32 devices in a mesh: groups: 2 (over y), fsdp: 4 (over z), dp: 4 (over x, core).
Axes of the slice: x: 2, y: 2, z: 4, core: 2. Of those that a mesh axis runs over, the one named last changes fastest.
Arguments:
- output_gradient: bfloat16 [6144, 4096], P(('groups', 'dp'), 'fsdp'), parts along dimension 0, may hold values from -6 to 6
- hidden: bfloat16 [6144, 16384], P(('groups', 'dp'), 'fsdp'), parts along dimension 0, may hold values from -6 to 6
- frozen_down_weight: bfloat16 [16384, 4096], P('fsdp', 'dp'), may hold values from -0.09375 to 0.09375
- adapter_first_factors: bfloat16 [64, 16384, 64], P(('groups', 'dp'), 'fsdp'), parts along dimension 0, may hold values from -0.046875 to 0.046875
- adapter_second_factors: bfloat16 [64, 64, 4096], P(('groups', 'dp'), None, 'fsdp'), parts along dimension 0, may hold values from -0.09375 to 0.09375
- island_live_rows: int32 [24], P(('groups', 'dp')), parts along dimension 0, may hold values from 33 to 256, as said below
- island_adapter_ids: int32 [24], P(('groups', 'dp')), parts along dimension 0, may hold values from 0 to 31
- owner_slot_adapters: int32 [64], P('groups'), parts along dimension 0, may hold values from 0 to 31, each once
Outputs:
- grad_hidden: bfloat16 [6144, 16384], P(('groups', 'dp'), 'fsdp'), parts along dimension 0
- grad_a: float32 [64, 16384, 64], P(('groups', 'dp'), 'fsdp'), parts along dimension 0
- grad_b: float32 [64, 64, 4096], P(('groups', 'dp'), None, 'fsdp'), parts along dimension 0
The draws below stay inside these ranges and needn't reach their ends.
There are 2 independent parts, one for each index of `groups`. The reference program is written for one: setup_inputs(seed, part) draws one part's arguments, and reference() takes and returns one part's arrays. A program takes and returns all parts, laid end to end along the dimension named above; an argument that names none is the same for every part. Nothing has to cross between parts.
Inputs may be any that keep to these rules, and one draw needn't show every extreme that they name: `island_live_rows`: at least one block in every draw has all 256 rows live. `owner_slot_adapters`: slot j belongs to index j // (32 / 4) of dp.
All inputs are finite; a program needn't handle non-finite values.
Results may differ from the reference program's by a relative error of at most 0.0029.
Values may be sent and summed in bfloat16 or wider, within the bound.
No kernel may reach another device: no remote copies, remote signals or barrier semaphores. Data moves between devices by JAX's collectives and lax.ppermute only.
A program may use at most 320 MiB of HBM per device.

```python
import math
import jax
import jax.numpy as jnp
import numpy as np
from jax import lax

MODEL_FEATURES = 4096
HIDDEN_UNITS = 16384
ADAPTER_RANK = 64
GROUP_ADAPTERS = 32
BLOCK = 256
BLOCKS = 12
ROWS = 3072


def draw_island_live_rows(key, part):
    key = jax.random.fold_in(key, 7)
    first, second = jax.random.split(key)
    live = jax.random.randint(first, (BLOCKS,), BLOCK // 8 + 1, BLOCK + 1)
    full = jax.random.randint(second, (), 0, BLOCKS)
    return jnp.where(jnp.arange(BLOCKS) == full, BLOCK, live).astype(jnp.int32)


def set_ends(result, key, low, top_value):
    place = [jax.random.randint(jax.random.fold_in(key, axis), (), 0, length) for axis, length in enumerate(result.shape)]
    longest = result.shape.index(max(result.shape))
    next_to = place[:longest] + [(place[longest] + 1) % result.shape[longest]] + place[longest + 1:]
    return result.at[tuple(place)].set(low).at[tuple(next_to)].set(top_value)


def steps_of(key, shape, cuts, smallest, high):
    def one(dim, shards_of):
        draws = jax.random.uniform(jax.random.fold_in(jax.random.fold_in(key, 6), dim), (shards_of,), jnp.float32, smallest / len(cuts), high / len(cuts))
        return jnp.repeat(jnp.exp(draws), shape[dim] // shards_of).reshape((-1,) + (1,) * (len(shape) - dim - 1))

    gain = one(*cuts[0])
    for cut in cuts[1:]:
        gain = gain * one(*cut)
    return gain


def cumulative_ranks(amount, lean):
    portions = [(1 << 20) // math.isqrt(standing ** lean) + 1 for standing in range(1, amount + 1)]
    scale = 1 + sum(portions) // (1 << 30)
    return np.cumsum(np.array([max(1, weight // scale) for weight in portions]))


def ranked(own_key, extent, amount, slope):
    listing = cumulative_ranks(amount, slope)
    lot = jax.random.randint(jax.random.fold_in(own_key, 1), extent, 0, int(listing[amount - 1]))
    standing = jnp.searchsorted(jnp.asarray(listing, jnp.int32), lot, side="right")
    return jax.random.permutation(jax.random.fold_in(own_key, 2), amount)[standing].astype(jnp.int32)


def centred(key, dims, width, most, cuts=(), kind=jnp.bfloat16):
    drawn = width * jax.random.normal(key, dims, jnp.float32)
    if cuts:
        drawn = drawn * steps_of(key, dims, cuts, -0.22, 0.18)
    return jnp.clip(drawn, -most, most).astype(kind)


def setup_inputs(seed: int = 0, part: int = 0) -> dict:
    key_list = jax.random.split(jax.random.key(seed), 9)
    part_splits = jax.random.split(jax.random.fold_in(key_list[8], part), 9)
    return {
        "output_gradient": centred(part_splits[0], (ROWS, MODEL_FEATURES), 1.0, 6.0, ((0, 4), (1, 4))),
        "hidden": centred(part_splits[1], (ROWS, HIDDEN_UNITS), 1.0, 6.0, ((0, 4), (1, 4))),
        "frozen_down_weight": centred(key_list[2], (HIDDEN_UNITS, MODEL_FEATURES), MODEL_FEATURES ** -0.5, 0.09375, ((0, 4), (1, 4))),
        "adapter_first_factors": centred(part_splits[3], (GROUP_ADAPTERS, HIDDEN_UNITS, ADAPTER_RANK), HIDDEN_UNITS ** -0.5, 0.046875, ((0, 4), (1, 4))),
        "adapter_second_factors": centred(part_splits[4], (GROUP_ADAPTERS, ADAPTER_RANK, MODEL_FEATURES), MODEL_FEATURES ** -0.5, 0.09375, ((0, 4), (2, 4))),
        "island_live_rows": draw_island_live_rows(jax.random.fold_in(jax.random.fold_in(key_list[8], part), 71), part),
        "island_adapter_ids": set_ends(ranked(part_splits[6], (BLOCKS,), GROUP_ADAPTERS, 2), jax.random.fold_in(part_splits[6], 3), 0, GROUP_ADAPTERS - 1).astype(jnp.int32),
        "owner_slot_adapters": jax.random.permutation(part_splits[7], GROUP_ADAPTERS).astype(jnp.int32),
    }


adapter_scale = 2.0
factor_gradient = 0.0625


def reference(output_gradient, hidden, frozen_down_weight, adapter_first_factors, adapter_second_factors, island_live_rows, island_adapter_ids, owner_slot_adapters):
    offset = jnp.arange(ROWS, dtype=jnp.int32) % BLOCK
    valid = offset < jnp.repeat(island_live_rows, BLOCK)
    kept = jnp.where(valid[:, None], output_gradient, jnp.zeros((), jnp.bfloat16))
    match = island_adapter_ids[:, None] == owner_slot_adapters[None, :]
    slots = jnp.sum(jnp.where(match, jnp.arange(GROUP_ADAPTERS, dtype=jnp.int32)[None, :], 0), axis=1).astype(jnp.int32)

    def one_block(items):
        hid_rows, row_gradients, owner_slot = items
        first_factor = lax.dynamic_index_in_dim(adapter_first_factors, owner_slot, 0, keepdims=False)
        second_factor = lax.dynamic_index_in_dim(adapter_second_factors, owner_slot, 0, keepdims=False)
        low = jnp.dot(hid_rows, first_factor, preferred_element_type=jnp.float32)
        coefficient = adapter_scale * lax.dot_general(row_gradients, second_factor, (((1,), (1,)), ((), ())), preferred_element_type=jnp.float32)
        reduced_second = low.astype(jnp.bfloat16)
        coef_b = coefficient.astype(jnp.bfloat16)
        base = lax.dot_general(row_gradients, frozen_down_weight, (((1,), (1,)), ((), ())), preferred_element_type=jnp.float32)
        extra = lax.dot_general(coef_b, first_factor, (((1,), (1,)), ((), ())), preferred_element_type=jnp.float32)
        grad_rows_h = (base + extra).astype(jnp.bfloat16)
        term_a = factor_gradient * jnp.dot(hid_rows.T, coef_b, preferred_element_type=jnp.float32)
        second_term = (factor_gradient * adapter_scale) * jnp.dot(reduced_second.T, row_gradients, preferred_element_type=jnp.float32)
        return grad_rows_h, term_a, second_term

    hid_blocks = hidden.reshape(BLOCKS, BLOCK, HIDDEN_UNITS)
    grad_blocks = kept.reshape(BLOCKS, BLOCK, MODEL_FEATURES)
    grad_hidden, terms_a, terms_b = lax.map(one_block, (hid_blocks, grad_blocks, slots))
    select = (jnp.arange(GROUP_ADAPTERS, dtype=jnp.int32)[:, None] == slots[None, :]).astype(jnp.float32)
    grad_a = jnp.einsum("jk,kfr->jfr", select, terms_a, precision=lax.Precision.HIGHEST)
    grad_b = jnp.einsum("jk,krd->jrd", select, terms_b, precision=lax.Precision.HIGHEST)
    return grad_hidden.reshape(ROWS, HIDDEN_UNITS), grad_a, grad_b
```

```python
import functools

import jax
import jax.numpy as jnp
from jax import lax
from jax.experimental import pallas as pl
from jax.experimental.pallas import tpu as pltpu
from jax.sharding import PartitionSpec as P

adapter_scale = 2.0
factor_gradient = 0.0625
vmem_bytes = 50 * 1024 * 1024
bf16, f32, i32 = jnp.bfloat16, jnp.float32, jnp.int32


def params(cost):
    return dict(
        compiler_params=pltpu.CompilerParams(vmem_limit_bytes=vmem_bytes),
        cost_estimate=pl.CostEstimate(flops=cost[0], bytes_accessed=cost[1], transcendentals=0),
    )


def pick_kernel(pieces, index_ref, source_ref, *refs):
    a_refs, b_refs, out_ref = refs[:pieces], refs[pieces : 2 * pieces], refs[-1]
    source = source_ref[pl.program_id(0)]
    a, b = a_refs[0][0], b_refs[0][0]
    for r in range(1, pieces):
        a = jnp.where(source == r, a_refs[r][0], a)
        b = jnp.where(source == r, b_refs[r][0], b)
    ff = a.shape[1]
    out_ref[0, :, :ff] = a
    out_ref[0, :, ff:] = b


def factor_specs(pieces, count, rank, width):
    return [
        pl.BlockSpec(
            (1, rank, width), lambda i, index, source, r=r: (index[r * count + i], 0, 0)
        )
        for r in range(pieces)
    ]


def pick(index, source, a_pieces, b_pieces):
    count, pieces = source.shape[0], len(a_pieces)
    _, rank, ff = a_pieces[0].shape
    d = b_pieces[0].shape[2]
    return pl.pallas_call(
        functools.partial(pick_kernel, pieces),
        grid_spec=pltpu.PrefetchScalarGridSpec(
            num_scalar_prefetch=2,
            grid=(count,),
            in_specs=factor_specs(pieces, count, rank, ff) + factor_specs(pieces, count, rank, d),
            out_specs=pl.BlockSpec((1, rank, ff + d), lambda i, index, source: (i, 0, 0)),
        ),
        out_shape=jax.ShapeDtypeStruct((count, rank, ff + d), bf16),
        **params((0, 2 * (pieces + 1) * count * rank * (ff + d))),
    )(index, source, *a_pieces, *b_pieces)


def project_kernel(pieces, index_ref, source_ref, *refs):
    a_refs, b_refs = refs[:pieces], refs[pieces : 2 * pieces]
    far_ref, hid_ref, grad_ref, part_ref, block_ref = refs[2 * pieces :]
    source = source_ref[pl.program_id(0)]
    ff = hid_ref.shape[1]
    a, b = far_ref[0, :, :ff], far_ref[0, :, ff:]
    for r in range(pieces):
        a = jnp.where(source == r, a_refs[r][0], a)
        b = jnp.where(source == r, b_refs[r][0], b)
    block_ref[0] = a
    over_last = (((1,), (1,)), ((), ()))
    rank = a.shape[0]
    part_ref[0, :, :rank] = lax.dot_general(
        hid_ref[...], a, over_last, preferred_element_type=f32
    )
    part_ref[0, :, rank:] = lax.dot_general(
        grad_ref[...], b, over_last, preferred_element_type=f32
    )


def project(index, source, a_pieces, b_pieces, far, hidden, grad):
    count, pieces = source.shape[0], len(a_pieces)
    _, rank, ff = a_pieces[0].shape
    d = b_pieces[0].shape[2]
    rows = hidden.shape[0]
    height = rows // count
    own = lambda i, index, source: (i, 0)
    own3 = lambda i, index, source: (i, 0, 0)
    return pl.pallas_call(
        functools.partial(project_kernel, pieces),
        grid_spec=pltpu.PrefetchScalarGridSpec(
            num_scalar_prefetch=2,
            grid=(count,),
            in_specs=factor_specs(pieces, count, rank, ff)
            + factor_specs(pieces, count, rank, d)
            + [
                pl.BlockSpec((1, rank, ff + d), own3),
                pl.BlockSpec((height, ff), own),
                pl.BlockSpec((height, d), own),
            ],
            out_specs=[
                pl.BlockSpec((1, height, 2 * rank), own3),
                pl.BlockSpec((1, rank, ff), own3),
            ],
        ),
        out_shape=[
            jax.ShapeDtypeStruct((count, height, 2 * rank), f32),
            jax.ShapeDtypeStruct((count, rank, ff), bf16),
        ],
        **params((2 * rows * rank * (ff + d), 2 * (rows + (pieces + 2) * count * rank) * (ff + d))),
    )(index, source, *a_pieces, *b_pieces, far, hidden, grad)


def terms_kernel(live_ref, here_ref, there_ref, hid_ref, grad_ref, terms_ref, coef_ref):
    ff = hid_ref.shape[1]
    rank = coef_ref.shape[2]
    total = here_ref[0] + there_ref[0]
    valid = lax.broadcasted_iota(i32, total.shape, 0) < live_ref[pl.program_id(0)]
    total = jnp.where(valid, total, 0.0)
    low = total[:, :rank].astype(bf16)
    coef = (adapter_scale * total[:, rank:]).astype(bf16)
    coef_ref[0] = coef
    over_rows = (((0,), (0,)), ((), ()))
    terms_ref[0, :, :ff] = (
        factor_gradient
        * lax.dot_general(coef, hid_ref[...], over_rows, preferred_element_type=f32)
    ).astype(bf16)
    terms_ref[0, :, ff:] = (
        factor_gradient
        * adapter_scale
        * lax.dot_general(low, grad_ref[...], over_rows, preferred_element_type=f32)
    ).astype(bf16)


def block_terms(live, here, there, hidden, grad):
    count, height, both = here.shape
    rank = both // 2
    rows, ff = hidden.shape
    d = grad.shape[1]
    own = lambda i, live: (i, 0)
    own3 = lambda i, live: (i, 0, 0)
    return pl.pallas_call(
        terms_kernel,
        grid_spec=pltpu.PrefetchScalarGridSpec(
            num_scalar_prefetch=1,
            grid=(count,),
            in_specs=[
                pl.BlockSpec((1, height, both), own3),
                pl.BlockSpec((1, height, both), own3),
                pl.BlockSpec((height, ff), own),
                pl.BlockSpec((height, d), own),
            ],
            out_specs=[
                pl.BlockSpec((1, rank, ff + d), own3),
                pl.BlockSpec((1, height, rank), own3),
            ],
        ),
        out_shape=[
            jax.ShapeDtypeStruct((count, rank, ff + d), bf16),
            jax.ShapeDtypeStruct((count, height, rank), bf16),
        ],
        **params((2 * rows * rank * (ff + d), 2 * (rows + count * rank) * (ff + d))),
    )(live, here, there, hidden, grad)


def base_kernel(pieces, count, scalars_ref, kept_ref, *refs):
    w_refs = refs[:pieces]
    coef_ref, block_ref = refs[pieces : pieces + 2]
    out_ref = refs[-1]
    deep = w_refs[0].shape[1]
    height = coef_ref.shape[1]
    total = None
    for r in range(pieces):
        start = pl.multiple_of(scalars_ref[1 + r] * deep, deep)
        part = lax.dot_general(
            kept_ref[:, pl.ds(start, deep)],
            w_refs[r][...],
            (((1,), (1,)), ((), ())),
            preferred_element_type=f32,
        )
        total = part if total is None else total + part
    for b in range(count):
        extra = jnp.dot(coef_ref[b], block_ref[b], preferred_element_type=f32)
        here = total[b * height : (b + 1) * height] + extra
        valid = lax.broadcasted_iota(i32, here.shape, 0) < scalars_ref[1 + pieces + b]
        out_ref[b * height : (b + 1) * height, :] = jnp.where(valid, here, 0.0).astype(bf16)


def base(scalars, kept, whole, chunk, coef, block_a, held, size, tile):
    rows, depth = kept.shape
    count, rank, ff = block_a.shape
    pieces = len(whole) + len(chunk)
    deep = depth // pieces
    height = rows // count
    once2 = lambda i, s: (0, 0)
    placed = lambda i, s: (s[0] + i, 0)
    in_specs = [pl.BlockSpec((rows, depth), once2)]
    operands = [kept]
    for r in range(pieces):
        if r in whole:
            in_specs.append(pl.BlockSpec((tile, deep), placed))
            operands.append(whole[r])
        else:
            in_specs.append(pl.BlockSpec((tile, deep), lambda i, s: (i, 0)))
            operands.append(chunk[r])
    in_specs += [
        pl.BlockSpec((count, height, rank), lambda i, s: (0, 0, 0)),
        pl.BlockSpec((count, rank, tile), lambda i, s: (0, 0, s[0] + i)),
    ]
    operands += [coef, block_a]
    aliases = {}
    if held is not None:
        in_specs.append(pl.BlockSpec(memory_space=pl.ANY))
        operands.append(held)
        aliases = {len(operands): 0}
    return pl.pallas_call(
        functools.partial(base_kernel, pieces, count),
        grid_spec=pltpu.PrefetchScalarGridSpec(
            num_scalar_prefetch=1,
            grid=(size // tile,),
            in_specs=in_specs,
            out_specs=pl.BlockSpec((rows, tile), lambda i, s: (0, s[0] + i)),
        ),
        out_shape=jax.ShapeDtypeStruct((rows, ff), bf16),
        input_output_aliases=aliases,
        **params((2 * rows * depth * size, 2 * (rows * depth + (rows + depth) * size))),
    )(scalars, *operands)


def merge_kernel(pieces, count, tiles, slots_ref, *refs):
    term_refs, (a_ref, b_ref) = refs[:pieces], refs[pieces:]
    step = pl.program_id(0)

    def put(out_ref):
        out_ref[...] = jnp.zeros_like(out_ref)
        for r in range(pieces):
            for k in range(count):
                slot = slots_ref[r * count + k]

                @pl.when((slot >= 0) & (slot < out_ref.shape[0]))
                def _():
                    out_ref[slot] += term_refs[r][k].astype(f32)

    pl.when(step < tiles)(lambda: put(a_ref))
    pl.when(step >= tiles)(lambda: put(b_ref))


def merge(slots, pieces, local, ff, tile):
    count, rank, both = pieces[0].shape
    tiles = ff // tile
    d = both - ff
    return pl.pallas_call(
        functools.partial(merge_kernel, len(pieces), count, tiles),
        grid_spec=pltpu.PrefetchScalarGridSpec(
            num_scalar_prefetch=1,
            grid=(both // tile,),
            in_specs=[pl.BlockSpec((count, rank, tile), lambda i, s: (0, 0, i))] * len(pieces),
            out_specs=[
                pl.BlockSpec((local, rank, tile), lambda i, s: (0, 0, jnp.minimum(i, tiles - 1))),
                pl.BlockSpec((local, rank, tile), lambda i, s: (0, 0, jnp.maximum(i - tiles, 0))),
            ],
        ),
        out_shape=[
            jax.ShapeDtypeStruct((local, rank, ff), f32),
            jax.ShapeDtypeStruct((local, rank, d), f32),
        ],
        **params((0, both * rank * (2 * len(pieces) * count + 4 * local))),
    )(slots, *pieces)


def on_device(
    n_groups,
    n_fsdp,
    n_dp,
    output_gradient,
    hidden,
    frozen_down_weight,
    adapter_first_factors,
    adapter_second_factors,
    island_live_rows,
    island_adapter_ids,
    owner_slot_adapters,
):
    rows, ff = hidden.shape
    d = output_gradient.shape[1]
    count = island_live_rows.shape[0]
    local = adapter_first_factors.shape[0]
    n_slots = owner_slot_adapters.shape[0]
    top = n_dp // 2
    me = lax.axis_index("dp")
    group = lax.axis_index("groups")

    def swap(value, bit, axis="dp", size=n_dp):
        return lax.ppermute(value, axis, [(i, i ^ bit) for i in range(size)])

    def spread(held):
        held = dict(held)
        bit = top // 2
        while bit:
            for r in list(held):
                held[r ^ bit] = swap(held[r], bit)
            bit //= 2
        return held

    match = island_adapter_ids[:, None] == owner_slot_adapters[None, :]
    slots = jnp.sum(jnp.where(match, jnp.arange(n_slots, dtype=i32)[None, :], 0), axis=1)
    far_slots = swap(slots, top)

    kept = lax.all_gather(output_gradient, "fsdp", axis=1, tiled=True)

    first = jnp.swapaxes(adapter_first_factors, 1, 2)
    a_near = spread({0: first})
    b_near = spread({0: adapter_second_factors})
    near = sorted(a_near)
    a_near = [a_near[r] for r in near]
    b_near = [b_near[r] for r in near]

    def places(wanted):
        owner = wanted // local
        index = jnp.concatenate([wanted % local] * len(near))
        return index, jnp.where((owner ^ me) < top, owner ^ me, len(near))

    far = swap(pick(*places(far_slots), a_near, b_near), top)

    share = ff // n_groups
    size = max(min(share, 256), share // 4)
    tile = min(512, size)
    shares = []
    for j in range(share // size):
        shares.append(
            swap(
                lax.dynamic_slice_in_dim(
                    frozen_down_weight, group * share + j * size, size, axis=0
                ),
                top,
            )
        )
    whole = spread({0: frozen_down_weight})

    part, block_a = project(*places(slots), a_near, b_near, far, hidden, output_gradient)
    bit = 1
    total = None
    while bit < n_fsdp:
        total = part if total is None else total + other
        other = swap(total, bit, "fsdp", n_fsdp)
        bit *= 2
    terms, coef = block_terms(island_live_rows, total, other, hidden, output_gradient)
    far_terms = swap(terms, top)

    order = [me ^ r for r in range(n_dp)]
    grad_hidden = None
    for shift in range(n_groups):
        for j, piece in enumerate(shares):
            if shift:
                piece = lax.ppermute(
                    piece, "groups", [(i, (i + shift) % n_groups) for i in range(n_groups)]
                )
            start = lax.rem(group + n_groups - shift, n_groups) * share + j * size
            scalars = jnp.stack([start // tile] + order).astype(i32)
            grad_hidden = base(
                jnp.concatenate([scalars, island_live_rows]),
                kept,
                whole,
                spread({top: piece}),
                coef,
                block_a,
                grad_hidden,
                size,
                tile,
            )

    all_slots = spread({0: slots, top: far_slots})
    all_terms = spread({0: terms, top: far_terms})
    keys = sorted(all_terms)
    relative = jnp.concatenate([all_slots[r] for r in keys]) - me * local
    grad_a, grad_b = merge(relative, [all_terms[r] for r in keys], local, ff, min(d, 512))
    return grad_hidden, jnp.swapaxes(grad_a, 1, 2), grad_b


def solution(mesh):
    placed = (
        P(("groups", "dp"), "fsdp"),
        P(("groups", "dp"), "fsdp"),
        P("fsdp", "dp"),
        P(("groups", "dp"), "fsdp", None),
        P(("groups", "dp"), None, "fsdp"),
        P(("groups", "dp")),
        P(("groups", "dp")),
        P("groups"),
    )
    sizes = [mesh.shape[name] for name in ("groups", "fsdp", "dp")]
    return jax.shard_map(
        functools.partial(on_device, *sizes),
        mesh=mesh,
        in_specs=placed,
        out_specs=(
            P(("groups", "dp"), "fsdp"),
            P(("groups", "dp"), "fsdp", None),
            P(("groups", "dp"), None, "fsdp"),
        ),
        check_vma=False,
    )
```

```python
import functools

import jax
import jax.numpy as jnp
from jax import lax
from jax.experimental import pallas as pl
from jax.experimental.pallas import tpu as pltpu
from jax.sharding import PartitionSpec as P

adapter_scale = 2.0
factor_gradient = 0.0625
vmem_bytes = 60 * 1024 * 1024
bf16, f32, i32 = jnp.bfloat16, jnp.float32, jnp.int32


def behind(value, *after):
    if not after:
        return value
    return lax.optimization_barrier((value, *after))[0]


def params(cost):
    return dict(
        compiler_params=pltpu.CompilerParams(vmem_limit_bytes=vmem_bytes),
        cost_estimate=pl.CostEstimate(flops=cost[0], bytes_accessed=cost[1], transcendentals=0),
    )


def pick_kernel(pieces, index_ref, source_ref, *refs):
    a_refs, b_refs, out_ref = refs[:pieces], refs[pieces : 2 * pieces], refs[-1]
    source = source_ref[pl.program_id(0)]
    a, b = a_refs[0][0], b_refs[0][0]
    for r in range(1, pieces):
        a = jnp.where(source == r, a_refs[r][0], a)
        b = jnp.where(source == r, b_refs[r][0], b)
    ff = a.shape[1]
    out_ref[0, :, :ff] = a
    out_ref[0, :, ff:] = b


def factor_specs(pieces, count, rank, width):
    return [
        pl.BlockSpec(
            (1, rank, width), lambda i, index, source, r=r: (index[r * count + i], 0, 0)
        )
        for r in range(pieces)
    ]


def pick(index, source, a_pieces, b_pieces):
    count, pieces = source.shape[0], len(a_pieces)
    _, rank, ff = a_pieces[0].shape
    d = b_pieces[0].shape[2]
    return pl.pallas_call(
        functools.partial(pick_kernel, pieces),
        grid_spec=pltpu.PrefetchScalarGridSpec(
            num_scalar_prefetch=2,
            grid=(count,),
            in_specs=factor_specs(pieces, count, rank, ff) + factor_specs(pieces, count, rank, d),
            out_specs=pl.BlockSpec((1, rank, ff + d), lambda i, index, source: (i, 0, 0)),
        ),
        out_shape=jax.ShapeDtypeStruct((count, rank, ff + d), bf16),
        **params((0, 2 * (pieces + 1) * count * rank * (ff + d))),
    )(index, source, *a_pieces, *b_pieces)


def project_kernel(pieces, index_ref, source_ref, *refs):
    a_refs, b_refs = refs[:pieces], refs[pieces : 2 * pieces]
    far_ref, hid_ref, grad_ref, part_ref, block_ref = refs[2 * pieces :]
    source = source_ref[pl.program_id(0)]
    ff = hid_ref.shape[1]
    a, b = far_ref[0, :, :ff], far_ref[0, :, ff:]
    for r in range(pieces):
        a = jnp.where(source == r, a_refs[r][0], a)
        b = jnp.where(source == r, b_refs[r][0], b)
    block_ref[0] = a
    over_last = (((1,), (1,)), ((), ()))
    rank = a.shape[0]
    part_ref[0, :, :rank] = lax.dot_general(
        hid_ref[...], a, over_last, preferred_element_type=f32
    )
    part_ref[0, :, rank:] = lax.dot_general(
        grad_ref[...], b, over_last, preferred_element_type=f32
    )


def project(index, source, a_pieces, b_pieces, far, hidden, grad):
    count, pieces = source.shape[0], len(a_pieces)
    _, rank, ff = a_pieces[0].shape
    d = b_pieces[0].shape[2]
    rows = hidden.shape[0]
    height = rows // count
    own = lambda i, index, source: (i, 0)
    own3 = lambda i, index, source: (i, 0, 0)
    return pl.pallas_call(
        functools.partial(project_kernel, pieces),
        grid_spec=pltpu.PrefetchScalarGridSpec(
            num_scalar_prefetch=2,
            grid=(count,),
            in_specs=factor_specs(pieces, count, rank, ff)
            + factor_specs(pieces, count, rank, d)
            + [
                pl.BlockSpec((1, rank, ff + d), own3),
                pl.BlockSpec((height, ff), own),
                pl.BlockSpec((height, d), own),
            ],
            out_specs=[
                pl.BlockSpec((1, height, 2 * rank), own3),
                pl.BlockSpec((1, rank, ff), own3),
            ],
        ),
        out_shape=[
            jax.ShapeDtypeStruct((count, height, 2 * rank), f32),
            jax.ShapeDtypeStruct((count, rank, ff), bf16),
        ],
        **params((2 * rows * rank * (ff + d), 2 * (rows + (pieces + 2) * count * rank) * (ff + d))),
    )(index, source, *a_pieces, *b_pieces, far, hidden, grad)


def terms_kernel(live_ref, here_ref, there_ref, hid_ref, grad_ref, terms_ref, coef_ref):
    ff = hid_ref.shape[1]
    rank = coef_ref.shape[2]
    total = here_ref[0] + there_ref[0]
    valid = lax.broadcasted_iota(i32, total.shape, 0) < live_ref[pl.program_id(0)]
    total = jnp.where(valid, total, 0.0)
    low = total[:, :rank].astype(bf16)
    coef = (adapter_scale * total[:, rank:]).astype(bf16)
    coef_ref[0] = coef
    over_rows = (((0,), (0,)), ((), ()))
    terms_ref[0, :, :ff] = (
        factor_gradient
        * lax.dot_general(coef, hid_ref[...], over_rows, preferred_element_type=f32)
    ).astype(bf16)
    terms_ref[0, :, ff:] = (
        factor_gradient
        * adapter_scale
        * lax.dot_general(low, grad_ref[...], over_rows, preferred_element_type=f32)
    ).astype(bf16)


def block_terms(live, here, there, hidden, grad):
    count, height, both = here.shape
    rank = both // 2
    rows, ff = hidden.shape
    d = grad.shape[1]
    own = lambda i, live: (i, 0)
    own3 = lambda i, live: (i, 0, 0)
    return pl.pallas_call(
        terms_kernel,
        grid_spec=pltpu.PrefetchScalarGridSpec(
            num_scalar_prefetch=1,
            grid=(count,),
            in_specs=[
                pl.BlockSpec((1, height, both), own3),
                pl.BlockSpec((1, height, both), own3),
                pl.BlockSpec((height, ff), own),
                pl.BlockSpec((height, d), own),
            ],
            out_specs=[
                pl.BlockSpec((1, rank, ff + d), own3),
                pl.BlockSpec((1, height, rank), own3),
            ],
        ),
        out_shape=[
            jax.ShapeDtypeStruct((count, rank, ff + d), bf16),
            jax.ShapeDtypeStruct((count, height, rank), bf16),
        ],
        **params((2 * rows * rank * (ff + d), 2 * (rows + count * rank) * (ff + d))),
    )(live, here, there, hidden, grad)


def base_kernel(near, bounds, count, scalars_ref, kept_ref, *refs):
    near_refs = refs[:near]
    coef_ref, block_ref = refs[near * len(bounds) : near * len(bounds) + 2]
    out_ref = refs[-1]
    deep = near_refs[0].shape[1]
    height = coef_ref.shape[1]
    step = pl.program_id(0)

    def part(r, w_ref):
        start = pl.multiple_of(scalars_ref[1 + r] * deep, deep)
        return lax.dot_general(
            kept_ref[:, pl.ds(start, deep)],
            w_ref[...],
            (((1,), (1,)), ((), ())),
            preferred_element_type=f32,
        )

    def whole_sum(far_refs):
        total = part(0, near_refs[0])
        for r in range(1, near):
            total += part(r, near_refs[r])
        for r in range(near):
            total += part(near + r, far_refs[r])
        for b in range(count):
            extra = jnp.dot(coef_ref[b], block_ref[b], preferred_element_type=f32)
            here = total[b * height : (b + 1) * height] + extra
            valid = lax.broadcasted_iota(i32, here.shape, 0) < scalars_ref[1 + 2 * near + b]
            out_ref[b * height : (b + 1) * height, :] = jnp.where(valid, here, 0.0).astype(bf16)

    for j in range(len(bounds) - 1):
        far_refs = refs[near * (j + 1) : near * (j + 2)]
        pl.when((step >= bounds[j]) & (step < bounds[j + 1]))(
            functools.partial(whole_sum, far_refs)
        )


def base(scalars, kept, near, chunks, coef, block_a, held, tile):
    rows, depth = kept.shape
    count, rank, ff = block_a.shape
    top = len(near)
    deep = depth // (2 * top)
    height = rows // count
    bounds = [0]
    in_specs = [pl.BlockSpec((rows, depth), lambda i, s: (0, 0))]
    in_specs += [pl.BlockSpec((tile, deep), lambda i, s: (s[0] + i, 0))] * top
    operands = [kept] + [near[r] for r in range(top)]
    for chunk in chunks:
        low = bounds[-1]
        last = chunk[top].shape[0] // tile - 1
        bounds.append(low + last + 1)
        place = lambda i, s, low=low, last=last: (jnp.clip(i - low, 0, last), 0)
        in_specs += [pl.BlockSpec((tile, deep), place)] * top
        operands += [chunk[r] for r in range(top, 2 * top)]
    in_specs += [
        pl.BlockSpec((count, height, rank), lambda i, s: (0, 0, 0)),
        pl.BlockSpec((count, rank, tile), lambda i, s: (0, 0, s[0] + i)),
    ]
    operands += [coef, block_a]
    aliases = {}
    if held is not None:
        in_specs.append(pl.BlockSpec(memory_space=pl.ANY))
        operands.append(held)
        aliases = {len(operands): 0}
    span = bounds[-1] * tile
    return pl.pallas_call(
        functools.partial(base_kernel, top, bounds, count),
        grid_spec=pltpu.PrefetchScalarGridSpec(
            num_scalar_prefetch=1,
            grid=(bounds[-1],),
            in_specs=in_specs,
            out_specs=pl.BlockSpec((rows, tile), lambda i, s: (0, s[0] + i)),
        ),
        out_shape=jax.ShapeDtypeStruct((rows, ff), bf16),
        input_output_aliases=aliases,
        **params((2 * rows * depth * span, 2 * (rows * depth + (rows + depth) * span))),
    )(scalars, *operands)


def merge_kernel(pieces, count, tiles, slots_ref, *refs):
    term_refs, (a_ref, b_ref) = refs[:pieces], refs[pieces:]
    step = pl.program_id(0)

    def put(out_ref):
        out_ref[...] = jnp.zeros_like(out_ref)
        for r in range(pieces):
            for k in range(count):
                slot = slots_ref[r * count + k]

                @pl.when((slot >= 0) & (slot < out_ref.shape[0]))
                def _():
                    out_ref[slot] += term_refs[r][k].astype(f32)

    pl.when(step < tiles)(lambda: put(a_ref))
    pl.when(step >= tiles)(lambda: put(b_ref))


def merge(slots, pieces, local, ff, tile):
    count, rank, both = pieces[0].shape
    tiles = ff // tile
    d = both - ff
    return pl.pallas_call(
        functools.partial(merge_kernel, len(pieces), count, tiles),
        grid_spec=pltpu.PrefetchScalarGridSpec(
            num_scalar_prefetch=1,
            grid=(both // tile,),
            in_specs=[pl.BlockSpec((count, rank, tile), lambda i, s: (0, 0, i))] * len(pieces),
            out_specs=[
                pl.BlockSpec((local, rank, tile), lambda i, s: (0, 0, jnp.minimum(i, tiles - 1))),
                pl.BlockSpec((local, rank, tile), lambda i, s: (0, 0, jnp.maximum(i - tiles, 0))),
            ],
        ),
        out_shape=[
            jax.ShapeDtypeStruct((local, rank, ff), f32),
            jax.ShapeDtypeStruct((local, rank, d), f32),
        ],
        **params((0, both * rank * (2 * len(pieces) * count + 4 * local))),
    )(slots, *pieces)


def on_device(
    n_groups,
    n_fsdp,
    n_dp,
    output_gradient,
    hidden,
    frozen_down_weight,
    adapter_first_factors,
    adapter_second_factors,
    island_live_rows,
    island_adapter_ids,
    owner_slot_adapters,
):
    rows, ff = hidden.shape
    d = output_gradient.shape[1]
    count = island_live_rows.shape[0]
    local = adapter_first_factors.shape[0]
    n_slots = owner_slot_adapters.shape[0]
    top = n_dp // 2
    me = lax.axis_index("dp")
    group = lax.axis_index("groups")

    def swap(value, bit, axis="dp", size=n_dp):
        return lax.ppermute(value, axis, [(i, i ^ bit) for i in range(size)])

    def spread(held):
        held = dict(held)
        bit = top // 2
        while bit:
            for r in list(held):
                held[r ^ bit] = swap(held[r], bit)
            bit //= 2
        return held

    match = island_adapter_ids[:, None] == owner_slot_adapters[None, :]
    slots = jnp.sum(jnp.where(match, jnp.arange(n_slots, dtype=i32)[None, :], 0), axis=1)
    far_slots = swap(slots, top)

    kept = lax.all_gather(output_gradient, "fsdp", axis=1, tiled=True)

    share = ff // n_groups
    unit = share // 8 if share % 2048 == 0 else share
    sizes = [unit, 2 * unit, 2 * unit, 2 * unit, unit] if unit < share else [share]
    tile = min(256, unit)
    starts = [sum(sizes[:j]) for j in range(len(sizes))]
    crossed, turned = [], []

    def cross(*after):
        j = len(crossed)
        if j == len(sizes):
            return
        piece = lax.dynamic_slice_in_dim(
            frozen_down_weight, group * share + starts[j], sizes[j], axis=0
        )
        crossed.append(swap(behind(piece, *after), top))

    def turn(*after):
        j = len(turned)
        if j == len(sizes):
            return
        turned.append(
            [
                lax.ppermute(
                    behind(crossed[j], *after),
                    "groups",
                    [(i, (i + shift) % n_groups) for i in range(n_groups)],
                )
                for shift in range(1, n_groups)
            ]
        )

    cross()

    first = jnp.swapaxes(adapter_first_factors, 1, 2)
    a_near = spread({0: first})
    b_near = spread({0: adapter_second_factors})
    near = sorted(a_near)
    a_near = [a_near[r] for r in near]
    b_near = [b_near[r] for r in near]
    whole = spread({0: frozen_down_weight})

    def places(wanted):
        owner = wanted // local
        index = jnp.concatenate([wanted % local] * len(near))
        return index, jnp.where((owner ^ me) < top, owner ^ me, len(near))

    far = swap(pick(*places(behind(far_slots, *crossed)), a_near, b_near), top)
    both_slots = spread({0: jnp.concatenate([slots, far_slots])})
    cross(far)
    turn()

    ready = behind(slots, *whole.values(), *turned[0], *both_slots.values())
    part, block_a = project(*places(ready), a_near, b_near, far, hidden, output_gradient)
    cross(part)
    turn(part)
    bit = 1
    total = None
    while bit < n_fsdp:
        total = part if total is None else total + other
        other = swap(total, bit, "fsdp", n_fsdp)
        bit *= 2
    cross(total, *crossed[:2])
    live = behind(island_live_rows, *crossed[:2], *sum(turned[:1], []))
    terms, coef = block_terms(live, total, other, hidden, output_gradient)
    far_terms = swap(terms, top)
    cross(terms, *crossed[:3])
    turn(total)
    turn(terms)
    turn(terms)

    order = [me ^ r for r in range(n_dp)]
    grad_hidden = None
    for shift in range(n_groups):
        pieces = [
            spread({top: turned[j][shift - 1] if shift else crossed[j]}) for j in range(len(sizes))
        ]
        start = lax.rem(group + n_groups - shift, n_groups) * share
        cuts = [0, len(sizes)] if shift == 0 or len(sizes) == 1 else [0, len(sizes) - 1, len(sizes)]
        for low, high in zip(cuts, cuts[1:]):
            scalars = jnp.stack([(start + starts[low]) // tile] + order).astype(i32)
            grad_hidden = base(
                jnp.concatenate([scalars, island_live_rows]),
                kept,
                whole,
                pieces[low:high],
                coef,
                block_a,
                grad_hidden,
                tile,
            )

    all_terms = spread({0: terms, top: far_terms})
    keys = sorted(all_terms)
    relative = [both_slots[r][:count] for r in near] + [both_slots[r][count:] for r in near]
    relative = jnp.concatenate(relative) - me * local
    grad_a, grad_b = merge(relative, [all_terms[r] for r in keys], local, ff, d)
    return grad_hidden, jnp.swapaxes(grad_a, 1, 2), grad_b


def solution(mesh):
    placed = (
        P(("groups", "dp"), "fsdp"),
        P(("groups", "dp"), "fsdp"),
        P("fsdp", "dp"),
        P(("groups", "dp"), "fsdp", None),
        P(("groups", "dp"), None, "fsdp"),
        P(("groups", "dp")),
        P(("groups", "dp")),
        P("groups"),
    )
    sizes = [mesh.shape[name] for name in ("groups", "fsdp", "dp")]
    return jax.shard_map(
        functools.partial(on_device, *sizes),
        mesh=mesh,
        in_specs=placed,
        out_specs=(
            P(("groups", "dp"), "fsdp"),
            P(("groups", "dp"), "fsdp", None),
            P(("groups", "dp"), None, "fsdp"),
        ),
        check_vma=False,
    )
```

```python
import functools

import jax
import jax.numpy as jnp
from jax import lax
from jax.experimental import pallas as pl
from jax.experimental.pallas import tpu as pltpu
from jax.sharding import PartitionSpec as P

adapter_scale = 2.0
factor_gradient = 0.0625
vmem_bytes = 60 * 1024 * 1024
bf16, f32, i32 = jnp.bfloat16, jnp.float32, jnp.int32


def behind(value, *after):
    if not after:
        return value
    return lax.optimization_barrier((value, *after))[0]


def params(cost):
    return dict(
        compiler_params=pltpu.CompilerParams(vmem_limit_bytes=vmem_bytes),
        cost_estimate=pl.CostEstimate(flops=cost[0], bytes_accessed=cost[1], transcendentals=0),
    )


def pick_kernel(pieces, index_ref, source_ref, *refs):
    a_refs, b_refs, out_ref = refs[:pieces], refs[pieces : 2 * pieces], refs[-1]
    source = source_ref[pl.program_id(0)]
    a, b = a_refs[0][0], b_refs[0][0]
    for r in range(1, pieces):
        a = jnp.where(source == r, a_refs[r][0], a)
        b = jnp.where(source == r, b_refs[r][0], b)
    ff = a.shape[1]
    out_ref[0, :, :ff] = a
    out_ref[0, :, ff:] = b


def factor_specs(pieces, count, rank, width):
    return [
        pl.BlockSpec(
            (1, rank, width), lambda i, index, source, r=r: (index[r * count + i], 0, 0)
        )
        for r in range(pieces)
    ]


def pick(index, source, a_pieces, b_pieces):
    count, pieces = source.shape[0], len(a_pieces)
    _, rank, ff = a_pieces[0].shape
    d = b_pieces[0].shape[2]
    return pl.pallas_call(
        functools.partial(pick_kernel, pieces),
        grid_spec=pltpu.PrefetchScalarGridSpec(
            num_scalar_prefetch=2,
            grid=(count,),
            in_specs=factor_specs(pieces, count, rank, ff) + factor_specs(pieces, count, rank, d),
            out_specs=pl.BlockSpec((1, rank, ff + d), lambda i, index, source: (i, 0, 0)),
        ),
        out_shape=jax.ShapeDtypeStruct((count, rank, ff + d), bf16),
        **params((0, 2 * (pieces + 1) * count * rank * (ff + d))),
    )(index, source, *a_pieces, *b_pieces)


def project_kernel(pieces, index_ref, source_ref, *refs):
    a_refs, b_refs = refs[:pieces], refs[pieces : 2 * pieces]
    far_ref, hid_ref, grad_ref, part_ref, block_ref = refs[2 * pieces :]
    source = source_ref[pl.program_id(0)]
    ff = hid_ref.shape[1]
    a, b = far_ref[0, :, :ff], far_ref[0, :, ff:]
    for r in range(pieces):
        a = jnp.where(source == r, a_refs[r][0], a)
        b = jnp.where(source == r, b_refs[r][0], b)
    block_ref[0] = a
    over_last = (((1,), (1,)), ((), ()))
    rank = a.shape[0]
    part_ref[0, :, :rank] = lax.dot_general(
        hid_ref[...], a, over_last, preferred_element_type=f32
    )
    part_ref[0, :, rank:] = lax.dot_general(
        grad_ref[...], b, over_last, preferred_element_type=f32
    )


def project(index, source, a_pieces, b_pieces, far, hidden, grad):
    count, pieces = source.shape[0], len(a_pieces)
    _, rank, ff = a_pieces[0].shape
    d = b_pieces[0].shape[2]
    rows = hidden.shape[0]
    height = rows // count
    own = lambda i, index, source: (i, 0)
    own3 = lambda i, index, source: (i, 0, 0)
    return pl.pallas_call(
        functools.partial(project_kernel, pieces),
        grid_spec=pltpu.PrefetchScalarGridSpec(
            num_scalar_prefetch=2,
            grid=(count,),
            in_specs=factor_specs(pieces, count, rank, ff)
            + factor_specs(pieces, count, rank, d)
            + [
                pl.BlockSpec((1, rank, ff + d), own3),
                pl.BlockSpec((height, ff), own),
                pl.BlockSpec((height, d), own),
            ],
            out_specs=[
                pl.BlockSpec((1, height, 2 * rank), own3),
                pl.BlockSpec((1, rank, ff), own3),
            ],
        ),
        out_shape=[
            jax.ShapeDtypeStruct((count, height, 2 * rank), f32),
            jax.ShapeDtypeStruct((count, rank, ff), bf16),
        ],
        **params((2 * rows * rank * (ff + d), 2 * (rows + (pieces + 2) * count * rank) * (ff + d))),
    )(index, source, *a_pieces, *b_pieces, far, hidden, grad)


def terms_kernel(live_ref, here_ref, there_ref, hid_ref, grad_ref, terms_ref, coef_ref):
    ff = hid_ref.shape[1]
    rank = coef_ref.shape[2]
    total = here_ref[0] + there_ref[0]
    valid = lax.broadcasted_iota(i32, total.shape, 0) < live_ref[pl.program_id(0)]
    total = jnp.where(valid, total, 0.0)
    low = total[:, :rank].astype(bf16)
    coef = (adapter_scale * total[:, rank:]).astype(bf16)
    coef_ref[0] = coef
    over_rows = (((0,), (0,)), ((), ()))
    terms_ref[0, :, :ff] = (
        factor_gradient
        * lax.dot_general(coef, hid_ref[...], over_rows, preferred_element_type=f32)
    ).astype(bf16)
    terms_ref[0, :, ff:] = (
        factor_gradient
        * adapter_scale
        * lax.dot_general(low, grad_ref[...], over_rows, preferred_element_type=f32)
    ).astype(bf16)


def block_terms(live, here, there, hidden, grad):
    count, height, both = here.shape
    rank = both // 2
    rows, ff = hidden.shape
    d = grad.shape[1]
    own = lambda i, live: (i, 0)
    own3 = lambda i, live: (i, 0, 0)
    return pl.pallas_call(
        terms_kernel,
        grid_spec=pltpu.PrefetchScalarGridSpec(
            num_scalar_prefetch=1,
            grid=(count,),
            in_specs=[
                pl.BlockSpec((1, height, both), own3),
                pl.BlockSpec((1, height, both), own3),
                pl.BlockSpec((height, ff), own),
                pl.BlockSpec((height, d), own),
            ],
            out_specs=[
                pl.BlockSpec((1, rank, ff + d), own3),
                pl.BlockSpec((1, height, rank), own3),
            ],
        ),
        out_shape=[
            jax.ShapeDtypeStruct((count, rank, ff + d), bf16),
            jax.ShapeDtypeStruct((count, height, rank), bf16),
        ],
        **params((2 * rows * rank * (ff + d), 2 * (rows + count * rank) * (ff + d))),
    )(live, here, there, hidden, grad)


def base_kernel(n_dp, tiles, count, scalars_ref, kept_ref, *refs):
    near = n_dp // 2
    near_refs = refs[:near]
    far_refs = refs[near : near + sum(tiles) * near]
    coef_ref, block_ref = refs[near + sum(tiles) * near : near + sum(tiles) * near + 2]
    out_ref, kept, weight, factor, result, kept_sem, in_sem, factor_sem, out_sem = refs[-9:]
    _, tile, depth = weight.shape
    deep = depth // n_dp
    height = coef_ref.shape[1]
    steps = len(tiles)

    def lanes(r):
        return pl.ds(pl.multiple_of(scalars_ref[steps + r] * deep, deep), deep)

    def span(j):
        return pl.ds(pl.multiple_of(scalars_ref[j] * tile, tile), tile)

    def loads(j, slot):
        copies = [
            pltpu.make_async_copy(
                near_refs[r].at[span(j), :], weight.at[slot, :, lanes(r)], in_sem.at[slot, r]
            )
            for r in range(near)
        ]
        first = sum(tiles[:j]) * near
        part = tile // tiles[j]
        for k in range(tiles[j]):
            for r in range(near):
                copies.append(
                    pltpu.make_async_copy(
                        far_refs[first + k * near + r],
                        weight.at[slot, pl.ds(k * part, part), lanes(near + r)],
                        in_sem.at[slot, (k + 1) * near + r],
                    )
                )
        copies.append(
            pltpu.make_async_copy(
                block_ref.at[:, :, span(j)], factor.at[slot], factor_sem.at[slot]
            )
        )
        return copies

    def store(j, slot):
        return pltpu.make_async_copy(
            result.at[slot], out_ref.at[:, span(j)], out_sem.at[slot]
        )

    whole = pltpu.make_async_copy(kept_ref, kept, kept_sem)
    whole.start()
    for copy in loads(0, 0):
        copy.start()
    whole.wait()

    @pl.loop(0, steps)
    def _(step):
        slot = lax.rem(step, 2)
        for j in range(steps):

            @pl.when(step == j)
            def _():
                if j + 1 < steps:
                    for copy in loads(j + 1, (j + 1) % 2):
                        copy.start()
                for copy in loads(j, j % 2):
                    copy.wait()
                if j >= 2:
                    store(j - 2, j % 2).wait()

        total = lax.dot_general(
            kept[...], weight[slot], (((1,), (1,)), ((), ())), preferred_element_type=f32
        )
        for b in range(count):
            extra = jnp.dot(coef_ref[b], factor[slot, b], preferred_element_type=f32)
            here = total[b * height : (b + 1) * height] + extra
            valid = lax.broadcasted_iota(i32, here.shape, 0) < scalars_ref[steps + n_dp + b]
            result[slot, b * height : (b + 1) * height, :] = jnp.where(valid, here, 0.0).astype(
                bf16
            )
        for j in range(steps):
            pl.when(step == j)(lambda j=j: store(j, j % 2).start())

    for j in range(max(steps - 2, 0), steps):
        store(j, j % 2).wait()


def base(places, scalars, kept, near, tiles, coef, block_a, held):
    rows, depth = kept.shape
    count, rank, ff = block_a.shape
    top = len(near)
    tile = sum(piece[top].shape[0] for piece in tiles[0])
    anywhere = pl.BlockSpec(memory_space=pl.ANY)
    operands = [kept] + [near[r] for r in range(top)]
    for pieces in tiles:
        for piece in pieces:
            operands += [piece[r] for r in range(top, 2 * top)]
    in_specs = [anywhere] * len(operands)
    in_specs += [pl.BlockSpec(coef.shape, lambda i, s: (0, 0, 0)), anywhere]
    operands += [coef, block_a]
    aliases = {}
    if held is not None:
        in_specs.append(anywhere)
        operands.append(held)
        aliases = {len(operands): 0}
    most = max(len(pieces) for pieces in tiles)
    span = tile * len(tiles)
    return pl.pallas_call(
        functools.partial(base_kernel, 2 * top, [len(pieces) for pieces in tiles], count),
        grid_spec=pltpu.PrefetchScalarGridSpec(
            num_scalar_prefetch=1,
            grid=(1,),
            in_specs=in_specs,
            out_specs=anywhere,
            scratch_shapes=[
                pltpu.VMEM((rows, depth), bf16),
                pltpu.VMEM((2, tile, depth), bf16),
                pltpu.VMEM((2, count, rank, tile), bf16),
                pltpu.VMEM((2, rows, tile), bf16),
                pltpu.SemaphoreType.DMA,
                pltpu.SemaphoreType.DMA((2, (1 + most) * top)),
                pltpu.SemaphoreType.DMA((2,)),
                pltpu.SemaphoreType.DMA((2,)),
            ],
        ),
        out_shape=jax.ShapeDtypeStruct((rows, ff), bf16),
        input_output_aliases=aliases,
        **params((2 * rows * depth * span, 2 * (rows * depth + (rows + depth) * span))),
    )(jnp.concatenate([jnp.stack(places).astype(i32), scalars]), *operands)


def merge_kernel(pieces, count, tiles, slots_ref, *refs):
    term_refs, (a_ref, b_ref) = refs[:pieces], refs[pieces:]
    step = pl.program_id(0)

    def put(out_ref):
        out_ref[...] = jnp.zeros_like(out_ref)
        for r in range(pieces):
            for k in range(count):
                slot = slots_ref[r * count + k]

                @pl.when((slot >= 0) & (slot < out_ref.shape[0]))
                def _():
                    out_ref[slot] += term_refs[r][k].astype(f32)

    pl.when(step < tiles)(lambda: put(a_ref))
    pl.when(step >= tiles)(lambda: put(b_ref))


def merge(slots, pieces, local, ff, tile):
    count, rank, both = pieces[0].shape
    tiles = ff // tile
    d = both - ff
    return pl.pallas_call(
        functools.partial(merge_kernel, len(pieces), count, tiles),
        grid_spec=pltpu.PrefetchScalarGridSpec(
            num_scalar_prefetch=1,
            grid=(both // tile,),
            in_specs=[pl.BlockSpec((count, rank, tile), lambda i, s: (0, 0, i))] * len(pieces),
            out_specs=[
                pl.BlockSpec((local, rank, tile), lambda i, s: (0, 0, jnp.minimum(i, tiles - 1))),
                pl.BlockSpec((local, rank, tile), lambda i, s: (0, 0, jnp.maximum(i - tiles, 0))),
            ],
        ),
        out_shape=[
            jax.ShapeDtypeStruct((local, rank, ff), f32),
            jax.ShapeDtypeStruct((local, rank, d), f32),
        ],
        **params((0, both * rank * (2 * len(pieces) * count + 4 * local))),
    )(slots, *pieces)


def add_kernel(pieces, count, slots_ref, *refs):
    term_refs = refs[:pieces]
    a_ref, b_ref, term, a, b, term_sem, a_sem, b_sem = refs[pieces + 2 :]
    ff = a.shape[1]
    for r in range(pieces):
        for k in range(count):
            slot = slots_ref[r * count + k]

            @pl.when((slot >= 0) & (slot < a_ref.shape[0]))
            def _():
                loads = [
                    pltpu.make_async_copy(term_refs[r].at[k], term, term_sem),
                    pltpu.make_async_copy(a_ref.at[slot], a, a_sem),
                    pltpu.make_async_copy(b_ref.at[slot], b, b_sem),
                ]
                for copy in loads:
                    copy.start()
                for copy in loads:
                    copy.wait()
                a[...] += term[:, :ff].astype(f32)
                b[...] += term[:, ff:].astype(f32)
                stores = [
                    pltpu.make_async_copy(a, a_ref.at[slot], a_sem),
                    pltpu.make_async_copy(b, b_ref.at[slot], b_sem),
                ]
                for copy in stores:
                    copy.start()
                for copy in stores:
                    copy.wait()


def add_far(slots, pieces, grad_a, grad_b):
    count, rank, both = pieces[0].shape
    ff, d = grad_a.shape[2], grad_b.shape[2]
    anywhere = pl.BlockSpec(memory_space=pl.ANY)
    n = len(pieces)
    return pl.pallas_call(
        functools.partial(add_kernel, n, count),
        grid_spec=pltpu.PrefetchScalarGridSpec(
            num_scalar_prefetch=1,
            grid=(1,),
            in_specs=[anywhere] * (n + 2),
            out_specs=[anywhere] * 2,
            scratch_shapes=[
                pltpu.VMEM((rank, both), bf16),
                pltpu.VMEM((rank, ff), f32),
                pltpu.VMEM((rank, d), f32),
                pltpu.SemaphoreType.DMA,
                pltpu.SemaphoreType.DMA,
                pltpu.SemaphoreType.DMA,
            ],
        ),
        out_shape=[
            jax.ShapeDtypeStruct(grad_a.shape, f32),
            jax.ShapeDtypeStruct(grad_b.shape, f32),
        ],
        input_output_aliases={n + 1: 0, n + 2: 1},
        **params((0, n * count * 10 * rank * both)),
    )(slots, *pieces, grad_a, grad_b)


def on_device(
    n_groups,
    n_fsdp,
    n_dp,
    output_gradient,
    hidden,
    frozen_down_weight,
    adapter_first_factors,
    adapter_second_factors,
    island_live_rows,
    island_adapter_ids,
    owner_slot_adapters,
):
    rows, ff = hidden.shape
    d = output_gradient.shape[1]
    count = island_live_rows.shape[0]
    local = adapter_first_factors.shape[0]
    n_slots = owner_slot_adapters.shape[0]
    top = n_dp // 2
    me = lax.axis_index("dp")
    group = lax.axis_index("groups")

    def swap(value, bit, axis="dp", size=n_dp):
        return lax.ppermute(value, axis, [(i, i ^ bit) for i in range(size)])

    def spread(held):
        held = dict(held)
        bit = top // 2
        while bit:
            for r in list(held):
                held[r ^ bit] = swap(held[r], bit)
            bit //= 2
        return held

    match = island_adapter_ids[:, None] == owner_slot_adapters[None, :]
    slots = jnp.sum(jnp.where(match, jnp.arange(n_slots, dtype=i32)[None, :], 0), axis=1)
    far_slots = swap(slots, top)

    kept = lax.all_gather(output_gradient, "fsdp", axis=1, tiled=True)

    share = ff // n_groups
    if share % 1024 == 0:
        tile = 512
        rest = [(k * tile, tile) for k in range(1, share // tile)]
        parts = [(0, tile // 2), *rest, (tile // 2, tile // 2)]
        groups = [[k] for k in range(1, share // tile)] + [[0, share // tile]]
    else:
        tile = share
        parts = [(0, share)]
        groups = [[0]]
    crossed = [None] * len(parts)
    turned = [[] for _ in parts]
    done = []

    def flat(*pieces):
        return [v for piece in pieces for v in piece.values()]

    def sends(j, *after):
        after = [*after, *done]
        done.clear()
        if j < len(parts):
            start, size = parts[j]
            piece = lax.dynamic_slice_in_dim(
                frozen_down_weight, group * share + start, size, axis=0
            )
            crossed[j] = {top: swap(behind(piece, *after), top)}
            done.extend(flat(crossed[j]))
        if 0 <= j - 1 < len(parts):
            piece = behind(crossed[j - 1][top], *after)
            for shift in range(1, n_groups):
                ring = [(i, (i + shift) % n_groups) for i in range(n_groups)]
                turned[j - 1].append({top: lax.ppermute(piece, "groups", ring)})
            crossed[j - 1] = spread({top: piece})
            done.extend(flat(*turned[j - 1], crossed[j - 1]))
        if 0 <= j - 2 < len(parts):
            turned[j - 2] = [spread({top: behind(p[top], *after)}) for p in turned[j - 2]]
            done.extend(flat(*turned[j - 2]))

    sends(0, far_slots)

    first = jnp.swapaxes(adapter_first_factors, 1, 2)
    a_near = spread({0: first})
    b_near = spread({0: adapter_second_factors})
    near = sorted(a_near)
    a_near = [a_near[r] for r in near]
    b_near = [b_near[r] for r in near]
    whole = spread({0: behind(frozen_down_weight, *a_near, *b_near)})

    def places(wanted):
        owner = wanted // local
        index = jnp.concatenate([wanted % local] * len(near))
        return index, jnp.where((owner ^ me) < top, owner ^ me, len(near))

    far = swap(pick(*places(behind(far_slots, *done)), a_near, b_near), top)
    both_slots = spread({0: jnp.concatenate([slots, far_slots])})
    sends(1, far)

    ready = behind(slots, *whole.values(), *both_slots.values())
    part, block_a = project(*places(ready), a_near, b_near, far, hidden, output_gradient)
    sends(2, part)
    bit = 1
    total = None
    while bit < n_fsdp:
        total = part if total is None else total + other
        other = swap(total, bit, "fsdp", n_fsdp)
        bit *= 2
    sends(3, total)
    terms, coef = block_terms(island_live_rows, total, other, hidden, output_gradient)
    far_terms = swap(behind(terms, *done), top)
    for j in range(4, len(parts) + 2):
        sends(j)
    near_terms = spread({0: terms})

    relative = [both_slots[r][:count] for r in near] + [both_slots[r][count:] for r in near]
    relative = jnp.concatenate(relative) - me * local
    edge = count * len(near)
    grad_a, grad_b = merge(relative[:edge], [near_terms[r] for r in near], local, ff, d)

    scalars = jnp.concatenate([jnp.stack([me ^ r for r in range(n_dp)]).astype(i32), island_live_rows])
    arrived = []
    for shift in range(n_groups):
        pieces = [turned[j][shift - 1] if shift else crossed[j] for j in range(len(parts))]
        start = lax.rem(group + n_groups - shift, n_groups) * share
        arrived.append(
            [((start + parts[g[0]][0]) // tile, [pieces[j] for j in g]) for g in groups]
        )
    if len(groups) > 1:
        calls = [tiles[:-1] for tiles in arrived] + [[tiles[-1] for tiles in arrived]]
    else:
        calls = arrived
    grad_hidden = None
    stages = [grad_a]
    for tiles in calls:
        where = [place for place, _ in tiles]
        pieces = [piece for _, piece in tiles]
        grad_hidden = base(where, scalars, kept, whole, pieces, coef, block_a, grad_hidden)
        stages.append(grad_hidden)

    far_terms = behind(far_terms, *stages[:3:2], *flat(*sum(turned, [])))
    all_far = spread({top: far_terms})
    grad_a, grad_b = add_far(
        relative[edge:], [all_far[r + top] for r in near], grad_a, grad_b
    )
    return grad_hidden, jnp.swapaxes(grad_a, 1, 2), grad_b


def solution(mesh):
    placed = (
        P(("groups", "dp"), "fsdp"),
        P(("groups", "dp"), "fsdp"),
        P("fsdp", "dp"),
        P(("groups", "dp"), "fsdp", None),
        P(("groups", "dp"), None, "fsdp"),
        P(("groups", "dp")),
        P(("groups", "dp")),
        P("groups"),
    )
    sizes = [mesh.shape[name] for name in ("groups", "fsdp", "dp")]
    return jax.shard_map(
        functools.partial(on_device, *sizes),
        mesh=mesh,
        in_specs=placed,
        out_specs=(
            P(("groups", "dp"), "fsdp"),
            P(("groups", "dp"), "fsdp", None),
            P(("groups", "dp"), None, "fsdp"),
        ),
        check_vma=False,
    )
```

```python
import functools

import jax
import jax.numpy as jnp
from jax import lax
from jax.experimental import pallas as pl
from jax.experimental.pallas import tpu as pltpu
from jax.sharding import PartitionSpec as P

adapter_scale = 2.0
factor_gradient = 0.0625
vmem_bytes = 60 * 1024 * 1024
bf16, f32, i32 = jnp.bfloat16, jnp.float32, jnp.int32


def behind(value, *after):
    if not after:
        return value
    return lax.optimization_barrier((value, *after))[0]


def params(cost):
    return dict(
        compiler_params=pltpu.CompilerParams(vmem_limit_bytes=vmem_bytes),
        cost_estimate=pl.CostEstimate(flops=cost[0], bytes_accessed=cost[1], transcendentals=0),
    )


def pick_kernel(pieces, index_ref, source_ref, *refs):
    a_refs, b_refs, out_ref = refs[:pieces], refs[pieces : 2 * pieces], refs[-1]
    source = source_ref[pl.program_id(0)]
    a, b = a_refs[0][0], b_refs[0][0]
    for r in range(1, pieces):
        a = jnp.where(source == r, a_refs[r][0], a)
        b = jnp.where(source == r, b_refs[r][0], b)
    ff = a.shape[1]
    out_ref[0, :, :ff] = a
    out_ref[0, :, ff:] = b


def factor_specs(pieces, count, rank, width):
    return [
        pl.BlockSpec(
            (1, rank, width), lambda i, index, source, r=r: (index[r * count + i], 0, 0)
        )
        for r in range(pieces)
    ]


def pick(index, source, a_pieces, b_pieces):
    count, pieces = source.shape[0], len(a_pieces)
    _, rank, ff = a_pieces[0].shape
    d = b_pieces[0].shape[2]
    return pl.pallas_call(
        functools.partial(pick_kernel, pieces),
        grid_spec=pltpu.PrefetchScalarGridSpec(
            num_scalar_prefetch=2,
            grid=(count,),
            in_specs=factor_specs(pieces, count, rank, ff) + factor_specs(pieces, count, rank, d),
            out_specs=pl.BlockSpec((1, rank, ff + d), lambda i, index, source: (i, 0, 0)),
        ),
        out_shape=jax.ShapeDtypeStruct((count, rank, ff + d), bf16),
        **params((0, 2 * (pieces + 1) * count * rank * (ff + d))),
    )(index, source, *a_pieces, *b_pieces)


def project_kernel(pieces, index_ref, source_ref, *refs):
    a_refs, b_refs = refs[:pieces], refs[pieces : 2 * pieces]
    far_ref, hid_ref, grad_ref, part_ref, block_ref, grad_a_ref, grad_b_ref = refs[
        2 * pieces : 2 * pieces + 7
    ]
    zeros, zero_sem = refs[2 * pieces + 7 :]
    step = pl.program_id(0)
    source = source_ref[step]
    ff = hid_ref.shape[1]
    d = grad_ref.shape[1]

    fills = []
    for slot in range(grad_a_ref.shape[0]):
        fills.append(pltpu.make_async_copy(zeros, grad_a_ref.at[slot], zero_sem.at[2 * slot]))
        fills.append(
            pltpu.make_async_copy(
                zeros.at[:, pl.ds(0, d)], grad_b_ref.at[slot], zero_sem.at[2 * slot + 1]
            )
        )

    @pl.when(step == 0)
    def _():
        zeros[...] = jnp.zeros_like(zeros)
        for fill in fills:
            fill.start()

    a, b = far_ref[0, :, :ff], far_ref[0, :, ff:]
    for r in range(pieces):
        a = jnp.where(source == r, a_refs[r][0], a)
        b = jnp.where(source == r, b_refs[r][0], b)
    block_ref[0] = a
    over_last = (((1,), (1,)), ((), ()))
    rank = a.shape[0]
    part_ref[0, :, :rank] = lax.dot_general(
        hid_ref[...], a, over_last, preferred_element_type=f32
    )
    part_ref[0, :, rank:] = lax.dot_general(
        grad_ref[...], b, over_last, preferred_element_type=f32
    )

    @pl.when(step == pl.num_programs(0) - 1)
    def _():
        for fill in fills:
            fill.wait()


def project(index, source, a_pieces, b_pieces, far, hidden, grad):
    count, pieces = source.shape[0], len(a_pieces)
    local, rank, ff = a_pieces[0].shape
    d = b_pieces[0].shape[2]
    rows = hidden.shape[0]
    height = rows // count
    own = lambda i, index, source: (i, 0)
    own3 = lambda i, index, source: (i, 0, 0)
    return pl.pallas_call(
        functools.partial(project_kernel, pieces),
        grid_spec=pltpu.PrefetchScalarGridSpec(
            num_scalar_prefetch=2,
            grid=(count,),
            in_specs=factor_specs(pieces, count, rank, ff)
            + factor_specs(pieces, count, rank, d)
            + [
                pl.BlockSpec((1, rank, ff + d), own3),
                pl.BlockSpec((height, ff), own),
                pl.BlockSpec((height, d), own),
            ],
            out_specs=[
                pl.BlockSpec((1, height, 2 * rank), own3),
                pl.BlockSpec((1, rank, ff), own3),
                pl.BlockSpec(memory_space=pl.ANY),
                pl.BlockSpec(memory_space=pl.ANY),
            ],
            scratch_shapes=[
                pltpu.VMEM((rank, ff), f32),
                pltpu.SemaphoreType.DMA((2 * local,)),
            ],
        ),
        out_shape=[
            jax.ShapeDtypeStruct((count, height, 2 * rank), f32),
            jax.ShapeDtypeStruct((count, rank, ff), bf16),
            jax.ShapeDtypeStruct((local, rank, ff), f32),
            jax.ShapeDtypeStruct((local, rank, d), f32),
        ],
        **params((2 * rows * rank * (ff + d), 2 * (rows + (pieces + 2) * count * rank) * (ff + d))),
    )(index, source, *a_pieces, *b_pieces, far, hidden, grad)


def terms_kernel(live_ref, here_ref, there_ref, hid_ref, grad_ref, terms_ref, coef_ref):
    ff = hid_ref.shape[1]
    rank = coef_ref.shape[2]
    total = here_ref[0] + there_ref[0]
    valid = lax.broadcasted_iota(i32, total.shape, 0) < live_ref[pl.program_id(0)]
    total = jnp.where(valid, total, 0.0)
    low = total[:, :rank].astype(bf16)
    coef = (adapter_scale * total[:, rank:]).astype(bf16)
    coef_ref[0] = coef
    over_rows = (((0,), (0,)), ((), ()))
    terms_ref[0, :, :ff] = (
        factor_gradient
        * lax.dot_general(coef, hid_ref[...], over_rows, preferred_element_type=f32)
    ).astype(bf16)
    terms_ref[0, :, ff:] = (
        factor_gradient
        * adapter_scale
        * lax.dot_general(low, grad_ref[...], over_rows, preferred_element_type=f32)
    ).astype(bf16)


def block_terms(live, here, there, hidden, grad):
    count, height, both = here.shape
    rank = both // 2
    rows, ff = hidden.shape
    d = grad.shape[1]
    own = lambda i, live: (i, 0)
    own3 = lambda i, live: (i, 0, 0)
    return pl.pallas_call(
        terms_kernel,
        grid_spec=pltpu.PrefetchScalarGridSpec(
            num_scalar_prefetch=1,
            grid=(count,),
            in_specs=[
                pl.BlockSpec((1, height, both), own3),
                pl.BlockSpec((1, height, both), own3),
                pl.BlockSpec((height, ff), own),
                pl.BlockSpec((height, d), own),
            ],
            out_specs=[
                pl.BlockSpec((1, rank, ff + d), own3),
                pl.BlockSpec((1, height, rank), own3),
            ],
        ),
        out_shape=[
            jax.ShapeDtypeStruct((count, rank, ff + d), bf16),
            jax.ShapeDtypeStruct((count, height, rank), bf16),
        ],
        **params((2 * rows * rank * (ff + d), 2 * (rows + count * rank) * (ff + d))),
    )(live, here, there, hidden, grad)


def base_kernel(n_dp, tiles, n_chunks, count, scalars_ref, kept_ref, *refs):
    near = n_dp // 2
    near_refs = refs[:near]
    far_refs = refs[near : near + n_chunks * near]
    coef_ref, block_ref = refs[near + n_chunks * near : near + n_chunks * near + 2]
    out_ref, kept, weight, factor, result, kept_sem, in_sem, factor_sem, out_sem = refs[-9:]
    _, tile, depth = weight.shape
    deep = depth // n_dp
    height = coef_ref.shape[1]
    steps = len(tiles)

    def lanes(r):
        return pl.ds(pl.multiple_of(scalars_ref[steps + r] * deep, deep), deep)

    def span(j):
        return pl.ds(pl.multiple_of(scalars_ref[j] * tile, tile), tile)

    def loads(j, slot, r):
        if r < near:
            return [
                pltpu.make_async_copy(
                    near_refs[r].at[span(j), :], weight.at[slot, :, lanes(r)], in_sem.at[slot, r, 0]
                )
            ]
        copies, low = [], 0
        for k, (chunk, start, size) in enumerate(tiles[j]):
            copies.append(
                pltpu.make_async_copy(
                    far_refs[chunk * near + r - near].at[pl.ds(start, size)],
                    weight.at[slot, pl.ds(low, size), lanes(r)],
                    in_sem.at[slot, r, k],
                )
            )
            low += size
        return copies

    def factors(j, slot):
        return pltpu.make_async_copy(
            block_ref.at[:, :, span(j)], factor.at[slot], factor_sem.at[slot]
        )

    def columns(r):
        return pltpu.make_async_copy(kept_ref.at[:, lanes(r)], kept.at[:, lanes(r)], kept_sem.at[r])

    def store(j, slot):
        return pltpu.make_async_copy(result.at[slot], out_ref.at[:, span(j)], out_sem.at[slot])

    def load(j, slot):
        for r in range(n_dp):
            for copy in loads(j, slot, r):
                copy.start()
        factors(j, slot).start()

    over_last = (((1,), (1,)), ((), ()))

    def finish(slot, total):
        for b in range(count):
            extra = jnp.dot(coef_ref[b], factor[slot, b], preferred_element_type=f32)
            here = total[b * height : (b + 1) * height] + extra
            valid = lax.broadcasted_iota(i32, here.shape, 0) < scalars_ref[steps + n_dp + b]
            result[slot, b * height : (b + 1) * height, :] = jnp.where(valid, here, 0.0).astype(
                bf16
            )

    for r in range(n_dp):
        columns(r).start()
        for copy in loads(0, 0, r):
            copy.start()
    factors(0, 0).start()
    if steps > 1:
        load(1, 1)
    total = None
    for r in range(n_dp):
        columns(r).wait()
        for copy in loads(0, 0, r):
            copy.wait()
        part = lax.dot_general(
            kept[:, lanes(r)], weight[0, :, lanes(r)], over_last, preferred_element_type=f32
        )
        total = part if total is None else total + part
    factors(0, 0).wait()
    finish(0, total)
    store(0, 0).start()

    @pl.loop(1, steps)
    def _(step):
        slot = lax.rem(step, 2)
        for j in range(1, steps):

            @pl.when(step == j)
            def _():
                if j + 1 < steps:
                    load(j + 1, (j + 1) % 2)
                for r in range(n_dp):
                    for copy in loads(j, j % 2, r):
                        copy.wait()
                factors(j, j % 2).wait()
                if j >= 2:
                    store(j - 2, j % 2).wait()

        finish(
            slot,
            lax.dot_general(kept[...], weight[slot], over_last, preferred_element_type=f32),
        )
        for j in range(1, steps):
            pl.when(step == j)(lambda j=j: store(j, j % 2).start())

    for j in range(max(steps - 2, 0), steps):
        store(j, j % 2).wait()


def base(places, scalars, kept, near, chunks, tiles, tile, coef, block_a, held):
    rows, depth = kept.shape
    count, rank, ff = block_a.shape
    top = len(near)
    anywhere = pl.BlockSpec(memory_space=pl.ANY)
    operands = [kept] + [near[r] for r in range(top)]
    for piece in chunks:
        operands += [piece[r] for r in range(top, 2 * top)]
    in_specs = [anywhere] * len(operands)
    in_specs += [pl.BlockSpec(coef.shape, lambda i, s: (0, 0, 0)), anywhere]
    operands += [coef, block_a]
    aliases = {}
    if held is not None:
        in_specs.append(anywhere)
        operands.append(held)
        aliases = {len(operands): 0}
    most = max(len(segments) for segments in tiles)
    span = tile * len(tiles)
    return pl.pallas_call(
        functools.partial(base_kernel, 2 * top, tiles, len(chunks), count),
        grid_spec=pltpu.PrefetchScalarGridSpec(
            num_scalar_prefetch=1,
            grid=(1,),
            in_specs=in_specs,
            out_specs=anywhere,
            scratch_shapes=[
                pltpu.VMEM((rows, depth), bf16),
                pltpu.VMEM((2, tile, depth), bf16),
                pltpu.VMEM((2, count, rank, tile), bf16),
                pltpu.VMEM((2, rows, tile), bf16),
                pltpu.SemaphoreType.DMA((2 * top,)),
                pltpu.SemaphoreType.DMA((2, 2 * top, most)),
                pltpu.SemaphoreType.DMA((2,)),
                pltpu.SemaphoreType.DMA((2,)),
            ],
        ),
        out_shape=jax.ShapeDtypeStruct((rows, ff), bf16),
        input_output_aliases=aliases,
        **params((2 * rows * depth * span, 2 * (rows * depth + (rows + depth) * span))),
    )(jnp.concatenate([jnp.stack(places).astype(i32), scalars]), *operands)


def add_kernel(pieces, count, slots_ref, *refs):
    term_refs = refs[:pieces]
    a_ref, b_ref, term, a, b, term_sem, a_sem, b_sem = refs[pieces + 2 :]
    ff = a.shape[1]
    for r in range(pieces):
        for k in range(count):
            slot = slots_ref[r * count + k]

            @pl.when((slot >= 0) & (slot < a_ref.shape[0]))
            def _():
                loads = [
                    pltpu.make_async_copy(term_refs[r].at[k], term, term_sem),
                    pltpu.make_async_copy(a_ref.at[slot], a, a_sem),
                    pltpu.make_async_copy(b_ref.at[slot], b, b_sem),
                ]
                for copy in loads:
                    copy.start()
                for copy in loads:
                    copy.wait()
                a[...] += term[:, :ff].astype(f32)
                b[...] += term[:, ff:].astype(f32)
                stores = [
                    pltpu.make_async_copy(a, a_ref.at[slot], a_sem),
                    pltpu.make_async_copy(b, b_ref.at[slot], b_sem),
                ]
                for copy in stores:
                    copy.start()
                for copy in stores:
                    copy.wait()


def add_terms(slots, pieces, grad_a, grad_b):
    count, rank, both = pieces[0].shape
    ff, d = grad_a.shape[2], grad_b.shape[2]
    anywhere = pl.BlockSpec(memory_space=pl.ANY)
    n = len(pieces)
    return pl.pallas_call(
        functools.partial(add_kernel, n, count),
        grid_spec=pltpu.PrefetchScalarGridSpec(
            num_scalar_prefetch=1,
            grid=(1,),
            in_specs=[anywhere] * (n + 2),
            out_specs=[anywhere] * 2,
            scratch_shapes=[
                pltpu.VMEM((rank, both), bf16),
                pltpu.VMEM((rank, ff), f32),
                pltpu.VMEM((rank, d), f32),
                pltpu.SemaphoreType.DMA,
                pltpu.SemaphoreType.DMA,
                pltpu.SemaphoreType.DMA,
            ],
        ),
        out_shape=[
            jax.ShapeDtypeStruct(grad_a.shape, f32),
            jax.ShapeDtypeStruct(grad_b.shape, f32),
        ],
        input_output_aliases={n + 1: 0, n + 2: 1},
        **params((0, n * count * 10 * rank * both)),
    )(slots, *pieces, grad_a, grad_b)


def on_device(
    n_groups,
    n_fsdp,
    n_dp,
    output_gradient,
    hidden,
    frozen_down_weight,
    adapter_first_factors,
    adapter_second_factors,
    island_live_rows,
    island_adapter_ids,
    owner_slot_adapters,
):
    rows, ff = hidden.shape
    d = output_gradient.shape[1]
    count = island_live_rows.shape[0]
    local = adapter_first_factors.shape[0]
    n_slots = owner_slot_adapters.shape[0]
    top = n_dp // 2
    me = lax.axis_index("dp")
    group = lax.axis_index("groups")

    def swap(value, bit, axis="dp", size=n_dp):
        return lax.ppermute(value, axis, [(i, i ^ bit) for i in range(size)])

    def spread(held):
        held = dict(held)
        bit = top // 2
        while bit:
            for r in list(held):
                held[r ^ bit] = swap(held[r], bit)
            bit //= 2
        return held

    match = island_adapter_ids[:, None] == owner_slot_adapters[None, :]
    slots = jnp.sum(jnp.where(match, jnp.arange(n_slots, dtype=i32)[None, :], 0), axis=1)
    far_slots = swap(slots, top)

    kept = lax.all_gather(output_gradient, "fsdp", axis=1, tiled=True)

    share = ff // n_groups
    if share % 2048 == 0:
        unit, tile = share // 8, share // 4
        sizes = [unit, 3 * unit, 2 * unit, 2 * unit]
    else:
        tile = share
        sizes = [share]
    parts = [(sum(sizes[:j]), size) for j, size in enumerate(sizes)]

    crossed = []
    turned = []

    def flat(*pieces):
        return [v for piece in pieces for v in piece.values()]

    def cross(*after):
        j = len(crossed)
        if j < len(parts):
            start, size = parts[j]
            piece = lax.dynamic_slice_in_dim(
                frozen_down_weight, group * share + start, size, axis=0
            )
            crossed.append({top: swap(behind(piece, *after), top)})

    def turn(*after):
        j = len(turned)
        if j < len(parts):
            piece = behind(crossed[j][top], *after)
            turned.append([])
            for shift in range(1, n_groups):
                ring = [(i, (i + shift) % n_groups) for i in range(n_groups)]
                turned[j].append({top: lax.ppermute(piece, "groups", ring)})

    def fill(chunks, *after):
        for piece in chunks:
            piece.update(spread({top: behind(piece[top], *after)}))

    cross()

    first = jnp.swapaxes(adapter_first_factors, 1, 2)
    a_near = spread({0: first})
    b_near = spread({0: adapter_second_factors})
    near = sorted(a_near)
    a_near = [a_near[r] for r in near]
    b_near = [b_near[r] for r in near]
    def places(wanted):
        owner = wanted // local
        index = jnp.concatenate([wanted % local] * len(near))
        return index, jnp.where((owner ^ me) < top, owner ^ me, len(near))

    far = swap(pick(*places(behind(far_slots, *flat(*crossed))), a_near, b_near), top)
    whole = spread({0: behind(frozen_down_weight, *a_near, *b_near)})
    both_slots = spread({0: jnp.concatenate([slots, far_slots])})
    turn()

    ready = behind(slots, *flat(whole, both_slots, *turned[0]))
    part, block_a, grad_a, grad_b = project(
        *places(ready), a_near, b_near, far, hidden, output_gradient
    )
    cross(far, *flat(*turned[0]))
    fill(crossed[:1], far)
    fill(turned[0], far)
    sums = [part]
    bit = 1
    while bit < n_fsdp:
        sums.append(swap(sums[-1], bit, "fsdp", n_fsdp))
        if 2 * bit < n_fsdp:
            sums.append(sums[-2] + sums[-1])
        bit *= 2
    total, other = sums[-2:]
    past = [sums[2], *flat(*crossed[:2], *turned[0])]
    cross(*past)
    turn(*past)
    fill(crossed[1:2], *past)
    past = [other, *flat(*crossed[:3], *sum(turned, []))]
    cross(*past)
    turn(*past)
    fill(crossed[2:3], *past)
    for pieces in turned[1:2]:
        fill(pieces, *past)
    terms, coef = block_terms(island_live_rows, total, other, hidden, output_gradient)
    far_terms = swap(terms, top)
    past = flat(*crossed, *sum(turned, []))
    turn(*past)
    fill(crossed[3:], *past)
    for pieces in turned[2:3]:
        fill(pieces, *past)
    near_terms = spread({0: behind(terms, *past)})
    past = [*flat(near_terms, *crossed, *sum(turned, []))]
    for pieces in turned[3:]:
        fill(pieces, *past)

    relative = [both_slots[r][:count] for r in near] + [both_slots[r][count:] for r in near]
    relative = jnp.concatenate(relative) - me * local
    edge = count * len(near)
    grad_a, grad_b = add_terms(
        relative[:edge], [near_terms[r] for r in near], grad_a, grad_b
    )

    scalars = jnp.concatenate([jnp.stack([me ^ r for r in range(n_dp)]).astype(i32), island_live_rows])
    order = [(shift, t) for shift in range(n_groups) for t in range(share // tile)]
    if share > tile:
        order.sort(key=lambda k: (k[1] + 1 == share // tile, k[0] > 0 and k[1] + 2 == share // tile))
        calls = [order[: len(order) - 3], order[len(order) - 3 :]]
    else:
        calls = [order]
    grad_hidden = None
    stages = [grad_a]
    for call in calls:
        chunks, tiles, where = [], [], []
        for shift, t in call:
            start = lax.rem(group + n_groups - shift, n_groups) * share
            where.append(start // tile + t)
            tiles.append([])
            for j, (first, size) in enumerate(parts):
                low, high = max(first, t * tile), min(first + size, (t + 1) * tile)
                if low < high:
                    if (shift, j) not in chunks:
                        chunks.append((shift, j))
                    tiles[-1].append((chunks.index((shift, j)), low - first, high - low))
        pieces = [turned[j][shift - 1] if shift else crossed[j] for shift, j in chunks]
        grad_hidden = base(
            where, scalars, kept, whole, pieces, tiles, tile, coef, block_a, grad_hidden
        )
        stages.append(grad_hidden)

    far_terms = behind(far_terms, *stages[:2], *flat(*sum(turned, [])))
    all_far = spread({top: far_terms})
    grad_a, grad_b = add_terms(
        relative[edge:], [all_far[r + top] for r in near], grad_a, grad_b
    )
    return grad_hidden, jnp.swapaxes(grad_a, 1, 2), grad_b


def solution(mesh):
    placed = (
        P(("groups", "dp"), "fsdp"),
        P(("groups", "dp"), "fsdp"),
        P("fsdp", "dp"),
        P(("groups", "dp"), "fsdp", None),
        P(("groups", "dp"), None, "fsdp"),
        P(("groups", "dp")),
        P(("groups", "dp")),
        P("groups"),
    )
    sizes = [mesh.shape[name] for name in ("groups", "fsdp", "dp")]
    return jax.shard_map(
        functools.partial(on_device, *sizes),
        mesh=mesh,
        in_specs=placed,
        out_specs=(
            P(("groups", "dp"), "fsdp"),
            P(("groups", "dp"), "fsdp", None),
            P(("groups", "dp"), None, "fsdp"),
        ),
        check_vma=False,
    )
```

```python
import functools

import jax
import jax.numpy as jnp
from jax import lax
from jax.experimental import pallas as pl
from jax.experimental.pallas import tpu as pltpu
from jax.sharding import PartitionSpec as P

adapter_scale = 2.0
factor_gradient = 0.0625
vmem_bytes = 60 * 1024 * 1024
bf16, f32, i32 = jnp.bfloat16, jnp.float32, jnp.int32


def behind(value, *after):
    if not after:
        return value
    return lax.optimization_barrier((value, *after))[0]


def params(cost):
    return dict(
        compiler_params=pltpu.CompilerParams(vmem_limit_bytes=vmem_bytes),
        cost_estimate=pl.CostEstimate(flops=cost[0], bytes_accessed=cost[1], transcendentals=0),
    )


def pick_kernel(pieces, index_ref, source_ref, *refs):
    a_refs, b_refs, out_ref = refs[:pieces], refs[pieces : 2 * pieces], refs[-1]
    source = source_ref[pl.program_id(0)]
    a, b = a_refs[0][0], b_refs[0][0]
    for r in range(1, pieces):
        a = jnp.where(source == r, a_refs[r][0], a)
        b = jnp.where(source == r, b_refs[r][0], b)
    ff = a.shape[1]
    out_ref[0, :, :ff] = a
    out_ref[0, :, ff:] = b


def factor_specs(pieces, count, rank, width):
    return [
        pl.BlockSpec(
            (1, rank, width), lambda i, index, source, r=r: (index[r * count + i], 0, 0)
        )
        for r in range(pieces)
    ]


def pick(index, source, a_pieces, b_pieces):
    count, pieces = source.shape[0], len(a_pieces)
    _, rank, ff = a_pieces[0].shape
    d = b_pieces[0].shape[2]
    return pl.pallas_call(
        functools.partial(pick_kernel, pieces),
        grid_spec=pltpu.PrefetchScalarGridSpec(
            num_scalar_prefetch=2,
            grid=(count,),
            in_specs=factor_specs(pieces, count, rank, ff) + factor_specs(pieces, count, rank, d),
            out_specs=pl.BlockSpec((1, rank, ff + d), lambda i, index, source: (i, 0, 0)),
        ),
        out_shape=jax.ShapeDtypeStruct((count, rank, ff + d), bf16),
        **params((0, 2 * (pieces + 1) * count * rank * (ff + d))),
    )(index, source, *a_pieces, *b_pieces)


def project_kernel(pieces, index_ref, source_ref, *refs):
    a_refs, b_refs = refs[:pieces], refs[pieces : 2 * pieces]
    far_ref, hid_ref, grad_ref, part_ref, block_ref, grad_a_ref, grad_b_ref = refs[
        2 * pieces : 2 * pieces + 7
    ]
    zeros, zero_sem = refs[2 * pieces + 7 :]
    step = pl.program_id(0)
    source = source_ref[step]
    ff = hid_ref.shape[1]
    d = grad_ref.shape[1]

    fills = []
    for slot in range(grad_a_ref.shape[0]):
        fills.append(pltpu.make_async_copy(zeros, grad_a_ref.at[slot], zero_sem.at[2 * slot]))
        fills.append(
            pltpu.make_async_copy(
                zeros.at[:, pl.ds(0, d)], grad_b_ref.at[slot], zero_sem.at[2 * slot + 1]
            )
        )

    @pl.when(step == 0)
    def _():
        zeros[...] = jnp.zeros_like(zeros)
        for fill in fills:
            fill.start()

    a, b = far_ref[0, :, :ff], far_ref[0, :, ff:]
    for r in range(pieces):
        a = jnp.where(source == r, a_refs[r][0], a)
        b = jnp.where(source == r, b_refs[r][0], b)
    block_ref[0] = a
    over_last = (((1,), (1,)), ((), ()))
    rank = a.shape[0]
    part_ref[0, :, :rank] = lax.dot_general(
        hid_ref[...], a, over_last, preferred_element_type=f32
    )
    part_ref[0, :, rank:] = lax.dot_general(
        grad_ref[...], b, over_last, preferred_element_type=f32
    )

    @pl.when(step == pl.num_programs(0) - 1)
    def _():
        for fill in fills:
            fill.wait()


def project(index, source, a_pieces, b_pieces, far, hidden, grad):
    count, pieces = source.shape[0], len(a_pieces)
    local, rank, ff = a_pieces[0].shape
    d = b_pieces[0].shape[2]
    rows = hidden.shape[0]
    height = rows // count
    own = lambda i, index, source: (i, 0)
    own3 = lambda i, index, source: (i, 0, 0)
    return pl.pallas_call(
        functools.partial(project_kernel, pieces),
        grid_spec=pltpu.PrefetchScalarGridSpec(
            num_scalar_prefetch=2,
            grid=(count,),
            in_specs=factor_specs(pieces, count, rank, ff)
            + factor_specs(pieces, count, rank, d)
            + [
                pl.BlockSpec((1, rank, ff + d), own3),
                pl.BlockSpec((height, ff), own),
                pl.BlockSpec((height, d), own),
            ],
            out_specs=[
                pl.BlockSpec((1, height, 2 * rank), own3),
                pl.BlockSpec((1, rank, ff), own3),
                pl.BlockSpec(memory_space=pl.ANY),
                pl.BlockSpec(memory_space=pl.ANY),
            ],
            scratch_shapes=[
                pltpu.VMEM((rank, ff), f32),
                pltpu.SemaphoreType.DMA((2 * local,)),
            ],
        ),
        out_shape=[
            jax.ShapeDtypeStruct((count, height, 2 * rank), f32),
            jax.ShapeDtypeStruct((count, rank, ff), bf16),
            jax.ShapeDtypeStruct((local, rank, ff), f32),
            jax.ShapeDtypeStruct((local, rank, d), f32),
        ],
        **params((2 * rows * rank * (ff + d), 2 * (rows + (pieces + 2) * count * rank) * (ff + d))),
    )(index, source, *a_pieces, *b_pieces, far, hidden, grad)


def terms_kernel(live_ref, here_ref, there_ref, hid_ref, grad_ref, terms_ref, coef_ref):
    ff = hid_ref.shape[1]
    rank = coef_ref.shape[2]
    total = here_ref[0] + there_ref[0]
    valid = lax.broadcasted_iota(i32, total.shape, 0) < live_ref[pl.program_id(0)]
    total = jnp.where(valid, total, 0.0)
    low = total[:, :rank].astype(bf16)
    coef = (adapter_scale * total[:, rank:]).astype(bf16)
    coef_ref[0] = coef
    over_rows = (((0,), (0,)), ((), ()))
    terms_ref[0, :, :ff] = (
        factor_gradient
        * lax.dot_general(coef, hid_ref[...], over_rows, preferred_element_type=f32)
    ).astype(bf16)
    terms_ref[0, :, ff:] = (
        factor_gradient
        * adapter_scale
        * lax.dot_general(low, grad_ref[...], over_rows, preferred_element_type=f32)
    ).astype(bf16)


def block_terms(live, here, there, hidden, grad):
    count, height, both = here.shape
    rank = both // 2
    rows, ff = hidden.shape
    d = grad.shape[1]
    own = lambda i, live: (i, 0)
    own3 = lambda i, live: (i, 0, 0)
    return pl.pallas_call(
        terms_kernel,
        grid_spec=pltpu.PrefetchScalarGridSpec(
            num_scalar_prefetch=1,
            grid=(count,),
            in_specs=[
                pl.BlockSpec((1, height, both), own3),
                pl.BlockSpec((1, height, both), own3),
                pl.BlockSpec((height, ff), own),
                pl.BlockSpec((height, d), own),
            ],
            out_specs=[
                pl.BlockSpec((1, rank, ff + d), own3),
                pl.BlockSpec((1, height, rank), own3),
            ],
        ),
        out_shape=[
            jax.ShapeDtypeStruct((count, rank, ff + d), bf16),
            jax.ShapeDtypeStruct((count, height, rank), bf16),
        ],
        **params((2 * rows * rank * (ff + d), 2 * (rows + count * rank) * (ff + d))),
    )(live, here, there, hidden, grad)


def base_kernel(n_dp, tiles, n_chunks, blocks, scalars_ref, kept_ref, *refs):
    near = n_dp // 2
    near_refs = refs[:near]
    far_refs = refs[near : near + n_chunks * near]
    coef_ref, block_ref = refs[near + n_chunks * near : near + n_chunks * near + 2]
    out_ref, token_ref, kept, weight, factor, result = refs[-10:-4]
    kept_sem, in_sem, factor_sem, out_sem = refs[-4:]
    _, tile, depth = weight.shape
    deep = depth // n_dp
    height = coef_ref.shape[1]
    steps = len(tiles)
    rows = pl.ds(blocks[0] * height, len(blocks) * height)
    token_ref[...] = jnp.zeros_like(token_ref)

    def lanes(r):
        return pl.ds(pl.multiple_of(scalars_ref[steps + r] * deep, deep), deep)

    def span(j):
        return pl.ds(pl.multiple_of(scalars_ref[j] * tile, tile), tile)

    def loads(j, slot, r):
        if r < near:
            return [
                pltpu.make_async_copy(
                    near_refs[r].at[span(j), :], weight.at[slot, :, lanes(r)], in_sem.at[slot, r, 0]
                )
            ]
        copies, low = [], 0
        for k, (chunk, start, size) in enumerate(tiles[j]):
            copies.append(
                pltpu.make_async_copy(
                    far_refs[chunk * near + r - near].at[pl.ds(start, size)],
                    weight.at[slot, pl.ds(low, size), lanes(r)],
                    in_sem.at[slot, r, k],
                )
            )
            low += size
        return copies

    def factors(j, slot):
        return pltpu.make_async_copy(
            block_ref.at[:, :, span(j)], factor.at[slot], factor_sem.at[slot]
        )

    def columns(r):
        return pltpu.make_async_copy(kept_ref.at[:, lanes(r)], kept.at[:, lanes(r)], kept_sem.at[r])

    def store(j, slot):
        return pltpu.make_async_copy(result.at[slot], out_ref.at[rows, span(j)], out_sem.at[slot])

    def load(j, slot):
        for r in range(n_dp):
            for copy in loads(j, slot, r):
                copy.start()
        factors(j, slot).start()

    over_last = (((1,), (1,)), ((), ()))

    def finish(slot, total):
        for k, b in enumerate(blocks):
            extra = jnp.dot(coef_ref[b], factor[slot, b], preferred_element_type=f32)
            here = total[k * height : (k + 1) * height] + extra
            valid = lax.broadcasted_iota(i32, here.shape, 0) < scalars_ref[steps + n_dp + b]
            result[slot, k * height : (k + 1) * height, :] = jnp.where(valid, here, 0.0).astype(
                bf16
            )

    for r in range(n_dp):
        columns(r).start()
        for copy in loads(0, 0, r):
            copy.start()
    factors(0, 0).start()
    if steps > 1:
        load(1, 1)
    total = None
    for r in range(n_dp):
        columns(r).wait()
        for copy in loads(0, 0, r):
            copy.wait()
        part = lax.dot_general(
            kept[:, lanes(r)], weight[0, :, lanes(r)], over_last, preferred_element_type=f32
        )
        total = part if total is None else total + part
    factors(0, 0).wait()
    finish(0, total)
    store(0, 0).start()

    @pl.loop(1, steps)
    def _(step):
        slot = lax.rem(step, 2)
        for j in range(1, steps):

            @pl.when(step == j)
            def _():
                if j + 1 < steps:
                    load(j + 1, (j + 1) % 2)
                for r in range(n_dp):
                    for copy in loads(j, j % 2, r):
                        copy.wait()
                factors(j, j % 2).wait()
                if j >= 2:
                    store(j - 2, j % 2).wait()

        finish(
            slot,
            lax.dot_general(kept[...], weight[slot], over_last, preferred_element_type=f32),
        )
        for j in range(1, steps):
            pl.when(step == j)(lambda j=j: store(j, j % 2).start())

    for j in range(max(steps - 2, 0), steps):
        store(j, j % 2).wait()


def base(places, scalars, kept, near, chunks, tiles, tile, coef, block_a, blocks, held, token):
    rows, depth = kept.shape
    count, rank, ff = block_a.shape
    top = len(near)
    anywhere = pl.BlockSpec(memory_space=pl.ANY)
    operands = [kept] + [near[r] for r in range(top)]
    for piece in chunks:
        operands += [piece[r] for r in range(top, 2 * top)]
    in_specs = [anywhere] * len(operands)
    in_specs += [pl.BlockSpec(coef.shape, lambda i, s: (0, 0, 0)), anywhere]
    operands += [coef, block_a]
    aliases = {}
    if held is not None:
        in_specs += [anywhere, anywhere]
        operands += [token, held]
        aliases = {len(operands): 0}
    most = max(len(segments) for segments in tiles)
    span = tile * len(tiles)
    return pl.pallas_call(
        functools.partial(base_kernel, 2 * top, tiles, len(chunks), blocks),
        grid_spec=pltpu.PrefetchScalarGridSpec(
            num_scalar_prefetch=1,
            grid=(1,),
            in_specs=in_specs,
            out_specs=[anywhere, pl.BlockSpec((8, 128), lambda i, s: (0, 0))],
            scratch_shapes=[
                pltpu.VMEM((rows, depth), bf16),
                pltpu.VMEM((2, tile, depth), bf16),
                pltpu.VMEM((2, count, rank, tile), bf16),
                pltpu.VMEM((2, rows, tile), bf16),
                pltpu.SemaphoreType.DMA((2 * top,)),
                pltpu.SemaphoreType.DMA((2, 2 * top, most)),
                pltpu.SemaphoreType.DMA((2,)),
                pltpu.SemaphoreType.DMA((2,)),
            ],
        ),
        out_shape=[
            jax.ShapeDtypeStruct((rows // len(blocks) * count, ff), bf16),
            jax.ShapeDtypeStruct((8, 128), f32),
        ],
        input_output_aliases=aliases,
        **params((2 * rows * depth * span, 2 * (rows * depth + (rows + depth) * span))),
    )(jnp.concatenate([jnp.stack(places).astype(i32), scalars]), *operands)


def add_kernel(pieces, count, slots_ref, *refs):
    term_refs = refs[:pieces]
    a_ref, b_ref, terms, a, b, term_sem, a_sem, b_sem = refs[pieces + 2 :]
    local, _, ff = a.shape

    def load(k):
        return pltpu.make_async_copy(
            term_refs[k // count].at[k % count], terms.at[k], term_sem.at[k]
        )

    def whole(slot, inward):
        pairs = [(a_ref.at[slot], a.at[slot]), (b_ref.at[slot], b.at[slot])]
        return [
            pltpu.make_async_copy(*(pair if inward else pair[::-1]), sem.at[slot])
            for pair, sem in zip(pairs, (a_sem, b_sem))
        ]

    wanted = [slots_ref[k] for k in range(pieces * count)]
    owned = [(slot >= 0) & (slot < local) for slot in wanted]
    hit = []
    for j in range(local):
        any_here = wanted[0] == j
        for slot in wanted[1:]:
            any_here = any_here | (slot == j)
        hit.append(any_here)

    def start(copies):
        for copy in copies:
            copy.start()

    def wait(copies):
        for copy in copies:
            copy.wait()

    for j in range(local):
        pl.when(hit[j])(lambda j=j: start(whole(j, True)))
    for k in range(pieces * count):
        pl.when(owned[k])(lambda k=k: start([load(k)]))
    for j in range(local):
        pl.when(hit[j])(lambda j=j: wait(whole(j, True)))

    def add(k):
        wait([load(k)])
        a[wanted[k]] += terms[k, :, :ff].astype(f32)
        b[wanted[k]] += terms[k, :, ff:].astype(f32)

    for k in range(pieces * count):
        pl.when(owned[k])(lambda k=k: add(k))
    for j in range(local):
        pl.when(hit[j])(lambda j=j: start(whole(j, False)))
    for j in range(local):
        pl.when(hit[j])(lambda j=j: wait(whole(j, False)))


def add_terms(slots, pieces, grad_a, grad_b):
    count, rank, both = pieces[0].shape
    anywhere = pl.BlockSpec(memory_space=pl.ANY)
    n = len(pieces)
    local = grad_a.shape[0]
    return pl.pallas_call(
        functools.partial(add_kernel, n, count),
        grid_spec=pltpu.PrefetchScalarGridSpec(
            num_scalar_prefetch=1,
            grid=(1,),
            in_specs=[anywhere] * (n + 2),
            out_specs=[anywhere] * 2,
            scratch_shapes=[
                pltpu.VMEM((n * count, rank, both), bf16),
                pltpu.VMEM(grad_a.shape, f32),
                pltpu.VMEM(grad_b.shape, f32),
                pltpu.SemaphoreType.DMA((n * count,)),
                pltpu.SemaphoreType.DMA((local,)),
                pltpu.SemaphoreType.DMA((local,)),
            ],
        ),
        out_shape=[
            jax.ShapeDtypeStruct(grad_a.shape, f32),
            jax.ShapeDtypeStruct(grad_b.shape, f32),
        ],
        input_output_aliases={n + 1: 0, n + 2: 1},
        **params((0, n * count * 10 * rank * both)),
    )(slots, *pieces, grad_a, grad_b)


def on_device(
    n_groups,
    n_fsdp,
    n_dp,
    output_gradient,
    hidden,
    frozen_down_weight,
    adapter_first_factors,
    adapter_second_factors,
    island_live_rows,
    island_adapter_ids,
    owner_slot_adapters,
):
    rows, ff = hidden.shape
    d = output_gradient.shape[1]
    count = island_live_rows.shape[0]
    local = adapter_first_factors.shape[0]
    n_slots = owner_slot_adapters.shape[0]
    top = n_dp // 2
    me = lax.axis_index("dp")
    group = lax.axis_index("groups")

    def swap(value, bit, axis="dp", size=n_dp):
        return lax.ppermute(value, axis, [(i, i ^ bit) for i in range(size)])

    def spread(held):
        held = dict(held)
        bit = top // 2
        while bit:
            for r in list(held):
                held[r ^ bit] = swap(held[r], bit)
            bit //= 2
        return held

    match = island_adapter_ids[:, None] == owner_slot_adapters[None, :]
    slots = jnp.sum(jnp.where(match, jnp.arange(n_slots, dtype=i32)[None, :], 0), axis=1)
    far_slots = swap(slots, top)

    cut = (2 * count + 2) // 3
    row_parts = [range(cut), range(cut, count)] if cut < count else [range(count)]
    height = rows // count
    kept = []

    def gather(*after):
        k = len(kept)
        if k < len(row_parts):
            part = row_parts[k]
            mine = output_gradient[part[0] * height : (part[-1] + 1) * height]
            kept.append(lax.all_gather(behind(mine, *after), "fsdp", axis=1, tiled=True))

    gather()

    share = ff // n_groups
    if share % 2048 == 0:
        unit, tile = share // 8, share // 4
        sizes = [unit, 2 * unit, 3 * unit, 2 * unit]
    else:
        tile = share
        sizes = [share]
    parts = [(sum(sizes[:j]), size) for j, size in enumerate(sizes)]

    crossed = []
    turned = []

    def flat(*pieces):
        return [v for piece in pieces for v in piece.values()]

    def cross(*after):
        j = len(crossed)
        if j < len(parts):
            start, size = parts[j]
            piece = lax.dynamic_slice_in_dim(
                frozen_down_weight, group * share + start, size, axis=0
            )
            crossed.append({top: swap(behind(piece, *after), top)})

    def turn(*after):
        j = len(turned)
        if j < len(parts):
            piece = behind(crossed[j][top], *after)
            turned.append([])
            for shift in range(1, n_groups):
                ring = [(i, (i + shift) % n_groups) for i in range(n_groups)]
                turned[j].append({top: lax.ppermute(piece, "groups", ring)})

    def fill(chunks, *after):
        for piece in chunks:
            piece.update(spread({top: behind(piece[top], *after)}))

    cross()

    first = jnp.swapaxes(adapter_first_factors, 1, 2)
    a_near = spread({0: first})
    b_near = spread({0: adapter_second_factors})
    near = sorted(a_near)
    a_near = [a_near[r] for r in near]
    b_near = [b_near[r] for r in near]
    def places(wanted):
        owner = wanted // local
        index = jnp.concatenate([wanted % local] * len(near))
        return index, jnp.where((owner ^ me) < top, owner ^ me, len(near))

    picked = pick(*places(behind(far_slots, *flat(*crossed))), a_near, b_near)
    far = swap(picked, top)
    whole = spread({0: behind(frozen_down_weight, picked)})
    both_slots = spread({0: jnp.concatenate([slots, far_slots])})
    turn()

    ready = behind(slots, *flat(whole, both_slots, *turned[0]))
    part, block_a, grad_a, grad_b = project(
        *places(ready), a_near, b_near, far, hidden, output_gradient
    )
    cross(far, *flat(*turned[0]))
    fill(crossed[:1], far)
    fill(turned[0], far)
    sums = [part]
    bit = 1
    while bit < n_fsdp:
        sums.append(swap(sums[-1], bit, "fsdp", n_fsdp))
        if 2 * bit < n_fsdp:
            sums.append(sums[-2] + sums[-1])
        bit *= 2
    total, other = sums[-2:]
    past = [sums[2], *flat(*crossed[:2], *turned[0])]
    cross(*past)
    turn(*past)
    fill(crossed[1:2], *past)
    gather(other)
    past = [other, *flat(*crossed[:3], *sum(turned, []))]
    cross(*past)
    turn(*past)
    fill(crossed[2:3], *past)
    for pieces in turned[1:2]:
        fill(pieces, *past)
    terms, coef = block_terms(island_live_rows, total, other, hidden, output_gradient)
    far_terms = swap(terms, top)
    near_terms = spread({0: behind(terms, *flat(*crossed[:3]))})

    relative = [both_slots[r][:count] for r in near] + [both_slots[r][count:] for r in near]
    relative = jnp.concatenate(relative) - me * local
    edge = count * len(near)
    grad_a, grad_b = add_terms(
        relative[:edge], [near_terms[r] for r in near], grad_a, grad_b
    )

    scalars = jnp.concatenate([jnp.stack([me ^ r for r in range(n_dp)]).astype(i32), island_live_rows])
    grad_hidden = token = None

    def multiply(k, *where):
        nonlocal grad_hidden, token
        chunks, tiles, places = [], [], []
        for shift, t in where:
            start = lax.rem(group + n_groups - shift, n_groups) * share
            places.append(start // tile + t)
            tiles.append([])
            for j, (first, size) in enumerate(parts):
                low, high = max(first, t * tile), min(first + size, (t + 1) * tile)
                if low < high:
                    if (shift, j) not in chunks:
                        chunks.append((shift, j))
                    tiles[-1].append((chunks.index((shift, j)), low - first, high - low))
        pieces = [turned[j][shift - 1] if shift else crossed[j] for shift, j in chunks]
        grad_hidden, token = base(
            places, scalars, kept[k], whole, pieces, tiles, tile, coef, block_a,
            list(row_parts[k]), grad_hidden, token,
        )

    last = share // tile - 1
    others = range(1, n_groups)
    if last:
        multiply(0, *[(0, t) for t in range(last)], *[(g, 0) for g in others])
        past = [token, *flat(*crossed)]
        turn(*past)
        fill(crossed[3:], *past)
        for pieces in turned[2:3]:
            fill(pieces, *flat(*crossed))
        multiply(0, (0, last), *[(g, t) for g in others for t in range(1, last)])
        for k in range(1, len(row_parts)):
            multiply(
                k, *[(0, t) for t in range(last + 1)], *[(g, t) for g in others for t in range(last)]
            )
        for pieces in turned[3:]:
            fill(pieces, token)
        early = token
        for k in range(len(row_parts)):
            multiply(k, *[(g, last) for g in others])
    else:
        for k in range(len(row_parts)):
            multiply(k, *[(g, 0) for g in range(n_groups)])
        early = token

    all_far = spread({top: behind(far_terms, early)})
    grad_a, grad_b = add_terms(
        relative[edge:], [all_far[r + top] for r in near], grad_a, grad_b
    )
    return grad_hidden, jnp.swapaxes(grad_a, 1, 2), grad_b


def solution(mesh):
    placed = (
        P(("groups", "dp"), "fsdp"),
        P(("groups", "dp"), "fsdp"),
        P("fsdp", "dp"),
        P(("groups", "dp"), "fsdp", None),
        P(("groups", "dp"), None, "fsdp"),
        P(("groups", "dp")),
        P(("groups", "dp")),
        P("groups"),
    )
    sizes = [mesh.shape[name] for name in ("groups", "fsdp", "dp")]
    return jax.shard_map(
        functools.partial(on_device, *sizes),
        mesh=mesh,
        in_specs=placed,
        out_specs=(
            P(("groups", "dp"), "fsdp"),
            P(("groups", "dp"), "fsdp", None),
            P(("groups", "dp"), None, "fsdp"),
        ),
        check_vma=False,
    )
```

```python
import functools

import jax
import jax.numpy as jnp
from jax import lax
from jax.experimental import pallas as pl
from jax.experimental.pallas import tpu as pltpu
from jax.sharding import PartitionSpec as P

adapter_scale = 2.0
factor_gradient = 0.0625
vmem_bytes = 60 * 1024 * 1024
bf16, f32, i32 = jnp.bfloat16, jnp.float32, jnp.int32


def behind(value, *after):
    if not after:
        return value
    return lax.optimization_barrier((value, *after))[0]


def params(cost):
    return dict(
        compiler_params=pltpu.CompilerParams(vmem_limit_bytes=vmem_bytes),
        cost_estimate=pl.CostEstimate(flops=cost[0], bytes_accessed=cost[1], transcendentals=0),
    )


def pick_kernel(pieces, index_ref, source_ref, *refs):
    a_refs, b_refs, out_ref = refs[:pieces], refs[pieces : 2 * pieces], refs[-1]
    source = source_ref[pl.program_id(0)]
    a, b = a_refs[0][0], b_refs[0][0]
    for r in range(1, pieces):
        a = jnp.where(source == r, a_refs[r][0], a)
        b = jnp.where(source == r, b_refs[r][0], b)
    ff = a.shape[1]
    out_ref[0, :, :ff] = a
    out_ref[0, :, ff:] = b


def factor_specs(pieces, count, rank, width):
    return [
        pl.BlockSpec(
            (1, rank, width), lambda i, index, source, r=r: (index[r * count + i], 0, 0)
        )
        for r in range(pieces)
    ]


def pick(index, source, a_pieces, b_pieces):
    count, pieces = source.shape[0], len(a_pieces)
    _, rank, ff = a_pieces[0].shape
    d = b_pieces[0].shape[2]
    return pl.pallas_call(
        functools.partial(pick_kernel, pieces),
        grid_spec=pltpu.PrefetchScalarGridSpec(
            num_scalar_prefetch=2,
            grid=(count,),
            in_specs=factor_specs(pieces, count, rank, ff) + factor_specs(pieces, count, rank, d),
            out_specs=pl.BlockSpec((1, rank, ff + d), lambda i, index, source: (i, 0, 0)),
        ),
        out_shape=jax.ShapeDtypeStruct((count, rank, ff + d), bf16),
        **params((0, 2 * (pieces + 1) * count * rank * (ff + d))),
    )(index, source, *a_pieces, *b_pieces)


def project_kernel(pieces, index_ref, source_ref, *refs):
    a_refs, b_refs = refs[:pieces], refs[pieces : 2 * pieces]
    far_ref, hid_ref, grad_ref, part_ref, block_ref, grad_a_ref, grad_b_ref = refs[
        2 * pieces : 2 * pieces + 7
    ]
    zeros, zero_sem = refs[2 * pieces + 7 :]
    step = pl.program_id(0)
    source = source_ref[step]
    ff = hid_ref.shape[1]
    d = grad_ref.shape[1]

    fills = []
    for slot in range(grad_a_ref.shape[0]):
        fills.append(pltpu.make_async_copy(zeros, grad_a_ref.at[slot], zero_sem.at[2 * slot]))
        fills.append(
            pltpu.make_async_copy(
                zeros.at[:, pl.ds(0, d)], grad_b_ref.at[slot], zero_sem.at[2 * slot + 1]
            )
        )

    @pl.when(step == 0)
    def _():
        zeros[...] = jnp.zeros_like(zeros)
        for fill in fills:
            fill.start()

    a, b = far_ref[0, :, :ff], far_ref[0, :, ff:]
    for r in range(pieces):
        a = jnp.where(source == r, a_refs[r][0], a)
        b = jnp.where(source == r, b_refs[r][0], b)
    block_ref[0] = a
    over_last = (((1,), (1,)), ((), ()))
    rank = a.shape[0]
    part_ref[0, :, :rank] = lax.dot_general(
        hid_ref[...], a, over_last, preferred_element_type=f32
    )
    part_ref[0, :, rank:] = lax.dot_general(
        grad_ref[...], b, over_last, preferred_element_type=f32
    )

    @pl.when(step == pl.num_programs(0) - 1)
    def _():
        for fill in fills:
            fill.wait()


def project(index, source, a_pieces, b_pieces, far, hidden, grad):
    count, pieces = source.shape[0], len(a_pieces)
    local, rank, ff = a_pieces[0].shape
    d = b_pieces[0].shape[2]
    rows = hidden.shape[0]
    height = rows // count
    own = lambda i, index, source: (i, 0)
    own3 = lambda i, index, source: (i, 0, 0)
    return pl.pallas_call(
        functools.partial(project_kernel, pieces),
        grid_spec=pltpu.PrefetchScalarGridSpec(
            num_scalar_prefetch=2,
            grid=(count,),
            in_specs=factor_specs(pieces, count, rank, ff)
            + factor_specs(pieces, count, rank, d)
            + [
                pl.BlockSpec((1, rank, ff + d), own3),
                pl.BlockSpec((height, ff), own),
                pl.BlockSpec((height, d), own),
            ],
            out_specs=[
                pl.BlockSpec((1, height, 2 * rank), own3),
                pl.BlockSpec((1, rank, ff), own3),
                pl.BlockSpec(memory_space=pl.ANY),
                pl.BlockSpec(memory_space=pl.ANY),
            ],
            scratch_shapes=[
                pltpu.VMEM((rank, ff), f32),
                pltpu.SemaphoreType.DMA((2 * local,)),
            ],
        ),
        out_shape=[
            jax.ShapeDtypeStruct((count, height, 2 * rank), f32),
            jax.ShapeDtypeStruct((count, rank, ff), bf16),
            jax.ShapeDtypeStruct((local, rank, ff), f32),
            jax.ShapeDtypeStruct((local, rank, d), f32),
        ],
        **params((2 * rows * rank * (ff + d), 2 * (rows + (pieces + 2) * count * rank) * (ff + d))),
    )(index, source, *a_pieces, *b_pieces, far, hidden, grad)


def terms_kernel(live_ref, here_ref, there_ref, hid_ref, grad_ref, terms_ref, coef_ref):
    ff = hid_ref.shape[1]
    rank = coef_ref.shape[2]
    total = here_ref[0] + there_ref[0]
    valid = lax.broadcasted_iota(i32, total.shape, 0) < live_ref[pl.program_id(0)]
    total = jnp.where(valid, total, 0.0)
    low = total[:, :rank].astype(bf16)
    coef = (adapter_scale * total[:, rank:]).astype(bf16)
    coef_ref[0] = coef
    over_rows = (((0,), (0,)), ((), ()))
    terms_ref[0, :, :ff] = (
        factor_gradient
        * lax.dot_general(coef, hid_ref[...], over_rows, preferred_element_type=f32)
    ).astype(bf16)
    terms_ref[0, :, ff:] = (
        factor_gradient
        * adapter_scale
        * lax.dot_general(low, grad_ref[...], over_rows, preferred_element_type=f32)
    ).astype(bf16)


def block_terms(live, here, there, hidden, grad):
    count, height, both = here.shape
    rank = both // 2
    rows, ff = hidden.shape
    d = grad.shape[1]
    own = lambda i, live: (i, 0)
    own3 = lambda i, live: (i, 0, 0)
    return pl.pallas_call(
        terms_kernel,
        grid_spec=pltpu.PrefetchScalarGridSpec(
            num_scalar_prefetch=1,
            grid=(count,),
            in_specs=[
                pl.BlockSpec((1, height, both), own3),
                pl.BlockSpec((1, height, both), own3),
                pl.BlockSpec((height, ff), own),
                pl.BlockSpec((height, d), own),
            ],
            out_specs=[
                pl.BlockSpec((1, rank, ff + d), own3),
                pl.BlockSpec((1, height, rank), own3),
            ],
        ),
        out_shape=[
            jax.ShapeDtypeStruct((count, rank, ff + d), bf16),
            jax.ShapeDtypeStruct((count, height, rank), bf16),
        ],
        **params((2 * rows * rank * (ff + d), 2 * (rows + count * rank) * (ff + d))),
    )(live, here, there, hidden, grad)


def join_kernel(n, *refs):
    at_ref, piece_refs, (out_ref, sem) = refs[0], refs[1 : 1 + n], refs[1 + n :]
    deep = piece_refs[0].shape[1]

    def copy(k):
        lanes = pl.ds(pl.multiple_of(at_ref[k] * deep, deep), deep)
        return pltpu.make_async_copy(piece_refs[k], out_ref.at[:, lanes], sem.at[k])

    for k in range(n):
        pl.when(at_ref[k] >= 0)(lambda k=k: copy(k).start())
    for k in range(n):
        pl.when(at_ref[k] >= 0)(lambda k=k: copy(k).wait())


def join(at, pieces, parts):
    rows, deep = pieces[0].shape
    anywhere = pl.BlockSpec(memory_space=pl.ANY)
    return pl.pallas_call(
        functools.partial(join_kernel, len(pieces)),
        grid_spec=pltpu.PrefetchScalarGridSpec(
            num_scalar_prefetch=1,
            grid=(1,),
            in_specs=[anywhere] * len(pieces),
            out_specs=anywhere,
            scratch_shapes=[pltpu.SemaphoreType.DMA((len(pieces),))],
        ),
        out_shape=jax.ShapeDtypeStruct((rows, parts * deep), bf16),
        **params((0, 4 * rows * parts * deep)),
    )(at, *pieces)


def base_kernel(n_dp, tiles, n_chunks, blocks, scalars_ref, kept_ref, *refs):
    near = n_dp // 2
    near_refs = refs[:near]
    far_refs = refs[near : near + n_chunks * near]
    coef_ref, block_ref = refs[near + n_chunks * near : near + n_chunks * near + 2]
    out_ref, token_ref, kept, weight, factor, result = refs[-10:-4]
    kept_sem, in_sem, factor_sem, out_sem = refs[-4:]
    _, tile, depth = weight.shape
    deep = depth // n_dp
    height = coef_ref.shape[1]
    steps = len(tiles)
    rows = pl.ds(blocks[0] * height, len(blocks) * height)
    token_ref[...] = jnp.zeros_like(token_ref)

    def lanes(r):
        return pl.ds(pl.multiple_of(scalars_ref[steps + r] * deep, deep), deep)

    def span(j):
        return pl.ds(pl.multiple_of(scalars_ref[j] * tile, tile), tile)

    def loads(j, slot, r):
        if r < near:
            return [
                pltpu.make_async_copy(
                    near_refs[r].at[span(j), :], weight.at[slot, :, lanes(r)], in_sem.at[slot, r, 0]
                )
            ]
        copies, low = [], 0
        for k, (chunk, start, size) in enumerate(tiles[j]):
            copies.append(
                pltpu.make_async_copy(
                    far_refs[chunk * near + r - near].at[pl.ds(start, size)],
                    weight.at[slot, pl.ds(low, size), lanes(r)],
                    in_sem.at[slot, r, k],
                )
            )
            low += size
        return copies

    def factors(j, slot):
        return pltpu.make_async_copy(
            block_ref.at[:, :, span(j)], factor.at[slot], factor_sem.at[slot]
        )

    def columns(r):
        return pltpu.make_async_copy(kept_ref.at[:, lanes(r)], kept.at[:, lanes(r)], kept_sem.at[r])

    def store(j, slot):
        return pltpu.make_async_copy(result.at[slot], out_ref.at[rows, span(j)], out_sem.at[slot])

    def load(j, slot):
        for r in range(n_dp):
            for copy in loads(j, slot, r):
                copy.start()
        factors(j, slot).start()

    over_last = (((1,), (1,)), ((), ()))

    def finish(slot, total):
        for k, b in enumerate(blocks):
            extra = jnp.dot(coef_ref[b], factor[slot, b], preferred_element_type=f32)
            here = total[k * height : (k + 1) * height] + extra
            valid = lax.broadcasted_iota(i32, here.shape, 0) < scalars_ref[steps + n_dp + b]
            result[slot, k * height : (k + 1) * height, :] = jnp.where(valid, here, 0.0).astype(
                bf16
            )

    for r in range(n_dp):
        columns(r).start()
        for copy in loads(0, 0, r):
            copy.start()
    factors(0, 0).start()
    if steps > 1:
        load(1, 1)
    total = None
    for r in range(n_dp):
        columns(r).wait()
        for copy in loads(0, 0, r):
            copy.wait()
        part = lax.dot_general(
            kept[:, lanes(r)], weight[0, :, lanes(r)], over_last, preferred_element_type=f32
        )
        total = part if total is None else total + part
    factors(0, 0).wait()
    finish(0, total)
    store(0, 0).start()

    @pl.loop(1, steps)
    def _(step):
        slot = lax.rem(step, 2)
        for j in range(1, steps):

            @pl.when(step == j)
            def _():
                if j + 1 < steps:
                    load(j + 1, (j + 1) % 2)
                for r in range(n_dp):
                    for copy in loads(j, j % 2, r):
                        copy.wait()
                factors(j, j % 2).wait()
                if j >= 2:
                    store(j - 2, j % 2).wait()

        finish(
            slot,
            lax.dot_general(kept[...], weight[slot], over_last, preferred_element_type=f32),
        )
        for j in range(1, steps):
            pl.when(step == j)(lambda j=j: store(j, j % 2).start())

    for j in range(max(steps - 2, 0), steps):
        store(j, j % 2).wait()


def base(places, scalars, kept, near, chunks, tiles, tile, coef, block_a, blocks, held, token):
    rows, depth = kept.shape
    count, rank, ff = block_a.shape
    top = len(near)
    anywhere = pl.BlockSpec(memory_space=pl.ANY)
    operands = [kept] + [near[r] for r in range(top)]
    for piece in chunks:
        operands += [piece[r] for r in range(top, 2 * top)]
    in_specs = [anywhere] * len(operands)
    in_specs += [pl.BlockSpec(coef.shape, lambda i, s: (0, 0, 0)), anywhere]
    operands += [coef, block_a]
    aliases = {}
    if held is not None:
        in_specs += [anywhere, anywhere]
        operands += [token, held]
        aliases = {len(operands): 0}
    most = max(len(segments) for segments in tiles)
    span = tile * len(tiles)
    return pl.pallas_call(
        functools.partial(base_kernel, 2 * top, tiles, len(chunks), blocks),
        grid_spec=pltpu.PrefetchScalarGridSpec(
            num_scalar_prefetch=1,
            grid=(1,),
            in_specs=in_specs,
            out_specs=[anywhere, pl.BlockSpec((8, 128), lambda i, s: (0, 0))],
            scratch_shapes=[
                pltpu.VMEM((rows, depth), bf16),
                pltpu.VMEM((2, tile, depth), bf16),
                pltpu.VMEM((2, count, rank, tile), bf16),
                pltpu.VMEM((2, rows, tile), bf16),
                pltpu.SemaphoreType.DMA((2 * top,)),
                pltpu.SemaphoreType.DMA((2, 2 * top, most)),
                pltpu.SemaphoreType.DMA((2,)),
                pltpu.SemaphoreType.DMA((2,)),
            ],
        ),
        out_shape=[
            jax.ShapeDtypeStruct((rows // len(blocks) * count, ff), bf16),
            jax.ShapeDtypeStruct((8, 128), f32),
        ],
        input_output_aliases=aliases,
        **params((1, 1)),
    )(jnp.concatenate([jnp.stack(places).astype(i32), scalars]), *operands)


def add_kernel(pieces, count, slots_ref, *refs):
    term_refs = refs[:pieces]
    a_ref, b_ref, terms, a, b, term_sem, a_sem, b_sem = refs[pieces + 2 :]
    local, _, ff = a.shape

    def load(k):
        return pltpu.make_async_copy(
            term_refs[k // count].at[k % count], terms.at[k], term_sem.at[k]
        )

    def whole(slot, inward):
        pairs = [(a_ref.at[slot], a.at[slot]), (b_ref.at[slot], b.at[slot])]
        return [
            pltpu.make_async_copy(*(pair if inward else pair[::-1]), sem.at[slot])
            for pair, sem in zip(pairs, (a_sem, b_sem))
        ]

    wanted = [slots_ref[k] for k in range(pieces * count)]
    owned = [(slot >= 0) & (slot < local) for slot in wanted]
    hit = []
    for j in range(local):
        any_here = wanted[0] == j
        for slot in wanted[1:]:
            any_here = any_here | (slot == j)
        hit.append(any_here)

    def start(copies):
        for copy in copies:
            copy.start()

    def wait(copies):
        for copy in copies:
            copy.wait()

    for j in range(local):
        pl.when(hit[j])(lambda j=j: start(whole(j, True)))
    for k in range(pieces * count):
        pl.when(owned[k])(lambda k=k: start([load(k)]))
    for j in range(local):
        pl.when(hit[j])(lambda j=j: wait(whole(j, True)))

    def add(k):
        wait([load(k)])
        a[wanted[k]] += terms[k, :, :ff].astype(f32)
        b[wanted[k]] += terms[k, :, ff:].astype(f32)

    for k in range(pieces * count):
        pl.when(owned[k])(lambda k=k: add(k))
    for j in range(local):
        pl.when(hit[j])(lambda j=j: start(whole(j, False)))
    for j in range(local):
        pl.when(hit[j])(lambda j=j: wait(whole(j, False)))


def add_terms(slots, pieces, grad_a, grad_b):
    count, rank, both = pieces[0].shape
    anywhere = pl.BlockSpec(memory_space=pl.ANY)
    n = len(pieces)
    local = grad_a.shape[0]
    return pl.pallas_call(
        functools.partial(add_kernel, n, count),
        grid_spec=pltpu.PrefetchScalarGridSpec(
            num_scalar_prefetch=1,
            grid=(1,),
            in_specs=[anywhere] * (n + 2),
            out_specs=[anywhere] * 2,
            scratch_shapes=[
                pltpu.VMEM((n * count, rank, both), bf16),
                pltpu.VMEM(grad_a.shape, f32),
                pltpu.VMEM(grad_b.shape, f32),
                pltpu.SemaphoreType.DMA((n * count,)),
                pltpu.SemaphoreType.DMA((local,)),
                pltpu.SemaphoreType.DMA((local,)),
            ],
        ),
        out_shape=[
            jax.ShapeDtypeStruct(grad_a.shape, f32),
            jax.ShapeDtypeStruct(grad_b.shape, f32),
        ],
        input_output_aliases={n + 1: 0, n + 2: 1},
        **params((1, 1)),
    )(slots, *pieces, grad_a, grad_b)


def on_device(
    n_groups,
    n_fsdp,
    n_dp,
    output_gradient,
    hidden,
    frozen_down_weight,
    adapter_first_factors,
    adapter_second_factors,
    island_live_rows,
    island_adapter_ids,
    owner_slot_adapters,
):
    rows, ff = hidden.shape
    d = output_gradient.shape[1]
    count = island_live_rows.shape[0]
    local = adapter_first_factors.shape[0]
    n_slots = owner_slot_adapters.shape[0]
    top = n_dp // 2
    me = lax.axis_index("dp")
    group = lax.axis_index("groups")

    def swap(value, bit, axis="dp", size=n_dp):
        return lax.ppermute(value, axis, [(i, i ^ bit) for i in range(size)])

    def spread(held):
        held = dict(held)
        bit = top // 2
        while bit:
            for r in list(held):
                held[r ^ bit] = swap(held[r], bit)
            bit //= 2
        return held

    match = island_adapter_ids[:, None] == owner_slot_adapters[None, :]
    slots = jnp.sum(jnp.where(match, jnp.arange(n_slots, dtype=i32)[None, :], 0), axis=1)
    far_slots = swap(slots, top)

    place = lax.axis_index("fsdp")
    line = n_fsdp <= 4
    pieces_of_kept, at = [output_gradient], [place]

    def hop(*after):
        k = len(pieces_of_kept) // 2
        if not line or k + 1 >= n_fsdp:
            return []
        right = [(i, i + 1) for i in range(n_fsdp - 1)]
        left = [(i + 1, i) for i in range(n_fsdp - 1)]
        ends = pieces_of_kept[-2:] if k else pieces_of_kept * 2
        for piece, pairs in zip(ends, (right, left)):
            pieces_of_kept.append(lax.ppermute(behind(piece, *after), "fsdp", pairs))
        at.append(place - k - 1)
        at.append(jnp.where(place + k + 1 < n_fsdp, place + k + 1, -1))
        return pieces_of_kept[-2:]

    first_hop = hop()

    share = ff // n_groups
    if share % 2048 == 0:
        unit, tile = share // 8, share // 4
        sizes = [3 * unit, 3 * unit, 2 * unit]
    else:
        tile = share
        sizes = [share]
    parts = [(sum(sizes[:j]), size) for j, size in enumerate(sizes)]

    crossed = []
    turned = []

    def flat(*pieces):
        return [v for piece in pieces for v in piece.values()]

    def cross(*after):
        j = len(crossed)
        if j < len(parts):
            start, size = parts[j]
            piece = lax.dynamic_slice_in_dim(
                frozen_down_weight, group * share + start, size, axis=0
            )
            crossed.append({top: swap(behind(piece, *after), top)})

    def turn(*after):
        j = len(turned)
        if j < len(parts):
            piece = behind(crossed[j][top], *after)
            turned.append([])
            for shift in range(1, n_groups):
                ring = [(i, (i + shift) % n_groups) for i in range(n_groups)]
                turned[j].append({top: lax.ppermute(piece, "groups", ring)})

    def fill(chunks, *after):
        for piece in chunks:
            piece.update(spread({top: behind(piece[top], *after)}))

    cross(far_slots)

    first = jnp.swapaxes(adapter_first_factors, 1, 2)
    a_near = spread({0: first})
    b_near = spread({0: adapter_second_factors})
    near = sorted(a_near)
    a_near = [a_near[r] for r in near]
    b_near = [b_near[r] for r in near]
    def places(wanted):
        owner = wanted // local
        index = jnp.concatenate([wanted % local] * len(near))
        return index, jnp.where((owner ^ me) < top, owner ^ me, len(near))

    picked = pick(*places(far_slots), a_near, b_near)
    both_slots = spread({0: behind(jnp.concatenate([slots, far_slots]), picked)})
    past = [picked, *first_hop, *flat(both_slots, *crossed)]
    far = swap(behind(picked, *past[1:]), top)
    whole = spread({0: behind(frozen_down_weight, *past)})
    turn(*past)
    past = [far, *hop(*past), *flat(*turned[0])]

    ready = behind(slots, *flat(whole, both_slots), *past)
    part, block_a, grad_a, grad_b = project(
        *places(ready), a_near, b_near, far, hidden, output_gradient
    )
    cross(*past)
    fill(crossed[:1], *past)
    third_hop = hop(*past)
    sums = [part]
    bit = 1
    while bit < n_fsdp:
        sums.append(swap(sums[-1], bit, "fsdp", n_fsdp))
        if 2 * bit < n_fsdp:
            sums.append(sums[-2] + sums[-1])
        bit *= 2
    total, other = sums[-2:]
    past = [sums[2], *flat(*crossed), *third_hop]
    cross(*past)
    turn(*past)
    fill(crossed[1:2], *past)
    fill(turned[0], *past)
    past = [other, *flat(*crossed)]
    fill(crossed[2:], *past)
    terms, coef = block_terms(island_live_rows, total, other, hidden, output_gradient)
    far_terms = swap(terms, top)
    near_terms = spread({0: behind(terms, *past)})
    turn(*past)
    for pieces in turned[1:2]:
        fill(pieces, *past)
    if line:
        kept = join(jnp.stack(at).astype(i32), pieces_of_kept, n_fsdp)
    else:
        kept = lax.all_gather(output_gradient, "fsdp", axis=1, tiled=True)

    relative = [both_slots[r][:count] for r in near] + [both_slots[r][count:] for r in near]
    relative = jnp.concatenate(relative) - me * local
    edge = count * len(near)
    grad_a, grad_b = add_terms(
        relative[:edge], [near_terms[r] for r in near], grad_a, grad_b
    )

    scalars = jnp.concatenate([jnp.stack([me ^ r for r in range(n_dp)]).astype(i32), island_live_rows])
    grad_hidden = token = None

    def multiply(*where):
        nonlocal grad_hidden, token
        chunks, tiles, places = [], [], []
        for shift, t in where:
            start = lax.rem(group + n_groups - shift, n_groups) * share
            places.append(start // tile + t)
            tiles.append([])
            for j, (first, size) in enumerate(parts):
                low, high = max(first, t * tile), min(first + size, (t + 1) * tile)
                if low < high:
                    if (shift, j) not in chunks:
                        chunks.append((shift, j))
                    tiles[-1].append((chunks.index((shift, j)), low - first, high - low))
        pieces = [turned[j][shift - 1] if shift else crossed[j] for shift, j in chunks]
        grad_hidden, token = base(
            places, scalars, kept, whole, pieces, tiles, tile, coef, block_a, list(range(count)),
            grad_hidden, token,
        )

    others = range(1, n_groups)
    if share > tile:
        multiply((0, 0), (0, 1), (0, 2))
        multiply((0, 3), *[(g, t) for g in others for t in range(3)])
        for pieces in turned[2:]:
            fill(pieces, token)
        early = token
        multiply(*[(g, 3) for g in others])
    else:
        multiply(*[(g, 0) for g in range(n_groups)])
        early = token

    all_far = spread({top: behind(far_terms, early)})
    grad_a, grad_b = add_terms(
        relative[edge:], [all_far[r + top] for r in near], grad_a, grad_b
    )
    return grad_hidden, jnp.swapaxes(grad_a, 1, 2), grad_b


def solution(mesh):
    placed = (
        P(("groups", "dp"), "fsdp"),
        P(("groups", "dp"), "fsdp"),
        P("fsdp", "dp"),
        P(("groups", "dp"), "fsdp", None),
        P(("groups", "dp"), None, "fsdp"),
        P(("groups", "dp")),
        P(("groups", "dp")),
        P("groups"),
    )
    sizes = [mesh.shape[name] for name in ("groups", "fsdp", "dp")]
    return jax.shard_map(
        functools.partial(on_device, *sizes),
        mesh=mesh,
        in_specs=placed,
        out_specs=(
            P(("groups", "dp"), "fsdp"),
            P(("groups", "dp"), "fsdp", None),
            P(("groups", "dp"), None, "fsdp"),
        ),
        check_vma=False,
    )
```

```python
import functools

import jax
import jax.numpy as jnp
from jax import lax
from jax.experimental import pallas as pl
from jax.experimental.pallas import tpu as pltpu
from jax.sharding import PartitionSpec as P

adapter_scale = 2.0
factor_gradient = 0.0625
vmem_bytes = 60 * 1024 * 1024
bf16, f32, i32 = jnp.bfloat16, jnp.float32, jnp.int32


def behind(value, *after):
    if not after:
        return value
    return lax.optimization_barrier((value, *after))[0]


def params(cost):
    return dict(
        compiler_params=pltpu.CompilerParams(vmem_limit_bytes=vmem_bytes),
        cost_estimate=pl.CostEstimate(flops=cost[0], bytes_accessed=cost[1], transcendentals=0),
    )


def pick_kernel(pieces, index_ref, source_ref, *refs):
    a_refs, b_refs, out_ref = refs[:pieces], refs[pieces : 2 * pieces], refs[-1]
    source = source_ref[pl.program_id(0)]
    a, b = a_refs[0][0], b_refs[0][0]
    for r in range(1, pieces):
        a = jnp.where(source == r, a_refs[r][0], a)
        b = jnp.where(source == r, b_refs[r][0], b)
    ff = a.shape[1]
    out_ref[0, :, :ff] = a
    out_ref[0, :, ff:] = b


def factor_specs(pieces, count, rank, width):
    return [
        pl.BlockSpec(
            (1, rank, width), lambda i, index, source, r=r: (index[r * count + i], 0, 0)
        )
        for r in range(pieces)
    ]


def pick(index, source, a_pieces, b_pieces):
    count, pieces = source.shape[0], len(a_pieces)
    _, rank, ff = a_pieces[0].shape
    d = b_pieces[0].shape[2]
    return pl.pallas_call(
        functools.partial(pick_kernel, pieces),
        grid_spec=pltpu.PrefetchScalarGridSpec(
            num_scalar_prefetch=2,
            grid=(count,),
            in_specs=factor_specs(pieces, count, rank, ff) + factor_specs(pieces, count, rank, d),
            out_specs=pl.BlockSpec((1, rank, ff + d), lambda i, index, source: (i, 0, 0)),
        ),
        out_shape=jax.ShapeDtypeStruct((count, rank, ff + d), bf16),
        **params((0, 2 * (pieces + 1) * count * rank * (ff + d))),
    )(index, source, *a_pieces, *b_pieces)


def project_kernel(pieces, index_ref, source_ref, *refs):
    a_refs, b_refs = refs[:pieces], refs[pieces : 2 * pieces]
    far_ref, hid_ref, grad_ref, part_ref, block_ref, grad_a_ref, grad_b_ref = refs[
        2 * pieces : 2 * pieces + 7
    ]
    zeros, zero_sem = refs[2 * pieces + 7 :]
    step = pl.program_id(0)
    source = source_ref[step]
    ff = hid_ref.shape[1]
    d = grad_ref.shape[1]

    fills = []
    for slot in range(grad_a_ref.shape[0]):
        fills.append(pltpu.make_async_copy(zeros, grad_a_ref.at[slot], zero_sem.at[2 * slot]))
        fills.append(
            pltpu.make_async_copy(
                zeros.at[:, pl.ds(0, d)], grad_b_ref.at[slot], zero_sem.at[2 * slot + 1]
            )
        )

    @pl.when(step == 0)
    def _():
        zeros[...] = jnp.zeros_like(zeros)
        for fill in fills:
            fill.start()

    a, b = far_ref[0, :, :ff], far_ref[0, :, ff:]
    for r in range(pieces):
        a = jnp.where(source == r, a_refs[r][0], a)
        b = jnp.where(source == r, b_refs[r][0], b)
    block_ref[0] = a
    over_last = (((1,), (1,)), ((), ()))
    rank = a.shape[0]
    part_ref[0, :, :rank] = lax.dot_general(
        hid_ref[...], a, over_last, preferred_element_type=f32
    )
    part_ref[0, :, rank:] = lax.dot_general(
        grad_ref[...], b, over_last, preferred_element_type=f32
    )

    @pl.when(step == pl.num_programs(0) - 1)
    def _():
        for fill in fills:
            fill.wait()


def project(index, source, a_pieces, b_pieces, far, hidden, grad):
    count, pieces = source.shape[0], len(a_pieces)
    local, rank, ff = a_pieces[0].shape
    d = b_pieces[0].shape[2]
    rows = hidden.shape[0]
    height = rows // count
    own = lambda i, index, source: (i, 0)
    own3 = lambda i, index, source: (i, 0, 0)
    return pl.pallas_call(
        functools.partial(project_kernel, pieces),
        grid_spec=pltpu.PrefetchScalarGridSpec(
            num_scalar_prefetch=2,
            grid=(count,),
            in_specs=factor_specs(pieces, count, rank, ff)
            + factor_specs(pieces, count, rank, d)
            + [
                pl.BlockSpec((1, rank, ff + d), own3),
                pl.BlockSpec((height, ff), own),
                pl.BlockSpec((height, d), own),
            ],
            out_specs=[
                pl.BlockSpec((1, height, 2 * rank), own3),
                pl.BlockSpec((1, rank, ff), own3),
                pl.BlockSpec(memory_space=pl.ANY),
                pl.BlockSpec(memory_space=pl.ANY),
            ],
            scratch_shapes=[
                pltpu.VMEM((rank, ff), f32),
                pltpu.SemaphoreType.DMA((2 * local,)),
            ],
        ),
        out_shape=[
            jax.ShapeDtypeStruct((count, height, 2 * rank), f32),
            jax.ShapeDtypeStruct((count, rank, ff), bf16),
            jax.ShapeDtypeStruct((local, rank, ff), f32),
            jax.ShapeDtypeStruct((local, rank, d), f32),
        ],
        **params((2 * rows * rank * (ff + d), 2 * (rows + (pieces + 2) * count * rank) * (ff + d))),
    )(index, source, *a_pieces, *b_pieces, far, hidden, grad)


def terms_kernel(live_ref, here_ref, there_ref, hid_ref, grad_ref, terms_ref, coef_ref):
    ff = hid_ref.shape[1]
    rank = coef_ref.shape[2]
    total = here_ref[0] + there_ref[0]
    valid = lax.broadcasted_iota(i32, total.shape, 0) < live_ref[pl.program_id(0)]
    total = jnp.where(valid, total, 0.0)
    low = total[:, :rank].astype(bf16)
    coef = (adapter_scale * total[:, rank:]).astype(bf16)
    coef_ref[0] = coef
    over_rows = (((0,), (0,)), ((), ()))
    terms_ref[0, :, :ff] = (
        factor_gradient
        * lax.dot_general(coef, hid_ref[...], over_rows, preferred_element_type=f32)
    ).astype(bf16)
    terms_ref[0, :, ff:] = (
        factor_gradient
        * adapter_scale
        * lax.dot_general(low, grad_ref[...], over_rows, preferred_element_type=f32)
    ).astype(bf16)


def block_terms(live, here, there, hidden, grad):
    count, height, both = here.shape
    rank = both // 2
    rows, ff = hidden.shape
    d = grad.shape[1]
    own = lambda i, live: (i, 0)
    own3 = lambda i, live: (i, 0, 0)
    return pl.pallas_call(
        terms_kernel,
        grid_spec=pltpu.PrefetchScalarGridSpec(
            num_scalar_prefetch=1,
            grid=(count,),
            in_specs=[
                pl.BlockSpec((1, height, both), own3),
                pl.BlockSpec((1, height, both), own3),
                pl.BlockSpec((height, ff), own),
                pl.BlockSpec((height, d), own),
            ],
            out_specs=[
                pl.BlockSpec((1, rank, ff + d), own3),
                pl.BlockSpec((1, height, rank), own3),
            ],
        ),
        out_shape=[
            jax.ShapeDtypeStruct((count, rank, ff + d), bf16),
            jax.ShapeDtypeStruct((count, height, rank), bf16),
        ],
        **params((2 * rows * rank * (ff + d), 2 * (rows + count * rank) * (ff + d))),
    )(live, here, there, hidden, grad)


def base_kernel(n_dp, tiles, n_chunks, n_kept, count, scalars_ref, *refs):
    near = n_dp // 2
    kept_refs, refs = refs[:n_kept], refs[n_kept:]
    near_refs = refs[:near]
    far_refs = refs[near : near + n_chunks * near]
    coef_ref, block_ref = refs[near + n_chunks * near : near + n_chunks * near + 2]
    out_ref, token_ref, kept, weight, factor, result = refs[-10:-4]
    kept_sem, in_sem, factor_sem, out_sem = refs[-4:]
    _, tile, depth = weight.shape
    deep = depth // n_dp
    height = coef_ref.shape[1]
    steps = len(tiles)
    token_ref[...] = jnp.zeros_like(token_ref)

    def lanes(r):
        return pl.ds(pl.multiple_of(scalars_ref[steps + r] * deep, deep), deep)

    def span(j):
        return pl.ds(pl.multiple_of(scalars_ref[j] * tile, tile), tile)

    def loads(j, slot, r):
        if r < near:
            return [
                pltpu.make_async_copy(
                    near_refs[r].at[span(j), :], weight.at[slot, :, lanes(r)], in_sem.at[slot, r, 0]
                )
            ]
        copies, low = [], 0
        for k, (chunk, start, size) in enumerate(tiles[j]):
            copies.append(
                pltpu.make_async_copy(
                    far_refs[chunk * near + r - near].at[pl.ds(start, size)],
                    weight.at[slot, pl.ds(low, size), lanes(r)],
                    in_sem.at[slot, r, k],
                )
            )
            low += size
        return copies

    def factors(j, slot):
        return pltpu.make_async_copy(
            block_ref.at[:, :, span(j)], factor.at[slot], factor_sem.at[slot]
        )

    at = [scalars_ref[steps + n_dp + count + k] for k in range(n_kept)]

    def columns(k):
        wide = kept_refs[k].shape[1]
        place = pl.ds(pl.multiple_of(at[k] * wide, wide), wide)
        return pltpu.make_async_copy(kept_refs[k], kept.at[:, place], kept_sem.at[k])

    def store(j, slot):
        return pltpu.make_async_copy(result.at[slot], out_ref.at[:, span(j)], out_sem.at[slot])

    def load(j, slot):
        for r in range(n_dp):
            for copy in loads(j, slot, r):
                copy.start()
        factors(j, slot).start()

    over_last = (((1,), (1,)), ((), ()))

    def finish(slot, total):
        for b in range(count):
            extra = jnp.dot(coef_ref[b], factor[slot, b], preferred_element_type=f32)
            here = total[b * height : (b + 1) * height] + extra
            valid = lax.broadcasted_iota(i32, here.shape, 0) < scalars_ref[steps + n_dp + b]
            result[slot, b * height : (b + 1) * height, :] = jnp.where(valid, here, 0.0).astype(
                bf16
            )

    for k in range(n_kept):
        pl.when(at[k] >= 0)(lambda k=k: columns(k).start())
    for r in range(n_dp):
        for copy in loads(0, 0, r):
            copy.start()
    factors(0, 0).start()
    if steps > 1:
        load(1, 1)
    matching = kept_refs[0].shape[1] == deep
    if not matching:
        for k in range(n_kept):
            pl.when(at[k] >= 0)(lambda k=k: columns(k).wait())
    total = None
    for r in range(n_dp):
        if matching:
            for k in range(n_kept):
                pl.when(at[k] == scalars_ref[steps + r])(lambda k=k: columns(k).wait())
        for copy in loads(0, 0, r):
            copy.wait()
        part = lax.dot_general(
            kept[:, lanes(r)], weight[0, :, lanes(r)], over_last, preferred_element_type=f32
        )
        total = part if total is None else total + part
    factors(0, 0).wait()
    finish(0, total)
    store(0, 0).start()

    @pl.loop(1, steps)
    def _(step):
        slot = lax.rem(step, 2)
        for j in range(1, steps):

            @pl.when(step == j)
            def _():
                if j + 1 < steps:
                    load(j + 1, (j + 1) % 2)
                for r in range(n_dp):
                    for copy in loads(j, j % 2, r):
                        copy.wait()
                factors(j, j % 2).wait()
                if j >= 2:
                    store(j - 2, j % 2).wait()

        finish(
            slot,
            lax.dot_general(kept[...], weight[slot], over_last, preferred_element_type=f32),
        )
        for j in range(1, steps):
            pl.when(step == j)(lambda j=j: store(j, j % 2).start())

    for j in range(max(steps - 2, 0), steps):
        store(j, j % 2).wait()


def base(places, scalars, kept, near, chunks, tiles, tile, coef, block_a, held, token):
    rows = kept[0].shape[0]
    count, rank, ff = block_a.shape
    top = len(near)
    depth = 2 * top * near[0].shape[1]
    anywhere = pl.BlockSpec(memory_space=pl.ANY)
    operands = [*kept, *[near[r] for r in range(top)]]
    for piece in chunks:
        operands += [piece[r] for r in range(top, 2 * top)]
    in_specs = [anywhere] * len(operands)
    in_specs += [pl.BlockSpec(coef.shape, lambda i, s: (0, 0, 0)), anywhere]
    operands += [coef, block_a]
    aliases = {}
    if held is not None:
        in_specs += [anywhere, anywhere]
        operands += [token, held]
        aliases = {len(operands): 0}
    most = max(len(segments) for segments in tiles)
    span = tile * len(tiles)
    return pl.pallas_call(
        functools.partial(base_kernel, 2 * top, tiles, len(chunks), len(kept), count),
        grid_spec=pltpu.PrefetchScalarGridSpec(
            num_scalar_prefetch=1,
            grid=(1,),
            in_specs=in_specs,
            out_specs=[anywhere, pl.BlockSpec((8, 128), lambda i, s: (0, 0))],
            scratch_shapes=[
                pltpu.VMEM((rows, depth), bf16),
                pltpu.VMEM((2, tile, depth), bf16),
                pltpu.VMEM((2, count, rank, tile), bf16),
                pltpu.VMEM((2, rows, tile), bf16),
                pltpu.SemaphoreType.DMA((len(kept),)),
                pltpu.SemaphoreType.DMA((2, 2 * top, most)),
                pltpu.SemaphoreType.DMA((2,)),
                pltpu.SemaphoreType.DMA((2,)),
            ],
        ),
        out_shape=[
            jax.ShapeDtypeStruct((rows, ff), bf16),
            jax.ShapeDtypeStruct((8, 128), f32),
        ],
        input_output_aliases=aliases,
        **params((1, 1)),
    )(jnp.concatenate([jnp.stack(places).astype(i32), scalars]), *operands)


def add_kernel(pieces, count, slots_ref, *refs):
    term_refs = refs[:pieces]
    a_ref, b_ref, terms, a, b, term_sem, a_sem, b_sem = refs[pieces + 3 :]
    local, _, ff = a.shape

    def load(k):
        return pltpu.make_async_copy(
            term_refs[k // count].at[k % count], terms.at[k], term_sem.at[k]
        )

    def whole(slot, inward):
        pairs = [(a_ref.at[slot], a.at[slot]), (b_ref.at[slot], b.at[slot])]
        return [
            pltpu.make_async_copy(*(pair if inward else pair[::-1]), sem.at[slot])
            for pair, sem in zip(pairs, (a_sem, b_sem))
        ]

    wanted = [slots_ref[k] for k in range(pieces * count)]
    owned = [(slot >= 0) & (slot < local) for slot in wanted]
    hit = []
    for j in range(local):
        any_here = wanted[0] == j
        for slot in wanted[1:]:
            any_here = any_here | (slot == j)
        hit.append(any_here)

    def start(copies):
        for copy in copies:
            copy.start()

    def wait(copies):
        for copy in copies:
            copy.wait()

    for j in range(local):
        pl.when(hit[j])(lambda j=j: start(whole(j, True)))
    for k in range(pieces * count):
        pl.when(owned[k])(lambda k=k: start([load(k)]))
    for j in range(local):
        pl.when(hit[j])(lambda j=j: wait(whole(j, True)))

    def add(k):
        wait([load(k)])
        a[wanted[k]] += terms[k, :, :ff].astype(f32)
        b[wanted[k]] += terms[k, :, ff:].astype(f32)

    for k in range(pieces * count):
        pl.when(owned[k])(lambda k=k: add(k))
    for j in range(local):
        pl.when(hit[j])(lambda j=j: start(whole(j, False)))
    for j in range(local):
        pl.when(hit[j])(lambda j=j: wait(whole(j, False)))


def add_terms(slots, pieces, grad_a, grad_b, token):
    count, rank, both = pieces[0].shape
    anywhere = pl.BlockSpec(memory_space=pl.ANY)
    n = len(pieces)
    local = grad_a.shape[0]
    return pl.pallas_call(
        functools.partial(add_kernel, n, count),
        grid_spec=pltpu.PrefetchScalarGridSpec(
            num_scalar_prefetch=1,
            grid=(1,),
            in_specs=[anywhere] * (n + 3),
            out_specs=[anywhere] * 2,
            scratch_shapes=[
                pltpu.VMEM((n * count, rank, both), bf16),
                pltpu.VMEM(grad_a.shape, f32),
                pltpu.VMEM(grad_b.shape, f32),
                pltpu.SemaphoreType.DMA((n * count,)),
                pltpu.SemaphoreType.DMA((local,)),
                pltpu.SemaphoreType.DMA((local,)),
            ],
        ),
        out_shape=[
            jax.ShapeDtypeStruct(grad_a.shape, f32),
            jax.ShapeDtypeStruct(grad_b.shape, f32),
        ],
        input_output_aliases={n + 2: 0, n + 3: 1},
        **params((1, 1)),
    )(slots, *pieces, token, grad_a, grad_b)


def on_device(
    n_groups,
    n_fsdp,
    n_dp,
    output_gradient,
    hidden,
    frozen_down_weight,
    adapter_first_factors,
    adapter_second_factors,
    island_live_rows,
    island_adapter_ids,
    owner_slot_adapters,
):
    rows, ff = hidden.shape
    d = output_gradient.shape[1]
    count = island_live_rows.shape[0]
    local = adapter_first_factors.shape[0]
    n_slots = owner_slot_adapters.shape[0]
    top = n_dp // 2
    me = lax.axis_index("dp")
    group = lax.axis_index("groups")

    def swap(value, bit, axis="dp", size=n_dp):
        return lax.ppermute(value, axis, [(i, i ^ bit) for i in range(size)])

    def spread(held):
        held = dict(held)
        bit = top // 2
        while bit:
            for r in list(held):
                held[r ^ bit] = swap(held[r], bit)
            bit //= 2
        return held

    match = island_adapter_ids[:, None] == owner_slot_adapters[None, :]
    slots = jnp.sum(jnp.where(match, jnp.arange(n_slots, dtype=i32)[None, :], 0), axis=1)
    far_slots = swap(slots, top)

    place = lax.axis_index("fsdp")
    line = n_fsdp <= 4
    pieces_of_kept, at = [output_gradient], [place]

    def hop(*after):
        k = len(pieces_of_kept) // 2
        if not line or k + 1 >= n_fsdp:
            return []
        right = [(i, i + 1) for i in range(n_fsdp - 1)]
        left = [(i + 1, i) for i in range(n_fsdp - 1)]
        ends = pieces_of_kept[-2:] if k else pieces_of_kept * 2
        for piece, pairs in zip(ends, (right, left)):
            pieces_of_kept.append(lax.ppermute(behind(piece, *after), "fsdp", pairs))
        at.append(place - k - 1)
        at.append(jnp.where(place + k + 1 < n_fsdp, place + k + 1, -1))
        return pieces_of_kept[-2:]

    first_hop = hop()

    share = ff // n_groups
    if share % 2048 == 0:
        unit, tile = share // 8, share // 4
        sizes = [2 * unit] * 4
    else:
        tile = share
        sizes = [share]
    parts = [(sum(sizes[:j]), size) for j, size in enumerate(sizes)]

    crossed = []
    turned = []

    def flat(*pieces):
        return [v for piece in pieces for v in piece.values()]

    def cross(*after):
        j = len(crossed)
        if j < len(parts):
            start, size = parts[j]
            piece = lax.dynamic_slice_in_dim(
                frozen_down_weight, group * share + start, size, axis=0
            )
            crossed.append({top: swap(behind(piece, *after), top)})

    def turn(*after):
        j = len(turned)
        if j < len(parts):
            piece = behind(crossed[j][top], *after)
            turned.append([])
            for shift in range(1, n_groups):
                ring = [(i, (i + shift) % n_groups) for i in range(n_groups)]
                turned[j].append({top: lax.ppermute(piece, "groups", ring)})

    def fill(chunks, *after):
        for piece in chunks:
            piece.update(spread({top: behind(piece[top], *after)}))

    cross(far_slots)

    first = jnp.swapaxes(adapter_first_factors, 1, 2)
    a_near = spread({0: first})
    b_near = spread({0: adapter_second_factors})
    near = sorted(a_near)
    a_near = [a_near[r] for r in near]
    b_near = [b_near[r] for r in near]
    def places(wanted):
        owner = wanted // local
        index = jnp.concatenate([wanted % local] * len(near))
        return index, jnp.where((owner ^ me) < top, owner ^ me, len(near))

    picked = pick(*places(far_slots), a_near, b_near)
    both_slots = spread({0: behind(jnp.concatenate([slots, far_slots]), picked)})
    past = [picked, *first_hop, *flat(both_slots, *crossed)]
    far = swap(behind(picked, *past[1:]), top)
    whole = spread({0: behind(frozen_down_weight, *past)})
    turn(*past)
    past = [far, *hop(*past), *flat(*turned[0])]

    ready = behind(slots, *flat(whole, both_slots), *past)
    part, block_a, grad_a, grad_b = project(
        *places(ready), a_near, b_near, far, hidden, output_gradient
    )
    third_hop = hop(*past)
    cross(*past)
    cross(*past)
    sums = [part]
    bit = 1
    while bit < n_fsdp:
        sums.append(swap(sums[-1], bit, "fsdp", n_fsdp))
        if 2 * bit < n_fsdp:
            sums.append(sums[-2] + sums[-1])
        bit *= 2
    total, other = sums[-2:]
    turn(part)
    past = [sums[2], *flat(*crossed[:3], *sum(turned[:2], [])), *third_hop]
    cross(*past)
    turn(*past)
    fill(crossed[:2], *past)
    past = [other, *flat(*crossed, *sum(turned, []))]
    terms, coef = block_terms(island_live_rows, total, other, hidden, output_gradient)
    far_terms = swap(terms, top)
    turn(*past)
    fill(crossed[2:3], *past)
    for pieces in turned[:2]:
        fill(pieces, *past)
    near_terms = spread({0: behind(terms, *past)})
    if line:
        at = jnp.stack(at).astype(i32)
    else:
        pieces_of_kept = [lax.all_gather(output_gradient, "fsdp", axis=1, tiled=True)]
        at = jnp.zeros((1,), i32)

    relative = [both_slots[r][:count] for r in near] + [both_slots[r][count:] for r in near]
    relative = jnp.concatenate(relative) - me * local
    edge = count * len(near)
    grad_a, grad_b = add_terms(
        relative[:edge], [near_terms[r] for r in near], grad_a, grad_b, coef[0, :8]
    )

    scalars = jnp.concatenate(
        [jnp.stack([me ^ r for r in range(n_dp)]).astype(i32), island_live_rows, at]
    )
    grad_hidden = token = None

    def multiply(*where):
        nonlocal grad_hidden, token
        chunks, tiles, places = [], [], []
        for shift, t in where:
            start = lax.rem(group + n_groups - shift, n_groups) * share
            places.append(start // tile + t)
            tiles.append([])
            for j, (first, size) in enumerate(parts):
                low, high = max(first, t * tile), min(first + size, (t + 1) * tile)
                if low < high:
                    if (shift, j) not in chunks:
                        chunks.append((shift, j))
                    tiles[-1].append((chunks.index((shift, j)), low - first, high - low))
        pieces = [turned[j][shift - 1] if shift else crossed[j] for shift, j in chunks]
        grad_hidden, token = base(
            places, scalars, pieces_of_kept, whole, pieces, tiles, tile, coef, block_a,
            grad_hidden, token,
        )

    others = range(1, n_groups)
    if share > tile:
        multiply((0, 0), (0, 1), (0, 2), *[(g, t) for g in others for t in range(2)])
        fill(crossed[3:], token)
        for pieces in turned[2:]:
            fill(pieces, token)
        scalars = behind(scalars, grad_b)
        multiply((0, 3), *[(g, t) for g in others for t in range(2, 4)])
    else:
        multiply(*[(g, 0) for g in range(n_groups)])

    all_far = spread({top: behind(far_terms, token)})
    grad_a, grad_b = add_terms(
        relative[edge:], [all_far[r + top] for r in near], grad_a, grad_b, token
    )
    return grad_hidden, jnp.swapaxes(grad_a, 1, 2), grad_b


def solution(mesh):
    placed = (
        P(("groups", "dp"), "fsdp"),
        P(("groups", "dp"), "fsdp"),
        P("fsdp", "dp"),
        P(("groups", "dp"), "fsdp", None),
        P(("groups", "dp"), None, "fsdp"),
        P(("groups", "dp")),
        P(("groups", "dp")),
        P("groups"),
    )
    sizes = [mesh.shape[name] for name in ("groups", "fsdp", "dp")]
    return jax.shard_map(
        functools.partial(on_device, *sizes),
        mesh=mesh,
        in_specs=placed,
        out_specs=(
            P(("groups", "dp"), "fsdp"),
            P(("groups", "dp"), "fsdp", None),
            P(("groups", "dp"), None, "fsdp"),
        ),
        check_vma=False,
    )
```

```python
import functools

import jax
import jax.numpy as jnp
from jax import lax
from jax.experimental import pallas as pl
from jax.experimental.pallas import tpu as pltpu
from jax.sharding import PartitionSpec as P

adapter_scale = 2.0
factor_gradient = 0.0625
vmem_bytes = 60 * 1024 * 1024
bf16, f32, i32 = jnp.bfloat16, jnp.float32, jnp.int32


def behind(value, *after):
    if not after:
        return value
    return lax.optimization_barrier((value, *after))[0]


def params(cost):
    return dict(
        compiler_params=pltpu.CompilerParams(vmem_limit_bytes=vmem_bytes),
        cost_estimate=pl.CostEstimate(flops=cost[0], bytes_accessed=cost[1], transcendentals=0),
    )


def pick_kernel(pieces, index_ref, source_ref, *refs):
    a_refs, b_refs, out_ref = refs[:pieces], refs[pieces : 2 * pieces], refs[-1]
    source = source_ref[pl.program_id(0)]
    a, b = a_refs[0][0], b_refs[0][0]
    for r in range(1, pieces):
        a = jnp.where(source == r, a_refs[r][0], a)
        b = jnp.where(source == r, b_refs[r][0], b)
    ff = a.shape[1]
    out_ref[0, :, :ff] = a
    out_ref[0, :, ff:] = b


def factor_specs(pieces, count, rank, width):
    return [
        pl.BlockSpec(
            (1, rank, width), lambda i, index, source, r=r: (index[r * count + i], 0, 0)
        )
        for r in range(pieces)
    ]


def pick(index, source, a_pieces, b_pieces):
    count, pieces = source.shape[0], len(a_pieces)
    _, rank, ff = a_pieces[0].shape
    d = b_pieces[0].shape[2]
    return pl.pallas_call(
        functools.partial(pick_kernel, pieces),
        grid_spec=pltpu.PrefetchScalarGridSpec(
            num_scalar_prefetch=2,
            grid=(count,),
            in_specs=factor_specs(pieces, count, rank, ff) + factor_specs(pieces, count, rank, d),
            out_specs=pl.BlockSpec((1, rank, ff + d), lambda i, index, source: (i, 0, 0)),
        ),
        out_shape=jax.ShapeDtypeStruct((count, rank, ff + d), bf16),
        **params((0, 2 * (pieces + 1) * count * rank * (ff + d))),
    )(index, source, *a_pieces, *b_pieces)


def project_kernel(pieces, index_ref, source_ref, *refs):
    a_refs, b_refs = refs[:pieces], refs[pieces : 2 * pieces]
    far_ref, hid_ref, grad_ref, part_ref, block_ref, grad_a_ref, grad_b_ref = refs[
        2 * pieces : 2 * pieces + 7
    ]
    zeros, zero_sem = refs[2 * pieces + 7 :]
    step = pl.program_id(0)
    source = source_ref[step]
    ff = hid_ref.shape[1]
    d = grad_ref.shape[1]

    fills = []
    for slot in range(grad_a_ref.shape[0]):
        fills.append(pltpu.make_async_copy(zeros, grad_a_ref.at[slot], zero_sem.at[2 * slot]))
        fills.append(
            pltpu.make_async_copy(
                zeros.at[:, pl.ds(0, d)], grad_b_ref.at[slot], zero_sem.at[2 * slot + 1]
            )
        )

    @pl.when(step == 0)
    def _():
        zeros[...] = jnp.zeros_like(zeros)
        for fill in fills:
            fill.start()

    a, b = far_ref[0, :, :ff], far_ref[0, :, ff:]
    for r in range(pieces):
        a = jnp.where(source == r, a_refs[r][0], a)
        b = jnp.where(source == r, b_refs[r][0], b)
    block_ref[0] = a
    over_last = (((1,), (1,)), ((), ()))
    rank = a.shape[0]
    part_ref[0, :, :rank] = lax.dot_general(
        hid_ref[...], a, over_last, preferred_element_type=f32
    )
    part_ref[0, :, rank:] = lax.dot_general(
        grad_ref[...], b, over_last, preferred_element_type=f32
    )

    @pl.when(step == pl.num_programs(0) - 1)
    def _():
        for fill in fills:
            fill.wait()


def project(index, source, a_pieces, b_pieces, far, hidden, grad):
    count, pieces = source.shape[0], len(a_pieces)
    local, rank, ff = a_pieces[0].shape
    d = b_pieces[0].shape[2]
    rows = hidden.shape[0]
    height = rows // count
    own = lambda i, index, source: (i, 0)
    own3 = lambda i, index, source: (i, 0, 0)
    return pl.pallas_call(
        functools.partial(project_kernel, pieces),
        grid_spec=pltpu.PrefetchScalarGridSpec(
            num_scalar_prefetch=2,
            grid=(count,),
            in_specs=factor_specs(pieces, count, rank, ff)
            + factor_specs(pieces, count, rank, d)
            + [
                pl.BlockSpec((1, rank, ff + d), own3),
                pl.BlockSpec((height, ff), own),
                pl.BlockSpec((height, d), own),
            ],
            out_specs=[
                pl.BlockSpec((1, height, 2 * rank), own3),
                pl.BlockSpec((1, rank, ff), own3),
                pl.BlockSpec(memory_space=pl.ANY),
                pl.BlockSpec(memory_space=pl.ANY),
            ],
            scratch_shapes=[
                pltpu.VMEM((rank, ff), f32),
                pltpu.SemaphoreType.DMA((2 * local,)),
            ],
        ),
        out_shape=[
            jax.ShapeDtypeStruct((count, height, 2 * rank), f32),
            jax.ShapeDtypeStruct((count, rank, ff), bf16),
            jax.ShapeDtypeStruct((local, rank, ff), f32),
            jax.ShapeDtypeStruct((local, rank, d), f32),
        ],
        **params((2 * rows * rank * (ff + d), 2 * (rows + (pieces + 2) * count * rank) * (ff + d))),
    )(index, source, *a_pieces, *b_pieces, far, hidden, grad)


def terms_kernel(live_ref, here_ref, there_ref, hid_ref, grad_ref, low_ref, high_ref, coef_ref):
    ff = hid_ref.shape[1]
    cut = low_ref.shape[2]
    rank = coef_ref.shape[2]
    total = here_ref[0] + there_ref[0]
    valid = lax.broadcasted_iota(i32, total.shape, 0) < live_ref[pl.program_id(0)]
    total = jnp.where(valid, total, 0.0)
    low = total[:, :rank].astype(bf16)
    coef = (adapter_scale * total[:, rank:]).astype(bf16)
    coef_ref[0] = coef
    over_rows = (((0,), (0,)), ((), ()))
    term_a = (
        factor_gradient
        * lax.dot_general(coef, hid_ref[...], over_rows, preferred_element_type=f32)
    ).astype(bf16)
    low_ref[0] = term_a[:, :cut]
    high_ref[0, :, : ff - cut] = term_a[:, cut:]
    high_ref[0, :, ff - cut :] = (
        factor_gradient
        * adapter_scale
        * lax.dot_general(low, grad_ref[...], over_rows, preferred_element_type=f32)
    ).astype(bf16)


def block_terms(live, here, there, hidden, grad):
    count, height, both = here.shape
    rank = both // 2
    rows, ff = hidden.shape
    d = grad.shape[1]
    cut = (ff + d) // 384 * 128
    own = lambda i, live: (i, 0)
    own3 = lambda i, live: (i, 0, 0)
    return pl.pallas_call(
        terms_kernel,
        grid_spec=pltpu.PrefetchScalarGridSpec(
            num_scalar_prefetch=1,
            grid=(count,),
            in_specs=[
                pl.BlockSpec((1, height, both), own3),
                pl.BlockSpec((1, height, both), own3),
                pl.BlockSpec((height, ff), own),
                pl.BlockSpec((height, d), own),
            ],
            out_specs=[
                pl.BlockSpec((1, rank, cut), own3),
                pl.BlockSpec((1, rank, ff + d - cut), own3),
                pl.BlockSpec((1, height, rank), own3),
            ],
        ),
        out_shape=[
            jax.ShapeDtypeStruct((count, rank, cut), bf16),
            jax.ShapeDtypeStruct((count, rank, ff + d - cut), bf16),
            jax.ShapeDtypeStruct((count, height, rank), bf16),
        ],
        **params((2 * rows * rank * (ff + d), 2 * (rows + count * rank) * (ff + d))),
    )(live, here, there, hidden, grad)


def base_kernel(n_dp, tiles, n_chunks, n_kept, count, scalars_ref, *refs):
    near = n_dp // 2
    kept_refs, refs = refs[:n_kept], refs[n_kept:]
    near_refs = refs[:near]
    far_refs = refs[near : near + n_chunks * near]
    coef_ref, block_ref = refs[near + n_chunks * near : near + n_chunks * near + 2]
    out_ref, token_ref, kept, weight, factor, result = refs[-10:-4]
    kept_sem, in_sem, factor_sem, out_sem = refs[-4:]
    _, tile, depth = weight.shape
    deep = depth // n_dp
    height = coef_ref.shape[1]
    steps = len(tiles)
    token_ref[...] = jnp.zeros_like(token_ref)

    def lanes(r):
        return pl.ds(pl.multiple_of(scalars_ref[steps + r] * deep, deep), deep)

    def span(j):
        return pl.ds(pl.multiple_of(scalars_ref[j] * tile, tile), tile)

    def loads(j, slot, r):
        if r < near:
            return [
                pltpu.make_async_copy(
                    near_refs[r].at[span(j), :], weight.at[slot, :, lanes(r)], in_sem.at[slot, r, 0]
                )
            ]
        copies, low = [], 0
        for k, (chunk, start, size) in enumerate(tiles[j]):
            copies.append(
                pltpu.make_async_copy(
                    far_refs[chunk * near + r - near].at[pl.ds(start, size)],
                    weight.at[slot, pl.ds(low, size), lanes(r)],
                    in_sem.at[slot, r, k],
                )
            )
            low += size
        return copies

    def factors(j, slot):
        return pltpu.make_async_copy(
            block_ref.at[:, :, span(j)], factor.at[slot], factor_sem.at[slot]
        )

    at = [scalars_ref[steps + n_dp + count + k] for k in range(n_kept)]

    def columns(k):
        wide = kept_refs[k].shape[1]
        place = pl.ds(pl.multiple_of(at[k] * wide, wide), wide)
        return pltpu.make_async_copy(kept_refs[k], kept.at[:, place], kept_sem.at[k])

    def store(j, slot):
        return pltpu.make_async_copy(result.at[slot], out_ref.at[:, span(j)], out_sem.at[slot])

    def load(j, slot):
        for r in range(n_dp):
            for copy in loads(j, slot, r):
                copy.start()
        factors(j, slot).start()

    over_last = (((1,), (1,)), ((), ()))

    def finish(slot, total):
        for b in range(count):
            extra = jnp.dot(coef_ref[b], factor[slot, b], preferred_element_type=f32)
            here = total[b * height : (b + 1) * height] + extra
            valid = lax.broadcasted_iota(i32, here.shape, 0) < scalars_ref[steps + n_dp + b]
            result[slot, b * height : (b + 1) * height, :] = jnp.where(valid, here, 0.0).astype(
                bf16
            )

    for k in range(n_kept):
        pl.when(at[k] >= 0)(lambda k=k: columns(k).start())
    for r in range(n_dp):
        for copy in loads(0, 0, r):
            copy.start()
    factors(0, 0).start()
    if steps > 1:
        load(1, 1)
    matching = kept_refs[0].shape[1] == deep
    if not matching:
        for k in range(n_kept):
            pl.when(at[k] >= 0)(lambda k=k: columns(k).wait())
    total = None
    for r in range(n_dp):
        if matching:
            for k in range(n_kept):
                pl.when(at[k] == scalars_ref[steps + r])(lambda k=k: columns(k).wait())
        for copy in loads(0, 0, r):
            copy.wait()
        part = lax.dot_general(
            kept[:, lanes(r)], weight[0, :, lanes(r)], over_last, preferred_element_type=f32
        )
        total = part if total is None else total + part
    factors(0, 0).wait()
    finish(0, total)
    store(0, 0).start()

    @pl.loop(1, steps)
    def _(step):
        slot = lax.rem(step, 2)
        for j in range(1, steps):

            @pl.when(step == j)
            def _():
                if j + 1 < steps:
                    load(j + 1, (j + 1) % 2)
                for r in range(n_dp):
                    for copy in loads(j, j % 2, r):
                        copy.wait()
                factors(j, j % 2).wait()
                if j >= 2:
                    store(j - 2, j % 2).wait()

        finish(
            slot,
            lax.dot_general(kept[...], weight[slot], over_last, preferred_element_type=f32),
        )
        for j in range(1, steps):
            pl.when(step == j)(lambda j=j: store(j, j % 2).start())

    for j in range(max(steps - 2, 0), steps):
        store(j, j % 2).wait()


def base(places, scalars, kept, near, chunks, tiles, tile, coef, block_a, held, token):
    rows = kept[0].shape[0]
    count, rank, ff = block_a.shape
    top = len(near)
    depth = 2 * top * near[0].shape[1]
    anywhere = pl.BlockSpec(memory_space=pl.ANY)
    operands = [*kept, *[near[r] for r in range(top)]]
    for piece in chunks:
        operands += [piece[r] for r in range(top, 2 * top)]
    in_specs = [anywhere] * len(operands)
    in_specs += [pl.BlockSpec(coef.shape, lambda i, s: (0, 0, 0)), anywhere]
    operands += [coef, block_a]
    aliases = {}
    if held is not None:
        in_specs += [anywhere, anywhere]
        operands += [token, held]
        aliases = {len(operands): 0}
    most = max(len(segments) for segments in tiles)
    span = tile * len(tiles)
    return pl.pallas_call(
        functools.partial(base_kernel, 2 * top, tiles, len(chunks), len(kept), count),
        grid_spec=pltpu.PrefetchScalarGridSpec(
            num_scalar_prefetch=1,
            grid=(1,),
            in_specs=in_specs,
            out_specs=[anywhere, pl.BlockSpec((8, 128), lambda i, s: (0, 0))],
            scratch_shapes=[
                pltpu.VMEM((rows, depth), bf16),
                pltpu.VMEM((2, tile, depth), bf16),
                pltpu.VMEM((2, count, rank, tile), bf16),
                pltpu.VMEM((2, rows, tile), bf16),
                pltpu.SemaphoreType.DMA((len(kept),)),
                pltpu.SemaphoreType.DMA((2, 2 * top, most)),
                pltpu.SemaphoreType.DMA((2,)),
                pltpu.SemaphoreType.DMA((2,)),
            ],
        ),
        out_shape=[
            jax.ShapeDtypeStruct((rows, ff), bf16),
            jax.ShapeDtypeStruct((8, 128), f32),
        ],
        input_output_aliases=aliases,
        **params((1, 1)),
    )(jnp.concatenate([jnp.stack(places).astype(i32), scalars]), *operands)


def add_kernel(pieces, count, slots_ref, *refs):
    term_refs = refs[: 2 * pieces]
    a_ref, b_ref, terms, a, b, term_sem, a_sem, b_sem = refs[2 * pieces + 3 :]
    local, _, ff = a.shape
    both = terms.shape[2]
    cut = term_refs[0].shape[2]

    def load(k):
        lanes = (pl.ds(0, cut), pl.ds(cut, both - cut))
        return [
            pltpu.make_async_copy(
                term_refs[k // count * 2 + part].at[k % count],
                terms.at[k, :, lanes[part]],
                term_sem.at[k, part],
            )
            for part in range(2)
        ]

    def whole(slot, inward):
        pairs = [(a_ref.at[slot], a.at[slot]), (b_ref.at[slot], b.at[slot])]
        return [
            pltpu.make_async_copy(*(pair if inward else pair[::-1]), sem.at[slot])
            for pair, sem in zip(pairs, (a_sem, b_sem))
        ]

    wanted = [slots_ref[k] for k in range(pieces * count)]
    owned = [(slot >= 0) & (slot < local) for slot in wanted]
    hit = []
    for j in range(local):
        any_here = wanted[0] == j
        for slot in wanted[1:]:
            any_here = any_here | (slot == j)
        hit.append(any_here)

    def start(copies):
        for copy in copies:
            copy.start()

    def wait(copies):
        for copy in copies:
            copy.wait()

    for j in range(local):
        pl.when(hit[j])(lambda j=j: start(whole(j, True)))
    for k in range(pieces * count):
        pl.when(owned[k])(lambda k=k: start(load(k)))
    for j in range(local):
        pl.when(hit[j])(lambda j=j: wait(whole(j, True)))

    def add(k):
        wait(load(k))
        a[wanted[k]] += terms[k, :, :ff].astype(f32)
        b[wanted[k]] += terms[k, :, ff:].astype(f32)

    for k in range(pieces * count):
        pl.when(owned[k])(lambda k=k: add(k))
    for j in range(local):
        pl.when(hit[j])(lambda j=j: start(whole(j, False)))
    for j in range(local):
        pl.when(hit[j])(lambda j=j: wait(whole(j, False)))


def add_terms(slots, pieces, grad_a, grad_b, token):
    count, rank, _ = pieces[0].shape
    both = pieces[0].shape[2] + pieces[1].shape[2]
    anywhere = pl.BlockSpec(memory_space=pl.ANY)
    n = len(pieces) // 2
    local = grad_a.shape[0]
    return pl.pallas_call(
        functools.partial(add_kernel, n, count),
        grid_spec=pltpu.PrefetchScalarGridSpec(
            num_scalar_prefetch=1,
            grid=(1,),
            in_specs=[anywhere] * (2 * n + 3),
            out_specs=[anywhere] * 2,
            scratch_shapes=[
                pltpu.VMEM((n * count, rank, both), bf16),
                pltpu.VMEM(grad_a.shape, f32),
                pltpu.VMEM(grad_b.shape, f32),
                pltpu.SemaphoreType.DMA((n * count, 2)),
                pltpu.SemaphoreType.DMA((local,)),
                pltpu.SemaphoreType.DMA((local,)),
            ],
        ),
        out_shape=[
            jax.ShapeDtypeStruct(grad_a.shape, f32),
            jax.ShapeDtypeStruct(grad_b.shape, f32),
        ],
        input_output_aliases={2 * n + 2: 0, 2 * n + 3: 1},
        **params((1, 1)),
    )(slots, *pieces, token, grad_a, grad_b)


def on_device(
    n_groups,
    n_fsdp,
    n_dp,
    output_gradient,
    hidden,
    frozen_down_weight,
    adapter_first_factors,
    adapter_second_factors,
    island_live_rows,
    island_adapter_ids,
    owner_slot_adapters,
):
    rows, ff = hidden.shape
    d = output_gradient.shape[1]
    count = island_live_rows.shape[0]
    local = adapter_first_factors.shape[0]
    n_slots = owner_slot_adapters.shape[0]
    top = n_dp // 2
    me = lax.axis_index("dp")
    group = lax.axis_index("groups")

    def swap(value, bit, axis="dp", size=n_dp):
        return lax.ppermute(value, axis, [(i, i ^ bit) for i in range(size)])

    def spread(held):
        held = dict(held)
        bit = top // 2
        while bit:
            for r in list(held):
                held[r ^ bit] = swap(held[r], bit)
            bit //= 2
        return held

    match = island_adapter_ids[:, None] == owner_slot_adapters[None, :]
    slots = jnp.sum(jnp.where(match, jnp.arange(n_slots, dtype=i32)[None, :], 0), axis=1)
    far_slots = swap(slots, top)

    place = lax.axis_index("fsdp")
    line = n_fsdp <= 4
    pieces_of_kept, at = [output_gradient], [place]

    def hop(*after):
        k = len(pieces_of_kept) // 2
        if not line or k + 1 >= n_fsdp:
            return []
        right = [(i, i + 1) for i in range(n_fsdp - 1)]
        left = [(i + 1, i) for i in range(n_fsdp - 1)]
        ends = pieces_of_kept[-2:] if k else pieces_of_kept * 2
        for piece, pairs in zip(ends, (right, left)):
            pieces_of_kept.append(lax.ppermute(behind(piece, *after), "fsdp", pairs))
        at.append(place - k - 1)
        at.append(jnp.where(place + k + 1 < n_fsdp, place + k + 1, -1))
        return pieces_of_kept[-2:]

    first_hop = hop()

    share = ff // n_groups
    if share % 2048 == 0:
        unit, tile = share // 8, share // 4
        sizes = [2 * unit] * 4
    else:
        tile = share
        sizes = [share]
    parts = [(sum(sizes[:j]), size) for j, size in enumerate(sizes)]

    crossed = []
    turned = []

    def flat(*pieces):
        return [v for piece in pieces for v in piece.values()]

    def cross(*after):
        j = len(crossed)
        if j < len(parts):
            start, size = parts[j]
            piece = lax.dynamic_slice_in_dim(
                frozen_down_weight, group * share + start, size, axis=0
            )
            crossed.append({top: swap(behind(piece, *after), top)})

    def turn(*after):
        j = len(turned)
        if j < len(parts):
            piece = behind(crossed[j][top], *after)
            turned.append([])
            for shift in range(1, n_groups):
                ring = [(i, (i + shift) % n_groups) for i in range(n_groups)]
                turned[j].append({top: lax.ppermute(piece, "groups", ring)})

    def fill(chunks, *after):
        for piece in chunks:
            piece.update(spread({top: behind(piece[top], *after)}))

    cross(far_slots)

    first = jnp.swapaxes(adapter_first_factors, 1, 2)
    a_near = spread({0: first})
    b_near = spread({0: adapter_second_factors})
    near = sorted(a_near)
    a_near = [a_near[r] for r in near]
    b_near = [b_near[r] for r in near]
    def places(wanted):
        owner = wanted // local
        index = jnp.concatenate([wanted % local] * len(near))
        return index, jnp.where((owner ^ me) < top, owner ^ me, len(near))

    picked = pick(*places(far_slots), a_near, b_near)
    both_slots = spread({0: behind(jnp.concatenate([slots, far_slots]), picked)})
    past = [picked, *first_hop, *flat(both_slots, *crossed)]
    far = swap(behind(picked, *past[1:]), top)
    whole = spread({0: behind(frozen_down_weight, *past)})
    turn(*past)
    past = [far, *hop(*past), *flat(*turned[0])]

    ready = behind(slots, *flat(whole, both_slots), *past)
    part, block_a, grad_a, grad_b = project(
        *places(ready), a_near, b_near, far, hidden, output_gradient
    )
    cross(*past)
    cross(*past)
    sums = [part]
    bit = 1
    while bit < n_fsdp:
        sums.append(swap(sums[-1], bit, "fsdp", n_fsdp))
        if 2 * bit < n_fsdp:
            sums.append(sums[-2] + sums[-1])
        bit *= 2
    total, other = sums[-2:]
    past = [sums[2], *flat(*crossed[1:2])]
    turn(*past)
    fill(crossed[:1], *past)
    fill(turned[0], *past)
    past = [other, *flat(*crossed, *sum(turned, []))]
    third_hop = hop(*past)
    cross(*past)
    turn(*past)
    low_terms, high_terms, coef = block_terms(
        island_live_rows, total, other, hidden, output_gradient
    )
    far_low = swap(behind(low_terms, *flat(*crossed)), top)
    past = flat(*crossed[3:])
    fill(crossed[1:], *past)
    for pieces in turned[1:3]:
        fill(pieces, *past)
    past = [far_low, *third_hop, *flat(*crossed, *sum(turned, []))]
    far_high = swap(behind(high_terms, *past), top)
    turn(*past)
    if line:
        at = jnp.stack(at).astype(i32)
    else:
        pieces_of_kept = [lax.all_gather(output_gradient, "fsdp", axis=1, tiled=True)]
        at = jnp.zeros((1,), i32)

    relative = [both_slots[r][:count] for r in near] + [both_slots[r][count:] for r in near]
    relative = jnp.concatenate(relative) - me * local

    scalars = jnp.concatenate(
        [jnp.stack([me ^ r for r in range(n_dp)]).astype(i32), island_live_rows, at]
    )
    grad_hidden = token = None

    def multiply(*where):
        nonlocal grad_hidden, token
        chunks, tiles, places = [], [], []
        for shift, t in where:
            start = lax.rem(group + n_groups - shift, n_groups) * share
            places.append(start // tile + t)
            tiles.append([])
            for j, (first, size) in enumerate(parts):
                low, high = max(first, t * tile), min(first + size, (t + 1) * tile)
                if low < high:
                    if (shift, j) not in chunks:
                        chunks.append((shift, j))
                    tiles[-1].append((chunks.index((shift, j)), low - first, high - low))
        pieces = [turned[j][shift - 1] if shift else crossed[j] for shift, j in chunks]
        grad_hidden, token = base(
            places, scalars, pieces_of_kept, whole, pieces, tiles, tile, coef, block_a,
            grad_hidden, token,
        )

    others = range(1, n_groups)
    if share > tile:
        multiply(*[(0, t) for t in range(4)], *[(g, t) for g in others for t in range(3)])
        past = [token, far_high]
        for pieces in turned[3:]:
            fill(pieces, *past)
        multiply(*[(g, 3) for g in others])
    else:
        multiply(*[(g, 0) for g in range(n_groups)])

    near_low = spread({0: behind(low_terms, *past)})
    near_high = spread({0: behind(high_terms, *past)})
    all_low = spread({top: behind(far_low, token)})
    all_high = spread({top: behind(far_high, token)})
    terms = [p for r in near for p in (near_low[r], near_high[r])]
    terms += [p for r in near for p in (all_low[r + top], all_high[r + top])]
    grad_a, grad_b = add_terms(relative, terms, grad_a, grad_b, token)
    return grad_hidden, jnp.swapaxes(grad_a, 1, 2), grad_b


def solution(mesh):
    placed = (
        P(("groups", "dp"), "fsdp"),
        P(("groups", "dp"), "fsdp"),
        P("fsdp", "dp"),
        P(("groups", "dp"), "fsdp", None),
        P(("groups", "dp"), None, "fsdp"),
        P(("groups", "dp")),
        P(("groups", "dp")),
        P("groups"),
    )
    sizes = [mesh.shape[name] for name in ("groups", "fsdp", "dp")]
    return jax.shard_map(
        functools.partial(on_device, *sizes),
        mesh=mesh,
        in_specs=placed,
        out_specs=(
            P(("groups", "dp"), "fsdp"),
            P(("groups", "dp"), "fsdp", None),
            P(("groups", "dp"), None, "fsdp"),
        ),
        check_vma=False,
    )
```

```python
import functools

import jax
import jax.numpy as jnp
from jax import lax
from jax.experimental import pallas as pl
from jax.experimental.pallas import tpu as pltpu
from jax.sharding import PartitionSpec as P

adapter_scale = 2.0
factor_gradient = 0.0625
vmem_bytes = 60 * 1024 * 1024
bf16, f32, i32 = jnp.bfloat16, jnp.float32, jnp.int32


def behind(value, *after):
    if not after:
        return value
    return lax.optimization_barrier((value, *after))[0]


def params(cost):
    return dict(
        compiler_params=pltpu.CompilerParams(vmem_limit_bytes=vmem_bytes),
        cost_estimate=pl.CostEstimate(flops=cost[0], bytes_accessed=cost[1], transcendentals=0),
    )


def pick_kernel(pieces, index_ref, source_ref, *refs):
    a_refs, b_refs, out_ref = refs[:pieces], refs[pieces : 2 * pieces], refs[-1]
    source = source_ref[pl.program_id(0)]
    a, b = a_refs[0][0], b_refs[0][0]
    for r in range(1, pieces):
        a = jnp.where(source == r, a_refs[r][0], a)
        b = jnp.where(source == r, b_refs[r][0], b)
    ff = a.shape[1]
    out_ref[0, :, :ff] = a
    out_ref[0, :, ff:] = b


def factor_specs(pieces, count, rank, width):
    return [
        pl.BlockSpec(
            (1, rank, width), lambda i, index, source, r=r: (index[r * count + i], 0, 0)
        )
        for r in range(pieces)
    ]


def pick(index, source, a_pieces, b_pieces):
    count, pieces = source.shape[0], len(a_pieces)
    _, rank, ff = a_pieces[0].shape
    d = b_pieces[0].shape[2]
    return pl.pallas_call(
        functools.partial(pick_kernel, pieces),
        grid_spec=pltpu.PrefetchScalarGridSpec(
            num_scalar_prefetch=2,
            grid=(count,),
            in_specs=factor_specs(pieces, count, rank, ff) + factor_specs(pieces, count, rank, d),
            out_specs=pl.BlockSpec((1, rank, ff + d), lambda i, index, source: (i, 0, 0)),
        ),
        out_shape=jax.ShapeDtypeStruct((count, rank, ff + d), bf16),
        **params((0, 2 * (pieces + 1) * count * rank * (ff + d))),
    )(index, source, *a_pieces, *b_pieces)


def project_kernel(pieces, index_ref, source_ref, *refs):
    a_refs, b_refs = refs[:pieces], refs[pieces : 2 * pieces]
    far_ref, hid_ref, grad_ref, part_ref, block_ref, grad_a_ref, grad_b_ref = refs[
        2 * pieces : 2 * pieces + 7
    ]
    zeros, zero_sem = refs[2 * pieces + 7 :]
    step = pl.program_id(0)
    source = source_ref[step]
    ff = hid_ref.shape[1]
    d = grad_ref.shape[1]

    fills = []
    for slot in range(grad_a_ref.shape[0]):
        fills.append(pltpu.make_async_copy(zeros, grad_a_ref.at[slot], zero_sem.at[2 * slot]))
        fills.append(
            pltpu.make_async_copy(
                zeros.at[:, pl.ds(0, d)], grad_b_ref.at[slot], zero_sem.at[2 * slot + 1]
            )
        )

    @pl.when(step == 0)
    def _():
        zeros[...] = jnp.zeros_like(zeros)
        for fill in fills:
            fill.start()

    a, b = far_ref[0, :, :ff], far_ref[0, :, ff:]
    for r in range(pieces):
        a = jnp.where(source == r, a_refs[r][0], a)
        b = jnp.where(source == r, b_refs[r][0], b)
    block_ref[0] = a
    over_last = (((1,), (1,)), ((), ()))
    rank = a.shape[0]
    part_ref[0, :, :rank] = lax.dot_general(
        hid_ref[...], a, over_last, preferred_element_type=f32
    )
    part_ref[0, :, rank:] = lax.dot_general(
        grad_ref[...], b, over_last, preferred_element_type=f32
    )

    @pl.when(step == pl.num_programs(0) - 1)
    def _():
        for fill in fills:
            fill.wait()


def project(index, source, a_pieces, b_pieces, far, hidden, grad):
    count, pieces = source.shape[0], len(a_pieces)
    local, rank, ff = a_pieces[0].shape
    d = b_pieces[0].shape[2]
    rows = hidden.shape[0]
    height = rows // count
    own = lambda i, index, source: (i, 0)
    own3 = lambda i, index, source: (i, 0, 0)
    return pl.pallas_call(
        functools.partial(project_kernel, pieces),
        grid_spec=pltpu.PrefetchScalarGridSpec(
            num_scalar_prefetch=2,
            grid=(count,),
            in_specs=factor_specs(pieces, count, rank, ff)
            + factor_specs(pieces, count, rank, d)
            + [
                pl.BlockSpec((1, rank, ff + d), own3),
                pl.BlockSpec((height, ff), own),
                pl.BlockSpec((height, d), own),
            ],
            out_specs=[
                pl.BlockSpec((1, height, 2 * rank), own3),
                pl.BlockSpec((1, rank, ff), own3),
                pl.BlockSpec(memory_space=pl.ANY),
                pl.BlockSpec(memory_space=pl.ANY),
            ],
            scratch_shapes=[
                pltpu.VMEM((rank, ff), f32),
                pltpu.SemaphoreType.DMA((2 * local,)),
            ],
        ),
        out_shape=[
            jax.ShapeDtypeStruct((count, height, 2 * rank), f32),
            jax.ShapeDtypeStruct((count, rank, ff), bf16),
            jax.ShapeDtypeStruct((local, rank, ff), f32),
            jax.ShapeDtypeStruct((local, rank, d), f32),
        ],
        **params((2 * rows * rank * (ff + d), 2 * (rows + (pieces + 2) * count * rank) * (ff + d))),
    )(index, source, *a_pieces, *b_pieces, far, hidden, grad)


def terms_kernel(live_ref, here_ref, there_ref, hid_ref, grad_ref, low_ref, high_ref, coef_ref):
    ff = hid_ref.shape[1]
    cut = low_ref.shape[2]
    rank = coef_ref.shape[2]
    total = here_ref[0] + there_ref[0]
    valid = lax.broadcasted_iota(i32, total.shape, 0) < live_ref[pl.program_id(0)]
    total = jnp.where(valid, total, 0.0)
    low = total[:, :rank].astype(bf16)
    coef = (adapter_scale * total[:, rank:]).astype(bf16)
    coef_ref[0] = coef
    over_rows = (((0,), (0,)), ((), ()))
    term_a = (
        factor_gradient
        * lax.dot_general(coef, hid_ref[...], over_rows, preferred_element_type=f32)
    ).astype(bf16)
    low_ref[0] = term_a[:, :cut]
    high_ref[0, :, : ff - cut] = term_a[:, cut:]
    high_ref[0, :, ff - cut :] = (
        factor_gradient
        * adapter_scale
        * lax.dot_general(low, grad_ref[...], over_rows, preferred_element_type=f32)
    ).astype(bf16)


def block_terms(live, here, there, hidden, grad):
    count, height, both = here.shape
    rank = both // 2
    rows, ff = hidden.shape
    d = grad.shape[1]
    cut = (ff + d) // 384 * 128
    own = lambda i, live: (i, 0)
    own3 = lambda i, live: (i, 0, 0)
    return pl.pallas_call(
        terms_kernel,
        grid_spec=pltpu.PrefetchScalarGridSpec(
            num_scalar_prefetch=1,
            grid=(count,),
            in_specs=[
                pl.BlockSpec((1, height, both), own3),
                pl.BlockSpec((1, height, both), own3),
                pl.BlockSpec((height, ff), own),
                pl.BlockSpec((height, d), own),
            ],
            out_specs=[
                pl.BlockSpec((1, rank, cut), own3),
                pl.BlockSpec((1, rank, ff + d - cut), own3),
                pl.BlockSpec((1, height, rank), own3),
            ],
        ),
        out_shape=[
            jax.ShapeDtypeStruct((count, rank, cut), bf16),
            jax.ShapeDtypeStruct((count, rank, ff + d - cut), bf16),
            jax.ShapeDtypeStruct((count, height, rank), bf16),
        ],
        **params((2 * rows * rank * (ff + d), 2 * (rows + count * rank) * (ff + d))),
    )(live, here, there, hidden, grad)


def base_kernel(n_dp, tiles, n_chunks, n_kept, count, scalars_ref, *refs):
    near = n_dp // 2
    kept_refs, refs = refs[:n_kept], refs[n_kept:]
    near_refs = refs[:near]
    far_refs = refs[near : near + n_chunks * near]
    coef_ref, block_ref = refs[near + n_chunks * near : near + n_chunks * near + 2]
    out_ref, token_ref, kept, weight, factor, result = refs[-10:-4]
    kept_sem, in_sem, factor_sem, out_sem = refs[-4:]
    _, tile, depth = weight.shape
    deep = depth // n_dp
    height = coef_ref.shape[1]
    steps = len(tiles)
    token_ref[...] = jnp.zeros_like(token_ref)

    def lanes(r):
        return pl.ds(pl.multiple_of(scalars_ref[steps + r] * deep, deep), deep)

    def span(j):
        return pl.ds(pl.multiple_of(scalars_ref[j] * tile, tile), tile)

    def loads(j, slot, r):
        if r < near:
            return [
                pltpu.make_async_copy(
                    near_refs[r].at[span(j), :], weight.at[slot, :, lanes(r)], in_sem.at[slot, r, 0]
                )
            ]
        copies, low = [], 0
        for k, (chunk, start, size) in enumerate(tiles[j]):
            copies.append(
                pltpu.make_async_copy(
                    far_refs[chunk * near + r - near].at[pl.ds(start, size)],
                    weight.at[slot, pl.ds(low, size), lanes(r)],
                    in_sem.at[slot, r, k],
                )
            )
            low += size
        return copies

    def factors(j, slot):
        return pltpu.make_async_copy(
            block_ref.at[:, :, span(j)], factor.at[slot], factor_sem.at[slot]
        )

    at = [scalars_ref[steps + n_dp + count + k] for k in range(n_kept)]

    def columns(k):
        wide = kept_refs[k].shape[1]
        place = pl.ds(pl.multiple_of(at[k] * wide, wide), wide)
        return pltpu.make_async_copy(kept_refs[k], kept.at[:, place], kept_sem.at[k])

    def store(j, slot):
        return pltpu.make_async_copy(result.at[slot], out_ref.at[:, span(j)], out_sem.at[slot])

    def load(j, slot):
        for r in range(n_dp):
            for copy in loads(j, slot, r):
                copy.start()
        factors(j, slot).start()

    over_last = (((1,), (1,)), ((), ()))

    def finish(slot, total):
        for b in range(count):
            extra = jnp.dot(coef_ref[b], factor[slot, b], preferred_element_type=f32)
            here = total[b * height : (b + 1) * height] + extra
            valid = lax.broadcasted_iota(i32, here.shape, 0) < scalars_ref[steps + n_dp + b]
            result[slot, b * height : (b + 1) * height, :] = jnp.where(valid, here, 0.0).astype(
                bf16
            )

    for k in range(n_kept):
        pl.when(at[k] >= 0)(lambda k=k: columns(k).start())
    for r in range(n_dp):
        for copy in loads(0, 0, r):
            copy.start()
    factors(0, 0).start()
    if steps > 1:
        load(1, 1)
    matching = kept_refs[0].shape[1] == deep
    if not matching:
        for k in range(n_kept):
            pl.when(at[k] >= 0)(lambda k=k: columns(k).wait())
    total = None
    for r in range(n_dp):
        if matching:
            for k in range(n_kept):
                pl.when(at[k] == scalars_ref[steps + r])(lambda k=k: columns(k).wait())
        for copy in loads(0, 0, r):
            copy.wait()
        part = lax.dot_general(
            kept[:, lanes(r)], weight[0, :, lanes(r)], over_last, preferred_element_type=f32
        )
        total = part if total is None else total + part
    factors(0, 0).wait()
    finish(0, total)
    store(0, 0).start()

    @pl.loop(1, steps)
    def _(step):
        slot = lax.rem(step, 2)
        for j in range(1, steps):

            @pl.when(step == j)
            def _():
                if j + 1 < steps:
                    load(j + 1, (j + 1) % 2)
                for r in range(n_dp):
                    for copy in loads(j, j % 2, r):
                        copy.wait()
                factors(j, j % 2).wait()
                if j >= 2:
                    store(j - 2, j % 2).wait()

        finish(
            slot,
            lax.dot_general(kept[...], weight[slot], over_last, preferred_element_type=f32),
        )
        for j in range(1, steps):
            pl.when(step == j)(lambda j=j: store(j, j % 2).start())

    for j in range(max(steps - 2, 0), steps):
        store(j, j % 2).wait()


def base(places, scalars, kept, near, chunks, tiles, tile, coef, block_a, held, token):
    rows = kept[0].shape[0]
    count, rank, ff = block_a.shape
    top = len(near)
    depth = 2 * top * near[0].shape[1]
    anywhere = pl.BlockSpec(memory_space=pl.ANY)
    operands = [*kept, *[near[r] for r in range(top)]]
    for piece in chunks:
        operands += [piece[r] for r in range(top, 2 * top)]
    in_specs = [anywhere] * len(operands)
    in_specs += [pl.BlockSpec(coef.shape, lambda i, s: (0, 0, 0)), anywhere]
    operands += [coef, block_a]
    aliases = {}
    if held is not None:
        in_specs += [anywhere, anywhere]
        operands += [token, held]
        aliases = {len(operands): 0}
    most = max(len(segments) for segments in tiles)
    span = tile * len(tiles)
    return pl.pallas_call(
        functools.partial(base_kernel, 2 * top, tiles, len(chunks), len(kept), count),
        grid_spec=pltpu.PrefetchScalarGridSpec(
            num_scalar_prefetch=1,
            grid=(1,),
            in_specs=in_specs,
            out_specs=[anywhere, pl.BlockSpec((8, 128), lambda i, s: (0, 0))],
            scratch_shapes=[
                pltpu.VMEM((rows, depth), bf16),
                pltpu.VMEM((2, tile, depth), bf16),
                pltpu.VMEM((2, count, rank, tile), bf16),
                pltpu.VMEM((2, rows, tile), bf16),
                pltpu.SemaphoreType.DMA((len(kept),)),
                pltpu.SemaphoreType.DMA((2, 2 * top, most)),
                pltpu.SemaphoreType.DMA((2,)),
                pltpu.SemaphoreType.DMA((2,)),
            ],
        ),
        out_shape=[
            jax.ShapeDtypeStruct((rows, ff), bf16),
            jax.ShapeDtypeStruct((8, 128), f32),
        ],
        input_output_aliases=aliases,
        **params((1, 1)),
    )(jnp.concatenate([jnp.stack(places).astype(i32), scalars]), *operands)


def add_kernel(pieces, count, slots_ref, *refs):
    term_refs = refs[: 2 * pieces]
    a_ref, b_ref, terms, a, b, term_sem, a_sem, b_sem = refs[2 * pieces + 3 :]
    local, _, ff = a.shape
    both = terms.shape[2]
    cut = term_refs[0].shape[2]

    def load(k):
        lanes = (pl.ds(0, cut), pl.ds(cut, both - cut))
        return [
            pltpu.make_async_copy(
                term_refs[k // count * 2 + part].at[k % count],
                terms.at[k, :, lanes[part]],
                term_sem.at[k, part],
            )
            for part in range(2)
        ]

    def whole(slot, inward):
        pairs = [(a_ref.at[slot], a.at[slot]), (b_ref.at[slot], b.at[slot])]
        return [
            pltpu.make_async_copy(*(pair if inward else pair[::-1]), sem.at[slot])
            for pair, sem in zip(pairs, (a_sem, b_sem))
        ]

    wanted = [slots_ref[k] for k in range(pieces * count)]
    owned = [(slot >= 0) & (slot < local) for slot in wanted]
    hit = []
    for j in range(local):
        any_here = wanted[0] == j
        for slot in wanted[1:]:
            any_here = any_here | (slot == j)
        hit.append(any_here)

    def start(copies):
        for copy in copies:
            copy.start()

    def wait(copies):
        for copy in copies:
            copy.wait()

    for j in range(local):
        pl.when(hit[j])(lambda j=j: start(whole(j, True)))
    for k in range(pieces * count):
        pl.when(owned[k])(lambda k=k: start(load(k)))
    for j in range(local):
        pl.when(hit[j])(lambda j=j: wait(whole(j, True)))

    def add(k):
        wait(load(k))
        a[wanted[k]] += terms[k, :, :ff].astype(f32)
        b[wanted[k]] += terms[k, :, ff:].astype(f32)

    for k in range(pieces * count):
        pl.when(owned[k])(lambda k=k: add(k))
    for j in range(local):
        pl.when(hit[j])(lambda j=j: start(whole(j, False)))
    for j in range(local):
        pl.when(hit[j])(lambda j=j: wait(whole(j, False)))


def add_terms(slots, pieces, grad_a, grad_b, token):
    count, rank, _ = pieces[0].shape
    both = pieces[0].shape[2] + pieces[1].shape[2]
    anywhere = pl.BlockSpec(memory_space=pl.ANY)
    n = len(pieces) // 2
    local = grad_a.shape[0]
    return pl.pallas_call(
        functools.partial(add_kernel, n, count),
        grid_spec=pltpu.PrefetchScalarGridSpec(
            num_scalar_prefetch=1,
            grid=(1,),
            in_specs=[anywhere] * (2 * n + 3),
            out_specs=[anywhere] * 2,
            scratch_shapes=[
                pltpu.VMEM((n * count, rank, both), bf16),
                pltpu.VMEM(grad_a.shape, f32),
                pltpu.VMEM(grad_b.shape, f32),
                pltpu.SemaphoreType.DMA((n * count, 2)),
                pltpu.SemaphoreType.DMA((local,)),
                pltpu.SemaphoreType.DMA((local,)),
            ],
        ),
        out_shape=[
            jax.ShapeDtypeStruct(grad_a.shape, f32),
            jax.ShapeDtypeStruct(grad_b.shape, f32),
        ],
        input_output_aliases={2 * n + 2: 0, 2 * n + 3: 1},
        **params((1, 1)),
    )(slots, *pieces, token, grad_a, grad_b)


def on_device(
    n_groups,
    n_fsdp,
    n_dp,
    output_gradient,
    hidden,
    frozen_down_weight,
    adapter_first_factors,
    adapter_second_factors,
    island_live_rows,
    island_adapter_ids,
    owner_slot_adapters,
):
    rows, ff = hidden.shape
    d = output_gradient.shape[1]
    count = island_live_rows.shape[0]
    local = adapter_first_factors.shape[0]
    n_slots = owner_slot_adapters.shape[0]
    top = n_dp // 2
    me = lax.axis_index("dp")
    group = lax.axis_index("groups")

    def swap(value, bit, axis="dp", size=n_dp):
        return lax.ppermute(value, axis, [(i, i ^ bit) for i in range(size)])

    def spread(held):
        held = dict(held)
        bit = top // 2
        while bit:
            for r in list(held):
                held[r ^ bit] = swap(held[r], bit)
            bit //= 2
        return held

    match = island_adapter_ids[:, None] == owner_slot_adapters[None, :]
    slots = jnp.sum(jnp.where(match, jnp.arange(n_slots, dtype=i32)[None, :], 0), axis=1)
    far_slots = swap(slots, top)

    place = lax.axis_index("fsdp")
    line = n_fsdp <= 4
    pieces_of_kept, at = [output_gradient], [place]

    def hop(*after):
        k = len(pieces_of_kept) // 2
        if not line or k + 1 >= n_fsdp:
            return []
        right = [(i, i + 1) for i in range(n_fsdp - 1)]
        left = [(i + 1, i) for i in range(n_fsdp - 1)]
        ends = pieces_of_kept[-2:] if k else pieces_of_kept * 2
        for piece, pairs in zip(ends, (right, left)):
            pieces_of_kept.append(lax.ppermute(behind(piece, *after), "fsdp", pairs))
        at.append(place - k - 1)
        at.append(jnp.where(place + k + 1 < n_fsdp, place + k + 1, -1))
        return pieces_of_kept[-2:]

    first_hop = hop()

    share = ff // n_groups
    if share % 2048 == 0:
        unit, tile = share // 8, share // 4
        sizes = [2 * unit] * 4
    else:
        tile = share
        sizes = [share]
    parts = [(sum(sizes[:j]), size) for j, size in enumerate(sizes)]

    crossed = []
    turned = []

    def flat(*pieces):
        return [v for piece in pieces for v in piece.values()]

    def cross(*after):
        j = len(crossed)
        if j < len(parts):
            start, size = parts[j]
            piece = lax.dynamic_slice_in_dim(
                frozen_down_weight, group * share + start, size, axis=0
            )
            crossed.append({top: swap(behind(piece, *after), top)})

    def turn(*after):
        j = len(turned)
        if j < len(parts):
            piece = behind(crossed[j][top], *after)
            turned.append([])
            for shift in range(1, n_groups):
                ring = [(i, (i + shift) % n_groups) for i in range(n_groups)]
                turned[j].append({top: lax.ppermute(piece, "groups", ring)})

    def fill(chunks, *after):
        for piece in chunks:
            piece.update(spread({top: behind(piece[top], *after)}))

    first = jnp.swapaxes(adapter_first_factors, 1, 2)
    a_near = spread({0: first})
    b_near = spread({0: adapter_second_factors})
    near = sorted(a_near)
    a_near = [a_near[r] for r in near]
    b_near = [b_near[r] for r in near]
    def places(wanted):
        owner = wanted // local
        index = jnp.concatenate([wanted % local] * len(near))
        return index, jnp.where((owner ^ me) < top, owner ^ me, len(near))

    picked = pick(*places(far_slots), a_near, b_near)
    far = swap(picked, top)
    whole = spread({0: behind(frozen_down_weight, picked)})
    both_slots = spread({0: behind(jnp.concatenate([slots, far_slots]), picked)})
    past = [far, *first_hop, *flat(whole, both_slots)]
    part, block_a, grad_a, grad_b = project(
        *places(behind(slots, *past)), a_near, b_near, far, hidden, output_gradient
    )
    second_hop = hop(*past)
    cross(*past)
    cross(*past)
    sums = [part]
    bit = 1
    while bit < n_fsdp:
        sums.append(swap(sums[-1], bit, "fsdp", n_fsdp))
        if 2 * bit < n_fsdp:
            sums.append(sums[-2] + sums[-1])
        bit *= 2
    total, other = sums[-2:]
    turn(*past)
    past = [sums[2], *second_hop, *flat(*crossed, *sum(turned, []))]
    cross(*past)
    turn(*past)
    fill(crossed[:1], *past)
    fill(turned[0], *past)
    past = [other, *flat(*crossed, *sum(turned, []))]
    third_hop = hop(*past)
    cross(*past)
    turn(*past)
    low_terms, high_terms, coef = block_terms(
        island_live_rows, total, other, hidden, output_gradient
    )
    far_low = swap(behind(low_terms, *flat(*crossed)), top)
    past = flat(*crossed[3:])
    turn(low_terms, *past)
    fill(crossed[1:], *past)
    for pieces in turned[1:3]:
        fill(pieces, *past)
    past = [far_low, *third_hop, *flat(*crossed, *sum(turned, []))]
    far_high = swap(behind(high_terms, *past), top)
    if line:
        at = jnp.stack(at).astype(i32)
    else:
        pieces_of_kept = [lax.all_gather(output_gradient, "fsdp", axis=1, tiled=True)]
        at = jnp.zeros((1,), i32)

    relative = [both_slots[r][:count] for r in near] + [both_slots[r][count:] for r in near]
    relative = jnp.concatenate(relative) - me * local

    scalars = jnp.concatenate(
        [jnp.stack([me ^ r for r in range(n_dp)]).astype(i32), island_live_rows, at]
    )
    grad_hidden = token = None

    def multiply(*where):
        nonlocal grad_hidden, token
        chunks, tiles, places = [], [], []
        for shift, t in where:
            start = lax.rem(group + n_groups - shift, n_groups) * share
            places.append(start // tile + t)
            tiles.append([])
            for j, (first, size) in enumerate(parts):
                low, high = max(first, t * tile), min(first + size, (t + 1) * tile)
                if low < high:
                    if (shift, j) not in chunks:
                        chunks.append((shift, j))
                    tiles[-1].append((chunks.index((shift, j)), low - first, high - low))
        pieces = [turned[j][shift - 1] if shift else crossed[j] for shift, j in chunks]
        grad_hidden, token = base(
            places, scalars, pieces_of_kept, whole, pieces, tiles, tile, coef, block_a,
            grad_hidden, token,
        )

    others = range(1, n_groups)
    if share > tile:
        multiply(*[(0, t) for t in range(4)], *[(g, t) for g in others for t in range(3)])
        past = [token, far_high]
        for pieces in turned[3:]:
            fill(pieces, *past)
        multiply(*[(g, 3) for g in others])
    else:
        multiply(*[(g, 0) for g in range(n_groups)])

    near_low = spread({0: behind(low_terms, *past)})
    near_high = spread({0: behind(high_terms, *past)})
    all_low = spread({top: behind(far_low, token)})
    all_high = spread({top: behind(far_high, token)})
    terms = [p for r in near for p in (near_low[r], near_high[r])]
    terms += [p for r in near for p in (all_low[r + top], all_high[r + top])]
    grad_a, grad_b = add_terms(relative, terms, grad_a, grad_b, token)
    return grad_hidden, jnp.swapaxes(grad_a, 1, 2), grad_b


def solution(mesh):
    placed = (
        P(("groups", "dp"), "fsdp"),
        P(("groups", "dp"), "fsdp"),
        P("fsdp", "dp"),
        P(("groups", "dp"), "fsdp", None),
        P(("groups", "dp"), None, "fsdp"),
        P(("groups", "dp")),
        P(("groups", "dp")),
        P("groups"),
    )
    sizes = [mesh.shape[name] for name in ("groups", "fsdp", "dp")]
    return jax.shard_map(
        functools.partial(on_device, *sizes),
        mesh=mesh,
        in_specs=placed,
        out_specs=(
            P(("groups", "dp"), "fsdp"),
            P(("groups", "dp"), "fsdp", None),
            P(("groups", "dp"), None, "fsdp"),
        ),
        check_vma=False,
    )
```

```python
import functools

import jax
import jax.numpy as jnp
from jax import lax
from jax.experimental import pallas as pl
from jax.experimental.pallas import tpu as pltpu
from jax.sharding import PartitionSpec as P

adapter_scale = 2.0
factor_gradient = 0.0625
vmem_bytes = 60 * 1024 * 1024
bf16, f32, i32 = jnp.bfloat16, jnp.float32, jnp.int32


def behind(value, *after):
    if not after:
        return value
    return lax.optimization_barrier((value, *after))[0]


def params(cost):
    return dict(
        compiler_params=pltpu.CompilerParams(vmem_limit_bytes=vmem_bytes),
        cost_estimate=pl.CostEstimate(flops=cost[0], bytes_accessed=cost[1], transcendentals=0),
    )


def pick_kernel(pieces, index_ref, source_ref, *refs):
    a_refs, b_refs, out_ref = refs[:pieces], refs[pieces : 2 * pieces], refs[-1]
    source = source_ref[pl.program_id(0)]
    a, b = a_refs[0][0], b_refs[0][0]
    for r in range(1, pieces):
        a = jnp.where(source == r, a_refs[r][0], a)
        b = jnp.where(source == r, b_refs[r][0], b)
    ff = a.shape[1]
    out_ref[0, :, :ff] = a
    out_ref[0, :, ff:] = b


def factor_specs(pieces, count, rank, width):
    return [
        pl.BlockSpec(
            (1, rank, width), lambda i, index, source, r=r: (index[r * count + i], 0, 0)
        )
        for r in range(pieces)
    ]


def pick(index, source, a_pieces, b_pieces):
    count, pieces = source.shape[0], len(a_pieces)
    _, rank, ff = a_pieces[0].shape
    d = b_pieces[0].shape[2]
    return pl.pallas_call(
        functools.partial(pick_kernel, pieces),
        grid_spec=pltpu.PrefetchScalarGridSpec(
            num_scalar_prefetch=2,
            grid=(count,),
            in_specs=factor_specs(pieces, count, rank, ff) + factor_specs(pieces, count, rank, d),
            out_specs=pl.BlockSpec((1, rank, ff + d), lambda i, index, source: (i, 0, 0)),
        ),
        out_shape=jax.ShapeDtypeStruct((count, rank, ff + d), bf16),
        **params((0, 2 * (pieces + 1) * count * rank * (ff + d))),
    )(index, source, *a_pieces, *b_pieces)


def project_kernel(pieces, index_ref, source_ref, *refs):
    a_refs, b_refs = refs[:pieces], refs[pieces : 2 * pieces]
    far_ref, hid_ref, grad_ref, part_ref, block_ref, grad_a_ref, grad_b_ref = refs[
        2 * pieces : 2 * pieces + 7
    ]
    zeros, zero_sem = refs[2 * pieces + 7 :]
    step = pl.program_id(0)
    source = source_ref[step]
    ff = hid_ref.shape[1]
    d = grad_ref.shape[1]

    fills = []
    for slot in range(grad_a_ref.shape[0]):
        fills.append(pltpu.make_async_copy(zeros, grad_a_ref.at[slot], zero_sem.at[2 * slot]))
        fills.append(
            pltpu.make_async_copy(
                zeros.at[:, pl.ds(0, d)], grad_b_ref.at[slot], zero_sem.at[2 * slot + 1]
            )
        )

    @pl.when(step == 0)
    def _():
        zeros[...] = jnp.zeros_like(zeros)
        for fill in fills:
            fill.start()

    a, b = far_ref[0, :, :ff], far_ref[0, :, ff:]
    for r in range(pieces):
        a = jnp.where(source == r, a_refs[r][0], a)
        b = jnp.where(source == r, b_refs[r][0], b)
    block_ref[0] = a
    over_last = (((1,), (1,)), ((), ()))
    rank = a.shape[0]
    part_ref[0, :, :rank] = lax.dot_general(
        hid_ref[...], a, over_last, preferred_element_type=f32
    )
    part_ref[0, :, rank:] = lax.dot_general(
        grad_ref[...], b, over_last, preferred_element_type=f32
    )

    @pl.when(step == pl.num_programs(0) - 1)
    def _():
        for fill in fills:
            fill.wait()


def project(index, source, a_pieces, b_pieces, far, hidden, grad):
    count, pieces = source.shape[0], len(a_pieces)
    local, rank, ff = a_pieces[0].shape
    d = b_pieces[0].shape[2]
    rows = hidden.shape[0]
    height = rows // count
    own = lambda i, index, source: (i, 0)
    own3 = lambda i, index, source: (i, 0, 0)
    return pl.pallas_call(
        functools.partial(project_kernel, pieces),
        grid_spec=pltpu.PrefetchScalarGridSpec(
            num_scalar_prefetch=2,
            grid=(count,),
            in_specs=factor_specs(pieces, count, rank, ff)
            + factor_specs(pieces, count, rank, d)
            + [
                pl.BlockSpec((1, rank, ff + d), own3),
                pl.BlockSpec((height, ff), own),
                pl.BlockSpec((height, d), own),
            ],
            out_specs=[
                pl.BlockSpec((1, height, 2 * rank), own3),
                pl.BlockSpec((1, rank, ff), own3),
                pl.BlockSpec(memory_space=pl.ANY),
                pl.BlockSpec(memory_space=pl.ANY),
            ],
            scratch_shapes=[
                pltpu.VMEM((rank, ff), f32),
                pltpu.SemaphoreType.DMA((2 * local,)),
            ],
        ),
        out_shape=[
            jax.ShapeDtypeStruct((count, height, 2 * rank), f32),
            jax.ShapeDtypeStruct((count, rank, ff), bf16),
            jax.ShapeDtypeStruct((local, rank, ff), f32),
            jax.ShapeDtypeStruct((local, rank, d), f32),
        ],
        **params((2 * rows * rank * (ff + d), 2 * (rows + (pieces + 2) * count * rank) * (ff + d))),
    )(index, source, *a_pieces, *b_pieces, far, hidden, grad)


def terms_kernel(live_ref, here_ref, there_ref, hid_ref, grad_ref, low_ref, high_ref, coef_ref):
    ff = hid_ref.shape[1]
    cut = low_ref.shape[2]
    rank = coef_ref.shape[2]
    total = here_ref[0] + there_ref[0]
    valid = lax.broadcasted_iota(i32, total.shape, 0) < live_ref[pl.program_id(0)]
    total = jnp.where(valid, total, 0.0)
    low = total[:, :rank].astype(bf16)
    coef = (adapter_scale * total[:, rank:]).astype(bf16)
    coef_ref[0] = coef
    over_rows = (((0,), (0,)), ((), ()))
    term_a = (
        factor_gradient
        * lax.dot_general(coef, hid_ref[...], over_rows, preferred_element_type=f32)
    ).astype(bf16)
    low_ref[0] = term_a[:, :cut]
    high_ref[0, :, : ff - cut] = term_a[:, cut:]
    high_ref[0, :, ff - cut :] = (
        factor_gradient
        * adapter_scale
        * lax.dot_general(low, grad_ref[...], over_rows, preferred_element_type=f32)
    ).astype(bf16)


def block_terms(live, here, there, hidden, grad):
    count, height, both = here.shape
    rank = both // 2
    rows, ff = hidden.shape
    d = grad.shape[1]
    cut = (ff + d) // 384 * 128
    own = lambda i, live: (i, 0)
    own3 = lambda i, live: (i, 0, 0)
    return pl.pallas_call(
        terms_kernel,
        grid_spec=pltpu.PrefetchScalarGridSpec(
            num_scalar_prefetch=1,
            grid=(count,),
            in_specs=[
                pl.BlockSpec((1, height, both), own3),
                pl.BlockSpec((1, height, both), own3),
                pl.BlockSpec((height, ff), own),
                pl.BlockSpec((height, d), own),
            ],
            out_specs=[
                pl.BlockSpec((1, rank, cut), own3),
                pl.BlockSpec((1, rank, ff + d - cut), own3),
                pl.BlockSpec((1, height, rank), own3),
            ],
        ),
        out_shape=[
            jax.ShapeDtypeStruct((count, rank, cut), bf16),
            jax.ShapeDtypeStruct((count, rank, ff + d - cut), bf16),
            jax.ShapeDtypeStruct((count, height, rank), bf16),
        ],
        **params((2 * rows * rank * (ff + d), 2 * (rows + count * rank) * (ff + d))),
    )(live, here, there, hidden, grad)


def base_kernel(n_dp, tiles, n_chunks, count, scalars_ref, kept_ref, *refs):
    near = n_dp // 2
    near_refs = refs[:near]
    far_refs = refs[near : near + n_chunks * near]
    coef_ref, block_ref = refs[near + n_chunks * near : near + n_chunks * near + 2]
    out_ref, token_ref, kept, weight, factor, result = refs[-10:-4]
    kept_sem, in_sem, factor_sem, out_sem = refs[-4:]
    _, tile, depth = weight.shape
    deep = depth // n_dp
    height = coef_ref.shape[1]
    steps = len(tiles)
    token_ref[...] = jnp.zeros_like(token_ref)

    def lanes(r):
        return pl.ds(pl.multiple_of(scalars_ref[steps + r] * deep, deep), deep)

    def span(j):
        return pl.ds(pl.multiple_of(scalars_ref[j] * tile, tile), tile)

    def loads(j, slot, r):
        if r < near:
            return [
                pltpu.make_async_copy(
                    near_refs[r].at[span(j), :], weight.at[slot, :, lanes(r)], in_sem.at[slot, r, 0]
                )
            ]
        copies, low = [], 0
        for k, (chunk, start, size) in enumerate(tiles[j]):
            copies.append(
                pltpu.make_async_copy(
                    far_refs[chunk * near + r - near].at[pl.ds(start, size)],
                    weight.at[slot, pl.ds(low, size), lanes(r)],
                    in_sem.at[slot, r, k],
                )
            )
            low += size
        return copies

    def factors(j, slot):
        return pltpu.make_async_copy(
            block_ref.at[:, :, span(j)], factor.at[slot], factor_sem.at[slot]
        )

    def columns(r):
        return pltpu.make_async_copy(kept_ref.at[:, lanes(r)], kept.at[:, lanes(r)], kept_sem.at[r])

    def store(j, slot):
        return pltpu.make_async_copy(result.at[slot], out_ref.at[:, span(j)], out_sem.at[slot])

    def load(j, slot):
        for r in range(n_dp):
            for copy in loads(j, slot, r):
                copy.start()
        factors(j, slot).start()

    over_last = (((1,), (1,)), ((), ()))

    def finish(slot, total):
        for b in range(count):
            extra = jnp.dot(coef_ref[b], factor[slot, b], preferred_element_type=f32)
            here = total[b * height : (b + 1) * height] + extra
            valid = lax.broadcasted_iota(i32, here.shape, 0) < scalars_ref[steps + n_dp + b]
            result[slot, b * height : (b + 1) * height, :] = jnp.where(valid, here, 0.0).astype(
                bf16
            )

    for r in range(n_dp):
        columns(r).start()
        for copy in loads(0, 0, r):
            copy.start()
    factors(0, 0).start()
    if steps > 1:
        load(1, 1)
    total = None
    for r in range(n_dp):
        columns(r).wait()
        for copy in loads(0, 0, r):
            copy.wait()
        part = lax.dot_general(
            kept[:, lanes(r)], weight[0, :, lanes(r)], over_last, preferred_element_type=f32
        )
        total = part if total is None else total + part
    factors(0, 0).wait()
    finish(0, total)
    store(0, 0).start()

    @pl.loop(1, steps)
    def _(step):
        slot = lax.rem(step, 2)
        for j in range(1, steps):

            @pl.when(step == j)
            def _():
                if j + 1 < steps:
                    load(j + 1, (j + 1) % 2)
                for r in range(n_dp):
                    for copy in loads(j, j % 2, r):
                        copy.wait()
                factors(j, j % 2).wait()
                if j >= 2:
                    store(j - 2, j % 2).wait()

        finish(
            slot,
            lax.dot_general(kept[...], weight[slot], over_last, preferred_element_type=f32),
        )
        for j in range(1, steps):
            pl.when(step == j)(lambda j=j: store(j, j % 2).start())

    for j in range(max(steps - 2, 0), steps):
        store(j, j % 2).wait()


def base(places, scalars, kept, near, chunks, tiles, tile, coef, block_a, held, token):
    rows, depth = kept.shape
    count, rank, ff = block_a.shape
    top = len(near)
    anywhere = pl.BlockSpec(memory_space=pl.ANY)
    operands = [kept, *[near[r] for r in range(top)]]
    for piece in chunks:
        operands += [piece[r] for r in range(top, 2 * top)]
    in_specs = [anywhere] * len(operands)
    in_specs += [pl.BlockSpec(coef.shape, lambda i, s: (0, 0, 0)), anywhere]
    operands += [coef, block_a]
    aliases = {}
    if held is not None:
        in_specs += [anywhere, anywhere]
        operands += [token, held]
        aliases = {len(operands): 0}
    most = max(len(segments) for segments in tiles)
    span = tile * len(tiles)
    return pl.pallas_call(
        functools.partial(base_kernel, 2 * top, tiles, len(chunks), count),
        grid_spec=pltpu.PrefetchScalarGridSpec(
            num_scalar_prefetch=1,
            grid=(1,),
            in_specs=in_specs,
            out_specs=[anywhere, pl.BlockSpec((8, 128), lambda i, s: (0, 0))],
            scratch_shapes=[
                pltpu.VMEM((rows, depth), bf16),
                pltpu.VMEM((2, tile, depth), bf16),
                pltpu.VMEM((2, count, rank, tile), bf16),
                pltpu.VMEM((2, rows, tile), bf16),
                pltpu.SemaphoreType.DMA((2 * top,)),
                pltpu.SemaphoreType.DMA((2, 2 * top, most)),
                pltpu.SemaphoreType.DMA((2,)),
                pltpu.SemaphoreType.DMA((2,)),
            ],
        ),
        out_shape=[
            jax.ShapeDtypeStruct((rows, ff), bf16),
            jax.ShapeDtypeStruct((8, 128), f32),
        ],
        input_output_aliases=aliases,
        **params((1, 1)),
    )(jnp.concatenate([jnp.stack(places).astype(i32), scalars]), *operands)


def add_kernel(pieces, count, slots_ref, *refs):
    term_refs = refs[: 2 * pieces]
    a_ref, b_ref, terms, a, b, term_sem, a_sem, b_sem = refs[2 * pieces + 3 :]
    local, _, ff = a.shape
    both = terms.shape[2]
    cut = term_refs[0].shape[2]

    def load(k):
        lanes = (pl.ds(0, cut), pl.ds(cut, both - cut))
        return [
            pltpu.make_async_copy(
                term_refs[k // count * 2 + part].at[k % count],
                terms.at[k, :, lanes[part]],
                term_sem.at[k, part],
            )
            for part in range(2)
        ]

    def whole(slot, inward):
        pairs = [(a_ref.at[slot], a.at[slot]), (b_ref.at[slot], b.at[slot])]
        return [
            pltpu.make_async_copy(*(pair if inward else pair[::-1]), sem.at[slot])
            for pair, sem in zip(pairs, (a_sem, b_sem))
        ]

    wanted = [slots_ref[k] for k in range(pieces * count)]
    owned = [(slot >= 0) & (slot < local) for slot in wanted]
    hit = []
    for j in range(local):
        any_here = wanted[0] == j
        for slot in wanted[1:]:
            any_here = any_here | (slot == j)
        hit.append(any_here)

    def start(copies):
        for copy in copies:
            copy.start()

    def wait(copies):
        for copy in copies:
            copy.wait()

    for j in range(local):
        pl.when(hit[j])(lambda j=j: start(whole(j, True)))
    for k in range(pieces * count):
        pl.when(owned[k])(lambda k=k: start(load(k)))
    for j in range(local):
        pl.when(hit[j])(lambda j=j: wait(whole(j, True)))

    def add(k):
        wait(load(k))
        a[wanted[k]] += terms[k, :, :ff].astype(f32)
        b[wanted[k]] += terms[k, :, ff:].astype(f32)

    for k in range(pieces * count):
        pl.when(owned[k])(lambda k=k: add(k))
    for j in range(local):
        pl.when(hit[j])(lambda j=j: start(whole(j, False)))
    for j in range(local):
        pl.when(hit[j])(lambda j=j: wait(whole(j, False)))


def add_terms(slots, pieces, grad_a, grad_b, token):
    count, rank, _ = pieces[0].shape
    both = pieces[0].shape[2] + pieces[1].shape[2]
    anywhere = pl.BlockSpec(memory_space=pl.ANY)
    n = len(pieces) // 2
    local = grad_a.shape[0]
    return pl.pallas_call(
        functools.partial(add_kernel, n, count),
        grid_spec=pltpu.PrefetchScalarGridSpec(
            num_scalar_prefetch=1,
            grid=(1,),
            in_specs=[anywhere] * (2 * n + 3),
            out_specs=[anywhere] * 2,
            scratch_shapes=[
                pltpu.VMEM((n * count, rank, both), bf16),
                pltpu.VMEM(grad_a.shape, f32),
                pltpu.VMEM(grad_b.shape, f32),
                pltpu.SemaphoreType.DMA((n * count, 2)),
                pltpu.SemaphoreType.DMA((local,)),
                pltpu.SemaphoreType.DMA((local,)),
            ],
        ),
        out_shape=[
            jax.ShapeDtypeStruct(grad_a.shape, f32),
            jax.ShapeDtypeStruct(grad_b.shape, f32),
        ],
        input_output_aliases={2 * n + 2: 0, 2 * n + 3: 1},
        **params((1, 1)),
    )(slots, *pieces, token, grad_a, grad_b)


def on_device(
    n_groups,
    n_fsdp,
    n_dp,
    output_gradient,
    hidden,
    frozen_down_weight,
    adapter_first_factors,
    adapter_second_factors,
    island_live_rows,
    island_adapter_ids,
    owner_slot_adapters,
):
    rows, ff = hidden.shape
    d = output_gradient.shape[1]
    count = island_live_rows.shape[0]
    local = adapter_first_factors.shape[0]
    n_slots = owner_slot_adapters.shape[0]
    top = n_dp // 2
    me = lax.axis_index("dp")
    group = lax.axis_index("groups")

    def swap(value, bit, axis="dp", size=n_dp):
        return lax.ppermute(value, axis, [(i, i ^ bit) for i in range(size)])

    def spread(held):
        held = dict(held)
        bit = top // 2
        while bit:
            for r in list(held):
                held[r ^ bit] = swap(held[r], bit)
            bit //= 2
        return held

    match = island_adapter_ids[:, None] == owner_slot_adapters[None, :]
    slots = jnp.sum(jnp.where(match, jnp.arange(n_slots, dtype=i32)[None, :], 0), axis=1)
    far_slots = swap(slots, top)

    kept = lax.all_gather(output_gradient, "fsdp", axis=1, tiled=True)

    share = ff // n_groups
    if share % 2048 == 0:
        unit, tile = share // 8, share // 4
        sizes = [2 * unit, 2 * unit, 3 * unit, unit]
    else:
        tile = share
        sizes = [share]
    parts = [(sum(sizes[:j]), size) for j, size in enumerate(sizes)]

    crossed = []
    turned = []

    def flat(*pieces):
        return [v for piece in pieces for v in piece.values()]

    def piece_of(j, shift, *after):
        start, size = parts[j]
        owner = lax.rem(group + n_groups - shift, n_groups)
        piece = lax.dynamic_slice_in_dim(frozen_down_weight, owner * share + start, size, axis=0)
        return {top: swap(behind(piece, *after), top)}

    def cross(*after):
        j = len(crossed)
        if j < len(parts):
            crossed.append(piece_of(j, 0, *after))
            if j and j + 1 == len(parts):
                turned.append([piece_of(j, shift, *after) for shift in range(1, n_groups)])

    def turn(*after):
        j = len(turned)
        if j < len(parts):
            piece = behind(crossed[j][top], *after)
            turned.append([])
            for shift in range(1, n_groups):
                ring = [(i, (i + shift) % n_groups) for i in range(n_groups)]
                turned[j].append({top: lax.ppermute(piece, "groups", ring)})

    def fill(chunks, *after):
        for piece in chunks:
            piece.update(spread({top: behind(piece[top], *after)}))

    first = jnp.swapaxes(adapter_first_factors, 1, 2)
    a_near = spread({0: first})
    b_near = spread({0: adapter_second_factors})
    near = sorted(a_near)
    a_near = [a_near[r] for r in near]
    b_near = [b_near[r] for r in near]
    def places(wanted):
        owner = wanted // local
        index = jnp.concatenate([wanted % local] * len(near))
        return index, jnp.where((owner ^ me) < top, owner ^ me, len(near))

    picked = pick(*places(far_slots), a_near, b_near)
    far = swap(picked, top)
    whole = spread({0: behind(frozen_down_weight, picked)})
    both_slots = spread({0: behind(jnp.concatenate([slots, far_slots]), picked)})
    past = [far, *flat(whole, both_slots)]
    part, block_a, grad_a, grad_b = project(
        *places(behind(slots, *past)), a_near, b_near, far, hidden, output_gradient
    )
    cross(far)
    cross(far)
    sums = [part]
    bit = 1
    while bit < n_fsdp:
        sums.append(swap(sums[-1], bit, "fsdp", n_fsdp))
        if 2 * bit < n_fsdp:
            sums.append(sums[-2] + sums[-1])
        bit *= 2
    total, other = sums[-2:]
    past = [part, *flat(*crossed[:1])]
    cross(*past)
    turn(*past)
    fill(crossed[:1], *past)
    past = [part, *flat(*crossed[:2], *turned[0])]
    turn(*past)
    fill(crossed[1:2], *past)
    fill(turned[0], *past)
    past = [sums[2], *flat(*crossed[:3], *sum(turned, []))]
    turn(*past)
    cross(*past)
    fill(crossed[2:3], *past)
    for pieces in turned[1:2]:
        fill(pieces, *past)
    low_terms, high_terms, coef = block_terms(
        island_live_rows, total, other, hidden, output_gradient
    )
    far_high = swap(behind(high_terms, *flat(*crossed[3:], *sum(turned[3:], []))), top)
    far_low = swap(low_terms, top)
    fill(crossed[3:], other)
    for pieces in turned[3:]:
        fill(pieces, other)

    relative = [both_slots[r][:count] for r in near] + [both_slots[r][count:] for r in near]
    relative = jnp.concatenate(relative) - me * local

    scalars = jnp.concatenate(
        [jnp.stack([me ^ r for r in range(n_dp)]).astype(i32), island_live_rows]
    )
    grad_hidden = token = None

    def multiply(*where):
        nonlocal grad_hidden, token
        chunks, tiles, places = [], [], []
        for shift, t in where:
            start = lax.rem(group + n_groups - shift, n_groups) * share
            places.append(start // tile + t)
            tiles.append([])
            for j, (first, size) in enumerate(parts):
                low, high = max(first, t * tile), min(first + size, (t + 1) * tile)
                if low < high:
                    if (shift, j) not in chunks:
                        chunks.append((shift, j))
                    tiles[-1].append((chunks.index((shift, j)), low - first, high - low))
        pieces = [turned[j][shift - 1] if shift else crossed[j] for shift, j in chunks]
        grad_hidden, token = base(
            places, scalars, kept, whole, pieces, tiles, tile, coef, block_a,
            grad_hidden, token,
        )

    others = range(1, n_groups)
    if share > tile:
        multiply(*[(0, t) for t in range(4)], *[(g, 0) for g in others])
        past = [token, far_high]
        for pieces in turned[2:3]:
            fill(pieces, *past)
        multiply(*[(g, t) for g in others for t in range(1, 4)])
    else:
        multiply(*[(g, 0) for g in range(n_groups)])

    near_low = spread({0: behind(low_terms, *past)})
    near_high = spread({0: behind(high_terms, *past)})
    all_high = spread({top: behind(far_high, *past)})
    all_low = spread({top: behind(far_low, token)})
    terms = [p for r in near for p in (near_low[r], near_high[r])]
    terms += [p for r in near for p in (all_low[r + top], all_high[r + top])]
    grad_a, grad_b = add_terms(relative, terms, grad_a, grad_b, token)
    return grad_hidden, jnp.swapaxes(grad_a, 1, 2), grad_b


def solution(mesh):
    placed = (
        P(("groups", "dp"), "fsdp"),
        P(("groups", "dp"), "fsdp"),
        P("fsdp", "dp"),
        P(("groups", "dp"), "fsdp", None),
        P(("groups", "dp"), None, "fsdp"),
        P(("groups", "dp")),
        P(("groups", "dp")),
        P("groups"),
    )
    sizes = [mesh.shape[name] for name in ("groups", "fsdp", "dp")]
    return jax.shard_map(
        functools.partial(on_device, *sizes),
        mesh=mesh,
        in_specs=placed,
        out_specs=(
            P(("groups", "dp"), "fsdp"),
            P(("groups", "dp"), "fsdp", None),
            P(("groups", "dp"), None, "fsdp"),
        ),
        check_vma=False,
    )
```

```python
import functools

import jax
import jax.numpy as jnp
from jax import lax
from jax.experimental import pallas as pl
from jax.experimental.pallas import tpu as pltpu
from jax.sharding import PartitionSpec as P

adapter_scale = 2.0
factor_gradient = 0.0625
vmem_bytes = 60 * 1024 * 1024
bf16, f32, i32 = jnp.bfloat16, jnp.float32, jnp.int32


def behind(value, *after):
    if not after:
        return value
    return lax.optimization_barrier((value, *after))[0]


def params(cost):
    return dict(
        compiler_params=pltpu.CompilerParams(vmem_limit_bytes=vmem_bytes),
        cost_estimate=pl.CostEstimate(flops=cost[0], bytes_accessed=cost[1], transcendentals=0),
    )


def pick_kernel(pieces, index_ref, source_ref, *refs):
    a_refs, b_refs, out_ref = refs[:pieces], refs[pieces : 2 * pieces], refs[-1]
    source = source_ref[pl.program_id(0)]
    a, b = a_refs[0][0], b_refs[0][0]
    for r in range(1, pieces):
        a = jnp.where(source == r, a_refs[r][0], a)
        b = jnp.where(source == r, b_refs[r][0], b)
    ff = a.shape[1]
    out_ref[0, :, :ff] = a
    out_ref[0, :, ff:] = b


def factor_specs(pieces, count, rank, width):
    return [
        pl.BlockSpec(
            (1, rank, width), lambda i, index, source, r=r: (index[r * count + i], 0, 0)
        )
        for r in range(pieces)
    ]


def pick(index, source, a_pieces, b_pieces):
    count, pieces = source.shape[0], len(a_pieces)
    _, rank, ff = a_pieces[0].shape
    d = b_pieces[0].shape[2]
    return pl.pallas_call(
        functools.partial(pick_kernel, pieces),
        grid_spec=pltpu.PrefetchScalarGridSpec(
            num_scalar_prefetch=2,
            grid=(count,),
            in_specs=factor_specs(pieces, count, rank, ff) + factor_specs(pieces, count, rank, d),
            out_specs=pl.BlockSpec((1, rank, ff + d), lambda i, index, source: (i, 0, 0)),
        ),
        out_shape=jax.ShapeDtypeStruct((count, rank, ff + d), bf16),
        **params((0, 2 * (pieces + 1) * count * rank * (ff + d))),
    )(index, source, *a_pieces, *b_pieces)


def project_kernel(pieces, index_ref, source_ref, *refs):
    a_refs, b_refs = refs[:pieces], refs[pieces : 2 * pieces]
    far_ref, hid_ref, grad_ref, part_ref, block_ref, grad_a_ref, grad_b_ref = refs[
        2 * pieces : 2 * pieces + 7
    ]
    zeros, zero_sem = refs[2 * pieces + 7 :]
    step = pl.program_id(0)
    source = source_ref[step]
    ff = hid_ref.shape[1]
    d = grad_ref.shape[1]

    fills = []
    for slot in range(grad_a_ref.shape[0]):
        fills.append(pltpu.make_async_copy(zeros, grad_a_ref.at[slot], zero_sem.at[2 * slot]))
        fills.append(
            pltpu.make_async_copy(
                zeros.at[:, pl.ds(0, d)], grad_b_ref.at[slot], zero_sem.at[2 * slot + 1]
            )
        )

    @pl.when(step == 0)
    def _():
        zeros[...] = jnp.zeros_like(zeros)
        for fill in fills:
            fill.start()

    a, b = far_ref[0, :, :ff], far_ref[0, :, ff:]
    for r in range(pieces):
        a = jnp.where(source == r, a_refs[r][0], a)
        b = jnp.where(source == r, b_refs[r][0], b)
    block_ref[0] = a
    over_last = (((1,), (1,)), ((), ()))
    rank = a.shape[0]
    part_ref[0, :, :rank] = lax.dot_general(
        hid_ref[...], a, over_last, preferred_element_type=f32
    )
    part_ref[0, :, rank:] = lax.dot_general(
        grad_ref[...], b, over_last, preferred_element_type=f32
    )

    @pl.when(step == pl.num_programs(0) - 1)
    def _():
        for fill in fills:
            fill.wait()


def project(index, source, a_pieces, b_pieces, far, hidden, grad):
    count, pieces = source.shape[0], len(a_pieces)
    local, rank, ff = a_pieces[0].shape
    d = b_pieces[0].shape[2]
    rows = hidden.shape[0]
    height = rows // count
    own = lambda i, index, source: (i, 0)
    own3 = lambda i, index, source: (i, 0, 0)
    return pl.pallas_call(
        functools.partial(project_kernel, pieces),
        grid_spec=pltpu.PrefetchScalarGridSpec(
            num_scalar_prefetch=2,
            grid=(count,),
            in_specs=factor_specs(pieces, count, rank, ff)
            + factor_specs(pieces, count, rank, d)
            + [
                pl.BlockSpec((1, rank, ff + d), own3),
                pl.BlockSpec((height, ff), own),
                pl.BlockSpec((height, d), own),
            ],
            out_specs=[
                pl.BlockSpec((1, height, 2 * rank), own3),
                pl.BlockSpec((1, rank, ff), own3),
                pl.BlockSpec(memory_space=pl.ANY),
                pl.BlockSpec(memory_space=pl.ANY),
            ],
            scratch_shapes=[
                pltpu.VMEM((rank, ff), f32),
                pltpu.SemaphoreType.DMA((2 * local,)),
            ],
        ),
        out_shape=[
            jax.ShapeDtypeStruct((count, height, 2 * rank), f32),
            jax.ShapeDtypeStruct((count, rank, ff), bf16),
            jax.ShapeDtypeStruct((local, rank, ff), f32),
            jax.ShapeDtypeStruct((local, rank, d), f32),
        ],
        **params((2 * rows * rank * (ff + d), 2 * (rows + (pieces + 2) * count * rank) * (ff + d))),
    )(index, source, *a_pieces, *b_pieces, far, hidden, grad)


def terms_kernel(live_ref, here_ref, there_ref, hid_ref, grad_ref, low_ref, high_ref, coef_ref):
    ff = hid_ref.shape[1]
    cut = low_ref.shape[2]
    rank = coef_ref.shape[2]
    total = here_ref[0] + there_ref[0]
    valid = lax.broadcasted_iota(i32, total.shape, 0) < live_ref[pl.program_id(0)]
    total = jnp.where(valid, total, 0.0)
    low = total[:, :rank].astype(bf16)
    coef = (adapter_scale * total[:, rank:]).astype(bf16)
    coef_ref[0] = coef
    over_rows = (((0,), (0,)), ((), ()))
    term_a = (
        factor_gradient
        * lax.dot_general(coef, hid_ref[...], over_rows, preferred_element_type=f32)
    ).astype(bf16)
    low_ref[0] = term_a[:, :cut]
    high_ref[0, :, : ff - cut] = term_a[:, cut:]
    high_ref[0, :, ff - cut :] = (
        factor_gradient
        * adapter_scale
        * lax.dot_general(low, grad_ref[...], over_rows, preferred_element_type=f32)
    ).astype(bf16)


def block_terms(live, here, there, hidden, grad):
    count, height, both = here.shape
    rank = both // 2
    rows, ff = hidden.shape
    d = grad.shape[1]
    cut = (ff + d) // 384 * 128
    own = lambda i, live: (i, 0)
    own3 = lambda i, live: (i, 0, 0)
    return pl.pallas_call(
        terms_kernel,
        grid_spec=pltpu.PrefetchScalarGridSpec(
            num_scalar_prefetch=1,
            grid=(count,),
            in_specs=[
                pl.BlockSpec((1, height, both), own3),
                pl.BlockSpec((1, height, both), own3),
                pl.BlockSpec((height, ff), own),
                pl.BlockSpec((height, d), own),
            ],
            out_specs=[
                pl.BlockSpec((1, rank, cut), own3),
                pl.BlockSpec((1, rank, ff + d - cut), own3),
                pl.BlockSpec((1, height, rank), own3),
            ],
        ),
        out_shape=[
            jax.ShapeDtypeStruct((count, rank, cut), bf16),
            jax.ShapeDtypeStruct((count, rank, ff + d - cut), bf16),
            jax.ShapeDtypeStruct((count, height, rank), bf16),
        ],
        **params((2 * rows * rank * (ff + d), 2 * (rows + count * rank) * (ff + d))),
    )(live, here, there, hidden, grad)


def base_kernel(n_dp, tiles, n_chunks, kept_rows, count, scalars_ref, *refs):
    near = n_dp // 2
    n_kept = len(kept_rows)
    kept_refs, refs = refs[:n_kept], refs[n_kept:]
    near_refs = refs[:near]
    far_refs = refs[near : near + n_chunks * near]
    coef_ref, block_ref = refs[near + n_chunks * near : near + n_chunks * near + 2]
    out_ref, token_ref, kept, weight, factor, result = refs[-10:-4]
    kept_sem, in_sem, factor_sem, out_sem = refs[-4:]
    _, tile, depth = weight.shape
    deep = depth // n_dp
    height = coef_ref.shape[1]
    steps = len(tiles)
    token_ref[...] = jnp.zeros_like(token_ref)

    def lanes(r):
        return pl.ds(pl.multiple_of(scalars_ref[steps + r] * deep, deep), deep)

    def span(j):
        return pl.ds(pl.multiple_of(scalars_ref[j] * tile, tile), tile)

    def loads(j, slot, r):
        if r < near:
            return [
                pltpu.make_async_copy(
                    near_refs[r].at[span(j), :], weight.at[slot, :, lanes(r)], in_sem.at[slot, r, 0]
                )
            ]
        copies, low = [], 0
        for k, (chunk, start, size) in enumerate(tiles[j]):
            copies.append(
                pltpu.make_async_copy(
                    far_refs[chunk * near + r - near].at[pl.ds(start, size)],
                    weight.at[slot, pl.ds(low, size), lanes(r)],
                    in_sem.at[slot, r, k],
                )
            )
            low += size
        return copies

    def factors(j, slot):
        return pltpu.make_async_copy(
            block_ref.at[:, :, span(j)], factor.at[slot], factor_sem.at[slot]
        )

    at = [scalars_ref[steps + n_dp + count + k] for k in range(n_kept)]

    def columns(k):
        wide = kept_refs[k].shape[1]
        place = pl.ds(pl.multiple_of(at[k] * wide, wide), wide)
        rows = pl.ds(kept_rows[k], kept_refs[k].shape[0])
        return pltpu.make_async_copy(kept_refs[k], kept.at[rows, place], kept_sem.at[k])

    def store(j, slot):
        return pltpu.make_async_copy(result.at[slot], out_ref.at[:, span(j)], out_sem.at[slot])

    def load(j, slot):
        for r in range(n_dp):
            for copy in loads(j, slot, r):
                copy.start()
        factors(j, slot).start()

    over_last = (((1,), (1,)), ((), ()))

    def finish(slot, total):
        for b in range(count):
            extra = jnp.dot(coef_ref[b], factor[slot, b], preferred_element_type=f32)
            here = total[b * height : (b + 1) * height] + extra
            valid = lax.broadcasted_iota(i32, here.shape, 0) < scalars_ref[steps + n_dp + b]
            result[slot, b * height : (b + 1) * height, :] = jnp.where(valid, here, 0.0).astype(
                bf16
            )

    for k in range(n_kept):
        pl.when(at[k] >= 0)(lambda k=k: columns(k).start())
    for r in range(n_dp):
        for copy in loads(0, 0, r):
            copy.start()
    factors(0, 0).start()
    if steps > 1:
        load(1, 1)
    matching = kept_refs[0].shape[1] == deep
    if not matching:
        for k in range(n_kept):
            pl.when(at[k] >= 0)(lambda k=k: columns(k).wait())
    total = None
    for r in range(n_dp):
        if matching:
            for k in range(n_kept):
                pl.when(at[k] == scalars_ref[steps + r])(lambda k=k: columns(k).wait())
        for copy in loads(0, 0, r):
            copy.wait()
        part = lax.dot_general(
            kept[:, lanes(r)], weight[0, :, lanes(r)], over_last, preferred_element_type=f32
        )
        total = part if total is None else total + part
    factors(0, 0).wait()
    finish(0, total)
    store(0, 0).start()

    @pl.loop(1, steps)
    def _(step):
        slot = lax.rem(step, 2)
        for j in range(1, steps):

            @pl.when(step == j)
            def _():
                if j + 1 < steps:
                    load(j + 1, (j + 1) % 2)
                for r in range(n_dp):
                    for copy in loads(j, j % 2, r):
                        copy.wait()
                factors(j, j % 2).wait()
                if j >= 2:
                    store(j - 2, j % 2).wait()

        finish(
            slot,
            lax.dot_general(kept[...], weight[slot], over_last, preferred_element_type=f32),
        )
        for j in range(1, steps):
            pl.when(step == j)(lambda j=j: store(j, j % 2).start())

    for j in range(max(steps - 2, 0), steps):
        store(j, j % 2).wait()


def base(places, scalars, kept, near, chunks, tiles, tile, coef, block_a, held, token):
    rows = kept[0][0].shape[0]
    count, rank, ff = block_a.shape
    top = len(near)
    depth = 2 * top * near[0].shape[1]
    anywhere = pl.BlockSpec(memory_space=pl.ANY)
    operands = [piece for piece, _ in kept] + [near[r] for r in range(top)]
    for piece in chunks:
        operands += [piece[r] for r in range(top, 2 * top)]
    in_specs = [anywhere] * len(operands)
    in_specs += [pl.BlockSpec(coef.shape, lambda i, s: (0, 0, 0)), anywhere]
    operands += [coef, block_a]
    aliases = {}
    if held is not None:
        in_specs += [anywhere, anywhere]
        operands += [token, held]
        aliases = {len(operands): 0}
    most = max(len(segments) for segments in tiles)
    span = tile * len(tiles)
    return pl.pallas_call(
        functools.partial(
            base_kernel, 2 * top, tiles, len(chunks), [low for _, low in kept], count
        ),
        grid_spec=pltpu.PrefetchScalarGridSpec(
            num_scalar_prefetch=1,
            grid=(1,),
            in_specs=in_specs,
            out_specs=[anywhere, pl.BlockSpec((8, 128), lambda i, s: (0, 0))],
            scratch_shapes=[
                pltpu.VMEM((rows, depth), bf16),
                pltpu.VMEM((2, tile, depth), bf16),
                pltpu.VMEM((2, count, rank, tile), bf16),
                pltpu.VMEM((2, rows, tile), bf16),
                pltpu.SemaphoreType.DMA((len(kept),)),
                pltpu.SemaphoreType.DMA((2, 2 * top, most)),
                pltpu.SemaphoreType.DMA((2,)),
                pltpu.SemaphoreType.DMA((2,)),
            ],
        ),
        out_shape=[
            jax.ShapeDtypeStruct((rows, ff), bf16),
            jax.ShapeDtypeStruct((8, 128), f32),
        ],
        input_output_aliases=aliases,
        **params((1, 1)),
    )(jnp.concatenate([jnp.stack(places).astype(i32), scalars]), *operands)


def add_kernel(pieces, count, slots_ref, *refs):
    term_refs = refs[: 2 * pieces]
    a_ref, b_ref, terms, a, b, term_sem, a_sem, b_sem = refs[2 * pieces + 3 :]
    local, _, ff = a.shape
    both = terms.shape[2]
    cut = term_refs[0].shape[2]

    def load(k):
        lanes = (pl.ds(0, cut), pl.ds(cut, both - cut))
        return [
            pltpu.make_async_copy(
                term_refs[k // count * 2 + part].at[k % count],
                terms.at[k, :, lanes[part]],
                term_sem.at[k, part],
            )
            for part in range(2)
        ]

    def whole(slot, inward):
        pairs = [(a_ref.at[slot], a.at[slot]), (b_ref.at[slot], b.at[slot])]
        return [
            pltpu.make_async_copy(*(pair if inward else pair[::-1]), sem.at[slot])
            for pair, sem in zip(pairs, (a_sem, b_sem))
        ]

    wanted = [slots_ref[k] for k in range(pieces * count)]
    owned = [(slot >= 0) & (slot < local) for slot in wanted]
    hit = []
    for j in range(local):
        any_here = wanted[0] == j
        for slot in wanted[1:]:
            any_here = any_here | (slot == j)
        hit.append(any_here)

    def start(copies):
        for copy in copies:
            copy.start()

    def wait(copies):
        for copy in copies:
            copy.wait()

    for j in range(local):
        pl.when(hit[j])(lambda j=j: start(whole(j, True)))
    for k in range(pieces * count):
        pl.when(owned[k])(lambda k=k: start(load(k)))
    for j in range(local):
        pl.when(hit[j])(lambda j=j: wait(whole(j, True)))

    def add(k):
        wait(load(k))
        a[wanted[k]] += terms[k, :, :ff].astype(f32)
        b[wanted[k]] += terms[k, :, ff:].astype(f32)

    for k in range(pieces * count):
        pl.when(owned[k])(lambda k=k: add(k))
    for j in range(local):
        pl.when(hit[j])(lambda j=j: start(whole(j, False)))
    for j in range(local):
        pl.when(hit[j])(lambda j=j: wait(whole(j, False)))


def add_terms(slots, pieces, grad_a, grad_b, token):
    count, rank, _ = pieces[0].shape
    both = pieces[0].shape[2] + pieces[1].shape[2]
    anywhere = pl.BlockSpec(memory_space=pl.ANY)
    n = len(pieces) // 2
    local = grad_a.shape[0]
    return pl.pallas_call(
        functools.partial(add_kernel, n, count),
        grid_spec=pltpu.PrefetchScalarGridSpec(
            num_scalar_prefetch=1,
            grid=(1,),
            in_specs=[anywhere] * (2 * n + 3),
            out_specs=[anywhere] * 2,
            scratch_shapes=[
                pltpu.VMEM((n * count, rank, both), bf16),
                pltpu.VMEM(grad_a.shape, f32),
                pltpu.VMEM(grad_b.shape, f32),
                pltpu.SemaphoreType.DMA((n * count, 2)),
                pltpu.SemaphoreType.DMA((local,)),
                pltpu.SemaphoreType.DMA((local,)),
            ],
        ),
        out_shape=[
            jax.ShapeDtypeStruct(grad_a.shape, f32),
            jax.ShapeDtypeStruct(grad_b.shape, f32),
        ],
        input_output_aliases={2 * n + 2: 0, 2 * n + 3: 1},
        **params((1, 1)),
    )(slots, *pieces, token, grad_a, grad_b)


def on_device(
    n_groups,
    n_fsdp,
    n_dp,
    output_gradient,
    hidden,
    frozen_down_weight,
    adapter_first_factors,
    adapter_second_factors,
    island_live_rows,
    island_adapter_ids,
    owner_slot_adapters,
):
    rows, ff = hidden.shape
    d = output_gradient.shape[1]
    count = island_live_rows.shape[0]
    local = adapter_first_factors.shape[0]
    n_slots = owner_slot_adapters.shape[0]
    top = n_dp // 2
    me = lax.axis_index("dp")
    group = lax.axis_index("groups")

    def swap(value, bit, axis="dp", size=n_dp):
        return lax.ppermute(value, axis, [(i, i ^ bit) for i in range(size)])

    def spread(held):
        held = dict(held)
        bit = top // 2
        while bit:
            for r in list(held):
                held[r ^ bit] = swap(held[r], bit)
            bit //= 2
        return held

    match = island_adapter_ids[:, None] == owner_slot_adapters[None, :]
    slots = jnp.sum(jnp.where(match, jnp.arange(n_slots, dtype=i32)[None, :], 0), axis=1)
    far_slots = swap(slots, top)

    place = lax.axis_index("fsdp")
    line = n_fsdp <= 4
    height = rows // count
    pieces_of_kept, at = [(output_gradient, 0)], [None]

    def hop(*after, low=0, high=None):
        step = len(at) // 2
        if not line or step + 1 >= n_fsdp:
            return []
        if low == 0:
            ends[:] = next_ends or [output_gradient] * 2
            next_ends.clear()
        right = [(i, i + 1) for i in range(n_fsdp - 1)]
        left = [(i + 1, i) for i in range(n_fsdp - 1)]
        sent = []
        for piece, pairs, place_of in zip(ends, (right, left), (place - step - 1, place + step + 1)):
            piece = behind(piece[low:high], *after)
            sent.append(lax.ppermute(piece, "fsdp", pairs))
            pieces_of_kept.append((sent[-1], low))
            where.append(jnp.where(place_of < n_fsdp, place_of, -1))
        if high is None:
            at.extend([None, None])
            next_ends.extend(sent)
        return sent

    ends, next_ends, where = [], [], [place]
    first_hop = hop()

    share = ff // n_groups
    if share % 2048 == 0:
        unit, tile = share // 8, share // 4
        sizes = [2 * unit] * 4
    else:
        tile = share
        sizes = [share]
    parts = [(sum(sizes[:j]), size) for j, size in enumerate(sizes)]

    crossed = []
    turned = []

    def flat(*pieces):
        return [v for piece in pieces for v in piece.values()]

    def cross(*after):
        j = len(crossed)
        if j < len(parts):
            start, size = parts[j]
            piece = lax.dynamic_slice_in_dim(
                frozen_down_weight, group * share + start, size, axis=0
            )
            crossed.append({top: swap(behind(piece, *after), top)})

    def turn(*after):
        j = len(turned)
        if j < len(parts):
            piece = behind(crossed[j][top], *after)
            turned.append([])
            for shift in range(1, n_groups):
                ring = [(i, (i + shift) % n_groups) for i in range(n_groups)]
                turned[j].append({top: lax.ppermute(piece, "groups", ring)})

    def fill(chunks, *after):
        for piece in chunks:
            piece.update(spread({top: behind(piece[top], *after)}))

    cross(far_slots)

    first = jnp.swapaxes(adapter_first_factors, 1, 2)
    a_near = spread({0: first})
    b_near = spread({0: adapter_second_factors})
    near = sorted(a_near)
    a_near = [a_near[r] for r in near]
    b_near = [b_near[r] for r in near]
    def places(wanted):
        owner = wanted // local
        index = jnp.concatenate([wanted % local] * len(near))
        return index, jnp.where((owner ^ me) < top, owner ^ me, len(near))

    picked = pick(*places(far_slots), a_near, b_near)
    both_slots = spread({0: behind(jnp.concatenate([slots, far_slots]), picked)})
    past = [picked, *first_hop, *flat(both_slots, *crossed)]
    far = swap(behind(picked, *past[1:]), top)
    whole = spread({0: behind(frozen_down_weight, *past)})
    turn(*past)
    past = [far, *hop(*past), *flat(*turned[0])]

    ready = behind(slots, *flat(whole, both_slots), *past)
    part, block_a, grad_a, grad_b = project(
        *places(ready), a_near, b_near, far, hidden, output_gradient
    )
    cross(*past)
    cross(*past)
    third = hop(*past, high=height)
    sums = [part]
    bit = 1
    while bit < n_fsdp:
        sums.append(swap(sums[-1], bit, "fsdp", n_fsdp))
        if 2 * bit < n_fsdp:
            sums.append(sums[-2] + sums[-1])
        bit *= 2
    total, other = sums[-2:]
    past = [sums[2], *third, *flat(*crossed[1:2])]
    turn(*past)
    fill(crossed[:1], *past)
    fill(turned[0], *past)
    past = [other, *flat(*crossed, *sum(turned, []))]
    third = hop(*past, low=height)
    cross(*past)
    turn(*past)
    low_terms, high_terms, coef = block_terms(
        island_live_rows, total, other, hidden, output_gradient
    )
    past = [coef, *third, *flat(*crossed[3:], *sum(turned[2:], []))]
    far_high = swap(behind(high_terms, *past), top)
    far_low = swap(behind(low_terms, *past), top)
    turn(*past)
    fill(crossed[1:], *past)
    if line:
        at = jnp.stack(where).astype(i32)
    else:
        pieces_of_kept = [(lax.all_gather(output_gradient, "fsdp", axis=1, tiled=True), 0)]
        at = jnp.zeros((1,), i32)

    relative = [both_slots[r][:count] for r in near] + [both_slots[r][count:] for r in near]
    relative = jnp.concatenate(relative) - me * local

    scalars = jnp.concatenate(
        [jnp.stack([me ^ r for r in range(n_dp)]).astype(i32), island_live_rows, at]
    )
    grad_hidden = token = None

    def multiply(*where):
        nonlocal grad_hidden, token
        chunks, tiles, places = [], [], []
        for shift, t in where:
            start = lax.rem(group + n_groups - shift, n_groups) * share
            places.append(start // tile + t)
            tiles.append([])
            for j, (first, size) in enumerate(parts):
                low, high = max(first, t * tile), min(first + size, (t + 1) * tile)
                if low < high:
                    if (shift, j) not in chunks:
                        chunks.append((shift, j))
                    tiles[-1].append((chunks.index((shift, j)), low - first, high - low))
        pieces = [turned[j][shift - 1] if shift else crossed[j] for shift, j in chunks]
        grad_hidden, token = base(
            places, scalars, pieces_of_kept, whole, pieces, tiles, tile, coef, block_a,
            grad_hidden, token,
        )

    others = range(1, n_groups)
    if share > tile:
        multiply(*[(0, t) for t in range(4)], *[(g, 0) for g in others])
        past = [token, far_high]
        for pieces in turned[1:]:
            fill(pieces, *past)
        multiply(*[(g, t) for g in others for t in range(1, 4)])
    else:
        multiply(*[(g, 0) for g in range(n_groups)])

    near_low = spread({0: behind(low_terms, *past)})
    near_high = spread({0: behind(high_terms, *past)})
    all_high = spread({top: behind(far_high, *past)})
    all_low = spread({top: behind(far_low, token)})
    terms = [p for r in near for p in (near_low[r], near_high[r])]
    terms += [p for r in near for p in (all_low[r + top], all_high[r + top])]
    grad_a, grad_b = add_terms(relative, terms, grad_a, grad_b, token)
    return grad_hidden, jnp.swapaxes(grad_a, 1, 2), grad_b


def solution(mesh):
    placed = (
        P(("groups", "dp"), "fsdp"),
        P(("groups", "dp"), "fsdp"),
        P("fsdp", "dp"),
        P(("groups", "dp"), "fsdp", None),
        P(("groups", "dp"), None, "fsdp"),
        P(("groups", "dp")),
        P(("groups", "dp")),
        P("groups"),
    )
    sizes = [mesh.shape[name] for name in ("groups", "fsdp", "dp")]
    return jax.shard_map(
        functools.partial(on_device, *sizes),
        mesh=mesh,
        in_specs=placed,
        out_specs=(
            P(("groups", "dp"), "fsdp"),
            P(("groups", "dp"), "fsdp", None),
            P(("groups", "dp"), None, "fsdp"),
        ),
        check_vma=False,
    )
```

```python
import functools

import jax
import jax.numpy as jnp
from jax import lax
from jax.experimental import pallas as pl
from jax.experimental.pallas import tpu as pltpu
from jax.sharding import PartitionSpec as P

adapter_scale = 2.0
factor_gradient = 0.0625
vmem_bytes = 60 * 1024 * 1024
bf16, f32, i32 = jnp.bfloat16, jnp.float32, jnp.int32


def behind(value, *after):
    if not after:
        return value
    return lax.optimization_barrier((value, *after))[0]


def params(cost):
    return dict(
        compiler_params=pltpu.CompilerParams(vmem_limit_bytes=vmem_bytes),
        cost_estimate=pl.CostEstimate(flops=cost[0], bytes_accessed=cost[1], transcendentals=0),
    )


def pick_kernel(pieces, index_ref, source_ref, *refs):
    a_refs, b_refs, out_ref = refs[:pieces], refs[pieces : 2 * pieces], refs[-1]
    source = source_ref[pl.program_id(0)]
    a, b = a_refs[0][0], b_refs[0][0]
    for r in range(1, pieces):
        a = jnp.where(source == r, a_refs[r][0], a)
        b = jnp.where(source == r, b_refs[r][0], b)
    ff = a.shape[1]
    out_ref[0, :, :ff] = a
    out_ref[0, :, ff:] = b


def factor_specs(pieces, count, rank, width):
    return [
        pl.BlockSpec(
            (1, rank, width), lambda i, index, source, r=r: (index[r * count + i], 0, 0)
        )
        for r in range(pieces)
    ]


def pick(index, source, a_pieces, b_pieces):
    count, pieces = source.shape[0], len(a_pieces)
    _, rank, ff = a_pieces[0].shape
    d = b_pieces[0].shape[2]
    return pl.pallas_call(
        functools.partial(pick_kernel, pieces),
        grid_spec=pltpu.PrefetchScalarGridSpec(
            num_scalar_prefetch=2,
            grid=(count,),
            in_specs=factor_specs(pieces, count, rank, ff) + factor_specs(pieces, count, rank, d),
            out_specs=pl.BlockSpec((1, rank, ff + d), lambda i, index, source: (i, 0, 0)),
        ),
        out_shape=jax.ShapeDtypeStruct((count, rank, ff + d), bf16),
        **params((0, 2 * (pieces + 1) * count * rank * (ff + d))),
    )(index, source, *a_pieces, *b_pieces)


def project_kernel(pieces, index_ref, source_ref, *refs):
    a_refs, b_refs = refs[:pieces], refs[pieces : 2 * pieces]
    far_ref, hid_ref, grad_ref, part_ref, block_ref, grad_a_ref, grad_b_ref = refs[
        2 * pieces : 2 * pieces + 7
    ]
    zeros, zero_sem = refs[2 * pieces + 7 :]
    step = pl.program_id(0)
    source = source_ref[step]
    ff = hid_ref.shape[1]
    d = grad_ref.shape[1]

    fills = []
    for slot in range(grad_a_ref.shape[0]):
        fills.append(pltpu.make_async_copy(zeros, grad_a_ref.at[slot], zero_sem.at[2 * slot]))
        fills.append(
            pltpu.make_async_copy(
                zeros.at[:, pl.ds(0, d)], grad_b_ref.at[slot], zero_sem.at[2 * slot + 1]
            )
        )

    @pl.when(step == 0)
    def _():
        zeros[...] = jnp.zeros_like(zeros)
        for fill in fills:
            fill.start()

    a, b = far_ref[0, :, :ff], far_ref[0, :, ff:]
    for r in range(pieces):
        a = jnp.where(source == r, a_refs[r][0], a)
        b = jnp.where(source == r, b_refs[r][0], b)
    block_ref[0] = a
    over_last = (((1,), (1,)), ((), ()))
    rank = a.shape[0]
    part_ref[0, :, :rank] = lax.dot_general(
        hid_ref[...], a, over_last, preferred_element_type=f32
    )
    part_ref[0, :, rank:] = lax.dot_general(
        grad_ref[...], b, over_last, preferred_element_type=f32
    )

    @pl.when(step == pl.num_programs(0) - 1)
    def _():
        for fill in fills:
            fill.wait()


def project(index, source, a_pieces, b_pieces, far, hidden, grad):
    count, pieces = source.shape[0], len(a_pieces)
    local, rank, ff = a_pieces[0].shape
    d = b_pieces[0].shape[2]
    rows = hidden.shape[0]
    height = rows // count
    own = lambda i, index, source: (i, 0)
    own3 = lambda i, index, source: (i, 0, 0)
    return pl.pallas_call(
        functools.partial(project_kernel, pieces),
        grid_spec=pltpu.PrefetchScalarGridSpec(
            num_scalar_prefetch=2,
            grid=(count,),
            in_specs=factor_specs(pieces, count, rank, ff)
            + factor_specs(pieces, count, rank, d)
            + [
                pl.BlockSpec((1, rank, ff + d), own3),
                pl.BlockSpec((height, ff), own),
                pl.BlockSpec((height, d), own),
            ],
            out_specs=[
                pl.BlockSpec((1, height, 2 * rank), own3),
                pl.BlockSpec((1, rank, ff), own3),
                pl.BlockSpec(memory_space=pl.ANY),
                pl.BlockSpec(memory_space=pl.ANY),
            ],
            scratch_shapes=[
                pltpu.VMEM((rank, ff), f32),
                pltpu.SemaphoreType.DMA((2 * local,)),
            ],
        ),
        out_shape=[
            jax.ShapeDtypeStruct((count, height, 2 * rank), f32),
            jax.ShapeDtypeStruct((count, rank, ff), bf16),
            jax.ShapeDtypeStruct((local, rank, ff), f32),
            jax.ShapeDtypeStruct((local, rank, d), f32),
        ],
        **params((2 * rows * rank * (ff + d), 2 * (rows + (pieces + 2) * count * rank) * (ff + d))),
    )(index, source, *a_pieces, *b_pieces, far, hidden, grad)


def terms_kernel(live_ref, here_ref, there_ref, hid_ref, grad_ref, low_ref, high_ref, coef_ref):
    ff = hid_ref.shape[1]
    cut = low_ref.shape[2]
    rank = coef_ref.shape[2]
    total = here_ref[0] + there_ref[0]
    valid = lax.broadcasted_iota(i32, total.shape, 0) < live_ref[pl.program_id(0)]
    total = jnp.where(valid, total, 0.0)
    low = total[:, :rank].astype(bf16)
    coef = (adapter_scale * total[:, rank:]).astype(bf16)
    coef_ref[0] = coef
    over_rows = (((0,), (0,)), ((), ()))
    term_a = (
        factor_gradient
        * lax.dot_general(coef, hid_ref[...], over_rows, preferred_element_type=f32)
    ).astype(bf16)
    low_ref[0] = term_a[:, :cut]
    high_ref[0, :, : ff - cut] = term_a[:, cut:]
    high_ref[0, :, ff - cut :] = (
        factor_gradient
        * adapter_scale
        * lax.dot_general(low, grad_ref[...], over_rows, preferred_element_type=f32)
    ).astype(bf16)


def block_terms(live, here, there, hidden, grad):
    count, height, both = here.shape
    rank = both // 2
    rows, ff = hidden.shape
    d = grad.shape[1]
    cut = (ff + d) // 384 * 128
    own = lambda i, live: (i, 0)
    own3 = lambda i, live: (i, 0, 0)
    return pl.pallas_call(
        terms_kernel,
        grid_spec=pltpu.PrefetchScalarGridSpec(
            num_scalar_prefetch=1,
            grid=(count,),
            in_specs=[
                pl.BlockSpec((1, height, both), own3),
                pl.BlockSpec((1, height, both), own3),
                pl.BlockSpec((height, ff), own),
                pl.BlockSpec((height, d), own),
            ],
            out_specs=[
                pl.BlockSpec((1, rank, cut), own3),
                pl.BlockSpec((1, rank, ff + d - cut), own3),
                pl.BlockSpec((1, height, rank), own3),
            ],
        ),
        out_shape=[
            jax.ShapeDtypeStruct((count, rank, cut), bf16),
            jax.ShapeDtypeStruct((count, rank, ff + d - cut), bf16),
            jax.ShapeDtypeStruct((count, height, rank), bf16),
        ],
        **params((2 * rows * rank * (ff + d), 2 * (rows + count * rank) * (ff + d))),
    )(live, here, there, hidden, grad)


class Tiles:
    def __init__(self, n_dp, tiles, n_chunks, kept_rows, scalars_ref, refs):
        self.near, self.n_dp, self.tiles, self.kept_rows = n_dp // 2, n_dp, tiles, kept_rows
        n_kept = len(kept_rows)
        self.scalars_ref, self.kept_refs, refs = scalars_ref, refs[:n_kept], refs[n_kept:]
        self.near_refs, refs = refs[: self.near], refs[self.near :]
        self.far_refs, self.rest = refs[: n_chunks * self.near], refs[n_chunks * self.near :]
        self.deep = self.near_refs[0].shape[1]
        self.at = [scalars_ref[len(tiles) + 2 * n_dp + k] for k in range(n_kept)]

    def lanes(self, r):
        start = self.scalars_ref[len(self.tiles) + r] * self.deep
        return pl.ds(pl.multiple_of(start, self.deep), self.deep)

    def early(self, r):
        return self.scalars_ref[len(self.tiles) + self.n_dp + r] == 1

    def span(self, j, tile):
        return pl.ds(pl.multiple_of(self.scalars_ref[j] * tile, tile), tile)

    def loads(self, j, r, weight, slot, sem):
        if r < self.near:
            rows = self.near_refs[r].at[self.span(j, weight.shape[1]), :]
            return [
                pltpu.make_async_copy(rows, weight.at[slot, :, self.lanes(r)], sem.at[slot, r, 0])
            ]
        copies, low = [], 0
        for k, (chunk, start, size) in enumerate(self.tiles[j]):
            copies.append(
                pltpu.make_async_copy(
                    self.far_refs[chunk * self.near + r - self.near].at[pl.ds(start, size)],
                    weight.at[slot, pl.ds(low, size), self.lanes(r)],
                    sem.at[slot, r, k],
                )
            )
            low += size
        return copies

    def columns(self, k, kept, sem):
        wide = self.kept_refs[k].shape[1]
        place = pl.ds(pl.multiple_of(self.at[k] * wide, wide), wide)
        rows = pl.ds(self.kept_rows[k], self.kept_refs[k].shape[0])
        return pltpu.make_async_copy(self.kept_refs[k], kept.at[rows, place], sem.at[k])

    def each_column(self, kept, sem, act):
        for k in range(len(self.kept_refs)):
            pl.when(self.at[k] >= 0)(lambda k=k: act(self.columns(k, kept, sem)))

    def part(self, r, kept, weight, slot):
        return lax.dot_general(
            kept[:, self.lanes(r)],
            weight[slot, :, self.lanes(r)],
            (((1,), (1,)), ((), ())),
            preferred_element_type=f32,
        )


def start(copies):
    for copy in copies:
        copy.start()


def wait(copies):
    for copy in copies:
        copy.wait()


def early_kernel(n_dp, tiles, n_chunks, kept_rows, scalars_ref, *refs):
    me = Tiles(n_dp, tiles, n_chunks, kept_rows, scalars_ref, refs)
    sums_refs, (kept, weight, total, kept_sem, in_sem, out_sem) = me.rest[:-6], me.rest[-6:]
    steps = len(tiles)

    def load(j, act):
        for r in range(n_dp):
            pl.when(me.early(r))(lambda r=r: act(me.loads(j, r, weight, j % 2, in_sem)))

    def store(j):
        return pltpu.make_async_copy(total.at[j % 2], sums_refs[j], out_sem.at[j % 2])

    me.each_column(kept, kept_sem, lambda copy: copy.start())
    load(0, start)
    me.each_column(kept, kept_sem, lambda copy: copy.wait())

    @pl.loop(0, steps)
    def _(step):
        slot = lax.rem(step, 2)
        for j in range(steps):

            @pl.when(step == j)
            def _():
                if j + 1 < steps:
                    load(j + 1, start)
                load(j, wait)
                if j >= 2:
                    store(j - 2).wait()

        total[slot] = jnp.zeros(total.shape[1:], f32)
        for r in range(n_dp):

            @pl.when(me.early(r))
            def _():
                total[slot] += me.part(r, kept, weight, slot)

        for j in range(steps):
            pl.when(step == j)(lambda j=j: store(j).start())

    for j in range(max(steps - 2, 0), steps):
        store(j).wait()


def base_kernel(n_dp, tiles, n_chunks, kept_rows, n_held, count, scalars_ref, *refs):
    me = Tiles(n_dp, tiles, n_chunks, kept_rows, scalars_ref, refs)
    held_refs, (coef_ref, block_ref) = me.rest[:n_held], me.rest[n_held : n_held + 2]
    out_ref, token_ref, kept, weight, factor, result, total = me.rest[-12:-5]
    kept_sem, in_sem, factor_sem, out_sem, held_sem = me.rest[-5:]
    _, tile, _ = weight.shape
    height = coef_ref.shape[1]
    steps = len(tiles)
    live = steps + 2 * n_dp + len(kept_rows)
    token_ref[...] = jnp.zeros_like(token_ref)

    def load(j, act):
        slot = j % 2
        for r in range(n_dp):
            if j < n_held:
                pl.when(jnp.logical_not(me.early(r)))(
                    lambda r=r: act(me.loads(j, r, weight, slot, in_sem))
                )
            else:
                act(me.loads(j, r, weight, slot, in_sem))
        if j < n_held:
            act([pltpu.make_async_copy(held_refs[j], total.at[slot], held_sem.at[slot])])
        act(
            [
                pltpu.make_async_copy(
                    block_ref.at[:, :, me.span(j, tile)], factor.at[slot], factor_sem.at[slot]
                )
            ]
        )

    def store(j):
        return pltpu.make_async_copy(
            result.at[j % 2], out_ref.at[:, me.span(j, tile)], out_sem.at[j % 2]
        )

    def finish(slot, sums):
        for b in range(count):
            extra = jnp.dot(coef_ref[b], factor[slot, b], preferred_element_type=f32)
            here = sums[b * height : (b + 1) * height] + extra
            valid = lax.broadcasted_iota(i32, here.shape, 0) < scalars_ref[live + b]
            result[slot, b * height : (b + 1) * height, :] = jnp.where(valid, here, 0.0).astype(
                bf16
            )

    load(0, start)
    me.each_column(kept, kept_sem, lambda copy: copy.start())
    if steps > 1:
        load(1, start)
    me.each_column(kept, kept_sem, lambda copy: copy.wait())

    @pl.loop(0, steps)
    def _(step):
        slot = lax.rem(step, 2)
        for j in range(steps):

            @pl.when(step == j)
            def _():
                if 1 < j + 1 < steps:
                    load(j + 1, start)
                load(j, wait)
                if j >= 2:
                    store(j - 2).wait()

        if n_held:

            @pl.when(step < n_held)
            def _():
                for r in range(n_dp):

                    @pl.when(jnp.logical_not(me.early(r)))
                    def _():
                        total[slot] += me.part(r, kept, weight, slot)

                finish(slot, total[slot])

        if n_held < steps:

            @pl.when(step >= n_held)
            def _():
                finish(
                    slot,
                    lax.dot_general(
                        kept[...],
                        weight[slot],
                        (((1,), (1,)), ((), ())),
                        preferred_element_type=f32,
                    ),
                )

        for j in range(steps):
            pl.when(step == j)(lambda j=j: store(j).start())

    for j in range(max(steps - 2, 0), steps):
        store(j).wait()


def tile_scratch(rows, tile, depth, n_kept, n_dp, tiles):
    most = max(len(segments) for segments in tiles)
    return [
        pltpu.VMEM((rows, depth), bf16),
        pltpu.VMEM((2, tile, depth), bf16),
    ], [
        pltpu.SemaphoreType.DMA((n_kept,)),
        pltpu.SemaphoreType.DMA((2, n_dp, most)),
    ]


def tile_operands(kept, near, chunks):
    top = len(near)
    operands = [piece for piece, _ in kept] + [near[r] for r in range(top)]
    for piece in chunks:
        operands += [piece[r] for r in range(top, 2 * top)]
    return operands


def early_sums(places, scalars, kept, near, chunks, tiles, tile):
    rows = kept[0][0].shape[0]
    n_dp = 2 * len(near)
    depth = n_dp * near[0].shape[1]
    anywhere = pl.BlockSpec(memory_space=pl.ANY)
    operands = tile_operands(kept, near, chunks)
    buffers, semaphores = tile_scratch(rows, tile, depth, len(kept), n_dp, tiles)
    return pl.pallas_call(
        functools.partial(early_kernel, n_dp, tiles, len(chunks), [low for _, low in kept]),
        grid_spec=pltpu.PrefetchScalarGridSpec(
            num_scalar_prefetch=1,
            grid=(1,),
            in_specs=[anywhere] * len(operands),
            out_specs=[anywhere] * len(tiles),
            scratch_shapes=[
                *buffers,
                pltpu.VMEM((2, rows, tile), f32),
                *semaphores,
                pltpu.SemaphoreType.DMA((2,)),
            ],
        ),
        out_shape=[jax.ShapeDtypeStruct((rows, tile), f32)] * len(tiles),
        **params((1, 1)),
    )(jnp.concatenate([jnp.stack(places).astype(i32), scalars]), *operands)


def base(places, scalars, kept, near, chunks, tiles, tile, early, coef, block_a, held, token):
    rows = kept[0][0].shape[0]
    count, rank, ff = block_a.shape
    n_dp = 2 * len(near)
    depth = n_dp * near[0].shape[1]
    anywhere = pl.BlockSpec(memory_space=pl.ANY)
    operands = tile_operands(kept, near, chunks) + early
    in_specs = [anywhere] * len(operands)
    in_specs += [pl.BlockSpec(coef.shape, lambda i, s: (0, 0, 0)), anywhere]
    operands += [coef, block_a]
    aliases = {}
    if held is not None:
        in_specs += [anywhere, anywhere]
        operands += [token, held]
        aliases = {len(operands): 0}
    buffers, semaphores = tile_scratch(rows, tile, depth, len(kept), n_dp, tiles)
    return pl.pallas_call(
        functools.partial(
            base_kernel, n_dp, tiles, len(chunks), [low for _, low in kept], len(early), count
        ),
        grid_spec=pltpu.PrefetchScalarGridSpec(
            num_scalar_prefetch=1,
            grid=(1,),
            in_specs=in_specs,
            out_specs=[anywhere, pl.BlockSpec((8, 128), lambda i, s: (0, 0))],
            scratch_shapes=[
                *buffers,
                pltpu.VMEM((2, count, rank, tile), bf16),
                pltpu.VMEM((2, rows, tile), bf16),
                pltpu.VMEM((2, rows, tile), f32),
                *semaphores,
                pltpu.SemaphoreType.DMA((2,)),
                pltpu.SemaphoreType.DMA((2,)),
                pltpu.SemaphoreType.DMA((2,)),
            ],
        ),
        out_shape=[
            jax.ShapeDtypeStruct((rows, ff), bf16),
            jax.ShapeDtypeStruct((8, 128), f32),
        ],
        input_output_aliases=aliases,
        **params((1, 1)),
    )(jnp.concatenate([jnp.stack(places).astype(i32), scalars]), *operands)


def add_kernel(pieces, count, slots_ref, *refs):
    term_refs = refs[: 2 * pieces]
    a_ref, b_ref, terms, a, b, term_sem, a_sem, b_sem = refs[2 * pieces + 3 :]
    local, _, ff = a.shape
    both = terms.shape[2]
    cut = term_refs[0].shape[2]

    def load(k):
        lanes = (pl.ds(0, cut), pl.ds(cut, both - cut))
        return [
            pltpu.make_async_copy(
                term_refs[k // count * 2 + part].at[k % count],
                terms.at[k, :, lanes[part]],
                term_sem.at[k, part],
            )
            for part in range(2)
        ]

    def whole(slot, inward):
        pairs = [(a_ref.at[slot], a.at[slot]), (b_ref.at[slot], b.at[slot])]
        return [
            pltpu.make_async_copy(*(pair if inward else pair[::-1]), sem.at[slot])
            for pair, sem in zip(pairs, (a_sem, b_sem))
        ]

    wanted = [slots_ref[k] for k in range(pieces * count)]
    owned = [(slot >= 0) & (slot < local) for slot in wanted]
    hit = []
    for j in range(local):
        any_here = wanted[0] == j
        for slot in wanted[1:]:
            any_here = any_here | (slot == j)
        hit.append(any_here)

    for j in range(local):
        pl.when(hit[j])(lambda j=j: start(whole(j, True)))
    for k in range(pieces * count):
        pl.when(owned[k])(lambda k=k: start(load(k)))
    for j in range(local):
        pl.when(hit[j])(lambda j=j: wait(whole(j, True)))

    def add(k):
        wait(load(k))
        a[wanted[k]] += terms[k, :, :ff].astype(f32)
        b[wanted[k]] += terms[k, :, ff:].astype(f32)

    for k in range(pieces * count):
        pl.when(owned[k])(lambda k=k: add(k))
    for j in range(local):
        pl.when(hit[j])(lambda j=j: start(whole(j, False)))
    for j in range(local):
        pl.when(hit[j])(lambda j=j: wait(whole(j, False)))


def add_terms(slots, pieces, grad_a, grad_b, token):
    count, rank, _ = pieces[0].shape
    both = pieces[0].shape[2] + pieces[1].shape[2]
    anywhere = pl.BlockSpec(memory_space=pl.ANY)
    n = len(pieces) // 2
    local = grad_a.shape[0]
    return pl.pallas_call(
        functools.partial(add_kernel, n, count),
        grid_spec=pltpu.PrefetchScalarGridSpec(
            num_scalar_prefetch=1,
            grid=(1,),
            in_specs=[anywhere] * (2 * n + 3),
            out_specs=[anywhere] * 2,
            scratch_shapes=[
                pltpu.VMEM((n * count, rank, both), bf16),
                pltpu.VMEM(grad_a.shape, f32),
                pltpu.VMEM(grad_b.shape, f32),
                pltpu.SemaphoreType.DMA((n * count, 2)),
                pltpu.SemaphoreType.DMA((local,)),
                pltpu.SemaphoreType.DMA((local,)),
            ],
        ),
        out_shape=[
            jax.ShapeDtypeStruct(grad_a.shape, f32),
            jax.ShapeDtypeStruct(grad_b.shape, f32),
        ],
        input_output_aliases={2 * n + 2: 0, 2 * n + 3: 1},
        **params((1, 1)),
    )(slots, *pieces, token, grad_a, grad_b)


def on_device(
    n_groups,
    n_fsdp,
    n_dp,
    output_gradient,
    hidden,
    frozen_down_weight,
    adapter_first_factors,
    adapter_second_factors,
    island_live_rows,
    island_adapter_ids,
    owner_slot_adapters,
):
    rows, ff = hidden.shape
    d = output_gradient.shape[1]
    count = island_live_rows.shape[0]
    local = adapter_first_factors.shape[0]
    n_slots = owner_slot_adapters.shape[0]
    top = n_dp // 2
    me = lax.axis_index("dp")
    group = lax.axis_index("groups")

    def swap(value, bit, axis="dp", size=n_dp):
        return lax.ppermute(value, axis, [(i, i ^ bit) for i in range(size)])

    def spread(held):
        held = dict(held)
        bit = top // 2
        while bit:
            for r in list(held):
                held[r ^ bit] = swap(held[r], bit)
            bit //= 2
        return held

    match = island_adapter_ids[:, None] == owner_slot_adapters[None, :]
    slots = jnp.sum(jnp.where(match, jnp.arange(n_slots, dtype=i32)[None, :], 0), axis=1)
    far_slots = swap(slots, top)

    place = lax.axis_index("fsdp")
    line = n_fsdp <= 4
    height = rows // count
    pieces_of_kept, at = [(output_gradient, 0)], [None]

    def hop(*after, low=0, high=None):
        step = len(at) // 2
        if not line or step + 1 >= n_fsdp:
            return []
        if low == 0:
            ends[:] = next_ends or [output_gradient] * 2
            next_ends.clear()
        right = [(i, i + 1) for i in range(n_fsdp - 1)]
        left = [(i + 1, i) for i in range(n_fsdp - 1)]
        sent = []
        for piece, pairs, place_of in zip(ends, (right, left), (place - step - 1, place + step + 1)):
            piece = behind(piece[low:high], *after)
            sent.append(lax.ppermute(piece, "fsdp", pairs))
            pieces_of_kept.append((sent[-1], low))
            where.append(jnp.where(place_of < n_fsdp, place_of, -1))
        if high is None:
            at.extend([None, None])
            next_ends.extend(sent)
        return sent

    ends, next_ends, where = [], [], [place]
    first_hop = hop()

    share = ff // n_groups
    if share % 2048 == 0:
        unit, tile = share // 16, share // 4
        sizes = [4 * unit, 5 * unit, 5 * unit, 2 * unit]
    else:
        tile = share
        sizes = [share]
    parts = [(sum(sizes[:j]), size) for j, size in enumerate(sizes)]

    crossed = []
    turned = []

    def flat(*pieces):
        return [v for piece in pieces for v in piece.values()]

    def piece_of(j, shift, *after):
        first_row, size = parts[j]
        owner = lax.rem(group + n_groups - shift, n_groups)
        piece = lax.dynamic_slice_in_dim(
            frozen_down_weight, owner * share + first_row, size, axis=0
        )
        return {top: swap(behind(piece, *after), top)}

    def cross(*after):
        j = len(crossed)
        if j < len(parts):
            crossed.append(piece_of(j, 0, *after))
            if j and j + 1 == len(parts):
                direct.extend(piece_of(j, shift, *after) for shift in range(1, n_groups))

    direct = []

    def turn(*after):
        j = len(turned)
        if j < len(parts):
            piece = behind(crossed[j][top], *after)
            turned.append([])
            for shift in range(1, n_groups):
                ring = [(i, (i + shift) % n_groups) for i in range(n_groups)]
                turned[j].append({top: lax.ppermute(piece, "groups", ring)})

    def fill(chunks, *after):
        for piece in chunks:
            piece.update(spread({top: behind(piece[top], *after)}))

    cross(far_slots)

    first = jnp.swapaxes(adapter_first_factors, 1, 2)
    a_near = spread({0: first})
    b_near = spread({0: adapter_second_factors})
    near = sorted(a_near)
    a_near = [a_near[r] for r in near]
    b_near = [b_near[r] for r in near]
    def places(wanted):
        owner = wanted // local
        index = jnp.concatenate([wanted % local] * len(near))
        return index, jnp.where((owner ^ me) < top, owner ^ me, len(near))

    picked = pick(*places(far_slots), a_near, b_near)
    both_slots = spread({0: behind(jnp.concatenate([slots, far_slots]), picked)})
    past = [picked, *first_hop, *flat(both_slots, *crossed)]
    far = swap(behind(picked, *past[1:]), top)
    whole = spread({0: behind(frozen_down_weight, *past)})
    turn(*past)
    past = [far, *hop(*past), *flat(*turned[0])]

    ready = behind(slots, *flat(whole, both_slots), *past)
    part, block_a, grad_a, grad_b = project(
        *places(ready), a_near, b_near, far, hidden, output_gradient
    )
    cross(*past)
    cross(part, *past)
    third = hop(*past, high=height)
    sums = [part]
    bit = 1
    while bit < n_fsdp:
        sums.append(swap(sums[-1], bit, "fsdp", n_fsdp))
        if 2 * bit < n_fsdp:
            sums.append(sums[-2] + sums[-1])
        bit *= 2
    total, other = sums[-2:]
    past = [sums[2], *third, *flat(*crossed[1:2])]
    turn(*past)
    fill(crossed[:2], *past)
    fill(turned[0], *past)

    order = [me ^ r for r in range(n_dp)]
    steps_away = [jnp.abs(place - q) for q in order]
    if line:
        early = jnp.stack([(steps < n_fsdp - 1).astype(i32) for steps in steps_away])
    else:
        early = jnp.zeros((n_dp,), i32)
    order = jnp.stack(order).astype(i32)

    def collect(named):
        chunks, tiles, places_of = [], [], []
        for shift, t in named:
            first_row = lax.rem(group + n_groups - shift, n_groups) * share
            places_of.append(first_row // tile + t)
            tiles.append([])
            for j, (first, size) in enumerate(parts):
                low, high = max(first, t * tile), min(first + size, (t + 1) * tile)
                if low < high:
                    if (shift, j) not in chunks:
                        chunks.append((shift, j))
                    tiles[-1].append((chunks.index((shift, j)), low - first, high - low))
        return places_of, [turned[j][shift - 1] if shift else crossed[j] for shift, j in chunks], tiles

    sums_of = {}

    def begin(*named):
        n = 2 * (n_fsdp - 2) + 1
        at = jnp.stack(where[:n]).astype(i32)
        places_of, chunks, tiles = collect(named)
        got = early_sums(
            places_of, jnp.concatenate([order, early, at]), pieces_of_kept[:n], whole, chunks, tiles, tile
        )
        sums_of.update(zip(named, got))
        return got

    others = range(1, n_groups)
    ahead = line and share > tile
    begun = begin((0, 0), (0, 1), *[(g, 0) for g in others]) if ahead else []
    past = [other, *begun, *flat(*crossed, *sum(turned, []))]
    third = hop(*past, low=height)
    cross(*past)
    turn(*past)
    if direct:
        turned.append(direct)
    live = behind(island_live_rows, *past)
    low_terms, high_terms, coef = block_terms(live, total, other, hidden, output_gradient)
    far_low = swap(behind(low_terms, *flat(*crossed[3:], *direct)), top)
    fill(crossed[3:])
    fill(direct)
    past = [coef, *third, *flat(*crossed, *sum(turned, []))]
    far_high = swap(behind(high_terms, *past), top)
    fill(crossed[2:3], *past)
    for pieces in turned[1:2]:
        fill(pieces, *past)
    if line:
        at = jnp.stack(where).astype(i32)
    else:
        pieces_of_kept = [(lax.all_gather(output_gradient, "fsdp", axis=1, tiled=True), 0)]
        at = jnp.zeros((1,), i32)

    relative = [both_slots[r][:count] for r in near] + [both_slots[r][count:] for r in near]
    relative = jnp.concatenate(relative) - me * local

    scalars = jnp.concatenate([order, early, at, island_live_rows])
    grad_hidden = token = None

    def multiply(*named):
        nonlocal grad_hidden, token
        named = sorted(named, key=lambda name: name not in sums_of)
        places_of, chunks, tiles = collect(named)
        grad_hidden, token = base(
            places_of, scalars, pieces_of_kept, whole, chunks, tiles, tile,
            [sums_of[name] for name in named if name in sums_of], coef, block_a, grad_hidden, token,
        )

    if share > tile:
        multiply(*[(0, t) for t in range(4)], *[(g, t) for g in others for t in range(2)])
        past = [token, far_high]
        for pieces in turned[2:3]:
            fill(pieces, *past)
        multiply(*[(g, t) for g in others for t in range(2, 4)])
    else:
        multiply(*[(g, 0) for g in range(n_groups)])

    near_low = spread({0: behind(low_terms, *past)})
    near_high = spread({0: behind(high_terms, *past)})
    all_high = spread({top: behind(far_high, *past)})
    all_low = spread({top: behind(far_low, token)})
    terms = [p for r in near for p in (near_low[r], near_high[r])]
    terms += [p for r in near for p in (all_low[r + top], all_high[r + top])]
    grad_a, grad_b = add_terms(relative, terms, grad_a, grad_b, token)
    return grad_hidden, jnp.swapaxes(grad_a, 1, 2), grad_b


def solution(mesh):
    placed = (
        P(("groups", "dp"), "fsdp"),
        P(("groups", "dp"), "fsdp"),
        P("fsdp", "dp"),
        P(("groups", "dp"), "fsdp", None),
        P(("groups", "dp"), None, "fsdp"),
        P(("groups", "dp")),
        P(("groups", "dp")),
        P("groups"),
    )
    sizes = [mesh.shape[name] for name in ("groups", "fsdp", "dp")]
    return jax.shard_map(
        functools.partial(on_device, *sizes),
        mesh=mesh,
        in_specs=placed,
        out_specs=(
            P(("groups", "dp"), "fsdp"),
            P(("groups", "dp"), "fsdp", None),
            P(("groups", "dp"), None, "fsdp"),
        ),
        check_vma=False,
    )
```

```python
import functools

import jax
import jax.numpy as jnp
from jax import lax
from jax.experimental import pallas as pl
from jax.experimental.pallas import tpu as pltpu
from jax.sharding import PartitionSpec as P

adapter_scale = 2.0
factor_gradient = 0.0625
vmem_bytes = 60 * 1024 * 1024
bf16, f32, i32 = jnp.bfloat16, jnp.float32, jnp.int32


def behind(value, *after):
    if not after:
        return value
    return lax.optimization_barrier((value, *after))[0]


def params(cost):
    return dict(
        compiler_params=pltpu.CompilerParams(vmem_limit_bytes=vmem_bytes),
        cost_estimate=pl.CostEstimate(flops=cost[0], bytes_accessed=cost[1], transcendentals=0),
    )


def pick_kernel(pieces, index_ref, source_ref, *refs):
    a_refs, b_refs, out_ref = refs[:pieces], refs[pieces : 2 * pieces], refs[-1]
    source = source_ref[pl.program_id(0)]
    a, b = a_refs[0][0], b_refs[0][0]
    for r in range(1, pieces):
        a = jnp.where(source == r, a_refs[r][0], a)
        b = jnp.where(source == r, b_refs[r][0], b)
    ff = a.shape[1]
    out_ref[0, :, :ff] = a
    out_ref[0, :, ff:] = b


def factor_specs(pieces, count, rank, width):
    return [
        pl.BlockSpec(
            (1, rank, width), lambda i, index, source, r=r: (index[r * count + i], 0, 0)
        )
        for r in range(pieces)
    ]


def pick(index, source, a_pieces, b_pieces):
    count, pieces = source.shape[0], len(a_pieces)
    _, rank, ff = a_pieces[0].shape
    d = b_pieces[0].shape[2]
    return pl.pallas_call(
        functools.partial(pick_kernel, pieces),
        grid_spec=pltpu.PrefetchScalarGridSpec(
            num_scalar_prefetch=2,
            grid=(count,),
            in_specs=factor_specs(pieces, count, rank, ff) + factor_specs(pieces, count, rank, d),
            out_specs=pl.BlockSpec((1, rank, ff + d), lambda i, index, source: (i, 0, 0)),
        ),
        out_shape=jax.ShapeDtypeStruct((count, rank, ff + d), bf16),
        **params((0, 2 * (pieces + 1) * count * rank * (ff + d))),
    )(index, source, *a_pieces, *b_pieces)


def project_kernel(pieces, index_ref, source_ref, *refs):
    a_refs, b_refs = refs[:pieces], refs[pieces : 2 * pieces]
    far_ref, hid_ref, grad_ref, part_ref, block_ref, grad_a_ref, grad_b_ref = refs[
        2 * pieces : 2 * pieces + 7
    ]
    zeros, zero_sem = refs[2 * pieces + 7 :]
    step = pl.program_id(0)
    source = source_ref[step]
    ff = hid_ref.shape[1]
    d = grad_ref.shape[1]

    fills = []
    for slot in range(grad_a_ref.shape[0]):
        fills.append(pltpu.make_async_copy(zeros, grad_a_ref.at[slot], zero_sem.at[2 * slot]))
        fills.append(
            pltpu.make_async_copy(
                zeros.at[:, pl.ds(0, d)], grad_b_ref.at[slot], zero_sem.at[2 * slot + 1]
            )
        )

    @pl.when(step == 0)
    def _():
        zeros[...] = jnp.zeros_like(zeros)
        for fill in fills:
            fill.start()

    a, b = far_ref[0, :, :ff], far_ref[0, :, ff:]
    for r in range(pieces):
        a = jnp.where(source == r, a_refs[r][0], a)
        b = jnp.where(source == r, b_refs[r][0], b)
    block_ref[0] = a
    over_last = (((1,), (1,)), ((), ()))
    rank = a.shape[0]
    part_ref[0, :, :rank] = lax.dot_general(
        hid_ref[...], a, over_last, preferred_element_type=f32
    )
    part_ref[0, :, rank:] = lax.dot_general(
        grad_ref[...], b, over_last, preferred_element_type=f32
    )

    @pl.when(step == pl.num_programs(0) - 1)
    def _():
        for fill in fills:
            fill.wait()


def project(index, source, a_pieces, b_pieces, far, hidden, grad):
    count, pieces = source.shape[0], len(a_pieces)
    local, rank, ff = a_pieces[0].shape
    d = b_pieces[0].shape[2]
    rows = hidden.shape[0]
    height = rows // count
    own = lambda i, index, source: (i, 0)
    own3 = lambda i, index, source: (i, 0, 0)
    return pl.pallas_call(
        functools.partial(project_kernel, pieces),
        grid_spec=pltpu.PrefetchScalarGridSpec(
            num_scalar_prefetch=2,
            grid=(count,),
            in_specs=factor_specs(pieces, count, rank, ff)
            + factor_specs(pieces, count, rank, d)
            + [
                pl.BlockSpec((1, rank, ff + d), own3),
                pl.BlockSpec((height, ff), own),
                pl.BlockSpec((height, d), own),
            ],
            out_specs=[
                pl.BlockSpec((1, height, 2 * rank), own3),
                pl.BlockSpec((1, rank, ff), own3),
                pl.BlockSpec(memory_space=pl.ANY),
                pl.BlockSpec(memory_space=pl.ANY),
            ],
            scratch_shapes=[
                pltpu.VMEM((rank, ff), f32),
                pltpu.SemaphoreType.DMA((2 * local,)),
            ],
        ),
        out_shape=[
            jax.ShapeDtypeStruct((count, height, 2 * rank), f32),
            jax.ShapeDtypeStruct((count, rank, ff), bf16),
            jax.ShapeDtypeStruct((local, rank, ff), f32),
            jax.ShapeDtypeStruct((local, rank, d), f32),
        ],
        **params((2 * rows * rank * (ff + d), 2 * (rows + (pieces + 2) * count * rank) * (ff + d))),
    )(index, source, *a_pieces, *b_pieces, far, hidden, grad)


def terms_kernel(live_ref, here_ref, there_ref, hid_ref, grad_ref, low_ref, high_ref, coef_ref):
    ff = hid_ref.shape[1]
    cut = low_ref.shape[2]
    rank = coef_ref.shape[2]
    total = here_ref[0] + there_ref[0]
    valid = lax.broadcasted_iota(i32, total.shape, 0) < live_ref[pl.program_id(0)]
    total = jnp.where(valid, total, 0.0)
    low = total[:, :rank].astype(bf16)
    coef = (adapter_scale * total[:, rank:]).astype(bf16)
    coef_ref[0] = coef
    over_rows = (((0,), (0,)), ((), ()))
    term_a = (
        factor_gradient
        * lax.dot_general(coef, hid_ref[...], over_rows, preferred_element_type=f32)
    ).astype(bf16)
    low_ref[0] = term_a[:, :cut]
    high_ref[0, :, : ff - cut] = term_a[:, cut:]
    high_ref[0, :, ff - cut :] = (
        factor_gradient
        * adapter_scale
        * lax.dot_general(low, grad_ref[...], over_rows, preferred_element_type=f32)
    ).astype(bf16)


def block_terms(live, here, there, hidden, grad):
    count, height, both = here.shape
    rank = both // 2
    rows, ff = hidden.shape
    d = grad.shape[1]
    cut = (ff + d) // 256 * 128
    own = lambda i, live: (i, 0)
    own3 = lambda i, live: (i, 0, 0)
    return pl.pallas_call(
        terms_kernel,
        grid_spec=pltpu.PrefetchScalarGridSpec(
            num_scalar_prefetch=1,
            grid=(count,),
            in_specs=[
                pl.BlockSpec((1, height, both), own3),
                pl.BlockSpec((1, height, both), own3),
                pl.BlockSpec((height, ff), own),
                pl.BlockSpec((height, d), own),
            ],
            out_specs=[
                pl.BlockSpec((1, rank, cut), own3),
                pl.BlockSpec((1, rank, ff + d - cut), own3),
                pl.BlockSpec((1, height, rank), own3),
            ],
        ),
        out_shape=[
            jax.ShapeDtypeStruct((count, rank, cut), bf16),
            jax.ShapeDtypeStruct((count, rank, ff + d - cut), bf16),
            jax.ShapeDtypeStruct((count, height, rank), bf16),
        ],
        **params((2 * rows * rank * (ff + d), 2 * (rows + count * rank) * (ff + d))),
    )(live, here, there, hidden, grad)


class Tiles:
    def __init__(self, n_dp, tiles, n_chunks, kept_rows, scalars_ref, refs):
        self.near, self.n_dp, self.tiles, self.kept_rows = n_dp // 2, n_dp, tiles, kept_rows
        n_kept = len(kept_rows)
        self.scalars_ref, self.kept_refs, refs = scalars_ref, refs[:n_kept], refs[n_kept:]
        self.near_refs, refs = refs[: self.near], refs[self.near :]
        self.far_refs, self.rest = refs[: n_chunks * self.near], refs[n_chunks * self.near :]
        self.deep = self.near_refs[0].shape[1]
        self.at = [scalars_ref[len(tiles) + 2 * n_dp + k] for k in range(n_kept)]

    def lanes(self, r):
        start = self.scalars_ref[len(self.tiles) + r] * self.deep
        return pl.ds(pl.multiple_of(start, self.deep), self.deep)

    def early(self, r):
        return self.scalars_ref[len(self.tiles) + self.n_dp + r] == 1

    def span(self, j, tile):
        return pl.ds(pl.multiple_of(self.scalars_ref[j] * tile, tile), tile)

    def loads(self, j, r, weight, slot, sem):
        if r < self.near:
            rows = self.near_refs[r].at[self.span(j, weight.shape[1]), :]
            return [
                pltpu.make_async_copy(rows, weight.at[slot, :, self.lanes(r)], sem.at[slot, r, 0])
            ]
        copies, low = [], 0
        for k, (chunk, start, size) in enumerate(self.tiles[j]):
            copies.append(
                pltpu.make_async_copy(
                    self.far_refs[chunk * self.near + r - self.near].at[pl.ds(start, size)],
                    weight.at[slot, pl.ds(low, size), self.lanes(r)],
                    sem.at[slot, r, k],
                )
            )
            low += size
        return copies

    def columns(self, k, kept, sem):
        wide = self.kept_refs[k].shape[1]
        place = pl.ds(pl.multiple_of(self.at[k] * wide, wide), wide)
        rows = pl.ds(self.kept_rows[k], self.kept_refs[k].shape[0])
        return pltpu.make_async_copy(self.kept_refs[k], kept.at[rows, place], sem.at[k])

    def each_column(self, kept, sem, act):
        for k in range(len(self.kept_refs)):
            pl.when(self.at[k] >= 0)(lambda k=k: act(self.columns(k, kept, sem)))

    def part(self, r, kept, weight, slot):
        return lax.dot_general(
            kept[:, self.lanes(r)],
            weight[slot, :, self.lanes(r)],
            (((1,), (1,)), ((), ())),
            preferred_element_type=f32,
        )


def start(copies):
    for copy in copies:
        copy.start()


def wait(copies):
    for copy in copies:
        copy.wait()


def early_kernel(n_dp, tiles, n_chunks, kept_rows, scalars_ref, *refs):
    me = Tiles(n_dp, tiles, n_chunks, kept_rows, scalars_ref, refs)
    sums_refs, (kept, weight, total, kept_sem, in_sem, out_sem) = me.rest[:-6], me.rest[-6:]
    steps = len(tiles)

    def load(j, act):
        for r in range(n_dp):
            pl.when(me.early(r))(lambda r=r: act(me.loads(j, r, weight, j % 2, in_sem)))

    def store(j):
        return pltpu.make_async_copy(total.at[j % 2], sums_refs[j], out_sem.at[j % 2])

    me.each_column(kept, kept_sem, lambda copy: copy.start())
    load(0, start)
    me.each_column(kept, kept_sem, lambda copy: copy.wait())

    @pl.loop(0, steps)
    def _(step):
        slot = lax.rem(step, 2)
        for j in range(steps):

            @pl.when(step == j)
            def _():
                if j + 1 < steps:
                    load(j + 1, start)
                load(j, wait)
                if j >= 2:
                    store(j - 2).wait()

        total[slot] = jnp.zeros(total.shape[1:], f32)
        for r in range(n_dp):

            @pl.when(me.early(r))
            def _():
                total[slot] += me.part(r, kept, weight, slot)

        for j in range(steps):
            pl.when(step == j)(lambda j=j: store(j).start())

    for j in range(max(steps - 2, 0), steps):
        store(j).wait()


def base_kernel(n_dp, tiles, n_chunks, kept_rows, n_held, count, scalars_ref, *refs):
    me = Tiles(n_dp, tiles, n_chunks, kept_rows, scalars_ref, refs)
    held_refs, (coef_ref, block_ref) = me.rest[:n_held], me.rest[n_held : n_held + 2]
    out_ref, token_ref, kept, weight, factor, result, total = me.rest[-12:-5]
    kept_sem, in_sem, factor_sem, out_sem, held_sem = me.rest[-5:]
    _, tile, _ = weight.shape
    height = coef_ref.shape[1]
    steps = len(tiles)
    live = steps + 2 * n_dp + len(kept_rows)
    token_ref[...] = jnp.zeros_like(token_ref)

    def load(j, act):
        slot = j % 2
        for r in range(n_dp):
            if j < n_held:
                pl.when(jnp.logical_not(me.early(r)))(
                    lambda r=r: act(me.loads(j, r, weight, slot, in_sem))
                )
            else:
                act(me.loads(j, r, weight, slot, in_sem))
        if j < n_held:
            act([pltpu.make_async_copy(held_refs[j], total.at[slot], held_sem.at[slot])])
        act(
            [
                pltpu.make_async_copy(
                    block_ref.at[:, :, me.span(j, tile)], factor.at[slot], factor_sem.at[slot]
                )
            ]
        )

    def store(j):
        return pltpu.make_async_copy(
            result.at[j % 2], out_ref.at[:, me.span(j, tile)], out_sem.at[j % 2]
        )

    def finish(slot, sums):
        for b in range(count):
            extra = jnp.dot(coef_ref[b], factor[slot, b], preferred_element_type=f32)
            here = sums[b * height : (b + 1) * height] + extra
            valid = lax.broadcasted_iota(i32, here.shape, 0) < scalars_ref[live + b]
            result[slot, b * height : (b + 1) * height, :] = jnp.where(valid, here, 0.0).astype(
                bf16
            )

    load(0, start)
    me.each_column(kept, kept_sem, lambda copy: copy.start())
    if steps > 1:
        load(1, start)
    me.each_column(kept, kept_sem, lambda copy: copy.wait())

    @pl.loop(0, steps)
    def _(step):
        slot = lax.rem(step, 2)
        for j in range(steps):

            @pl.when(step == j)
            def _():
                if 1 < j + 1 < steps:
                    load(j + 1, start)
                load(j, wait)
                if j >= 2:
                    store(j - 2).wait()

        if n_held:

            @pl.when(step < n_held)
            def _():
                for r in range(n_dp):

                    @pl.when(jnp.logical_not(me.early(r)))
                    def _():
                        total[slot] += me.part(r, kept, weight, slot)

                finish(slot, total[slot])

        if n_held < steps:

            @pl.when(step >= n_held)
            def _():
                finish(
                    slot,
                    lax.dot_general(
                        kept[...],
                        weight[slot],
                        (((1,), (1,)), ((), ())),
                        preferred_element_type=f32,
                    ),
                )

        for j in range(steps):
            pl.when(step == j)(lambda j=j: store(j).start())

    for j in range(max(steps - 2, 0), steps):
        store(j).wait()


def tile_scratch(rows, tile, depth, n_kept, n_dp, tiles):
    most = max(len(segments) for segments in tiles)
    return [
        pltpu.VMEM((rows, depth), bf16),
        pltpu.VMEM((2, tile, depth), bf16),
    ], [
        pltpu.SemaphoreType.DMA((n_kept,)),
        pltpu.SemaphoreType.DMA((2, n_dp, most)),
    ]


def tile_operands(kept, near, chunks):
    top = len(near)
    operands = [piece for piece, _ in kept] + [near[r] for r in range(top)]
    for piece in chunks:
        operands += [piece[r] for r in range(top, 2 * top)]
    return operands


def early_sums(places, scalars, kept, near, chunks, tiles, tile):
    rows = kept[0][0].shape[0]
    n_dp = 2 * len(near)
    depth = n_dp * near[0].shape[1]
    anywhere = pl.BlockSpec(memory_space=pl.ANY)
    operands = tile_operands(kept, near, chunks)
    buffers, semaphores = tile_scratch(rows, tile, depth, len(kept), n_dp, tiles)
    return pl.pallas_call(
        functools.partial(early_kernel, n_dp, tiles, len(chunks), [low for _, low in kept]),
        grid_spec=pltpu.PrefetchScalarGridSpec(
            num_scalar_prefetch=1,
            grid=(1,),
            in_specs=[anywhere] * len(operands),
            out_specs=[anywhere] * len(tiles),
            scratch_shapes=[
                *buffers,
                pltpu.VMEM((2, rows, tile), f32),
                *semaphores,
                pltpu.SemaphoreType.DMA((2,)),
            ],
        ),
        out_shape=[jax.ShapeDtypeStruct((rows, tile), f32)] * len(tiles),
        **params((1, 1)),
    )(jnp.concatenate([jnp.stack(places).astype(i32), scalars]), *operands)


def base(places, scalars, kept, near, chunks, tiles, tile, early, coef, block_a, held, token):
    rows = kept[0][0].shape[0]
    count, rank, ff = block_a.shape
    n_dp = 2 * len(near)
    depth = n_dp * near[0].shape[1]
    anywhere = pl.BlockSpec(memory_space=pl.ANY)
    operands = tile_operands(kept, near, chunks) + early
    in_specs = [anywhere] * len(operands)
    in_specs += [pl.BlockSpec(coef.shape, lambda i, s: (0, 0, 0)), anywhere]
    operands += [coef, block_a]
    aliases = {}
    if held is not None:
        in_specs += [anywhere, anywhere]
        operands += [token, held]
        aliases = {len(operands): 0}
    buffers, semaphores = tile_scratch(rows, tile, depth, len(kept), n_dp, tiles)
    return pl.pallas_call(
        functools.partial(
            base_kernel, n_dp, tiles, len(chunks), [low for _, low in kept], len(early), count
        ),
        grid_spec=pltpu.PrefetchScalarGridSpec(
            num_scalar_prefetch=1,
            grid=(1,),
            in_specs=in_specs,
            out_specs=[anywhere, pl.BlockSpec((8, 128), lambda i, s: (0, 0))],
            scratch_shapes=[
                *buffers,
                pltpu.VMEM((2, count, rank, tile), bf16),
                pltpu.VMEM((2, rows, tile), bf16),
                pltpu.VMEM((2, rows, tile), f32),
                *semaphores,
                pltpu.SemaphoreType.DMA((2,)),
                pltpu.SemaphoreType.DMA((2,)),
                pltpu.SemaphoreType.DMA((2,)),
            ],
        ),
        out_shape=[
            jax.ShapeDtypeStruct((rows, ff), bf16),
            jax.ShapeDtypeStruct((8, 128), f32),
        ],
        input_output_aliases=aliases,
        **params((1, 1)),
    )(jnp.concatenate([jnp.stack(places).astype(i32), scalars]), *operands)


def add_kernel(pieces, count, slots_ref, *refs):
    term_refs = refs[: 2 * pieces]
    a_ref, b_ref, terms, a, b, term_sem, a_sem, b_sem = refs[2 * pieces + 3 :]
    local, _, ff = a.shape
    both = terms.shape[2]
    cut = term_refs[0].shape[2]

    def load(k):
        lanes = (pl.ds(0, cut), pl.ds(cut, both - cut))
        return [
            pltpu.make_async_copy(
                term_refs[k // count * 2 + part].at[k % count],
                terms.at[k, :, lanes[part]],
                term_sem.at[k, part],
            )
            for part in range(2)
        ]

    def whole(slot, inward):
        pairs = [(a_ref.at[slot], a.at[slot]), (b_ref.at[slot], b.at[slot])]
        return [
            pltpu.make_async_copy(*(pair if inward else pair[::-1]), sem.at[slot])
            for pair, sem in zip(pairs, (a_sem, b_sem))
        ]

    wanted = [slots_ref[k] for k in range(pieces * count)]
    owned = [(slot >= 0) & (slot < local) for slot in wanted]
    hit = []
    for j in range(local):
        any_here = wanted[0] == j
        for slot in wanted[1:]:
            any_here = any_here | (slot == j)
        hit.append(any_here)

    for j in range(local):
        pl.when(hit[j])(lambda j=j: start(whole(j, True)))
    for k in range(pieces * count):
        pl.when(owned[k])(lambda k=k: start(load(k)))
    for j in range(local):
        pl.when(hit[j])(lambda j=j: wait(whole(j, True)))

    def add(k):
        wait(load(k))
        a[wanted[k]] += terms[k, :, :ff].astype(f32)
        b[wanted[k]] += terms[k, :, ff:].astype(f32)

    for k in range(pieces * count):
        pl.when(owned[k])(lambda k=k: add(k))
    for j in range(local):
        pl.when(hit[j])(lambda j=j: start(whole(j, False)))
    for j in range(local):
        pl.when(hit[j])(lambda j=j: wait(whole(j, False)))


def add_terms(slots, pieces, grad_a, grad_b, token):
    count, rank, _ = pieces[0].shape
    both = pieces[0].shape[2] + pieces[1].shape[2]
    anywhere = pl.BlockSpec(memory_space=pl.ANY)
    n = len(pieces) // 2
    local = grad_a.shape[0]
    return pl.pallas_call(
        functools.partial(add_kernel, n, count),
        grid_spec=pltpu.PrefetchScalarGridSpec(
            num_scalar_prefetch=1,
            grid=(1,),
            in_specs=[anywhere] * (2 * n + 3),
            out_specs=[anywhere] * 2,
            scratch_shapes=[
                pltpu.VMEM((n * count, rank, both), bf16),
                pltpu.VMEM(grad_a.shape, f32),
                pltpu.VMEM(grad_b.shape, f32),
                pltpu.SemaphoreType.DMA((n * count, 2)),
                pltpu.SemaphoreType.DMA((local,)),
                pltpu.SemaphoreType.DMA((local,)),
            ],
        ),
        out_shape=[
            jax.ShapeDtypeStruct(grad_a.shape, f32),
            jax.ShapeDtypeStruct(grad_b.shape, f32),
        ],
        input_output_aliases={2 * n + 2: 0, 2 * n + 3: 1},
        **params((1, 1)),
    )(slots, *pieces, token, grad_a, grad_b)


def on_device(
    n_groups,
    n_fsdp,
    n_dp,
    output_gradient,
    hidden,
    frozen_down_weight,
    adapter_first_factors,
    adapter_second_factors,
    island_live_rows,
    island_adapter_ids,
    owner_slot_adapters,
):
    rows, ff = hidden.shape
    d = output_gradient.shape[1]
    count = island_live_rows.shape[0]
    local = adapter_first_factors.shape[0]
    n_slots = owner_slot_adapters.shape[0]
    top = n_dp // 2
    me = lax.axis_index("dp")
    group = lax.axis_index("groups")

    def swap(value, bit, axis="dp", size=n_dp):
        return lax.ppermute(value, axis, [(i, i ^ bit) for i in range(size)])

    def spread(held):
        held = dict(held)
        bit = top // 2
        while bit:
            for r in list(held):
                held[r ^ bit] = swap(held[r], bit)
            bit //= 2
        return held

    match = island_adapter_ids[:, None] == owner_slot_adapters[None, :]
    slots = jnp.sum(jnp.where(match, jnp.arange(n_slots, dtype=i32)[None, :], 0), axis=1)
    far_slots = swap(slots, top)

    place = lax.axis_index("fsdp")
    line = n_fsdp <= 4
    height = rows // count
    pieces_of_kept, at = [(output_gradient, 0)], [None]

    def hop(*after, low=0, high=None):
        step = len(at) // 2
        if not line or step + 1 >= n_fsdp:
            return []
        if low == 0:
            ends[:] = next_ends or [output_gradient] * 2
            next_ends.clear()
        right = [(i, i + 1) for i in range(n_fsdp - 1)]
        left = [(i + 1, i) for i in range(n_fsdp - 1)]
        sent = []
        for piece, pairs, place_of in zip(ends, (right, left), (place - step - 1, place + step + 1)):
            piece = behind(piece[low:high], *after)
            sent.append(lax.ppermute(piece, "fsdp", pairs))
            pieces_of_kept.append((sent[-1], low))
            where.append(jnp.where(place_of < n_fsdp, place_of, -1))
        if high is None:
            at.extend([None, None])
            next_ends.extend(sent)
        return sent

    ends, next_ends, where = [], [], [place]
    first_hop = hop()

    share = ff // n_groups
    if share % 2048 == 0:
        unit, tile = share // 8, share // 4
        sizes = [2 * unit] * 4
    else:
        tile = share
        sizes = [share]
    parts = [(sum(sizes[:j]), size) for j, size in enumerate(sizes)]

    crossed = []
    turned = []

    def flat(*pieces):
        return [v for piece in pieces for v in piece.values()]

    def cross(*after):
        j = len(crossed)
        if j < len(parts):
            first_row, size = parts[j]
            piece = lax.dynamic_slice_in_dim(
                frozen_down_weight, group * share + first_row, size, axis=0
            )
            crossed.append({top: swap(behind(piece, *after), top)})

    def turn(*after):
        j = len(turned)
        if j < len(parts):
            piece = behind(crossed[j][top], *after)
            turned.append([])
            for shift in range(1, n_groups):
                ring = [(i, (i + shift) % n_groups) for i in range(n_groups)]
                turned[j].append({top: lax.ppermute(piece, "groups", ring)})

    def fill(chunks, *after):
        for piece in chunks:
            piece.update(spread({top: behind(piece[top], *after)}))

    cross(far_slots)

    first = jnp.swapaxes(adapter_first_factors, 1, 2)
    a_near = spread({0: first})
    b_near = spread({0: adapter_second_factors})
    near = sorted(a_near)
    a_near = [a_near[r] for r in near]
    b_near = [b_near[r] for r in near]
    def places(wanted):
        owner = wanted // local
        index = jnp.concatenate([wanted % local] * len(near))
        return index, jnp.where((owner ^ me) < top, owner ^ me, len(near))

    picked = pick(*places(far_slots), a_near, b_near)
    both_slots = spread({0: behind(jnp.concatenate([slots, far_slots]), picked)})
    past = [picked, *first_hop, *flat(both_slots, *crossed)]
    far = swap(behind(picked, *past[1:]), top)
    whole = spread({0: behind(frozen_down_weight, *past)})
    turn(*past)
    past = [far, *hop(*past), *flat(*turned[0])]

    ready = behind(slots, *flat(whole, both_slots), *past)
    part, block_a, grad_a, grad_b = project(
        *places(ready), a_near, b_near, far, hidden, output_gradient
    )
    third_hop = hop(*past)
    cross(*past)
    cross(*past)
    sums = [part]
    bit = 1
    while bit < n_fsdp:
        sums.append(swap(sums[-1], bit, "fsdp", n_fsdp))
        if 2 * bit < n_fsdp:
            sums.append(sums[-2] + sums[-1])
        bit *= 2
    total, other = sums[-2:]
    turn(part)
    past = [sums[2], *flat(*crossed[:3], *sum(turned[:2], [])), *third_hop]
    cross(*past)
    turn(*past)
    fill(crossed[:2], *past)
    fill(turned[0], *past)

    order = [me ^ r for r in range(n_dp)]
    early = jnp.full((n_dp,), int(line), i32)
    order = jnp.stack(order).astype(i32)

    def collect(named):
        chunks, tiles, places_of = [], [], []
        for shift, t in named:
            first_row = lax.rem(group + n_groups - shift, n_groups) * share
            places_of.append(first_row // tile + t)
            tiles.append([])
            for j, (first, size) in enumerate(parts):
                low, high = max(first, t * tile), min(first + size, (t + 1) * tile)
                if low < high:
                    if (shift, j) not in chunks:
                        chunks.append((shift, j))
                    tiles[-1].append((chunks.index((shift, j)), low - first, high - low))
        return places_of, [turned[j][shift - 1] if shift else crossed[j] for shift, j in chunks], tiles

    sums_of = {}

    def begin(*named):
        at = jnp.stack(where).astype(i32)
        places_of, chunks, tiles = collect(named)
        got = early_sums(
            places_of, jnp.concatenate([order, early, at]), pieces_of_kept, whole, chunks, tiles, tile
        )
        sums_of.update(zip(named, got))
        return got

    others = range(1, n_groups)
    ahead = line and share > tile
    begun = begin((0, 0), (0, 1), *[(g, 0) for g in others]) if ahead else []
    past = [other, *begun, *flat(*crossed, *sum(turned, []))]
    low_terms, high_terms, coef = block_terms(
        island_live_rows, total, other, hidden, output_gradient
    )
    far_high = swap(high_terms, top)
    far_low = swap(low_terms, top)
    turn(*past)
    fill(crossed[2:3], *past)
    for pieces in turned[1:2]:
        fill(pieces, *past)
    if line:
        at = jnp.stack(where).astype(i32)
    else:
        pieces_of_kept = [(lax.all_gather(output_gradient, "fsdp", axis=1, tiled=True), 0)]
        at = jnp.zeros((1,), i32)

    relative = [both_slots[r][:count] for r in near] + [both_slots[r][count:] for r in near]
    relative = jnp.concatenate(relative) - me * local

    scalars = jnp.concatenate([order, early, at, island_live_rows])
    grad_hidden = token = None

    def multiply(*named):
        nonlocal grad_hidden, token
        named = sorted(named, key=lambda name: name not in sums_of)
        places_of, chunks, tiles = collect(named)
        grad_hidden, token = base(
            places_of, scalars, pieces_of_kept, whole, chunks, tiles, tile,
            [sums_of[name] for name in named if name in sums_of], coef, block_a, grad_hidden, token,
        )

    if share > tile:
        multiply(*[(0, t) for t in range(3)], *[(g, t) for g in others for t in range(2)])
        past = [token]
        fill(crossed[3:], *past)
        for pieces in turned[2:]:
            fill(pieces, *past)
        past = [token, far_high]
        multiply((0, 3), *[(g, t) for g in others for t in range(2, 4)])
    else:
        multiply(*[(g, 0) for g in range(n_groups)])

    near_low = spread({0: behind(low_terms, *past)})
    near_high = spread({0: behind(high_terms, *past)})
    all_high = spread({top: behind(far_high, *past)})
    all_low = spread({top: behind(far_low, token)})
    terms = [p for r in near for p in (near_low[r], near_high[r])]
    terms += [p for r in near for p in (all_low[r + top], all_high[r + top])]
    grad_a, grad_b = add_terms(relative, terms, grad_a, grad_b, token)
    return grad_hidden, jnp.swapaxes(grad_a, 1, 2), grad_b


def solution(mesh):
    placed = (
        P(("groups", "dp"), "fsdp"),
        P(("groups", "dp"), "fsdp"),
        P("fsdp", "dp"),
        P(("groups", "dp"), "fsdp", None),
        P(("groups", "dp"), None, "fsdp"),
        P(("groups", "dp")),
        P(("groups", "dp")),
        P("groups"),
    )
    sizes = [mesh.shape[name] for name in ("groups", "fsdp", "dp")]
    return jax.shard_map(
        functools.partial(on_device, *sizes),
        mesh=mesh,
        in_specs=placed,
        out_specs=(
            P(("groups", "dp"), "fsdp"),
            P(("groups", "dp"), "fsdp", None),
            P(("groups", "dp"), None, "fsdp"),
        ),
        check_vma=False,
    )
```

```python
import functools

import jax
import jax.numpy as jnp
from jax import lax
from jax.experimental import pallas as pl
from jax.experimental.pallas import tpu as pltpu
from jax.sharding import PartitionSpec as P

adapter_scale = 2.0
factor_gradient = 0.0625
vmem_bytes = 60 * 1024 * 1024
bf16, f32, i32 = jnp.bfloat16, jnp.float32, jnp.int32


def behind(value, *after):
    if not after:
        return value
    return lax.optimization_barrier((value, *after))[0]


def params(cost):
    return dict(
        compiler_params=pltpu.CompilerParams(vmem_limit_bytes=vmem_bytes),
        cost_estimate=pl.CostEstimate(flops=cost[0], bytes_accessed=cost[1], transcendentals=0),
    )


def pick_kernel(pieces, index_ref, source_ref, *refs):
    a_refs, b_refs, out_ref = refs[:pieces], refs[pieces : 2 * pieces], refs[-1]
    source = source_ref[pl.program_id(0)]
    a, b = a_refs[0][0], b_refs[0][0]
    for r in range(1, pieces):
        a = jnp.where(source == r, a_refs[r][0], a)
        b = jnp.where(source == r, b_refs[r][0], b)
    ff = a.shape[1]
    out_ref[0, :, :ff] = a
    out_ref[0, :, ff:] = b


def factor_specs(pieces, count, rank, width):
    return [
        pl.BlockSpec(
            (1, rank, width), lambda i, index, source, r=r: (index[r * count + i], 0, 0)
        )
        for r in range(pieces)
    ]


def pick(index, source, a_pieces, b_pieces):
    count, pieces = source.shape[0], len(a_pieces)
    _, rank, ff = a_pieces[0].shape
    d = b_pieces[0].shape[2]
    return pl.pallas_call(
        functools.partial(pick_kernel, pieces),
        grid_spec=pltpu.PrefetchScalarGridSpec(
            num_scalar_prefetch=2,
            grid=(count,),
            in_specs=factor_specs(pieces, count, rank, ff) + factor_specs(pieces, count, rank, d),
            out_specs=pl.BlockSpec((1, rank, ff + d), lambda i, index, source: (i, 0, 0)),
        ),
        out_shape=jax.ShapeDtypeStruct((count, rank, ff + d), bf16),
        **params((0, 2 * (pieces + 1) * count * rank * (ff + d))),
    )(index, source, *a_pieces, *b_pieces)


def project_kernel(pieces, index_ref, source_ref, *refs):
    a_refs, b_refs = refs[:pieces], refs[pieces : 2 * pieces]
    far_ref, hid_ref, grad_ref, part_ref, block_ref, grad_a_ref, grad_b_ref = refs[
        2 * pieces : 2 * pieces + 7
    ]
    zeros, zero_sem = refs[2 * pieces + 7 :]
    step = pl.program_id(0)
    source = source_ref[step]
    ff = hid_ref.shape[1]
    d = grad_ref.shape[1]

    fills = []
    for slot in range(grad_a_ref.shape[0]):
        fills.append(pltpu.make_async_copy(zeros, grad_a_ref.at[slot], zero_sem.at[2 * slot]))
        fills.append(
            pltpu.make_async_copy(
                zeros.at[:, pl.ds(0, d)], grad_b_ref.at[slot], zero_sem.at[2 * slot + 1]
            )
        )

    @pl.when(step == 0)
    def _():
        zeros[...] = jnp.zeros_like(zeros)
        for fill in fills:
            fill.start()

    a, b = far_ref[0, :, :ff], far_ref[0, :, ff:]
    for r in range(pieces):
        a = jnp.where(source == r, a_refs[r][0], a)
        b = jnp.where(source == r, b_refs[r][0], b)
    block_ref[0] = a
    over_last = (((1,), (1,)), ((), ()))
    rank = a.shape[0]
    part_ref[0, :, :rank] = lax.dot_general(
        hid_ref[...], a, over_last, preferred_element_type=f32
    )
    part_ref[0, :, rank:] = lax.dot_general(
        grad_ref[...], b, over_last, preferred_element_type=f32
    )

    @pl.when(step == pl.num_programs(0) - 1)
    def _():
        for fill in fills:
            fill.wait()


def project(index, source, a_pieces, b_pieces, far, hidden, grad):
    count, pieces = source.shape[0], len(a_pieces)
    local, rank, ff = a_pieces[0].shape
    d = b_pieces[0].shape[2]
    rows = hidden.shape[0]
    height = rows // count
    own = lambda i, index, source: (i, 0)
    own3 = lambda i, index, source: (i, 0, 0)
    return pl.pallas_call(
        functools.partial(project_kernel, pieces),
        grid_spec=pltpu.PrefetchScalarGridSpec(
            num_scalar_prefetch=2,
            grid=(count,),
            in_specs=factor_specs(pieces, count, rank, ff)
            + factor_specs(pieces, count, rank, d)
            + [
                pl.BlockSpec((1, rank, ff + d), own3),
                pl.BlockSpec((height, ff), own),
                pl.BlockSpec((height, d), own),
            ],
            out_specs=[
                pl.BlockSpec((1, height, 2 * rank), own3),
                pl.BlockSpec((1, rank, ff), own3),
                pl.BlockSpec(memory_space=pl.ANY),
                pl.BlockSpec(memory_space=pl.ANY),
            ],
            scratch_shapes=[
                pltpu.VMEM((rank, ff), f32),
                pltpu.SemaphoreType.DMA((2 * local,)),
            ],
        ),
        out_shape=[
            jax.ShapeDtypeStruct((count, height, 2 * rank), f32),
            jax.ShapeDtypeStruct((count, rank, ff), bf16),
            jax.ShapeDtypeStruct((local, rank, ff), f32),
            jax.ShapeDtypeStruct((local, rank, d), f32),
        ],
        **params((2 * rows * rank * (ff + d), 2 * (rows + (pieces + 2) * count * rank) * (ff + d))),
    )(index, source, *a_pieces, *b_pieces, far, hidden, grad)


def terms_kernel(live_ref, here_ref, there_ref, hid_ref, grad_ref, low_ref, high_ref, coef_ref):
    ff = hid_ref.shape[1]
    cut = low_ref.shape[2]
    rank = coef_ref.shape[2]
    total = here_ref[0] + there_ref[0]
    valid = lax.broadcasted_iota(i32, total.shape, 0) < live_ref[pl.program_id(0)]
    total = jnp.where(valid, total, 0.0)
    low = total[:, :rank].astype(bf16)
    coef = (adapter_scale * total[:, rank:]).astype(bf16)
    coef_ref[0] = coef
    over_rows = (((0,), (0,)), ((), ()))
    term_a = (
        factor_gradient
        * lax.dot_general(coef, hid_ref[...], over_rows, preferred_element_type=f32)
    ).astype(bf16)
    low_ref[0] = term_a[:, :cut]
    high_ref[0, :, : ff - cut] = term_a[:, cut:]
    high_ref[0, :, ff - cut :] = (
        factor_gradient
        * adapter_scale
        * lax.dot_general(low, grad_ref[...], over_rows, preferred_element_type=f32)
    ).astype(bf16)


def block_terms(live, here, there, hidden, grad):
    count, height, both = here.shape
    rank = both // 2
    rows, ff = hidden.shape
    d = grad.shape[1]
    cut = (ff + d) // 256 * 128
    own = lambda i, live: (i, 0)
    own3 = lambda i, live: (i, 0, 0)
    return pl.pallas_call(
        terms_kernel,
        grid_spec=pltpu.PrefetchScalarGridSpec(
            num_scalar_prefetch=1,
            grid=(count,),
            in_specs=[
                pl.BlockSpec((1, height, both), own3),
                pl.BlockSpec((1, height, both), own3),
                pl.BlockSpec((height, ff), own),
                pl.BlockSpec((height, d), own),
            ],
            out_specs=[
                pl.BlockSpec((1, rank, cut), own3),
                pl.BlockSpec((1, rank, ff + d - cut), own3),
                pl.BlockSpec((1, height, rank), own3),
            ],
        ),
        out_shape=[
            jax.ShapeDtypeStruct((count, rank, cut), bf16),
            jax.ShapeDtypeStruct((count, rank, ff + d - cut), bf16),
            jax.ShapeDtypeStruct((count, height, rank), bf16),
        ],
        **params((2 * rows * rank * (ff + d), 2 * (rows + count * rank) * (ff + d))),
    )(live, here, there, hidden, grad)


class Tiles:
    def __init__(self, n_dp, tiles, n_chunks, kept_rows, scalars_ref, refs):
        self.near, self.n_dp, self.tiles, self.kept_rows = n_dp // 2, n_dp, tiles, kept_rows
        n_kept = len(kept_rows)
        self.scalars_ref, self.kept_refs, refs = scalars_ref, refs[:n_kept], refs[n_kept:]
        self.near_refs, refs = refs[: self.near], refs[self.near :]
        self.far_refs, self.rest = refs[: n_chunks * self.near], refs[n_chunks * self.near :]
        self.deep = self.near_refs[0].shape[1]
        self.at = [scalars_ref[len(tiles) + 2 * n_dp + k] for k in range(n_kept)]

    def lanes(self, r):
        start = self.scalars_ref[len(self.tiles) + r] * self.deep
        return pl.ds(pl.multiple_of(start, self.deep), self.deep)

    def early(self, r):
        return self.scalars_ref[len(self.tiles) + self.n_dp + r] == 1

    def span(self, j, tile):
        return pl.ds(pl.multiple_of(self.scalars_ref[j] * tile, tile), tile)

    def loads(self, j, r, weight, slot, sem):
        if r < self.near:
            rows = self.near_refs[r].at[self.span(j, weight.shape[1]), :]
            return [
                pltpu.make_async_copy(rows, weight.at[slot, :, self.lanes(r)], sem.at[slot, r, 0])
            ]
        copies, low = [], 0
        for k, (chunk, start, size) in enumerate(self.tiles[j]):
            copies.append(
                pltpu.make_async_copy(
                    self.far_refs[chunk * self.near + r - self.near].at[pl.ds(start, size)],
                    weight.at[slot, pl.ds(low, size), self.lanes(r)],
                    sem.at[slot, r, k],
                )
            )
            low += size
        return copies

    def columns(self, k, kept, sem):
        wide = self.kept_refs[k].shape[1]
        place = pl.ds(pl.multiple_of(self.at[k] * wide, wide), wide)
        rows = pl.ds(self.kept_rows[k], self.kept_refs[k].shape[0])
        return pltpu.make_async_copy(self.kept_refs[k], kept.at[rows, place], sem.at[k])

    def each_column(self, kept, sem, act):
        for k in range(len(self.kept_refs)):
            pl.when(self.at[k] >= 0)(lambda k=k: act(self.columns(k, kept, sem)))

    def part(self, r, kept, weight, slot):
        return lax.dot_general(
            kept[:, self.lanes(r)],
            weight[slot, :, self.lanes(r)],
            (((1,), (1,)), ((), ())),
            preferred_element_type=f32,
        )


def start(copies):
    for copy in copies:
        copy.start()


def wait(copies):
    for copy in copies:
        copy.wait()


def early_kernel(n_dp, tiles, n_chunks, kept_rows, scalars_ref, *refs):
    me = Tiles(n_dp, tiles, n_chunks, kept_rows, scalars_ref, refs)
    sums_refs, (kept, weight, total, kept_sem, in_sem, out_sem) = me.rest[:-6], me.rest[-6:]
    steps = len(tiles)

    def load(j, act):
        for r in range(n_dp):
            pl.when(me.early(r))(lambda r=r: act(me.loads(j, r, weight, j % 2, in_sem)))

    def store(j):
        return pltpu.make_async_copy(total.at[j % 2], sums_refs[j], out_sem.at[j % 2])

    me.each_column(kept, kept_sem, lambda copy: copy.start())
    load(0, start)
    me.each_column(kept, kept_sem, lambda copy: copy.wait())

    @pl.loop(0, steps)
    def _(step):
        slot = lax.rem(step, 2)
        for j in range(steps):

            @pl.when(step == j)
            def _():
                if j + 1 < steps:
                    load(j + 1, start)
                load(j, wait)
                if j >= 2:
                    store(j - 2).wait()

        total[slot] = jnp.zeros(total.shape[1:], f32)
        for r in range(n_dp):

            @pl.when(me.early(r))
            def _():
                total[slot] += me.part(r, kept, weight, slot)

        for j in range(steps):
            pl.when(step == j)(lambda j=j: store(j).start())

    for j in range(max(steps - 2, 0), steps):
        store(j).wait()


def base_kernel(n_dp, tiles, n_chunks, kept_rows, n_held, count, scalars_ref, *refs):
    me = Tiles(n_dp, tiles, n_chunks, kept_rows, scalars_ref, refs)
    held_refs, (coef_ref, block_ref) = me.rest[:n_held], me.rest[n_held : n_held + 2]
    out_ref, token_ref, kept, weight, factor, result, total = me.rest[-12:-5]
    kept_sem, in_sem, factor_sem, out_sem, held_sem = me.rest[-5:]
    _, tile, _ = weight.shape
    height = coef_ref.shape[1]
    steps = len(tiles)
    live = steps + 2 * n_dp + len(kept_rows)
    token_ref[...] = jnp.zeros_like(token_ref)

    def load(j, act):
        slot = j % 2
        for r in range(n_dp):
            if j < n_held:
                pl.when(jnp.logical_not(me.early(r)))(
                    lambda r=r: act(me.loads(j, r, weight, slot, in_sem))
                )
            else:
                act(me.loads(j, r, weight, slot, in_sem))
        if j < n_held:
            act([pltpu.make_async_copy(held_refs[j], total.at[slot], held_sem.at[slot])])
        act(
            [
                pltpu.make_async_copy(
                    block_ref.at[:, :, me.span(j, tile)], factor.at[slot], factor_sem.at[slot]
                )
            ]
        )

    def store(j):
        return pltpu.make_async_copy(
            result.at[j % 2], out_ref.at[:, me.span(j, tile)], out_sem.at[j % 2]
        )

    def finish(slot, sums):
        for b in range(count):
            extra = jnp.dot(coef_ref[b], factor[slot, b], preferred_element_type=f32)
            here = sums[b * height : (b + 1) * height] + extra
            valid = lax.broadcasted_iota(i32, here.shape, 0) < scalars_ref[live + b]
            result[slot, b * height : (b + 1) * height, :] = jnp.where(valid, here, 0.0).astype(
                bf16
            )

    load(0, start)
    me.each_column(kept, kept_sem, lambda copy: copy.start())
    if steps > 1:
        load(1, start)
    me.each_column(kept, kept_sem, lambda copy: copy.wait())

    @pl.loop(0, steps)
    def _(step):
        slot = lax.rem(step, 2)
        for j in range(steps):

            @pl.when(step == j)
            def _():
                if 1 < j + 1 < steps:
                    load(j + 1, start)
                load(j, wait)
                if j >= 2:
                    store(j - 2).wait()

        if n_held:

            @pl.when(step < n_held)
            def _():
                for r in range(n_dp):

                    @pl.when(jnp.logical_not(me.early(r)))
                    def _():
                        total[slot] += me.part(r, kept, weight, slot)

                finish(slot, total[slot])

        if n_held < steps:

            @pl.when(step >= n_held)
            def _():
                finish(
                    slot,
                    lax.dot_general(
                        kept[...],
                        weight[slot],
                        (((1,), (1,)), ((), ())),
                        preferred_element_type=f32,
                    ),
                )

        for j in range(steps):
            pl.when(step == j)(lambda j=j: store(j).start())

    for j in range(max(steps - 2, 0), steps):
        store(j).wait()


def tile_scratch(rows, tile, depth, n_kept, n_dp, tiles):
    most = max(len(segments) for segments in tiles)
    return [
        pltpu.VMEM((rows, depth), bf16),
        pltpu.VMEM((2, tile, depth), bf16),
    ], [
        pltpu.SemaphoreType.DMA((n_kept,)),
        pltpu.SemaphoreType.DMA((2, n_dp, most)),
    ]


def tile_operands(kept, near, chunks):
    top = len(near)
    operands = [piece for piece, _ in kept] + [near[r] for r in range(top)]
    for piece in chunks:
        operands += [piece[r] for r in range(top, 2 * top)]
    return operands


def early_sums(places, scalars, kept, near, chunks, tiles, tile):
    rows = kept[0][0].shape[0]
    n_dp = 2 * len(near)
    depth = n_dp * near[0].shape[1]
    anywhere = pl.BlockSpec(memory_space=pl.ANY)
    operands = tile_operands(kept, near, chunks)
    buffers, semaphores = tile_scratch(rows, tile, depth, len(kept), n_dp, tiles)
    return pl.pallas_call(
        functools.partial(early_kernel, n_dp, tiles, len(chunks), [low for _, low in kept]),
        grid_spec=pltpu.PrefetchScalarGridSpec(
            num_scalar_prefetch=1,
            grid=(1,),
            in_specs=[anywhere] * len(operands),
            out_specs=[anywhere] * len(tiles),
            scratch_shapes=[
                *buffers,
                pltpu.VMEM((2, rows, tile), f32),
                *semaphores,
                pltpu.SemaphoreType.DMA((2,)),
            ],
        ),
        out_shape=[jax.ShapeDtypeStruct((rows, tile), f32)] * len(tiles),
        **params((1, 1)),
    )(jnp.concatenate([jnp.stack(places).astype(i32), scalars]), *operands)


def base(places, scalars, kept, near, chunks, tiles, tile, early, coef, block_a, held, token):
    rows = kept[0][0].shape[0]
    count, rank, ff = block_a.shape
    n_dp = 2 * len(near)
    depth = n_dp * near[0].shape[1]
    anywhere = pl.BlockSpec(memory_space=pl.ANY)
    operands = tile_operands(kept, near, chunks) + early
    in_specs = [anywhere] * len(operands)
    in_specs += [pl.BlockSpec(coef.shape, lambda i, s: (0, 0, 0)), anywhere]
    operands += [coef, block_a]
    aliases = {}
    if held is not None:
        in_specs += [anywhere, anywhere]
        operands += [token, held]
        aliases = {len(operands): 0}
    buffers, semaphores = tile_scratch(rows, tile, depth, len(kept), n_dp, tiles)
    return pl.pallas_call(
        functools.partial(
            base_kernel, n_dp, tiles, len(chunks), [low for _, low in kept], len(early), count
        ),
        grid_spec=pltpu.PrefetchScalarGridSpec(
            num_scalar_prefetch=1,
            grid=(1,),
            in_specs=in_specs,
            out_specs=[anywhere, pl.BlockSpec((8, 128), lambda i, s: (0, 0))],
            scratch_shapes=[
                *buffers,
                pltpu.VMEM((2, count, rank, tile), bf16),
                pltpu.VMEM((2, rows, tile), bf16),
                pltpu.VMEM((2, rows, tile), f32),
                *semaphores,
                pltpu.SemaphoreType.DMA((2,)),
                pltpu.SemaphoreType.DMA((2,)),
                pltpu.SemaphoreType.DMA((2,)),
            ],
        ),
        out_shape=[
            jax.ShapeDtypeStruct((rows, ff), bf16),
            jax.ShapeDtypeStruct((8, 128), f32),
        ],
        input_output_aliases=aliases,
        **params((1, 1)),
    )(jnp.concatenate([jnp.stack(places).astype(i32), scalars]), *operands)


def add_kernel(pieces, count, slots_ref, *refs):
    term_refs = refs[: 2 * pieces]
    a_ref, b_ref, terms, a, b, term_sem, a_sem, b_sem = refs[2 * pieces + 3 :]
    local, _, ff = a.shape
    both = terms.shape[2]
    cut = term_refs[0].shape[2]

    def load(k):
        lanes = (pl.ds(0, cut), pl.ds(cut, both - cut))
        return [
            pltpu.make_async_copy(
                term_refs[k // count * 2 + part].at[k % count],
                terms.at[k, :, lanes[part]],
                term_sem.at[k, part],
            )
            for part in range(2)
        ]

    def whole(slot, inward):
        pairs = [(a_ref.at[slot], a.at[slot]), (b_ref.at[slot], b.at[slot])]
        return [
            pltpu.make_async_copy(*(pair if inward else pair[::-1]), sem.at[slot])
            for pair, sem in zip(pairs, (a_sem, b_sem))
        ]

    wanted = [slots_ref[k] for k in range(pieces * count)]
    owned = [(slot >= 0) & (slot < local) for slot in wanted]
    hit = []
    for j in range(local):
        any_here = wanted[0] == j
        for slot in wanted[1:]:
            any_here = any_here | (slot == j)
        hit.append(any_here)

    for j in range(local):
        pl.when(hit[j])(lambda j=j: start(whole(j, True)))
    for k in range(pieces * count):
        pl.when(owned[k])(lambda k=k: start(load(k)))
    for j in range(local):
        pl.when(hit[j])(lambda j=j: wait(whole(j, True)))

    def add(k):
        wait(load(k))
        a[wanted[k]] += terms[k, :, :ff].astype(f32)
        b[wanted[k]] += terms[k, :, ff:].astype(f32)

    for k in range(pieces * count):
        pl.when(owned[k])(lambda k=k: add(k))
    for j in range(local):
        pl.when(hit[j])(lambda j=j: start(whole(j, False)))
    for j in range(local):
        pl.when(hit[j])(lambda j=j: wait(whole(j, False)))


def add_terms(slots, pieces, grad_a, grad_b, token):
    count, rank, _ = pieces[0].shape
    both = pieces[0].shape[2] + pieces[1].shape[2]
    anywhere = pl.BlockSpec(memory_space=pl.ANY)
    n = len(pieces) // 2
    local = grad_a.shape[0]
    return pl.pallas_call(
        functools.partial(add_kernel, n, count),
        grid_spec=pltpu.PrefetchScalarGridSpec(
            num_scalar_prefetch=1,
            grid=(1,),
            in_specs=[anywhere] * (2 * n + 3),
            out_specs=[anywhere] * 2,
            scratch_shapes=[
                pltpu.VMEM((n * count, rank, both), bf16),
                pltpu.VMEM(grad_a.shape, f32),
                pltpu.VMEM(grad_b.shape, f32),
                pltpu.SemaphoreType.DMA((n * count, 2)),
                pltpu.SemaphoreType.DMA((local,)),
                pltpu.SemaphoreType.DMA((local,)),
            ],
        ),
        out_shape=[
            jax.ShapeDtypeStruct(grad_a.shape, f32),
            jax.ShapeDtypeStruct(grad_b.shape, f32),
        ],
        input_output_aliases={2 * n + 2: 0, 2 * n + 3: 1},
        **params((1, 1)),
    )(slots, *pieces, token, grad_a, grad_b)


def on_device(
    n_groups,
    n_fsdp,
    n_dp,
    output_gradient,
    hidden,
    frozen_down_weight,
    adapter_first_factors,
    adapter_second_factors,
    island_live_rows,
    island_adapter_ids,
    owner_slot_adapters,
):
    rows, ff = hidden.shape
    d = output_gradient.shape[1]
    count = island_live_rows.shape[0]
    local = adapter_first_factors.shape[0]
    n_slots = owner_slot_adapters.shape[0]
    top = n_dp // 2
    me = lax.axis_index("dp")
    group = lax.axis_index("groups")

    def swap(value, bit, axis="dp", size=n_dp):
        return lax.ppermute(value, axis, [(i, i ^ bit) for i in range(size)])

    def spread(held):
        held = dict(held)
        bit = top // 2
        while bit:
            for r in list(held):
                held[r ^ bit] = swap(held[r], bit)
            bit //= 2
        return held

    match = island_adapter_ids[:, None] == owner_slot_adapters[None, :]
    slots = jnp.sum(jnp.where(match, jnp.arange(n_slots, dtype=i32)[None, :], 0), axis=1)
    far_slots = swap(slots, top)

    place = lax.axis_index("fsdp")
    line = n_fsdp <= 4
    height = rows // count
    pieces_of_kept, at = [(output_gradient, 0)], [None]

    def hop(*after, low=0, high=None):
        step = len(at) // 2
        if not line or step + 1 >= n_fsdp:
            return []
        if low == 0:
            ends[:] = next_ends or [output_gradient] * 2
            next_ends.clear()
        right = [(i, i + 1) for i in range(n_fsdp - 1)]
        left = [(i + 1, i) for i in range(n_fsdp - 1)]
        sent = []
        for piece, pairs, place_of in zip(ends, (right, left), (place - step - 1, place + step + 1)):
            piece = behind(piece[low:high], *after)
            sent.append(lax.ppermute(piece, "fsdp", pairs))
            pieces_of_kept.append((sent[-1], low))
            where.append(jnp.where(place_of < n_fsdp, place_of, -1))
        if high is None:
            at.extend([None, None])
            next_ends.extend(sent)
        return sent

    ends, next_ends, where = [], [], [place]
    first_hop = hop()

    share = ff // n_groups
    if share % 2048 == 0:
        unit, tile = share // 8, share // 4
        sizes = [2 * unit] * 4
    else:
        tile = share
        sizes = [share]
    parts = [(sum(sizes[:j]), size) for j, size in enumerate(sizes)]

    crossed = []
    turned = []

    def flat(*pieces):
        return [v for piece in pieces for v in piece.values()]

    def cross(*after):
        j = len(crossed)
        if j < len(parts):
            first_row, size = parts[j]
            piece = lax.dynamic_slice_in_dim(
                frozen_down_weight, group * share + first_row, size, axis=0
            )
            crossed.append({top: swap(behind(piece, *after), top)})

    def turn(*after):
        j = len(turned)
        if j < len(parts):
            piece = behind(crossed[j][top], *after)
            turned.append([])
            for shift in range(1, n_groups):
                ring = [(i, (i + shift) % n_groups) for i in range(n_groups)]
                turned[j].append({top: lax.ppermute(piece, "groups", ring)})

    def fill(chunks, *after):
        for piece in chunks:
            piece.update(spread({top: behind(piece[top], *after)}))

    cross(far_slots)

    first = jnp.swapaxes(adapter_first_factors, 1, 2)
    a_near = spread({0: first})
    b_near = spread({0: adapter_second_factors})
    near = sorted(a_near)
    a_near = [a_near[r] for r in near]
    b_near = [b_near[r] for r in near]
    def places(wanted):
        owner = wanted // local
        index = jnp.concatenate([wanted % local] * len(near))
        return index, jnp.where((owner ^ me) < top, owner ^ me, len(near))

    picked = pick(*places(far_slots), a_near, b_near)
    both_slots = spread({0: behind(jnp.concatenate([slots, far_slots]), picked)})
    past = [picked, *first_hop, *flat(both_slots, *crossed)]
    far = swap(behind(picked, *past[1:]), top)
    whole = spread({0: behind(frozen_down_weight, *past)})
    turn(*past)
    past = [far, *hop(*past), *flat(*turned[0])]

    ready = behind(slots, *flat(whole, both_slots), *past)
    part, block_a, grad_a, grad_b = project(
        *places(ready), a_near, b_near, far, hidden, output_gradient
    )
    third_hop = hop(*past)
    cross(*past)
    cross(*past)
    sums = [part]
    bit = 1
    while bit < n_fsdp:
        sums.append(swap(sums[-1], bit, "fsdp", n_fsdp))
        if 2 * bit < n_fsdp:
            sums.append(sums[-2] + sums[-1])
        bit *= 2
    total, other = sums[-2:]
    turn(part)
    past = [sums[2], *flat(*crossed[:3], *sum(turned[:2], [])), *third_hop]
    cross(*past)
    turn(*past)
    fill(crossed[:2], *past)
    fill(turned[0], *past)

    order = [me ^ r for r in range(n_dp)]
    early = jnp.full((n_dp,), int(line), i32)
    order = jnp.stack(order).astype(i32)

    def collect(named):
        chunks, tiles, places_of = [], [], []
        for shift, t in named:
            first_row = lax.rem(group + n_groups - shift, n_groups) * share
            places_of.append(first_row // tile + t)
            tiles.append([])
            for j, (first, size) in enumerate(parts):
                low, high = max(first, t * tile), min(first + size, (t + 1) * tile)
                if low < high:
                    if (shift, j) not in chunks:
                        chunks.append((shift, j))
                    tiles[-1].append((chunks.index((shift, j)), low - first, high - low))
        return places_of, [turned[j][shift - 1] if shift else crossed[j] for shift, j in chunks], tiles

    sums_of = {}

    def begin(*named):
        at = jnp.stack(where).astype(i32)
        places_of, chunks, tiles = collect(named)
        got = early_sums(
            places_of, jnp.concatenate([order, early, at]), pieces_of_kept, whole, chunks, tiles, tile
        )
        sums_of.update(zip(named, got))
        return got

    others = range(1, n_groups)
    ahead = line and share > tile
    begun = begin((0, 0), (0, 1), *[(g, 0) for g in others]) if ahead else []
    past = [other, *begun, *flat(*crossed, *sum(turned, []))]
    low_terms, high_terms, coef = block_terms(
        island_live_rows, total, other, hidden, output_gradient
    )
    far_high = swap(high_terms, top)
    far_low = swap(low_terms, top)
    turn(*past)
    fill(crossed[2:3], *past)
    for pieces in turned[1:2]:
        fill(pieces, *past)
    if line:
        at = jnp.stack(where).astype(i32)
    else:
        pieces_of_kept = [(lax.all_gather(output_gradient, "fsdp", axis=1, tiled=True), 0)]
        at = jnp.zeros((1,), i32)

    relative = [both_slots[r][:count] for r in near] + [both_slots[r][count:] for r in near]
    relative = jnp.concatenate(relative) - me * local

    scalars = jnp.concatenate([order, early, at, island_live_rows])
    grad_hidden = token = None

    def multiply(*named):
        nonlocal grad_hidden, token
        named = sorted(named, key=lambda name: name not in sums_of)
        places_of, chunks, tiles = collect(named)
        grad_hidden, token = base(
            places_of, scalars, pieces_of_kept, whole, chunks, tiles, tile,
            [sums_of[name] for name in named if name in sums_of], coef, block_a, grad_hidden, token,
        )

    if share > tile:
        multiply(*[(0, t) for t in range(3)], *[(g, t) for g in others for t in range(2)])
        past = [token, far_high]
        fill(crossed[3:], *past)
        for pieces in turned[2:]:
            fill(pieces, *past)
        multiply((0, 3), *[(g, t) for g in others for t in range(2, 4)])
    else:
        multiply(*[(g, 0) for g in range(n_groups)])

    near_low = spread({0: behind(low_terms, *past)})
    near_high = spread({0: behind(high_terms, *past)})
    all_high = spread({top: behind(far_high, *past)})
    all_low = spread({top: behind(far_low, token)})
    terms = [p for r in near for p in (near_low[r], near_high[r])]
    terms += [p for r in near for p in (all_low[r + top], all_high[r + top])]
    grad_a, grad_b = add_terms(relative, terms, grad_a, grad_b, token)
    return grad_hidden, jnp.swapaxes(grad_a, 1, 2), grad_b


def solution(mesh):
    placed = (
        P(("groups", "dp"), "fsdp"),
        P(("groups", "dp"), "fsdp"),
        P("fsdp", "dp"),
        P(("groups", "dp"), "fsdp", None),
        P(("groups", "dp"), None, "fsdp"),
        P(("groups", "dp")),
        P(("groups", "dp")),
        P("groups"),
    )
    sizes = [mesh.shape[name] for name in ("groups", "fsdp", "dp")]
    return jax.shard_map(
        functools.partial(on_device, *sizes),
        mesh=mesh,
        in_specs=placed,
        out_specs=(
            P(("groups", "dp"), "fsdp"),
            P(("groups", "dp"), "fsdp", None),
            P(("groups", "dp"), None, "fsdp"),
        ),
        check_vma=False,
    )
```

```python
import functools

import jax
import jax.numpy as jnp
from jax import lax
from jax.experimental import pallas as pl
from jax.experimental.pallas import tpu as pltpu
from jax.sharding import PartitionSpec as P

adapter_scale = 2.0
factor_gradient = 0.0625
vmem_bytes = 60 * 1024 * 1024
bf16, f32, i32 = jnp.bfloat16, jnp.float32, jnp.int32


def behind(value, *after):
    if not after:
        return value
    return lax.optimization_barrier((value, *after))[0]


def params(cost):
    return dict(
        compiler_params=pltpu.CompilerParams(vmem_limit_bytes=vmem_bytes),
        cost_estimate=pl.CostEstimate(flops=cost[0], bytes_accessed=cost[1], transcendentals=0),
    )


def pick_kernel(pieces, index_ref, source_ref, *refs):
    a_refs, b_refs, out_ref = refs[:pieces], refs[pieces : 2 * pieces], refs[-1]
    source = source_ref[pl.program_id(0)]
    a, b = a_refs[0][0], b_refs[0][0]
    for r in range(1, pieces):
        a = jnp.where(source == r, a_refs[r][0], a)
        b = jnp.where(source == r, b_refs[r][0], b)
    ff = a.shape[1]
    out_ref[0, :, :ff] = a
    out_ref[0, :, ff:] = b


def factor_specs(pieces, count, rank, width):
    return [
        pl.BlockSpec(
            (1, rank, width), lambda i, index, source, r=r: (index[r * count + i], 0, 0)
        )
        for r in range(pieces)
    ]


def pick(index, source, a_pieces, b_pieces):
    count, pieces = source.shape[0], len(a_pieces)
    _, rank, ff = a_pieces[0].shape
    d = b_pieces[0].shape[2]
    return pl.pallas_call(
        functools.partial(pick_kernel, pieces),
        grid_spec=pltpu.PrefetchScalarGridSpec(
            num_scalar_prefetch=2,
            grid=(count,),
            in_specs=factor_specs(pieces, count, rank, ff) + factor_specs(pieces, count, rank, d),
            out_specs=pl.BlockSpec((1, rank, ff + d), lambda i, index, source: (i, 0, 0)),
        ),
        out_shape=jax.ShapeDtypeStruct((count, rank, ff + d), bf16),
        **params((0, 2 * (pieces + 1) * count * rank * (ff + d))),
    )(index, source, *a_pieces, *b_pieces)


def project_kernel(pieces, index_ref, source_ref, *refs):
    a_refs, b_refs = refs[:pieces], refs[pieces : 2 * pieces]
    far_ref, hid_ref, grad_ref, part_ref, block_ref, grad_a_ref, grad_b_ref = refs[
        2 * pieces : 2 * pieces + 7
    ]
    zeros, zero_sem = refs[2 * pieces + 7 :]
    step = pl.program_id(0)
    source = source_ref[step]
    ff = hid_ref.shape[1]
    d = grad_ref.shape[1]

    fills = []
    for slot in range(grad_a_ref.shape[0]):
        fills.append(pltpu.make_async_copy(zeros, grad_a_ref.at[slot], zero_sem.at[2 * slot]))
        fills.append(
            pltpu.make_async_copy(
                zeros.at[:, pl.ds(0, d)], grad_b_ref.at[slot], zero_sem.at[2 * slot + 1]
            )
        )

    @pl.when(step == 0)
    def _():
        zeros[...] = jnp.zeros_like(zeros)
        for fill in fills:
            fill.start()

    a, b = far_ref[0, :, :ff], far_ref[0, :, ff:]
    for r in range(pieces):
        a = jnp.where(source == r, a_refs[r][0], a)
        b = jnp.where(source == r, b_refs[r][0], b)
    block_ref[0] = a
    over_last = (((1,), (1,)), ((), ()))
    rank = a.shape[0]
    part_ref[0, :, :rank] = lax.dot_general(
        hid_ref[...], a, over_last, preferred_element_type=f32
    )
    part_ref[0, :, rank:] = lax.dot_general(
        grad_ref[...], b, over_last, preferred_element_type=f32
    )

    @pl.when(step == pl.num_programs(0) - 1)
    def _():
        for fill in fills:
            fill.wait()


def project(index, source, a_pieces, b_pieces, far, hidden, grad):
    count, pieces = source.shape[0], len(a_pieces)
    local, rank, ff = a_pieces[0].shape
    d = b_pieces[0].shape[2]
    rows = hidden.shape[0]
    height = rows // count
    own = lambda i, index, source: (i, 0)
    own3 = lambda i, index, source: (i, 0, 0)
    return pl.pallas_call(
        functools.partial(project_kernel, pieces),
        grid_spec=pltpu.PrefetchScalarGridSpec(
            num_scalar_prefetch=2,
            grid=(count,),
            in_specs=factor_specs(pieces, count, rank, ff)
            + factor_specs(pieces, count, rank, d)
            + [
                pl.BlockSpec((1, rank, ff + d), own3),
                pl.BlockSpec((height, ff), own),
                pl.BlockSpec((height, d), own),
            ],
            out_specs=[
                pl.BlockSpec((1, height, 2 * rank), own3),
                pl.BlockSpec((1, rank, ff), own3),
                pl.BlockSpec(memory_space=pl.ANY),
                pl.BlockSpec(memory_space=pl.ANY),
            ],
            scratch_shapes=[
                pltpu.VMEM((rank, ff), f32),
                pltpu.SemaphoreType.DMA((2 * local,)),
            ],
        ),
        out_shape=[
            jax.ShapeDtypeStruct((count, height, 2 * rank), f32),
            jax.ShapeDtypeStruct((count, rank, ff), bf16),
            jax.ShapeDtypeStruct((local, rank, ff), f32),
            jax.ShapeDtypeStruct((local, rank, d), f32),
        ],
        **params((2 * rows * rank * (ff + d), 2 * (rows + (pieces + 2) * count * rank) * (ff + d))),
    )(index, source, *a_pieces, *b_pieces, far, hidden, grad)


def terms_kernel(live_ref, here_ref, there_ref, hid_ref, grad_ref, low_ref, high_ref, coef_ref):
    ff = hid_ref.shape[1]
    cut = low_ref.shape[2]
    rank = coef_ref.shape[2]
    total = here_ref[0] + there_ref[0]
    valid = lax.broadcasted_iota(i32, total.shape, 0) < live_ref[pl.program_id(0)]
    total = jnp.where(valid, total, 0.0)
    low = total[:, :rank].astype(bf16)
    coef = (adapter_scale * total[:, rank:]).astype(bf16)
    coef_ref[0] = coef
    over_rows = (((0,), (0,)), ((), ()))
    term_a = (
        factor_gradient
        * lax.dot_general(coef, hid_ref[...], over_rows, preferred_element_type=f32)
    ).astype(bf16)
    low_ref[0] = term_a[:, :cut]
    high_ref[0, :, : ff - cut] = term_a[:, cut:]
    high_ref[0, :, ff - cut :] = (
        factor_gradient
        * adapter_scale
        * lax.dot_general(low, grad_ref[...], over_rows, preferred_element_type=f32)
    ).astype(bf16)


def block_terms(live, here, there, hidden, grad):
    count, height, both = here.shape
    rank = both // 2
    rows, ff = hidden.shape
    d = grad.shape[1]
    cut = (ff + d) // 256 * 128
    own = lambda i, live: (i, 0)
    own3 = lambda i, live: (i, 0, 0)
    return pl.pallas_call(
        terms_kernel,
        grid_spec=pltpu.PrefetchScalarGridSpec(
            num_scalar_prefetch=1,
            grid=(count,),
            in_specs=[
                pl.BlockSpec((1, height, both), own3),
                pl.BlockSpec((1, height, both), own3),
                pl.BlockSpec((height, ff), own),
                pl.BlockSpec((height, d), own),
            ],
            out_specs=[
                pl.BlockSpec((1, rank, cut), own3),
                pl.BlockSpec((1, rank, ff + d - cut), own3),
                pl.BlockSpec((1, height, rank), own3),
            ],
        ),
        out_shape=[
            jax.ShapeDtypeStruct((count, rank, cut), bf16),
            jax.ShapeDtypeStruct((count, rank, ff + d - cut), bf16),
            jax.ShapeDtypeStruct((count, height, rank), bf16),
        ],
        **params((2 * rows * rank * (ff + d), 2 * (rows + count * rank) * (ff + d))),
    )(live, here, there, hidden, grad)


class Tiles:
    def __init__(self, n_dp, tiles, n_chunks, kept_rows, scalars_ref, refs):
        self.near, self.n_dp, self.tiles, self.kept_rows = n_dp // 2, n_dp, tiles, kept_rows
        n_kept = len(kept_rows)
        self.scalars_ref, self.kept_refs, refs = scalars_ref, refs[:n_kept], refs[n_kept:]
        self.near_refs, refs = refs[: self.near], refs[self.near :]
        self.far_refs, self.rest = refs[: n_chunks * self.near], refs[n_chunks * self.near :]
        self.deep = self.near_refs[0].shape[1]
        self.at = [scalars_ref[len(tiles) + n_dp + k] for k in range(n_kept)]

    def lanes(self, r):
        start = self.scalars_ref[len(self.tiles) + r] * self.deep
        return pl.ds(pl.multiple_of(start, self.deep), self.deep)

    def span(self, j, tile):
        return pl.ds(pl.multiple_of(self.scalars_ref[j] * tile, tile), tile)

    def loads(self, j, r, weight, slot, sem):
        if r < self.near:
            rows = self.near_refs[r].at[self.span(j, weight.shape[1]), :]
            return [
                pltpu.make_async_copy(rows, weight.at[slot, :, self.lanes(r)], sem.at[slot, r, 0])
            ]
        copies, low = [], 0
        for k, (chunk, start, size) in enumerate(self.tiles[j]):
            copies.append(
                pltpu.make_async_copy(
                    self.far_refs[chunk * self.near + r - self.near].at[pl.ds(start, size)],
                    weight.at[slot, pl.ds(low, size), self.lanes(r)],
                    sem.at[slot, r, k],
                )
            )
            low += size
        return copies

    def columns(self, k, kept, sem):
        wide = self.kept_refs[k].shape[1]
        place = pl.ds(pl.multiple_of(self.at[k] * wide, wide), wide)
        rows = pl.ds(self.kept_rows[k], self.kept_refs[k].shape[0])
        return pltpu.make_async_copy(self.kept_refs[k], kept.at[rows, place], sem.at[k])

    def each_column(self, kept, sem, act):
        for k in range(len(self.kept_refs)):
            pl.when(self.at[k] >= 0)(lambda k=k: act(self.columns(k, kept, sem)))

    def part(self, r, kept, weight, slot):
        return lax.dot_general(
            kept[:, self.lanes(r)],
            weight[slot, :, self.lanes(r)],
            (((1,), (1,)), ((), ())),
            preferred_element_type=f32,
        )


    def product(self, kept, weight, slot):
        return lax.dot_general(
            kept[...], weight[slot], (((1,), (1,)), ((), ())), preferred_element_type=f32
        )


def start(copies):
    for copy in copies:
        copy.start()


def wait(copies):
    for copy in copies:
        copy.wait()


def early_kernel(n_dp, tiles, n_chunks, kept_rows, scalars_ref, *refs):
    me = Tiles(n_dp, tiles, n_chunks, kept_rows, scalars_ref, refs)
    sums_refs, (kept, weight, total, kept_sem, in_sem, out_sem) = me.rest[:-6], me.rest[-6:]
    steps = len(tiles)

    def load(j, act):
        for r in range(n_dp):
            act(me.loads(j, r, weight, j % 2, in_sem))

    def store(j):
        return pltpu.make_async_copy(total.at[j % 2], sums_refs[j], out_sem.at[j % 2])

    me.each_column(kept, kept_sem, lambda copy: copy.start())
    load(0, start)
    me.each_column(kept, kept_sem, lambda copy: copy.wait())

    @pl.loop(0, steps)
    def _(step):
        slot = lax.rem(step, 2)
        for j in range(steps):

            @pl.when(step == j)
            def _():
                if j + 1 < steps:
                    load(j + 1, start)
                load(j, wait)
                if j >= 2:
                    store(j - 2).wait()

        total[slot] = me.product(kept, weight, slot)
        for j in range(steps):
            pl.when(step == j)(lambda j=j: store(j).start())

    for j in range(max(steps - 2, 0), steps):
        store(j).wait()


def base_kernel(n_dp, tiles, n_chunks, kept_rows, n_held, count, scalars_ref, *refs):
    me = Tiles(n_dp, tiles, n_chunks, kept_rows, scalars_ref, refs)
    held_refs, (coef_ref, block_ref) = me.rest[:n_held], me.rest[n_held : n_held + 2]
    out_ref, token_ref, kept, weight, factor, result, total = me.rest[-12:-5]
    kept_sem, in_sem, factor_sem, out_sem, held_sem = me.rest[-5:]
    _, tile, _ = weight.shape
    height = coef_ref.shape[1]
    steps = len(tiles)
    live = steps + n_dp + len(kept_rows)
    token_ref[...] = jnp.zeros_like(token_ref)

    def load(j, act):
        slot = j % 2
        if j >= n_held:
            for r in range(n_dp):
                act(me.loads(j, r, weight, slot, in_sem))
        if j < n_held:
            act([pltpu.make_async_copy(held_refs[j], total.at[slot], held_sem.at[slot])])
        factors(j, act)

    def factors(j, act):
        slot = j % 2
        act(
            [
                pltpu.make_async_copy(
                    block_ref.at[:, :, me.span(j, tile)], factor.at[slot], factor_sem.at[slot]
                )
            ]
        )

    def store(j):
        return pltpu.make_async_copy(
            result.at[j % 2], out_ref.at[:, me.span(j, tile)], out_sem.at[j % 2]
        )

    def finish(slot, sums):
        for b in range(count):
            extra = jnp.dot(coef_ref[b], factor[slot, b], preferred_element_type=f32)
            here = sums[b * height : (b + 1) * height] + extra
            valid = lax.broadcasted_iota(i32, here.shape, 0) < scalars_ref[live + b]
            result[slot, b * height : (b + 1) * height, :] = jnp.where(valid, here, 0.0).astype(
                bf16
            )

    load(0, start)
    if n_held < steps:
        me.each_column(kept, kept_sem, lambda copy: copy.start())
    if steps > 1:
        load(1, start)
    first = 0
    if not n_held and me.kept_refs[0].shape[1] == me.deep:
        first, sums = 1, None
        for r in range(n_dp):
            for k in range(len(kept_rows)):
                pl.when(me.at[k] == scalars_ref[steps + r])(
                    lambda k=k: me.columns(k, kept, kept_sem).wait()
                )
            wait(me.loads(0, r, weight, 0, in_sem))
            part = me.part(r, kept, weight, 0)
            sums = part if sums is None else sums + part
        factors(0, wait)
        finish(0, sums)
        store(0).start()
    elif not n_held:
        me.each_column(kept, kept_sem, lambda copy: copy.wait())

    @pl.loop(first, steps)
    def _(step):
        slot = lax.rem(step, 2)
        for j in range(first, steps):

            @pl.when(step == j)
            def _():
                if 1 < j + 1 < steps:
                    load(j + 1, start)
                if 0 < j == n_held:
                    me.each_column(kept, kept_sem, lambda copy: copy.wait())
                load(j, wait)
                if j >= 2:
                    store(j - 2).wait()

        if n_held:
            pl.when(step < n_held)(lambda: finish(slot, total[slot]))
        if n_held < steps:
            pl.when(step >= n_held)(lambda: finish(slot, me.product(kept, weight, slot)))

        for j in range(steps):
            pl.when(step == j)(lambda j=j: store(j).start())

    for j in range(max(steps - 2, 0), steps):
        store(j).wait()


def tile_scratch(rows, tile, depth, n_kept, n_dp, tiles):
    most = max(len(segments) for segments in tiles)
    return [
        pltpu.VMEM((rows, depth), bf16),
        pltpu.VMEM((2, tile, depth), bf16),
    ], [
        pltpu.SemaphoreType.DMA((n_kept,)),
        pltpu.SemaphoreType.DMA((2, n_dp, most)),
    ]


def tile_operands(kept, near, chunks):
    top = len(near)
    operands = [piece for piece, _ in kept] + [near[r] for r in range(top)]
    for piece in chunks:
        operands += [piece[r] for r in range(top, 2 * top)]
    return operands


def early_sums(places, scalars, kept, near, chunks, tiles, tile):
    rows = kept[0][0].shape[0]
    n_dp = 2 * len(near)
    depth = n_dp * near[0].shape[1]
    anywhere = pl.BlockSpec(memory_space=pl.ANY)
    operands = tile_operands(kept, near, chunks)
    buffers, semaphores = tile_scratch(rows, tile, depth, len(kept), n_dp, tiles)
    return pl.pallas_call(
        functools.partial(early_kernel, n_dp, tiles, len(chunks), [low for _, low in kept]),
        grid_spec=pltpu.PrefetchScalarGridSpec(
            num_scalar_prefetch=1,
            grid=(1,),
            in_specs=[anywhere] * len(operands),
            out_specs=[anywhere] * len(tiles),
            scratch_shapes=[
                *buffers,
                pltpu.VMEM((2, rows, tile), f32),
                *semaphores,
                pltpu.SemaphoreType.DMA((2,)),
            ],
        ),
        out_shape=[jax.ShapeDtypeStruct((rows, tile), f32)] * len(tiles),
        **params((1, 1)),
    )(jnp.concatenate([jnp.stack(places).astype(i32), scalars]), *operands)


def base(places, scalars, kept, near, chunks, tiles, tile, early, coef, block_a, held, token):
    rows = kept[0][0].shape[0]
    count, rank, ff = block_a.shape
    n_dp = 2 * len(near)
    depth = n_dp * near[0].shape[1]
    anywhere = pl.BlockSpec(memory_space=pl.ANY)
    operands = tile_operands(kept, near, chunks) + early
    in_specs = [anywhere] * len(operands)
    in_specs += [pl.BlockSpec(coef.shape, lambda i, s: (0, 0, 0)), anywhere]
    operands += [coef, block_a]
    aliases = {}
    if held is not None:
        in_specs += [anywhere, anywhere]
        operands += [token, held]
        aliases = {len(operands): 0}
    buffers, semaphores = tile_scratch(rows, tile, depth, len(kept), n_dp, tiles)
    return pl.pallas_call(
        functools.partial(
            base_kernel, n_dp, tiles, len(chunks), [low for _, low in kept], len(early), count
        ),
        grid_spec=pltpu.PrefetchScalarGridSpec(
            num_scalar_prefetch=1,
            grid=(1,),
            in_specs=in_specs,
            out_specs=[anywhere, pl.BlockSpec((8, 128), lambda i, s: (0, 0))],
            scratch_shapes=[
                *buffers,
                pltpu.VMEM((2, count, rank, tile), bf16),
                pltpu.VMEM((2, rows, tile), bf16),
                pltpu.VMEM((2, rows, tile), f32),
                *semaphores,
                pltpu.SemaphoreType.DMA((2,)),
                pltpu.SemaphoreType.DMA((2,)),
                pltpu.SemaphoreType.DMA((2,)),
            ],
        ),
        out_shape=[
            jax.ShapeDtypeStruct((rows, ff), bf16),
            jax.ShapeDtypeStruct((8, 128), f32),
        ],
        input_output_aliases=aliases,
        **params((1, 1)),
    )(jnp.concatenate([jnp.stack(places).astype(i32), scalars]), *operands)


def add_kernel(pieces, count, slots_ref, *refs):
    term_refs = refs[: 2 * pieces]
    a_ref, b_ref, terms, a, b, term_sem, a_sem, b_sem = refs[2 * pieces + 3 :]
    local, _, ff = a.shape
    both = terms.shape[2]
    cut = term_refs[0].shape[2]

    def load(k):
        lanes = (pl.ds(0, cut), pl.ds(cut, both - cut))
        return [
            pltpu.make_async_copy(
                term_refs[k // count * 2 + part].at[k % count],
                terms.at[k, :, lanes[part]],
                term_sem.at[k, part],
            )
            for part in range(2)
        ]

    def whole(slot, inward):
        pairs = [(a_ref.at[slot], a.at[slot]), (b_ref.at[slot], b.at[slot])]
        return [
            pltpu.make_async_copy(*(pair if inward else pair[::-1]), sem.at[slot])
            for pair, sem in zip(pairs, (a_sem, b_sem))
        ]

    wanted = [slots_ref[k] for k in range(pieces * count)]
    owned = [(slot >= 0) & (slot < local) for slot in wanted]
    hit = []
    for j in range(local):
        any_here = wanted[0] == j
        for slot in wanted[1:]:
            any_here = any_here | (slot == j)
        hit.append(any_here)

    for j in range(local):
        pl.when(hit[j])(lambda j=j: start(whole(j, True)))
    for k in range(pieces * count):
        pl.when(owned[k])(lambda k=k: start(load(k)))
    for j in range(local):
        pl.when(hit[j])(lambda j=j: wait(whole(j, True)))

    def add(k):
        wait(load(k))
        a[wanted[k]] += terms[k, :, :ff].astype(f32)
        b[wanted[k]] += terms[k, :, ff:].astype(f32)

    for k in range(pieces * count):
        pl.when(owned[k])(lambda k=k: add(k))
    for j in range(local):
        pl.when(hit[j])(lambda j=j: start(whole(j, False)))
    for j in range(local):
        pl.when(hit[j])(lambda j=j: wait(whole(j, False)))


def add_terms(slots, pieces, grad_a, grad_b, token):
    count, rank, _ = pieces[0].shape
    both = pieces[0].shape[2] + pieces[1].shape[2]
    anywhere = pl.BlockSpec(memory_space=pl.ANY)
    n = len(pieces) // 2
    local = grad_a.shape[0]
    return pl.pallas_call(
        functools.partial(add_kernel, n, count),
        grid_spec=pltpu.PrefetchScalarGridSpec(
            num_scalar_prefetch=1,
            grid=(1,),
            in_specs=[anywhere] * (2 * n + 3),
            out_specs=[anywhere] * 2,
            scratch_shapes=[
                pltpu.VMEM((n * count, rank, both), bf16),
                pltpu.VMEM(grad_a.shape, f32),
                pltpu.VMEM(grad_b.shape, f32),
                pltpu.SemaphoreType.DMA((n * count, 2)),
                pltpu.SemaphoreType.DMA((local,)),
                pltpu.SemaphoreType.DMA((local,)),
            ],
        ),
        out_shape=[
            jax.ShapeDtypeStruct(grad_a.shape, f32),
            jax.ShapeDtypeStruct(grad_b.shape, f32),
        ],
        input_output_aliases={2 * n + 2: 0, 2 * n + 3: 1},
        **params((1, 1)),
    )(slots, *pieces, token, grad_a, grad_b)


def on_device(
    n_groups,
    n_fsdp,
    n_dp,
    output_gradient,
    hidden,
    frozen_down_weight,
    adapter_first_factors,
    adapter_second_factors,
    island_live_rows,
    island_adapter_ids,
    owner_slot_adapters,
):
    rows, ff = hidden.shape
    d = output_gradient.shape[1]
    count = island_live_rows.shape[0]
    local = adapter_first_factors.shape[0]
    n_slots = owner_slot_adapters.shape[0]
    top = n_dp // 2
    me = lax.axis_index("dp")
    group = lax.axis_index("groups")

    def swap(value, bit, axis="dp", size=n_dp):
        return lax.ppermute(value, axis, [(i, i ^ bit) for i in range(size)])

    def spread(held):
        held = dict(held)
        bit = top // 2
        while bit:
            for r in list(held):
                held[r ^ bit] = swap(held[r], bit)
            bit //= 2
        return held

    match = island_adapter_ids[:, None] == owner_slot_adapters[None, :]
    slots = jnp.sum(jnp.where(match, jnp.arange(n_slots, dtype=i32)[None, :], 0), axis=1)
    far_slots = swap(slots, top)

    place = lax.axis_index("fsdp")
    line = n_fsdp <= 4
    height = rows // count
    pieces_of_kept, at = [(output_gradient, 0)], [None]

    def hop(*after, low=0, high=None):
        step = len(at) // 2
        if not line or step + 1 >= n_fsdp:
            return []
        if low == 0:
            ends[:] = next_ends or [output_gradient] * 2
            next_ends.clear()
        right = [(i, i + 1) for i in range(n_fsdp - 1)]
        left = [(i + 1, i) for i in range(n_fsdp - 1)]
        sent = []
        for piece, pairs, place_of in zip(ends, (right, left), (place - step - 1, place + step + 1)):
            piece = behind(piece[low:high], *after)
            sent.append(lax.ppermute(piece, "fsdp", pairs))
            pieces_of_kept.append((sent[-1], low))
            where.append(jnp.where(place_of < n_fsdp, place_of, -1))
        if high is None:
            at.extend([None, None])
            next_ends.extend(sent)
        return sent

    ends, next_ends, where = [], [], [place]
    first_hop = hop()

    share = ff // n_groups
    if share % 2048 == 0:
        unit, tile = share // 8, share // 4
        sizes = [2 * unit] * 4
    else:
        tile = share
        sizes = [share]
    parts = [(sum(sizes[:j]), size) for j, size in enumerate(sizes)]

    crossed = []
    turned = []

    def flat(*pieces):
        return [v for piece in pieces for v in piece.values()]

    def cross(*after):
        j = len(crossed)
        if j < len(parts):
            first_row, size = parts[j]
            piece = lax.dynamic_slice_in_dim(
                frozen_down_weight, group * share + first_row, size, axis=0
            )
            crossed.append({top: swap(behind(piece, *after), top)})

    def turn(*after):
        j = len(turned)
        if j < len(parts):
            piece = behind(crossed[j][top], *after)
            turned.append([])
            for shift in range(1, n_groups):
                ring = [(i, (i + shift) % n_groups) for i in range(n_groups)]
                turned[j].append({top: lax.ppermute(piece, "groups", ring)})

    def fill(chunks, *after):
        for piece in chunks:
            piece.update(spread({top: behind(piece[top], *after)}))

    cross(far_slots)

    first = jnp.swapaxes(adapter_first_factors, 1, 2)
    a_near = spread({0: first})
    b_near = spread({0: adapter_second_factors})
    near = sorted(a_near)
    a_near = [a_near[r] for r in near]
    b_near = [b_near[r] for r in near]
    def places(wanted):
        owner = wanted // local
        index = jnp.concatenate([wanted % local] * len(near))
        return index, jnp.where((owner ^ me) < top, owner ^ me, len(near))

    picked = pick(*places(far_slots), a_near, b_near)
    both_slots = spread({0: behind(jnp.concatenate([slots, far_slots]), picked)})
    past = [picked, *first_hop, *flat(both_slots, *crossed)]
    far = swap(behind(picked, *past[1:]), top)
    whole = spread({0: behind(frozen_down_weight, *past)})
    turn(*past)
    past = [far, *hop(*past), *flat(*turned[0])]

    ready = behind(slots, *flat(whole, both_slots), *past)
    part, block_a, grad_a, grad_b = project(
        *places(ready), a_near, b_near, far, hidden, output_gradient
    )
    third_hop = hop(*past)
    cross(*past)
    cross(*past)
    sums = [part]
    bit = 1
    while bit < n_fsdp:
        sums.append(swap(sums[-1], bit, "fsdp", n_fsdp))
        if 2 * bit < n_fsdp:
            sums.append(sums[-2] + sums[-1])
        bit *= 2
    total, other = sums[-2:]
    turn(part)
    past = [sums[2], *flat(*crossed[:3], *sum(turned[:2], [])), *third_hop]
    cross(*past)
    turn(*past)
    fill(crossed[:2], *past)
    fill(turned[0], *past)

    order = [me ^ r for r in range(n_dp)]
    order = jnp.stack(order).astype(i32)

    def collect(named):
        chunks, tiles, places_of = [], [], []
        for shift, t in named:
            first_row = lax.rem(group + n_groups - shift, n_groups) * share
            places_of.append(first_row // tile + t)
            tiles.append([])
            for j, (first, size) in enumerate(parts):
                low, high = max(first, t * tile), min(first + size, (t + 1) * tile)
                if low < high:
                    if (shift, j) not in chunks:
                        chunks.append((shift, j))
                    tiles[-1].append((chunks.index((shift, j)), low - first, high - low))
        return places_of, [turned[j][shift - 1] if shift else crossed[j] for shift, j in chunks], tiles

    sums_of = {}

    def begin(*named):
        at = jnp.stack(where).astype(i32)
        places_of, chunks, tiles = collect(named)
        got = early_sums(
            places_of, jnp.concatenate([order, at]), pieces_of_kept, whole, chunks, tiles, tile
        )
        sums_of.update(zip(named, got))
        return got

    others = range(1, n_groups)
    ahead = line and share > tile
    begun = begin((0, 0), (0, 1), *[(g, 0) for g in others]) if ahead else []
    past = [other, *begun, *flat(*crossed, *sum(turned, []))]
    low_terms, high_terms, coef = block_terms(
        island_live_rows, total, other, hidden, output_gradient
    )
    far_high = swap(high_terms, top)
    far_low = swap(low_terms, top)
    turn(*past)
    fill(crossed[2:3], *past)
    for pieces in turned[1:2]:
        fill(pieces, *past)
    if line:
        at = jnp.stack(where).astype(i32)
    else:
        pieces_of_kept = [(lax.all_gather(output_gradient, "fsdp", axis=1, tiled=True), 0)]
        at = jnp.zeros((1,), i32)

    relative = [both_slots[r][:count] for r in near] + [both_slots[r][count:] for r in near]
    relative = jnp.concatenate(relative) - me * local

    scalars = jnp.concatenate([order, at, island_live_rows])
    grad_hidden = token = None

    def multiply(*named):
        nonlocal grad_hidden, token
        named = sorted(named, key=lambda name: name not in sums_of)
        places_of, chunks, tiles = collect(named)
        grad_hidden, token = base(
            places_of, scalars, pieces_of_kept, whole, chunks, tiles, tile,
            [sums_of[name] for name in named if name in sums_of], coef, block_a, grad_hidden, token,
        )

    def add_near(grad_a, grad_b):
        low, high = spread({0: low_terms}), spread({0: high_terms})
        pieces = [p for r in near for p in (low[r], high[r])]
        return add_terms(relative[:edge], pieces, grad_a, grad_b, coef)

    edge = count * len(near)
    if share > tile:
        multiply(*[(0, t) for t in range(3)], *[(g, t) for g in others for t in range(2)])
        past = [token, far_high]
        fill(crossed[3:], *past)
        for pieces in turned[2:]:
            fill(pieces, *past)
        grad_a, grad_b = add_near(grad_a, grad_b)
        scalars = behind(scalars, grad_b)
        multiply((0, 3), *[(g, t) for g in others for t in range(2, 4)])
    else:
        multiply(*[(g, 0) for g in range(n_groups)])
        grad_a, grad_b = add_near(grad_a, grad_b)

    all_high = spread({top: behind(far_high, *past)})
    all_low = spread({top: behind(far_low, token)})
    terms = [p for r in near for p in (all_low[r + top], all_high[r + top])]
    grad_a, grad_b = add_terms(relative[edge:], terms, grad_a, grad_b, token)
    return grad_hidden, jnp.swapaxes(grad_a, 1, 2), grad_b


def solution(mesh):
    placed = (
        P(("groups", "dp"), "fsdp"),
        P(("groups", "dp"), "fsdp"),
        P("fsdp", "dp"),
        P(("groups", "dp"), "fsdp", None),
        P(("groups", "dp"), None, "fsdp"),
        P(("groups", "dp")),
        P(("groups", "dp")),
        P("groups"),
    )
    sizes = [mesh.shape[name] for name in ("groups", "fsdp", "dp")]
    return jax.shard_map(
        functools.partial(on_device, *sizes),
        mesh=mesh,
        in_specs=placed,
        out_specs=(
            P(("groups", "dp"), "fsdp"),
            P(("groups", "dp"), "fsdp", None),
            P(("groups", "dp"), None, "fsdp"),
        ),
        check_vma=False,
    )
```

```python
import functools

import jax
import jax.numpy as jnp
from jax import lax
from jax.experimental import pallas as pl
from jax.experimental.pallas import tpu as pltpu
from jax.sharding import PartitionSpec as P

adapter_scale = 2.0
factor_gradient = 0.0625
vmem_bytes = 60 * 1024 * 1024
bf16, f32, i32 = jnp.bfloat16, jnp.float32, jnp.int32


def behind(value, *after):
    if not after:
        return value
    return lax.optimization_barrier((value, *after))[0]


def params(cost):
    return dict(
        compiler_params=pltpu.CompilerParams(vmem_limit_bytes=vmem_bytes),
        cost_estimate=pl.CostEstimate(flops=cost[0], bytes_accessed=cost[1], transcendentals=0),
    )


def pick_kernel(pieces, index_ref, source_ref, *refs):
    a_refs, b_refs, out_ref = refs[:pieces], refs[pieces : 2 * pieces], refs[-1]
    source = source_ref[pl.program_id(0)]
    a, b = a_refs[0][0], b_refs[0][0]
    for r in range(1, pieces):
        a = jnp.where(source == r, a_refs[r][0], a)
        b = jnp.where(source == r, b_refs[r][0], b)
    ff = a.shape[1]
    out_ref[0, :, :ff] = a
    out_ref[0, :, ff:] = b


def factor_specs(pieces, count, rank, width):
    return [
        pl.BlockSpec(
            (1, rank, width), lambda i, index, source, r=r: (index[r * count + i], 0, 0)
        )
        for r in range(pieces)
    ]


def pick(index, source, a_pieces, b_pieces):
    count, pieces = source.shape[0], len(a_pieces)
    _, rank, ff = a_pieces[0].shape
    d = b_pieces[0].shape[2]
    return pl.pallas_call(
        functools.partial(pick_kernel, pieces),
        grid_spec=pltpu.PrefetchScalarGridSpec(
            num_scalar_prefetch=2,
            grid=(count,),
            in_specs=factor_specs(pieces, count, rank, ff) + factor_specs(pieces, count, rank, d),
            out_specs=pl.BlockSpec((1, rank, ff + d), lambda i, index, source: (i, 0, 0)),
        ),
        out_shape=jax.ShapeDtypeStruct((count, rank, ff + d), bf16),
        **params((0, 2 * (pieces + 1) * count * rank * (ff + d))),
    )(index, source, *a_pieces, *b_pieces)


def project_kernel(pieces, index_ref, source_ref, *refs):
    a_refs, b_refs = refs[:pieces], refs[pieces : 2 * pieces]
    far_ref, hid_ref, grad_ref, part_ref, block_ref, grad_a_ref, grad_b_ref = refs[
        2 * pieces : 2 * pieces + 7
    ]
    zeros, zero_sem = refs[2 * pieces + 7 :]
    step = pl.program_id(0)
    source = source_ref[step]
    ff = hid_ref.shape[1]
    d = grad_ref.shape[1]

    fills = []
    for slot in range(grad_a_ref.shape[0]):
        fills.append(pltpu.make_async_copy(zeros, grad_a_ref.at[slot], zero_sem.at[2 * slot]))
        fills.append(
            pltpu.make_async_copy(
                zeros.at[:, pl.ds(0, d)], grad_b_ref.at[slot], zero_sem.at[2 * slot + 1]
            )
        )

    @pl.when(step == 0)
    def _():
        zeros[...] = jnp.zeros_like(zeros)
        for fill in fills:
            fill.start()

    a, b = far_ref[0, :, :ff], far_ref[0, :, ff:]
    for r in range(pieces):
        a = jnp.where(source == r, a_refs[r][0], a)
        b = jnp.where(source == r, b_refs[r][0], b)
    block_ref[0] = a
    over_last = (((1,), (1,)), ((), ()))
    rank = a.shape[0]
    part_ref[0, :, :rank] = lax.dot_general(
        hid_ref[...], a, over_last, preferred_element_type=f32
    )
    part_ref[0, :, rank:] = lax.dot_general(
        grad_ref[...], b, over_last, preferred_element_type=f32
    )

    @pl.when(step == pl.num_programs(0) - 1)
    def _():
        for fill in fills:
            fill.wait()


def project(index, source, a_pieces, b_pieces, far, hidden, grad):
    count, pieces = source.shape[0], len(a_pieces)
    local, rank, ff = a_pieces[0].shape
    d = b_pieces[0].shape[2]
    rows = hidden.shape[0]
    height = rows // count
    own = lambda i, index, source: (i, 0)
    own3 = lambda i, index, source: (i, 0, 0)
    return pl.pallas_call(
        functools.partial(project_kernel, pieces),
        grid_spec=pltpu.PrefetchScalarGridSpec(
            num_scalar_prefetch=2,
            grid=(count,),
            in_specs=factor_specs(pieces, count, rank, ff)
            + factor_specs(pieces, count, rank, d)
            + [
                pl.BlockSpec((1, rank, ff + d), own3),
                pl.BlockSpec((height, ff), own),
                pl.BlockSpec((height, d), own),
            ],
            out_specs=[
                pl.BlockSpec((1, height, 2 * rank), own3),
                pl.BlockSpec((1, rank, ff), own3),
                pl.BlockSpec(memory_space=pl.ANY),
                pl.BlockSpec(memory_space=pl.ANY),
            ],
            scratch_shapes=[
                pltpu.VMEM((rank, ff), f32),
                pltpu.SemaphoreType.DMA((2 * local,)),
            ],
        ),
        out_shape=[
            jax.ShapeDtypeStruct((count, height, 2 * rank), f32),
            jax.ShapeDtypeStruct((count, rank, ff), bf16),
            jax.ShapeDtypeStruct((local, rank, ff), f32),
            jax.ShapeDtypeStruct((local, rank, d), f32),
        ],
        **params((2 * rows * rank * (ff + d), 2 * (rows + (pieces + 2) * count * rank) * (ff + d))),
    )(index, source, *a_pieces, *b_pieces, far, hidden, grad)


def terms_kernel(live_ref, here_ref, there_ref, hid_ref, grad_ref, low_ref, high_ref, coef_ref):
    ff = hid_ref.shape[1]
    cut = low_ref.shape[2]
    rank = coef_ref.shape[2]
    total = here_ref[0] + there_ref[0]
    valid = lax.broadcasted_iota(i32, total.shape, 0) < live_ref[pl.program_id(0)]
    total = jnp.where(valid, total, 0.0)
    low = total[:, :rank].astype(bf16)
    coef = (adapter_scale * total[:, rank:]).astype(bf16)
    coef_ref[0] = coef
    over_rows = (((0,), (0,)), ((), ()))
    term_a = (
        factor_gradient
        * lax.dot_general(coef, hid_ref[...], over_rows, preferred_element_type=f32)
    ).astype(bf16)
    low_ref[0] = term_a[:, :cut]
    high_ref[0, :, : ff - cut] = term_a[:, cut:]
    high_ref[0, :, ff - cut :] = (
        factor_gradient
        * adapter_scale
        * lax.dot_general(low, grad_ref[...], over_rows, preferred_element_type=f32)
    ).astype(bf16)


def block_terms(live, here, there, hidden, grad):
    count, height, both = here.shape
    rank = both // 2
    rows, ff = hidden.shape
    d = grad.shape[1]
    cut = (ff + d) // 256 * 128
    own = lambda i, live: (i, 0)
    own3 = lambda i, live: (i, 0, 0)
    return pl.pallas_call(
        terms_kernel,
        grid_spec=pltpu.PrefetchScalarGridSpec(
            num_scalar_prefetch=1,
            grid=(count,),
            in_specs=[
                pl.BlockSpec((1, height, both), own3),
                pl.BlockSpec((1, height, both), own3),
                pl.BlockSpec((height, ff), own),
                pl.BlockSpec((height, d), own),
            ],
            out_specs=[
                pl.BlockSpec((1, rank, cut), own3),
                pl.BlockSpec((1, rank, ff + d - cut), own3),
                pl.BlockSpec((1, height, rank), own3),
            ],
        ),
        out_shape=[
            jax.ShapeDtypeStruct((count, rank, cut), bf16),
            jax.ShapeDtypeStruct((count, rank, ff + d - cut), bf16),
            jax.ShapeDtypeStruct((count, height, rank), bf16),
        ],
        **params((2 * rows * rank * (ff + d), 2 * (rows + count * rank) * (ff + d))),
    )(live, here, there, hidden, grad)


class Tiles:
    def __init__(self, n_dp, tiles, n_chunks, kept_rows, scalars_ref, refs):
        self.near, self.n_dp, self.tiles, self.kept_rows = n_dp // 2, n_dp, tiles, kept_rows
        n_kept = len(kept_rows)
        self.scalars_ref, self.kept_refs, refs = scalars_ref, refs[:n_kept], refs[n_kept:]
        self.near_refs, refs = refs[: self.near], refs[self.near :]
        self.far_refs, self.rest = refs[: n_chunks * self.near], refs[n_chunks * self.near :]
        self.deep = self.near_refs[0].shape[1]
        self.at = [scalars_ref[len(tiles) + n_dp + k] for k in range(n_kept)]

    def lanes(self, r):
        start = self.scalars_ref[len(self.tiles) + r] * self.deep
        return pl.ds(pl.multiple_of(start, self.deep), self.deep)

    def span(self, j, tile):
        return pl.ds(pl.multiple_of(self.scalars_ref[j] * tile, tile), tile)

    def loads(self, j, r, weight, slot, sem):
        if r < self.near:
            rows = self.near_refs[r].at[self.span(j, weight.shape[1]), :]
            return [
                pltpu.make_async_copy(rows, weight.at[slot, :, self.lanes(r)], sem.at[slot, r, 0])
            ]
        copies, low = [], 0
        for k, (chunk, start, size) in enumerate(self.tiles[j]):
            copies.append(
                pltpu.make_async_copy(
                    self.far_refs[chunk * self.near + r - self.near].at[pl.ds(start, size)],
                    weight.at[slot, pl.ds(low, size), self.lanes(r)],
                    sem.at[slot, r, k],
                )
            )
            low += size
        return copies

    def columns(self, k, kept, sem):
        wide = self.kept_refs[k].shape[1]
        place = pl.ds(pl.multiple_of(self.at[k] * wide, wide), wide)
        rows = pl.ds(self.kept_rows[k], self.kept_refs[k].shape[0])
        return pltpu.make_async_copy(self.kept_refs[k], kept.at[rows, place], sem.at[k])

    def each_column(self, kept, sem, act):
        for k in range(len(self.kept_refs)):
            pl.when(self.at[k] >= 0)(lambda k=k: act(self.columns(k, kept, sem)))

    def part(self, r, kept, weight, slot):
        return lax.dot_general(
            kept[:, self.lanes(r)],
            weight[slot, :, self.lanes(r)],
            (((1,), (1,)), ((), ())),
            preferred_element_type=f32,
        )


    def product(self, kept, weight, slot):
        return lax.dot_general(
            kept[...], weight[slot], (((1,), (1,)), ((), ())), preferred_element_type=f32
        )


def start(copies):
    for copy in copies:
        copy.start()


def wait(copies):
    for copy in copies:
        copy.wait()


def early_kernel(n_dp, tiles, n_chunks, kept_rows, scalars_ref, *refs):
    me = Tiles(n_dp, tiles, n_chunks, kept_rows, scalars_ref, refs)
    sums_refs, (kept, weight, total, kept_sem, in_sem, out_sem) = me.rest[:-6], me.rest[-6:]
    steps = len(tiles)

    def load(j, act):
        for r in range(n_dp):
            act(me.loads(j, r, weight, j % 2, in_sem))

    def store(j):
        return pltpu.make_async_copy(total.at[j % 2], sums_refs[j], out_sem.at[j % 2])

    me.each_column(kept, kept_sem, lambda copy: copy.start())
    load(0, start)
    me.each_column(kept, kept_sem, lambda copy: copy.wait())

    @pl.loop(0, steps)
    def _(step):
        slot = lax.rem(step, 2)
        for j in range(steps):

            @pl.when(step == j)
            def _():
                if j + 1 < steps:
                    load(j + 1, start)
                load(j, wait)
                if j >= 2:
                    store(j - 2).wait()

        total[slot] = me.product(kept, weight, slot)
        for j in range(steps):
            pl.when(step == j)(lambda j=j: store(j).start())

    for j in range(max(steps - 2, 0), steps):
        store(j).wait()


def base_kernel(n_dp, tiles, n_chunks, kept_rows, n_held, count, scalars_ref, *refs):
    me = Tiles(n_dp, tiles, n_chunks, kept_rows, scalars_ref, refs)
    held_refs, (coef_ref, block_ref) = me.rest[:n_held], me.rest[n_held : n_held + 2]
    out_ref, token_ref, kept, weight, factor, result, total = me.rest[-12:-5]
    kept_sem, in_sem, factor_sem, out_sem, held_sem = me.rest[-5:]
    _, tile, _ = weight.shape
    height = coef_ref.shape[1]
    steps = len(tiles)
    live = steps + n_dp + len(kept_rows)
    token_ref[...] = jnp.zeros_like(token_ref)

    def load(j, act):
        slot = j % 2
        if j >= n_held:
            for r in range(n_dp):
                act(me.loads(j, r, weight, slot, in_sem))
        if j < n_held:
            act([pltpu.make_async_copy(held_refs[j], total.at[slot], held_sem.at[slot])])
        factors(j, act)

    def factors(j, act):
        slot = j % 2
        act(
            [
                pltpu.make_async_copy(
                    block_ref.at[:, :, me.span(j, tile)], factor.at[slot], factor_sem.at[slot]
                )
            ]
        )

    def store(j):
        return pltpu.make_async_copy(
            result.at[j % 2], out_ref.at[:, me.span(j, tile)], out_sem.at[j % 2]
        )

    def finish(slot, sums):
        for b in range(count):
            extra = jnp.dot(coef_ref[b], factor[slot, b], preferred_element_type=f32)
            here = sums[b * height : (b + 1) * height] + extra
            valid = lax.broadcasted_iota(i32, here.shape, 0) < scalars_ref[live + b]
            result[slot, b * height : (b + 1) * height, :] = jnp.where(valid, here, 0.0).astype(
                bf16
            )

    load(0, start)
    if n_held < steps:
        me.each_column(kept, kept_sem, lambda copy: copy.start())
    if steps > 1:
        load(1, start)
    first = 0
    if not n_held and me.kept_refs[0].shape[1] == me.deep:
        first, sums = 1, None
        for r in range(n_dp):
            for k in range(len(kept_rows)):
                pl.when(me.at[k] == scalars_ref[steps + r])(
                    lambda k=k: me.columns(k, kept, kept_sem).wait()
                )
            wait(me.loads(0, r, weight, 0, in_sem))
            part = me.part(r, kept, weight, 0)
            sums = part if sums is None else sums + part
        factors(0, wait)
        finish(0, sums)
        store(0).start()
    elif not n_held:
        me.each_column(kept, kept_sem, lambda copy: copy.wait())

    @pl.loop(first, steps)
    def _(step):
        slot = lax.rem(step, 2)
        for j in range(first, steps):

            @pl.when(step == j)
            def _():
                if 1 < j + 1 < steps:
                    load(j + 1, start)
                if 0 < j == n_held:
                    me.each_column(kept, kept_sem, lambda copy: copy.wait())
                load(j, wait)
                if j >= 2:
                    store(j - 2).wait()

        if n_held:
            pl.when(step < n_held)(lambda: finish(slot, total[slot]))
        if n_held < steps:
            pl.when(step >= n_held)(lambda: finish(slot, me.product(kept, weight, slot)))

        for j in range(steps):
            pl.when(step == j)(lambda j=j: store(j).start())

    for j in range(max(steps - 2, 0), steps):
        store(j).wait()


def tile_scratch(rows, tile, depth, n_kept, n_dp, tiles):
    most = max(len(segments) for segments in tiles)
    return [
        pltpu.VMEM((rows, depth), bf16),
        pltpu.VMEM((2, tile, depth), bf16),
    ], [
        pltpu.SemaphoreType.DMA((n_kept,)),
        pltpu.SemaphoreType.DMA((2, n_dp, most)),
    ]


def tile_operands(kept, near, chunks):
    top = len(near)
    operands = [piece for piece, _ in kept] + [near[r] for r in range(top)]
    for piece in chunks:
        operands += [piece[r] for r in range(top, 2 * top)]
    return operands


def early_sums(places, scalars, kept, near, chunks, tiles, tile):
    rows = kept[0][0].shape[0]
    n_dp = 2 * len(near)
    depth = n_dp * near[0].shape[1]
    anywhere = pl.BlockSpec(memory_space=pl.ANY)
    operands = tile_operands(kept, near, chunks)
    buffers, semaphores = tile_scratch(rows, tile, depth, len(kept), n_dp, tiles)
    return pl.pallas_call(
        functools.partial(early_kernel, n_dp, tiles, len(chunks), [low for _, low in kept]),
        grid_spec=pltpu.PrefetchScalarGridSpec(
            num_scalar_prefetch=1,
            grid=(1,),
            in_specs=[anywhere] * len(operands),
            out_specs=[anywhere] * len(tiles),
            scratch_shapes=[
                *buffers,
                pltpu.VMEM((2, rows, tile), f32),
                *semaphores,
                pltpu.SemaphoreType.DMA((2,)),
            ],
        ),
        out_shape=[jax.ShapeDtypeStruct((rows, tile), f32)] * len(tiles),
        **params((1, 1)),
    )(jnp.concatenate([jnp.stack(places).astype(i32), scalars]), *operands)


def base(places, scalars, kept, near, chunks, tiles, tile, early, coef, block_a, held, token):
    rows = kept[0][0].shape[0]
    count, rank, ff = block_a.shape
    n_dp = 2 * len(near)
    depth = n_dp * near[0].shape[1]
    anywhere = pl.BlockSpec(memory_space=pl.ANY)
    operands = tile_operands(kept, near, chunks) + early
    in_specs = [anywhere] * len(operands)
    in_specs += [pl.BlockSpec(coef.shape, lambda i, s: (0, 0, 0)), anywhere]
    operands += [coef, block_a]
    aliases = {}
    if held is not None:
        in_specs += [anywhere, anywhere]
        operands += [token, held]
        aliases = {len(operands): 0}
    buffers, semaphores = tile_scratch(rows, tile, depth, len(kept), n_dp, tiles)
    return pl.pallas_call(
        functools.partial(
            base_kernel, n_dp, tiles, len(chunks), [low for _, low in kept], len(early), count
        ),
        grid_spec=pltpu.PrefetchScalarGridSpec(
            num_scalar_prefetch=1,
            grid=(1,),
            in_specs=in_specs,
            out_specs=[anywhere, pl.BlockSpec((8, 128), lambda i, s: (0, 0))],
            scratch_shapes=[
                *buffers,
                pltpu.VMEM((2, count, rank, tile), bf16),
                pltpu.VMEM((2, rows, tile), bf16),
                pltpu.VMEM((2, rows, tile), f32),
                *semaphores,
                pltpu.SemaphoreType.DMA((2,)),
                pltpu.SemaphoreType.DMA((2,)),
                pltpu.SemaphoreType.DMA((2,)),
            ],
        ),
        out_shape=[
            jax.ShapeDtypeStruct((rows, ff), bf16),
            jax.ShapeDtypeStruct((8, 128), f32),
        ],
        input_output_aliases=aliases,
        **params((1, 1)),
    )(jnp.concatenate([jnp.stack(places).astype(i32), scalars]), *operands)


def add_kernel(pieces, count, slots_ref, *refs):
    term_refs = refs[: 2 * pieces]
    a_ref, b_ref, terms, a, b, term_sem, a_sem, b_sem = refs[2 * pieces + 3 :]
    local, _, ff = a.shape
    both = terms.shape[2]
    cut = term_refs[0].shape[2]

    def load(k):
        lanes = (pl.ds(0, cut), pl.ds(cut, both - cut))
        return [
            pltpu.make_async_copy(
                term_refs[k // count * 2 + part].at[k % count],
                terms.at[k, :, lanes[part]],
                term_sem.at[k, part],
            )
            for part in range(2)
        ]

    def whole(slot, inward):
        pairs = [(a_ref.at[slot], a.at[slot]), (b_ref.at[slot], b.at[slot])]
        return [
            pltpu.make_async_copy(*(pair if inward else pair[::-1]), sem.at[slot])
            for pair, sem in zip(pairs, (a_sem, b_sem))
        ]

    wanted = [slots_ref[k] for k in range(pieces * count)]
    owned = [(slot >= 0) & (slot < local) for slot in wanted]
    hit = []
    for j in range(local):
        any_here = wanted[0] == j
        for slot in wanted[1:]:
            any_here = any_here | (slot == j)
        hit.append(any_here)

    for j in range(local):
        pl.when(hit[j])(lambda j=j: start(whole(j, True)))
    for k in range(pieces * count):
        pl.when(owned[k])(lambda k=k: start(load(k)))
    for j in range(local):
        pl.when(hit[j])(lambda j=j: wait(whole(j, True)))

    def add(k):
        wait(load(k))
        a[wanted[k]] += terms[k, :, :ff].astype(f32)
        b[wanted[k]] += terms[k, :, ff:].astype(f32)

    for k in range(pieces * count):
        pl.when(owned[k])(lambda k=k: add(k))
    for j in range(local):
        pl.when(hit[j])(lambda j=j: start(whole(j, False)))
    for j in range(local):
        pl.when(hit[j])(lambda j=j: wait(whole(j, False)))


def add_terms(slots, pieces, grad_a, grad_b, token):
    count, rank, _ = pieces[0].shape
    both = pieces[0].shape[2] + pieces[1].shape[2]
    anywhere = pl.BlockSpec(memory_space=pl.ANY)
    n = len(pieces) // 2
    local = grad_a.shape[0]
    return pl.pallas_call(
        functools.partial(add_kernel, n, count),
        grid_spec=pltpu.PrefetchScalarGridSpec(
            num_scalar_prefetch=1,
            grid=(1,),
            in_specs=[anywhere] * (2 * n + 3),
            out_specs=[anywhere] * 2,
            scratch_shapes=[
                pltpu.VMEM((n * count, rank, both), bf16),
                pltpu.VMEM(grad_a.shape, f32),
                pltpu.VMEM(grad_b.shape, f32),
                pltpu.SemaphoreType.DMA((n * count, 2)),
                pltpu.SemaphoreType.DMA((local,)),
                pltpu.SemaphoreType.DMA((local,)),
            ],
        ),
        out_shape=[
            jax.ShapeDtypeStruct(grad_a.shape, f32),
            jax.ShapeDtypeStruct(grad_b.shape, f32),
        ],
        input_output_aliases={2 * n + 2: 0, 2 * n + 3: 1},
        **params((1, 1)),
    )(slots, *pieces, token, grad_a, grad_b)


def on_device(
    n_groups,
    n_fsdp,
    n_dp,
    output_gradient,
    hidden,
    frozen_down_weight,
    adapter_first_factors,
    adapter_second_factors,
    island_live_rows,
    island_adapter_ids,
    owner_slot_adapters,
):
    rows, ff = hidden.shape
    d = output_gradient.shape[1]
    count = island_live_rows.shape[0]
    local = adapter_first_factors.shape[0]
    n_slots = owner_slot_adapters.shape[0]
    top = n_dp // 2
    me = lax.axis_index("dp")
    group = lax.axis_index("groups")

    def swap(value, bit, axis="dp", size=n_dp):
        return lax.ppermute(value, axis, [(i, i ^ bit) for i in range(size)])

    def spread(held):
        held = dict(held)
        bit = top // 2
        while bit:
            for r in list(held):
                held[r ^ bit] = swap(held[r], bit)
            bit //= 2
        return held

    match = island_adapter_ids[:, None] == owner_slot_adapters[None, :]
    slots = jnp.sum(jnp.where(match, jnp.arange(n_slots, dtype=i32)[None, :], 0), axis=1)
    far_slots = swap(slots, top)

    place = lax.axis_index("fsdp")
    line = n_fsdp <= 4
    height = rows // count
    pieces_of_kept, at = [(output_gradient, 0)], [None]

    def hop(*after, low=0, high=None):
        step = len(at) // 2
        if not line or step + 1 >= n_fsdp:
            return []
        if low == 0:
            ends[:] = next_ends or [output_gradient] * 2
            next_ends.clear()
        right = [(i, i + 1) for i in range(n_fsdp - 1)]
        left = [(i + 1, i) for i in range(n_fsdp - 1)]
        sent = []
        for piece, pairs, place_of in zip(ends, (right, left), (place - step - 1, place + step + 1)):
            piece = behind(piece[low:high], *after)
            sent.append(lax.ppermute(piece, "fsdp", pairs))
            pieces_of_kept.append((sent[-1], low))
            where.append(jnp.where(place_of < n_fsdp, place_of, -1))
        if high is None:
            at.extend([None, None])
            next_ends.extend(sent)
        return sent

    ends, next_ends, where = [], [], [place]
    first_hop = hop()

    share = ff // n_groups
    if share % 2048 == 0:
        unit, tile = share // 8, share // 4
        sizes = [2 * unit] * 4
    else:
        tile = share
        sizes = [share]
    parts = [(sum(sizes[:j]), size) for j, size in enumerate(sizes)]

    crossed = []
    turned = []

    def flat(*pieces):
        return [v for piece in pieces for v in piece.values()]

    def cross(*after):
        j = len(crossed)
        if j < len(parts):
            first_row, size = parts[j]
            piece = lax.dynamic_slice_in_dim(
                frozen_down_weight, group * share + first_row, size, axis=0
            )
            crossed.append({top: swap(behind(piece, *after), top)})

    def turn(*after):
        j = len(turned)
        if j < len(parts):
            piece = behind(crossed[j][top], *after)
            turned.append([])
            for shift in range(1, n_groups):
                ring = [(i, (i + shift) % n_groups) for i in range(n_groups)]
                turned[j].append({top: lax.ppermute(piece, "groups", ring)})

    def fill(chunks, *after):
        for piece in chunks:
            piece.update(spread({top: behind(piece[top], *after)}))

    cross(far_slots)

    first = jnp.swapaxes(adapter_first_factors, 1, 2)
    a_near = spread({0: first})
    b_near = spread({0: adapter_second_factors})
    near = sorted(a_near)
    a_near = [a_near[r] for r in near]
    b_near = [b_near[r] for r in near]
    def places(wanted):
        owner = wanted // local
        index = jnp.concatenate([wanted % local] * len(near))
        return index, jnp.where((owner ^ me) < top, owner ^ me, len(near))

    picked = pick(*places(far_slots), a_near, b_near)
    both_slots = spread({0: behind(jnp.concatenate([slots, far_slots]), picked)})
    past = [picked, *first_hop, *flat(both_slots, *crossed)]
    far = swap(behind(picked, *past[1:]), top)
    whole = spread({0: behind(frozen_down_weight, *past)})
    turn(*past)
    past = [far, *hop(*past), *flat(*turned[0])]

    ready = behind(slots, *flat(whole, both_slots), *past)
    part, block_a, grad_a, grad_b = project(
        *places(ready), a_near, b_near, far, hidden, output_gradient
    )
    third_hop = hop(*past)
    cross(*past)
    cross(*past)
    sums = [part]
    bit = 1
    while bit < n_fsdp:
        sums.append(swap(sums[-1], bit, "fsdp", n_fsdp))
        if 2 * bit < n_fsdp:
            sums.append(sums[-2] + sums[-1])
        bit *= 2
    total, other = sums[-2:]
    turn(part)
    past = [sums[2], *flat(*crossed[:3], *sum(turned[:2], [])), *third_hop]
    cross(*past)
    turn(*past)
    fill(crossed[:2], *past)
    fill(turned[0], *past)

    order = [me ^ r for r in range(n_dp)]
    order = jnp.stack(order).astype(i32)

    def collect(named):
        chunks, tiles, places_of = [], [], []
        for shift, t in named:
            first_row = lax.rem(group + n_groups - shift, n_groups) * share
            places_of.append(first_row // tile + t)
            tiles.append([])
            for j, (first, size) in enumerate(parts):
                low, high = max(first, t * tile), min(first + size, (t + 1) * tile)
                if low < high:
                    if (shift, j) not in chunks:
                        chunks.append((shift, j))
                    tiles[-1].append((chunks.index((shift, j)), low - first, high - low))
        return places_of, [turned[j][shift - 1] if shift else crossed[j] for shift, j in chunks], tiles

    sums_of = {}

    def begin(*named):
        at = jnp.stack(where).astype(i32)
        places_of, chunks, tiles = collect(named)
        got = early_sums(
            places_of, jnp.concatenate([order, at]), pieces_of_kept, whole, chunks, tiles, tile
        )
        sums_of.update(zip(named, got))
        return got

    others = range(1, n_groups)
    ahead = line and share > tile
    begun = begin((0, 0), (0, 1)) if ahead else []
    past = [other, *begun, *flat(*crossed, *sum(turned, []))]
    low_terms, high_terms, coef = block_terms(
        island_live_rows, total, other, hidden, output_gradient
    )
    far_high = swap(high_terms, top)
    far_low = swap(low_terms, top)
    turn(*past)
    fill(crossed[2:3], *past)
    for pieces in turned[1:2]:
        fill(pieces, *past)
    if line:
        at = jnp.stack(where).astype(i32)
    else:
        pieces_of_kept = [(lax.all_gather(output_gradient, "fsdp", axis=1, tiled=True), 0)]
        at = jnp.zeros((1,), i32)

    relative = [both_slots[r][:count] for r in near] + [both_slots[r][count:] for r in near]
    relative = jnp.concatenate(relative) - me * local

    scalars = jnp.concatenate([order, at, island_live_rows])
    grad_hidden = token = None

    def multiply(*named):
        nonlocal grad_hidden, token
        named = sorted(named, key=lambda name: name not in sums_of)
        places_of, chunks, tiles = collect(named)
        grad_hidden, token = base(
            places_of, scalars, pieces_of_kept, whole, chunks, tiles, tile,
            [sums_of[name] for name in named if name in sums_of], coef, block_a, grad_hidden, token,
        )

    if share > tile:
        multiply(*[(0, t) for t in range(3)], *[(g, t) for g in others for t in range(2)])
        past = [token, far_high]
        fill(crossed[3:], *past)
        for pieces in turned[2:]:
            fill(pieces, *past)
        multiply((0, 3), *[(g, t) for g in others for t in range(2, 4)])
    else:
        multiply(*[(g, 0) for g in range(n_groups)])

    near_low = spread({0: behind(low_terms, *past)})
    near_high = spread({0: behind(high_terms, *past)})
    all_high = spread({top: behind(far_high, *past)})
    all_low = spread({top: behind(far_low, token)})
    terms = [p for r in near for p in (near_low[r], near_high[r])]
    terms += [p for r in near for p in (all_low[r + top], all_high[r + top])]
    grad_a, grad_b = add_terms(relative, terms, grad_a, grad_b, token)
    return grad_hidden, jnp.swapaxes(grad_a, 1, 2), grad_b


def solution(mesh):
    placed = (
        P(("groups", "dp"), "fsdp"),
        P(("groups", "dp"), "fsdp"),
        P("fsdp", "dp"),
        P(("groups", "dp"), "fsdp", None),
        P(("groups", "dp"), None, "fsdp"),
        P(("groups", "dp")),
        P(("groups", "dp")),
        P("groups"),
    )
    sizes = [mesh.shape[name] for name in ("groups", "fsdp", "dp")]
    return jax.shard_map(
        functools.partial(on_device, *sizes),
        mesh=mesh,
        in_specs=placed,
        out_specs=(
            P(("groups", "dp"), "fsdp"),
            P(("groups", "dp"), "fsdp", None),
            P(("groups", "dp"), None, "fsdp"),
        ),
        check_vma=False,
    )
```

```python
import functools

import jax
import jax.numpy as jnp
from jax import lax
from jax.experimental import pallas as pl
from jax.experimental.pallas import tpu as pltpu
from jax.sharding import PartitionSpec as P

adapter_scale = 2.0
factor_gradient = 0.0625
vmem_bytes = 60 * 1024 * 1024
bf16, f32, i32 = jnp.bfloat16, jnp.float32, jnp.int32


def behind(value, *after):
    if not after:
        return value
    return lax.optimization_barrier((value, *after))[0]


def params(cost):
    return dict(
        compiler_params=pltpu.CompilerParams(vmem_limit_bytes=vmem_bytes),
        cost_estimate=pl.CostEstimate(flops=cost[0], bytes_accessed=cost[1], transcendentals=0),
    )


def pick_kernel(pieces, index_ref, source_ref, *refs):
    a_refs, b_refs, out_ref = refs[:pieces], refs[pieces : 2 * pieces], refs[-1]
    source = source_ref[pl.program_id(0)]
    a, b = a_refs[0][0], b_refs[0][0]
    for r in range(1, pieces):
        a = jnp.where(source == r, a_refs[r][0], a)
        b = jnp.where(source == r, b_refs[r][0], b)
    ff = a.shape[1]
    out_ref[0, :, :ff] = a
    out_ref[0, :, ff:] = b


def factor_specs(pieces, count, rank, width):
    return [
        pl.BlockSpec(
            (1, rank, width), lambda i, index, source, r=r: (index[r * count + i], 0, 0)
        )
        for r in range(pieces)
    ]


def pick(index, source, a_pieces, b_pieces):
    count, pieces = source.shape[0], len(a_pieces)
    _, rank, ff = a_pieces[0].shape
    d = b_pieces[0].shape[2]
    return pl.pallas_call(
        functools.partial(pick_kernel, pieces),
        grid_spec=pltpu.PrefetchScalarGridSpec(
            num_scalar_prefetch=2,
            grid=(count,),
            in_specs=factor_specs(pieces, count, rank, ff) + factor_specs(pieces, count, rank, d),
            out_specs=pl.BlockSpec((1, rank, ff + d), lambda i, index, source: (i, 0, 0)),
        ),
        out_shape=jax.ShapeDtypeStruct((count, rank, ff + d), bf16),
        **params((0, 2 * (pieces + 1) * count * rank * (ff + d))),
    )(index, source, *a_pieces, *b_pieces)


def project_kernel(pieces, index_ref, source_ref, *refs):
    a_refs, b_refs = refs[:pieces], refs[pieces : 2 * pieces]
    far_ref, hid_ref, grad_ref, part_ref, block_ref, grad_a_ref, grad_b_ref = refs[
        2 * pieces : 2 * pieces + 7
    ]
    zeros, zero_sem = refs[2 * pieces + 7 :]
    step = pl.program_id(0)
    source = source_ref[step]
    ff = hid_ref.shape[1]
    d = grad_ref.shape[1]

    fills = []
    for slot in range(grad_a_ref.shape[0]):
        fills.append(pltpu.make_async_copy(zeros, grad_a_ref.at[slot], zero_sem.at[2 * slot]))
        fills.append(
            pltpu.make_async_copy(
                zeros.at[:, pl.ds(0, d)], grad_b_ref.at[slot], zero_sem.at[2 * slot + 1]
            )
        )

    @pl.when(step == 0)
    def _():
        zeros[...] = jnp.zeros_like(zeros)
        for fill in fills:
            fill.start()

    a, b = far_ref[0, :, :ff], far_ref[0, :, ff:]
    for r in range(pieces):
        a = jnp.where(source == r, a_refs[r][0], a)
        b = jnp.where(source == r, b_refs[r][0], b)
    block_ref[0] = a
    over_last = (((1,), (1,)), ((), ()))
    rank = a.shape[0]
    part_ref[0, :, :rank] = lax.dot_general(
        hid_ref[...], a, over_last, preferred_element_type=f32
    )
    part_ref[0, :, rank:] = lax.dot_general(
        grad_ref[...], b, over_last, preferred_element_type=f32
    )

    @pl.when(step == pl.num_programs(0) - 1)
    def _():
        for fill in fills:
            fill.wait()


def project(index, source, a_pieces, b_pieces, far, hidden, grad):
    count, pieces = source.shape[0], len(a_pieces)
    local, rank, ff = a_pieces[0].shape
    d = b_pieces[0].shape[2]
    rows = hidden.shape[0]
    height = rows // count
    own = lambda i, index, source: (i, 0)
    own3 = lambda i, index, source: (i, 0, 0)
    return pl.pallas_call(
        functools.partial(project_kernel, pieces),
        grid_spec=pltpu.PrefetchScalarGridSpec(
            num_scalar_prefetch=2,
            grid=(count,),
            in_specs=factor_specs(pieces, count, rank, ff)
            + factor_specs(pieces, count, rank, d)
            + [
                pl.BlockSpec((1, rank, ff + d), own3),
                pl.BlockSpec((height, ff), own),
                pl.BlockSpec((height, d), own),
            ],
            out_specs=[
                pl.BlockSpec((1, height, 2 * rank), own3),
                pl.BlockSpec((1, rank, ff), own3),
                pl.BlockSpec(memory_space=pl.ANY),
                pl.BlockSpec(memory_space=pl.ANY),
            ],
            scratch_shapes=[
                pltpu.VMEM((rank, ff), f32),
                pltpu.SemaphoreType.DMA((2 * local,)),
            ],
        ),
        out_shape=[
            jax.ShapeDtypeStruct((count, height, 2 * rank), f32),
            jax.ShapeDtypeStruct((count, rank, ff), bf16),
            jax.ShapeDtypeStruct((local, rank, ff), f32),
            jax.ShapeDtypeStruct((local, rank, d), f32),
        ],
        **params((2 * rows * rank * (ff + d), 2 * (rows + (pieces + 2) * count * rank) * (ff + d))),
    )(index, source, *a_pieces, *b_pieces, far, hidden, grad)


def terms_kernel(live_ref, here_ref, there_ref, hid_ref, grad_ref, low_ref, high_ref, coef_ref):
    ff = hid_ref.shape[1]
    cut = low_ref.shape[2]
    rank = coef_ref.shape[2]
    total = here_ref[0] + there_ref[0]
    valid = lax.broadcasted_iota(i32, total.shape, 0) < live_ref[pl.program_id(0)]
    total = jnp.where(valid, total, 0.0)
    low = total[:, :rank].astype(bf16)
    coef = (adapter_scale * total[:, rank:]).astype(bf16)
    coef_ref[0] = coef
    over_rows = (((0,), (0,)), ((), ()))
    term_a = (
        factor_gradient
        * lax.dot_general(coef, hid_ref[...], over_rows, preferred_element_type=f32)
    ).astype(bf16)
    low_ref[0] = term_a[:, :cut]
    high_ref[0, :, : ff - cut] = term_a[:, cut:]
    high_ref[0, :, ff - cut :] = (
        factor_gradient
        * adapter_scale
        * lax.dot_general(low, grad_ref[...], over_rows, preferred_element_type=f32)
    ).astype(bf16)


def block_terms(live, here, there, hidden, grad):
    count, height, both = here.shape
    rank = both // 2
    rows, ff = hidden.shape
    d = grad.shape[1]
    cut = (ff + d) // 256 * 128
    own = lambda i, live: (i, 0)
    own3 = lambda i, live: (i, 0, 0)
    return pl.pallas_call(
        terms_kernel,
        grid_spec=pltpu.PrefetchScalarGridSpec(
            num_scalar_prefetch=1,
            grid=(count,),
            in_specs=[
                pl.BlockSpec((1, height, both), own3),
                pl.BlockSpec((1, height, both), own3),
                pl.BlockSpec((height, ff), own),
                pl.BlockSpec((height, d), own),
            ],
            out_specs=[
                pl.BlockSpec((1, rank, cut), own3),
                pl.BlockSpec((1, rank, ff + d - cut), own3),
                pl.BlockSpec((1, height, rank), own3),
            ],
        ),
        out_shape=[
            jax.ShapeDtypeStruct((count, rank, cut), bf16),
            jax.ShapeDtypeStruct((count, rank, ff + d - cut), bf16),
            jax.ShapeDtypeStruct((count, height, rank), bf16),
        ],
        **params((2 * rows * rank * (ff + d), 2 * (rows + count * rank) * (ff + d))),
    )(live, here, there, hidden, grad)


class Tiles:
    def __init__(self, n_dp, tiles, n_chunks, kept_rows, scalars_ref, refs):
        self.near, self.n_dp, self.tiles, self.kept_rows = n_dp // 2, n_dp, tiles, kept_rows
        n_kept = len(kept_rows)
        self.scalars_ref, self.kept_refs, refs = scalars_ref, refs[:n_kept], refs[n_kept:]
        self.near_refs, refs = refs[: self.near], refs[self.near :]
        self.far_refs, self.rest = refs[: n_chunks * self.near], refs[n_chunks * self.near :]
        self.deep = self.near_refs[0].shape[1]
        self.at = [scalars_ref[len(tiles) + n_dp + k] for k in range(n_kept)]

    def lanes(self, r):
        start = self.scalars_ref[len(self.tiles) + r] * self.deep
        return pl.ds(pl.multiple_of(start, self.deep), self.deep)

    def span(self, j, tile):
        return pl.ds(pl.multiple_of(self.scalars_ref[j] * tile, tile), tile)

    def loads(self, j, r, weight, slot, sem):
        if r < self.near:
            rows = self.near_refs[r].at[self.span(j, weight.shape[1]), :]
            return [
                pltpu.make_async_copy(rows, weight.at[slot, :, self.lanes(r)], sem.at[slot, r, 0])
            ]
        copies, low = [], 0
        for k, (chunk, start, size) in enumerate(self.tiles[j]):
            copies.append(
                pltpu.make_async_copy(
                    self.far_refs[chunk * self.near + r - self.near].at[pl.ds(start, size)],
                    weight.at[slot, pl.ds(low, size), self.lanes(r)],
                    sem.at[slot, r, k],
                )
            )
            low += size
        return copies

    def columns(self, k, kept, sem):
        wide = self.kept_refs[k].shape[1]
        place = pl.ds(pl.multiple_of(self.at[k] * wide, wide), wide)
        rows = pl.ds(self.kept_rows[k], self.kept_refs[k].shape[0])
        return pltpu.make_async_copy(self.kept_refs[k], kept.at[rows, place], sem.at[k])

    def each_column(self, kept, sem, act):
        for k in range(len(self.kept_refs)):
            pl.when(self.at[k] >= 0)(lambda k=k: act(self.columns(k, kept, sem)))

    def part(self, r, kept, weight, slot):
        return lax.dot_general(
            kept[:, self.lanes(r)],
            weight[slot, :, self.lanes(r)],
            (((1,), (1,)), ((), ())),
            preferred_element_type=f32,
        )


    def product(self, kept, weight, slot):
        return lax.dot_general(
            kept[...], weight[slot], (((1,), (1,)), ((), ())), preferred_element_type=f32
        )


def start(copies):
    for copy in copies:
        copy.start()


def wait(copies):
    for copy in copies:
        copy.wait()


def early_kernel(n_dp, tiles, n_chunks, kept_rows, scalars_ref, *refs):
    me = Tiles(n_dp, tiles, n_chunks, kept_rows, scalars_ref, refs)
    sums_refs, (kept, weight, total, kept_sem, in_sem, out_sem) = me.rest[:-6], me.rest[-6:]
    steps = len(tiles)

    def load(j, act):
        for r in range(n_dp):
            act(me.loads(j, r, weight, j % 2, in_sem))

    def store(j):
        return pltpu.make_async_copy(total.at[j % 2], sums_refs[j], out_sem.at[j % 2])

    me.each_column(kept, kept_sem, lambda copy: copy.start())
    load(0, start)
    me.each_column(kept, kept_sem, lambda copy: copy.wait())

    @pl.loop(0, steps)
    def _(step):
        slot = lax.rem(step, 2)
        for j in range(steps):

            @pl.when(step == j)
            def _():
                if j + 1 < steps:
                    load(j + 1, start)
                load(j, wait)
                if j >= 2:
                    store(j - 2).wait()

        total[slot] = me.product(kept, weight, slot)
        for j in range(steps):
            pl.when(step == j)(lambda j=j: store(j).start())

    for j in range(max(steps - 2, 0), steps):
        store(j).wait()


def base_kernel(n_dp, tiles, n_chunks, kept_rows, n_held, count, scalars_ref, *refs):
    me = Tiles(n_dp, tiles, n_chunks, kept_rows, scalars_ref, refs)
    held_refs, (coef_ref, block_ref) = me.rest[:n_held], me.rest[n_held : n_held + 2]
    out_ref, token_ref, kept, weight, factor, result, total = me.rest[-12:-5]
    kept_sem, in_sem, factor_sem, out_sem, held_sem = me.rest[-5:]
    _, tile, _ = weight.shape
    height = coef_ref.shape[1]
    steps = len(tiles)
    live = steps + n_dp + len(kept_rows)
    token_ref[...] = jnp.zeros_like(token_ref)

    def load(j, act):
        slot = j % 2
        if j >= n_held:
            for r in range(n_dp):
                act(me.loads(j, r, weight, slot, in_sem))
        if j < n_held:
            act([pltpu.make_async_copy(held_refs[j], total.at[slot], held_sem.at[slot])])
        factors(j, act)

    def factors(j, act):
        slot = j % 2
        act(
            [
                pltpu.make_async_copy(
                    block_ref.at[:, :, me.span(j, tile)], factor.at[slot], factor_sem.at[slot]
                )
            ]
        )

    def store(j):
        return pltpu.make_async_copy(
            result.at[j % 2], out_ref.at[:, me.span(j, tile)], out_sem.at[j % 2]
        )

    def finish(slot, sums):
        for b in range(count):
            extra = jnp.dot(coef_ref[b], factor[slot, b], preferred_element_type=f32)
            here = sums[b * height : (b + 1) * height] + extra
            valid = lax.broadcasted_iota(i32, here.shape, 0) < scalars_ref[live + b]
            result[slot, b * height : (b + 1) * height, :] = jnp.where(valid, here, 0.0).astype(
                bf16
            )

    load(0, start)
    if n_held < steps:
        me.each_column(kept, kept_sem, lambda copy: copy.start())
    if steps > 1:
        load(1, start)
    first = 0
    if not n_held and me.kept_refs[0].shape[1] == me.deep:
        first, sums = 1, None
        for r in range(n_dp):
            for k in range(len(kept_rows)):
                pl.when(me.at[k] == scalars_ref[steps + r])(
                    lambda k=k: me.columns(k, kept, kept_sem).wait()
                )
            wait(me.loads(0, r, weight, 0, in_sem))
            part = me.part(r, kept, weight, 0)
            sums = part if sums is None else sums + part
        factors(0, wait)
        finish(0, sums)
        store(0).start()
    elif not n_held:
        me.each_column(kept, kept_sem, lambda copy: copy.wait())

    @pl.loop(first, steps)
    def _(step):
        slot = lax.rem(step, 2)
        for j in range(first, steps):

            @pl.when(step == j)
            def _():
                if 1 < j + 1 < steps:
                    load(j + 1, start)
                if 0 < j == n_held:
                    me.each_column(kept, kept_sem, lambda copy: copy.wait())
                load(j, wait)
                if j >= 2:
                    store(j - 2).wait()

        if n_held:
            pl.when(step < n_held)(lambda: finish(slot, total[slot]))
        if n_held < steps:
            pl.when(step >= n_held)(lambda: finish(slot, me.product(kept, weight, slot)))

        for j in range(steps):
            pl.when(step == j)(lambda j=j: store(j).start())

    for j in range(max(steps - 2, 0), steps):
        store(j).wait()


def tile_scratch(rows, tile, depth, n_kept, n_dp, tiles):
    most = max(len(segments) for segments in tiles)
    return [
        pltpu.VMEM((rows, depth), bf16),
        pltpu.VMEM((2, tile, depth), bf16),
    ], [
        pltpu.SemaphoreType.DMA((n_kept,)),
        pltpu.SemaphoreType.DMA((2, n_dp, most)),
    ]


def tile_operands(kept, near, chunks):
    top = len(near)
    operands = [piece for piece, _ in kept] + [near[r] for r in range(top)]
    for piece in chunks:
        operands += [piece[r] for r in range(top, 2 * top)]
    return operands


def early_sums(places, scalars, kept, near, chunks, tiles, tile):
    rows = kept[0][0].shape[0]
    n_dp = 2 * len(near)
    depth = n_dp * near[0].shape[1]
    anywhere = pl.BlockSpec(memory_space=pl.ANY)
    operands = tile_operands(kept, near, chunks)
    buffers, semaphores = tile_scratch(rows, tile, depth, len(kept), n_dp, tiles)
    return pl.pallas_call(
        functools.partial(early_kernel, n_dp, tiles, len(chunks), [low for _, low in kept]),
        grid_spec=pltpu.PrefetchScalarGridSpec(
            num_scalar_prefetch=1,
            grid=(1,),
            in_specs=[anywhere] * len(operands),
            out_specs=[anywhere] * len(tiles),
            scratch_shapes=[
                *buffers,
                pltpu.VMEM((2, rows, tile), f32),
                *semaphores,
                pltpu.SemaphoreType.DMA((2,)),
            ],
        ),
        out_shape=[jax.ShapeDtypeStruct((rows, tile), f32)] * len(tiles),
        **params((1, 1)),
    )(jnp.concatenate([jnp.stack(places).astype(i32), scalars]), *operands)


def base(places, scalars, kept, near, chunks, tiles, tile, early, coef, block_a, held, token):
    rows = kept[0][0].shape[0]
    count, rank, ff = block_a.shape
    n_dp = 2 * len(near)
    depth = n_dp * near[0].shape[1]
    anywhere = pl.BlockSpec(memory_space=pl.ANY)
    operands = tile_operands(kept, near, chunks) + early
    in_specs = [anywhere] * len(operands)
    in_specs += [pl.BlockSpec(coef.shape, lambda i, s: (0, 0, 0)), anywhere]
    operands += [coef, block_a]
    aliases = {}
    if held is not None:
        in_specs += [anywhere, anywhere]
        operands += [token, held]
        aliases = {len(operands): 0}
    buffers, semaphores = tile_scratch(rows, tile, depth, len(kept), n_dp, tiles)
    return pl.pallas_call(
        functools.partial(
            base_kernel, n_dp, tiles, len(chunks), [low for _, low in kept], len(early), count
        ),
        grid_spec=pltpu.PrefetchScalarGridSpec(
            num_scalar_prefetch=1,
            grid=(1,),
            in_specs=in_specs,
            out_specs=[anywhere, pl.BlockSpec((8, 128), lambda i, s: (0, 0))],
            scratch_shapes=[
                *buffers,
                pltpu.VMEM((2, count, rank, tile), bf16),
                pltpu.VMEM((2, rows, tile), bf16),
                pltpu.VMEM((2, rows, tile), f32),
                *semaphores,
                pltpu.SemaphoreType.DMA((2,)),
                pltpu.SemaphoreType.DMA((2,)),
                pltpu.SemaphoreType.DMA((2,)),
            ],
        ),
        out_shape=[
            jax.ShapeDtypeStruct((rows, ff), bf16),
            jax.ShapeDtypeStruct((8, 128), f32),
        ],
        input_output_aliases=aliases,
        **params((1, 1)),
    )(jnp.concatenate([jnp.stack(places).astype(i32), scalars]), *operands)


def add_kernel(pieces, count, slots_ref, *refs):
    term_refs = refs[: 2 * pieces]
    a_ref, b_ref, terms, a, b, term_sem, a_sem, b_sem = refs[2 * pieces + 3 :]
    local, _, ff = a.shape
    both = terms.shape[2]
    cut = term_refs[0].shape[2]

    def load(k):
        lanes = (pl.ds(0, cut), pl.ds(cut, both - cut))
        return [
            pltpu.make_async_copy(
                term_refs[k // count * 2 + part].at[k % count],
                terms.at[k, :, lanes[part]],
                term_sem.at[k, part],
            )
            for part in range(2)
        ]

    def whole(slot):
        return [
            pltpu.make_async_copy(a.at[slot], a_ref.at[slot], a_sem.at[slot]),
            pltpu.make_async_copy(b.at[slot], b_ref.at[slot], b_sem.at[slot]),
        ]

    wanted = [slots_ref[k] for k in range(pieces * count)]
    owned = [(slot >= 0) & (slot < local) for slot in wanted]
    hit = []
    for j in range(local):
        any_here = wanted[0] == j
        for slot in wanted[1:]:
            any_here = any_here | (slot == j)
        hit.append(any_here)

    def clear(j):
        a[j] = jnp.zeros(a.shape[1:], f32)
        b[j] = jnp.zeros(b.shape[1:], f32)

    for k in range(pieces * count):
        pl.when(owned[k])(lambda k=k: start(load(k)))
    for j in range(local):
        pl.when(hit[j])(lambda j=j: clear(j))

    def add(k):
        wait(load(k))
        a[wanted[k]] += terms[k, :, :ff].astype(f32)
        b[wanted[k]] += terms[k, :, ff:].astype(f32)

    for k in range(pieces * count):
        pl.when(owned[k])(lambda k=k: add(k))
    for j in range(local):
        pl.when(hit[j])(lambda j=j: start(whole(j)))
    for j in range(local):
        pl.when(hit[j])(lambda j=j: wait(whole(j)))


def add_terms(slots, pieces, grad_a, grad_b, token):
    count, rank, _ = pieces[0].shape
    both = pieces[0].shape[2] + pieces[1].shape[2]
    anywhere = pl.BlockSpec(memory_space=pl.ANY)
    n = len(pieces) // 2
    local = grad_a.shape[0]
    return pl.pallas_call(
        functools.partial(add_kernel, n, count),
        grid_spec=pltpu.PrefetchScalarGridSpec(
            num_scalar_prefetch=1,
            grid=(1,),
            in_specs=[anywhere] * (2 * n + 3),
            out_specs=[anywhere] * 2,
            scratch_shapes=[
                pltpu.VMEM((n * count, rank, both), bf16),
                pltpu.VMEM(grad_a.shape, f32),
                pltpu.VMEM(grad_b.shape, f32),
                pltpu.SemaphoreType.DMA((n * count, 2)),
                pltpu.SemaphoreType.DMA((local,)),
                pltpu.SemaphoreType.DMA((local,)),
            ],
        ),
        out_shape=[
            jax.ShapeDtypeStruct(grad_a.shape, f32),
            jax.ShapeDtypeStruct(grad_b.shape, f32),
        ],
        input_output_aliases={2 * n + 2: 0, 2 * n + 3: 1},
        **params((1, 1)),
    )(slots, *pieces, token, grad_a, grad_b)


def on_device(
    n_groups,
    n_fsdp,
    n_dp,
    output_gradient,
    hidden,
    frozen_down_weight,
    adapter_first_factors,
    adapter_second_factors,
    island_live_rows,
    island_adapter_ids,
    owner_slot_adapters,
):
    rows, ff = hidden.shape
    d = output_gradient.shape[1]
    count = island_live_rows.shape[0]
    local = adapter_first_factors.shape[0]
    n_slots = owner_slot_adapters.shape[0]
    top = n_dp // 2
    me = lax.axis_index("dp")
    group = lax.axis_index("groups")

    def swap(value, bit, axis="dp", size=n_dp):
        return lax.ppermute(value, axis, [(i, i ^ bit) for i in range(size)])

    def spread(held):
        held = dict(held)
        bit = top // 2
        while bit:
            for r in list(held):
                held[r ^ bit] = swap(held[r], bit)
            bit //= 2
        return held

    match = island_adapter_ids[:, None] == owner_slot_adapters[None, :]
    slots = jnp.sum(jnp.where(match, jnp.arange(n_slots, dtype=i32)[None, :], 0), axis=1)
    far_slots = swap(slots, top)

    place = lax.axis_index("fsdp")
    line = n_fsdp <= 4
    height = rows // count
    pieces_of_kept, at = [(output_gradient, 0)], [None]

    def hop(*after, low=0, high=None):
        step = len(at) // 2
        if not line or step + 1 >= n_fsdp:
            return []
        if low == 0:
            ends[:] = next_ends or [output_gradient] * 2
            next_ends.clear()
        right = [(i, i + 1) for i in range(n_fsdp - 1)]
        left = [(i + 1, i) for i in range(n_fsdp - 1)]
        sent = []
        for piece, pairs, place_of in zip(ends, (right, left), (place - step - 1, place + step + 1)):
            piece = behind(piece[low:high], *after)
            sent.append(lax.ppermute(piece, "fsdp", pairs))
            pieces_of_kept.append((sent[-1], low))
            where.append(jnp.where(place_of < n_fsdp, place_of, -1))
        if high is None:
            at.extend([None, None])
            next_ends.extend(sent)
        return sent

    ends, next_ends, where = [], [], [place]
    first_hop = hop()

    share = ff // n_groups
    if share % 2048 == 0:
        unit, tile = share // 8, share // 4
        sizes = [2 * unit] * 4
    else:
        tile = share
        sizes = [share]
    parts = [(sum(sizes[:j]), size) for j, size in enumerate(sizes)]

    crossed = []
    turned = []

    def flat(*pieces):
        return [v for piece in pieces for v in piece.values()]

    def cross(*after):
        j = len(crossed)
        if j < len(parts):
            first_row, size = parts[j]
            piece = lax.dynamic_slice_in_dim(
                frozen_down_weight, group * share + first_row, size, axis=0
            )
            crossed.append({top: swap(behind(piece, *after), top)})

    def turn(*after):
        j = len(turned)
        if j < len(parts):
            piece = behind(crossed[j][top], *after)
            turned.append([])
            for shift in range(1, n_groups):
                ring = [(i, (i + shift) % n_groups) for i in range(n_groups)]
                turned[j].append({top: lax.ppermute(piece, "groups", ring)})

    def fill(chunks, *after):
        for piece in chunks:
            piece.update(spread({top: behind(piece[top], *after)}))

    cross(far_slots)

    first = jnp.swapaxes(adapter_first_factors, 1, 2)
    a_near = spread({0: first})
    b_near = spread({0: adapter_second_factors})
    near = sorted(a_near)
    a_near = [a_near[r] for r in near]
    b_near = [b_near[r] for r in near]
    def places(wanted):
        owner = wanted // local
        index = jnp.concatenate([wanted % local] * len(near))
        return index, jnp.where((owner ^ me) < top, owner ^ me, len(near))

    picked = pick(*places(far_slots), a_near, b_near)
    both_slots = spread({0: behind(jnp.concatenate([slots, far_slots]), picked)})
    past = [picked, *first_hop, *flat(both_slots, *crossed)]
    far = swap(behind(picked, *past[1:]), top)
    whole = spread({0: behind(frozen_down_weight, *past)})
    turn(*past)
    past = [far, *hop(*past), *flat(*turned[0])]

    ready = behind(slots, *flat(whole, both_slots), *past)
    part, block_a, grad_a, grad_b = project(
        *places(ready), a_near, b_near, far, hidden, output_gradient
    )
    third_hop = hop(*past)
    cross(*past)
    cross(*past)
    sums = [part]
    bit = 1
    while bit < n_fsdp:
        sums.append(swap(sums[-1], bit, "fsdp", n_fsdp))
        if 2 * bit < n_fsdp:
            sums.append(sums[-2] + sums[-1])
        bit *= 2
    total, other = sums[-2:]
    turn(part)
    past = [sums[2], *flat(*crossed[:3], *sum(turned[:2], [])), *third_hop]
    cross(*past)
    turn(*past)
    fill(crossed[:2], *past)
    fill(turned[0], *past)

    order = [me ^ r for r in range(n_dp)]
    order = jnp.stack(order).astype(i32)

    def collect(named):
        chunks, tiles, places_of = [], [], []
        for shift, t in named:
            first_row = lax.rem(group + n_groups - shift, n_groups) * share
            places_of.append(first_row // tile + t)
            tiles.append([])
            for j, (first, size) in enumerate(parts):
                low, high = max(first, t * tile), min(first + size, (t + 1) * tile)
                if low < high:
                    if (shift, j) not in chunks:
                        chunks.append((shift, j))
                    tiles[-1].append((chunks.index((shift, j)), low - first, high - low))
        return places_of, [turned[j][shift - 1] if shift else crossed[j] for shift, j in chunks], tiles

    sums_of = {}

    def begin(*named):
        at = jnp.stack(where).astype(i32)
        places_of, chunks, tiles = collect(named)
        got = early_sums(
            places_of, jnp.concatenate([order, at]), pieces_of_kept, whole, chunks, tiles, tile
        )
        sums_of.update(zip(named, got))
        return got

    others = range(1, n_groups)
    ahead = line and share > tile
    begun = begin((0, 0), (0, 1)) if ahead else []
    live = behind(island_live_rows, *begun)
    low_terms, high_terms, coef = block_terms(live, total, other, hidden, output_gradient)
    past = [coef, *flat(*crossed, *sum(turned, []))]
    far_high = swap(high_terms, top)
    far_low = swap(low_terms, top)
    turn(*past)
    fill(crossed[2:], *past)
    for pieces in turned[1:3]:
        fill(pieces, *past)
    if line:
        at = jnp.stack(where).astype(i32)
    else:
        pieces_of_kept = [(lax.all_gather(output_gradient, "fsdp", axis=1, tiled=True), 0)]
        at = jnp.zeros((1,), i32)

    relative = [both_slots[r][:count] for r in near] + [both_slots[r][count:] for r in near]
    relative = jnp.concatenate(relative) - me * local

    scalars = jnp.concatenate([order, at, island_live_rows])
    grad_hidden = token = None

    def multiply(*named):
        nonlocal grad_hidden, token
        named = sorted(named, key=lambda name: name not in sums_of)
        places_of, chunks, tiles = collect(named)
        grad_hidden, token = base(
            places_of, scalars, pieces_of_kept, whole, chunks, tiles, tile,
            [sums_of[name] for name in named if name in sums_of], coef, block_a, grad_hidden, token,
        )

    if share > tile:
        multiply(*[(0, t) for t in range(3)], *[(g, t) for g in others for t in range(2)])
        past = [token, far_high]
        for pieces in turned[3:]:
            fill(pieces, *past)
        multiply((0, 3), *[(g, t) for g in others for t in range(2, 4)])
    else:
        multiply(*[(g, 0) for g in range(n_groups)])

    near_low = spread({0: behind(low_terms, *past)})
    near_high = spread({0: behind(high_terms, *past)})
    all_high = spread({top: behind(far_high, *past)})
    all_low = spread({top: behind(far_low, token)})
    terms = [p for r in near for p in (near_low[r], near_high[r])]
    terms += [p for r in near for p in (all_low[r + top], all_high[r + top])]
    grad_a, grad_b = add_terms(relative, terms, grad_a, grad_b, token)
    return grad_hidden, jnp.swapaxes(grad_a, 1, 2), grad_b


def solution(mesh):
    placed = (
        P(("groups", "dp"), "fsdp"),
        P(("groups", "dp"), "fsdp"),
        P("fsdp", "dp"),
        P(("groups", "dp"), "fsdp", None),
        P(("groups", "dp"), None, "fsdp"),
        P(("groups", "dp")),
        P(("groups", "dp")),
        P("groups"),
    )
    sizes = [mesh.shape[name] for name in ("groups", "fsdp", "dp")]
    return jax.shard_map(
        functools.partial(on_device, *sizes),
        mesh=mesh,
        in_specs=placed,
        out_specs=(
            P(("groups", "dp"), "fsdp"),
            P(("groups", "dp"), "fsdp", None),
            P(("groups", "dp"), None, "fsdp"),
        ),
        check_vma=False,
    )
```

```python
import functools

import jax
import jax.numpy as jnp
from jax import lax
from jax.experimental import pallas as pl
from jax.experimental.pallas import tpu as pltpu
from jax.sharding import PartitionSpec as P

adapter_scale = 2.0
factor_gradient = 0.0625
vmem_bytes = 60 * 1024 * 1024
bf16, f32, i32 = jnp.bfloat16, jnp.float32, jnp.int32


def behind(value, *after):
    if not after:
        return value
    return lax.optimization_barrier((value, *after))[0]


def params(cost):
    return dict(
        compiler_params=pltpu.CompilerParams(vmem_limit_bytes=vmem_bytes),
        cost_estimate=pl.CostEstimate(flops=cost[0], bytes_accessed=cost[1], transcendentals=0),
    )


def pick_kernel(pieces, index_ref, source_ref, *refs):
    a_refs, b_refs, out_ref = refs[:pieces], refs[pieces : 2 * pieces], refs[-1]
    source = source_ref[pl.program_id(0)]
    a, b = a_refs[0][0], b_refs[0][0]
    for r in range(1, pieces):
        a = jnp.where(source == r, a_refs[r][0], a)
        b = jnp.where(source == r, b_refs[r][0], b)
    ff = a.shape[1]
    out_ref[0, :, :ff] = a
    out_ref[0, :, ff:] = b


def factor_specs(pieces, count, rank, width):
    return [
        pl.BlockSpec(
            (1, rank, width), lambda i, index, source, r=r: (index[r * count + i], 0, 0)
        )
        for r in range(pieces)
    ]


def pick(index, source, a_pieces, b_pieces):
    count, pieces = source.shape[0], len(a_pieces)
    _, rank, ff = a_pieces[0].shape
    d = b_pieces[0].shape[2]
    return pl.pallas_call(
        functools.partial(pick_kernel, pieces),
        grid_spec=pltpu.PrefetchScalarGridSpec(
            num_scalar_prefetch=2,
            grid=(count,),
            in_specs=factor_specs(pieces, count, rank, ff) + factor_specs(pieces, count, rank, d),
            out_specs=pl.BlockSpec((1, rank, ff + d), lambda i, index, source: (i, 0, 0)),
        ),
        out_shape=jax.ShapeDtypeStruct((count, rank, ff + d), bf16),
        **params((0, 2 * (pieces + 1) * count * rank * (ff + d))),
    )(index, source, *a_pieces, *b_pieces)


def project_kernel(pieces, index_ref, source_ref, *refs):
    a_refs, b_refs = refs[:pieces], refs[pieces : 2 * pieces]
    far_ref, hid_ref, grad_ref, part_ref, block_ref, grad_a_ref, grad_b_ref = refs[
        2 * pieces : 2 * pieces + 7
    ]
    zeros, zero_sem = refs[2 * pieces + 7 :]
    step = pl.program_id(0)
    source = source_ref[step]
    ff = hid_ref.shape[1]
    d = grad_ref.shape[1]

    fills = []
    for slot in range(grad_a_ref.shape[0]):
        fills.append(pltpu.make_async_copy(zeros, grad_a_ref.at[slot], zero_sem.at[2 * slot]))
        fills.append(
            pltpu.make_async_copy(
                zeros.at[:, pl.ds(0, d)], grad_b_ref.at[slot], zero_sem.at[2 * slot + 1]
            )
        )

    @pl.when(step == 0)
    def _():
        zeros[...] = jnp.zeros_like(zeros)
        for fill in fills:
            fill.start()

    a, b = far_ref[0, :, :ff], far_ref[0, :, ff:]
    for r in range(pieces):
        a = jnp.where(source == r, a_refs[r][0], a)
        b = jnp.where(source == r, b_refs[r][0], b)
    block_ref[0] = a
    over_last = (((1,), (1,)), ((), ()))
    rank = a.shape[0]
    part_ref[0, :, :rank] = lax.dot_general(
        hid_ref[...], a, over_last, preferred_element_type=f32
    )
    part_ref[0, :, rank:] = lax.dot_general(
        grad_ref[...], b, over_last, preferred_element_type=f32
    )

    @pl.when(step == pl.num_programs(0) - 1)
    def _():
        for fill in fills:
            fill.wait()


def project(index, source, a_pieces, b_pieces, far, hidden, grad):
    count, pieces = source.shape[0], len(a_pieces)
    local, rank, ff = a_pieces[0].shape
    d = b_pieces[0].shape[2]
    rows = hidden.shape[0]
    height = rows // count
    own = lambda i, index, source: (i, 0)
    own3 = lambda i, index, source: (i, 0, 0)
    return pl.pallas_call(
        functools.partial(project_kernel, pieces),
        grid_spec=pltpu.PrefetchScalarGridSpec(
            num_scalar_prefetch=2,
            grid=(count,),
            in_specs=factor_specs(pieces, count, rank, ff)
            + factor_specs(pieces, count, rank, d)
            + [
                pl.BlockSpec((1, rank, ff + d), own3),
                pl.BlockSpec((height, ff), own),
                pl.BlockSpec((height, d), own),
            ],
            out_specs=[
                pl.BlockSpec((1, height, 2 * rank), own3),
                pl.BlockSpec((1, rank, ff), own3),
                pl.BlockSpec(memory_space=pl.ANY),
                pl.BlockSpec(memory_space=pl.ANY),
            ],
            scratch_shapes=[
                pltpu.VMEM((rank, ff), f32),
                pltpu.SemaphoreType.DMA((2 * local,)),
            ],
        ),
        out_shape=[
            jax.ShapeDtypeStruct((count, height, 2 * rank), f32),
            jax.ShapeDtypeStruct((count, rank, ff), bf16),
            jax.ShapeDtypeStruct((local, rank, ff), f32),
            jax.ShapeDtypeStruct((local, rank, d), f32),
        ],
        **params((2 * rows * rank * (ff + d), 2 * (rows + (pieces + 2) * count * rank) * (ff + d))),
    )(index, source, *a_pieces, *b_pieces, far, hidden, grad)


def terms_kernel(live_ref, here_ref, there_ref, hid_ref, grad_ref, low_ref, high_ref, coef_ref):
    ff = hid_ref.shape[1]
    cut = low_ref.shape[2]
    rank = coef_ref.shape[2]
    total = here_ref[0] + there_ref[0]
    valid = lax.broadcasted_iota(i32, total.shape, 0) < live_ref[pl.program_id(0)]
    total = jnp.where(valid, total, 0.0)
    low = total[:, :rank].astype(bf16)
    coef = (adapter_scale * total[:, rank:]).astype(bf16)
    coef_ref[0] = coef
    over_rows = (((0,), (0,)), ((), ()))
    term_a = (
        factor_gradient
        * lax.dot_general(coef, hid_ref[...], over_rows, preferred_element_type=f32)
    ).astype(bf16)
    low_ref[0] = term_a[:, :cut]
    high_ref[0, :, : ff - cut] = term_a[:, cut:]
    high_ref[0, :, ff - cut :] = (
        factor_gradient
        * adapter_scale
        * lax.dot_general(low, grad_ref[...], over_rows, preferred_element_type=f32)
    ).astype(bf16)


def block_terms(live, here, there, hidden, grad):
    count, height, both = here.shape
    rank = both // 2
    rows, ff = hidden.shape
    d = grad.shape[1]
    cut = (ff + d) // 256 * 128
    own = lambda i, live: (i, 0)
    own3 = lambda i, live: (i, 0, 0)
    return pl.pallas_call(
        terms_kernel,
        grid_spec=pltpu.PrefetchScalarGridSpec(
            num_scalar_prefetch=1,
            grid=(count,),
            in_specs=[
                pl.BlockSpec((1, height, both), own3),
                pl.BlockSpec((1, height, both), own3),
                pl.BlockSpec((height, ff), own),
                pl.BlockSpec((height, d), own),
            ],
            out_specs=[
                pl.BlockSpec((1, rank, cut), own3),
                pl.BlockSpec((1, rank, ff + d - cut), own3),
                pl.BlockSpec((1, height, rank), own3),
            ],
        ),
        out_shape=[
            jax.ShapeDtypeStruct((count, rank, cut), bf16),
            jax.ShapeDtypeStruct((count, rank, ff + d - cut), bf16),
            jax.ShapeDtypeStruct((count, height, rank), bf16),
        ],
        **params((2 * rows * rank * (ff + d), 2 * (rows + count * rank) * (ff + d))),
    )(live, here, there, hidden, grad)


class Tiles:
    def __init__(self, n_dp, tiles, n_chunks, kept_rows, scalars_ref, refs):
        self.near, self.n_dp, self.tiles, self.kept_rows = n_dp // 2, n_dp, tiles, kept_rows
        n_kept = len(kept_rows)
        self.scalars_ref, self.kept_refs, refs = scalars_ref, refs[:n_kept], refs[n_kept:]
        self.near_refs, refs = refs[: self.near], refs[self.near :]
        self.far_refs, self.rest = refs[: n_chunks * self.near], refs[n_chunks * self.near :]
        self.deep = self.near_refs[0].shape[1]
        self.at = [scalars_ref[len(tiles) + n_dp + k] for k in range(n_kept)]

    def lanes(self, r):
        start = self.scalars_ref[len(self.tiles) + r] * self.deep
        return pl.ds(pl.multiple_of(start, self.deep), self.deep)

    def span(self, j, tile):
        return pl.ds(pl.multiple_of(self.scalars_ref[j] * tile, tile), tile)

    def loads(self, j, r, weight, slot, sem):
        if r < self.near:
            rows = self.near_refs[r].at[self.span(j, weight.shape[1]), :]
            return [
                pltpu.make_async_copy(rows, weight.at[slot, :, self.lanes(r)], sem.at[slot, r, 0])
            ]
        copies, low = [], 0
        for k, (chunk, start, size) in enumerate(self.tiles[j]):
            copies.append(
                pltpu.make_async_copy(
                    self.far_refs[chunk * self.near + r - self.near].at[pl.ds(start, size)],
                    weight.at[slot, pl.ds(low, size), self.lanes(r)],
                    sem.at[slot, r, k],
                )
            )
            low += size
        return copies

    def columns(self, k, kept, sem):
        wide = self.kept_refs[k].shape[1]
        place = pl.ds(pl.multiple_of(self.at[k] * wide, wide), wide)
        rows = pl.ds(self.kept_rows[k], self.kept_refs[k].shape[0])
        return pltpu.make_async_copy(self.kept_refs[k], kept.at[rows, place], sem.at[k])

    def each_column(self, kept, sem, act):
        for k in range(len(self.kept_refs)):
            pl.when(self.at[k] >= 0)(lambda k=k: act(self.columns(k, kept, sem)))

    def part(self, r, kept, weight, slot):
        return lax.dot_general(
            kept[:, self.lanes(r)],
            weight[slot, :, self.lanes(r)],
            (((1,), (1,)), ((), ())),
            preferred_element_type=f32,
        )


    def product(self, kept, weight, slot):
        return lax.dot_general(
            kept[...], weight[slot], (((1,), (1,)), ((), ())), preferred_element_type=f32
        )


def start(copies):
    for copy in copies:
        copy.start()


def wait(copies):
    for copy in copies:
        copy.wait()


def early_kernel(n_dp, tiles, n_chunks, kept_rows, scalars_ref, *refs):
    me = Tiles(n_dp, tiles, n_chunks, kept_rows, scalars_ref, refs)
    sums_refs, (kept, weight, total, kept_sem, in_sem, out_sem) = me.rest[:-6], me.rest[-6:]
    steps = len(tiles)

    def load(j, act):
        for r in range(n_dp):
            act(me.loads(j, r, weight, j % 2, in_sem))

    def store(j):
        return pltpu.make_async_copy(total.at[j % 2], sums_refs[j], out_sem.at[j % 2])

    me.each_column(kept, kept_sem, lambda copy: copy.start())
    load(0, start)
    me.each_column(kept, kept_sem, lambda copy: copy.wait())

    @pl.loop(0, steps)
    def _(step):
        slot = lax.rem(step, 2)
        for j in range(steps):

            @pl.when(step == j)
            def _():
                if j + 1 < steps:
                    load(j + 1, start)
                load(j, wait)
                if j >= 2:
                    store(j - 2).wait()

        total[slot] = me.product(kept, weight, slot)
        for j in range(steps):
            pl.when(step == j)(lambda j=j: store(j).start())

    for j in range(max(steps - 2, 0), steps):
        store(j).wait()


def base_kernel(n_dp, tiles, n_chunks, kept_rows, n_held, count, scalars_ref, *refs):
    me = Tiles(n_dp, tiles, n_chunks, kept_rows, scalars_ref, refs)
    held_refs, (coef_ref, block_ref) = me.rest[:n_held], me.rest[n_held : n_held + 2]
    out_ref, token_ref, kept, weight, factor, result, total = me.rest[-12:-5]
    kept_sem, in_sem, factor_sem, out_sem, held_sem = me.rest[-5:]
    _, tile, _ = weight.shape
    height = coef_ref.shape[1]
    steps = len(tiles)
    live = steps + n_dp + len(kept_rows)
    token_ref[...] = jnp.zeros_like(token_ref)

    def load(j, act):
        slot = j % 2
        if j >= n_held:
            for r in range(n_dp):
                act(me.loads(j, r, weight, slot, in_sem))
        if j < n_held:
            act([pltpu.make_async_copy(held_refs[j], total.at[slot], held_sem.at[slot])])
        factors(j, act)

    def factors(j, act):
        slot = j % 2
        act(
            [
                pltpu.make_async_copy(
                    block_ref.at[:, :, me.span(j, tile)], factor.at[slot], factor_sem.at[slot]
                )
            ]
        )

    def store(j):
        return pltpu.make_async_copy(
            result.at[j % 2], out_ref.at[:, me.span(j, tile)], out_sem.at[j % 2]
        )

    def finish(slot, sums):
        for b in range(count):
            extra = jnp.dot(coef_ref[b], factor[slot, b], preferred_element_type=f32)
            here = sums[b * height : (b + 1) * height] + extra
            valid = lax.broadcasted_iota(i32, here.shape, 0) < scalars_ref[live + b]
            result[slot, b * height : (b + 1) * height, :] = jnp.where(valid, here, 0.0).astype(
                bf16
            )

    load(0, start)
    if n_held < steps:
        me.each_column(kept, kept_sem, lambda copy: copy.start())
    if steps > 1:
        load(1, start)
    first = 0
    if not n_held and me.kept_refs[0].shape[1] == me.deep:
        first, sums = 1, None
        for r in range(n_dp):
            for k in range(len(kept_rows)):
                pl.when(me.at[k] == scalars_ref[steps + r])(
                    lambda k=k: me.columns(k, kept, kept_sem).wait()
                )
            wait(me.loads(0, r, weight, 0, in_sem))
            part = me.part(r, kept, weight, 0)
            sums = part if sums is None else sums + part
        factors(0, wait)
        finish(0, sums)
        store(0).start()
    elif not n_held:
        me.each_column(kept, kept_sem, lambda copy: copy.wait())

    @pl.loop(first, steps)
    def _(step):
        slot = lax.rem(step, 2)
        for j in range(first, steps):

            @pl.when(step == j)
            def _():
                if 1 < j + 1 < steps:
                    load(j + 1, start)
                if 0 < j == n_held:
                    me.each_column(kept, kept_sem, lambda copy: copy.wait())
                load(j, wait)
                if j >= 2:
                    store(j - 2).wait()

        if n_held:
            pl.when(step < n_held)(lambda: finish(slot, total[slot]))
        if n_held < steps:
            pl.when(step >= n_held)(lambda: finish(slot, me.product(kept, weight, slot)))

        for j in range(steps):
            pl.when(step == j)(lambda j=j: store(j).start())

    for j in range(max(steps - 2, 0), steps):
        store(j).wait()


def tile_scratch(rows, tile, depth, n_kept, n_dp, tiles):
    most = max(len(segments) for segments in tiles)
    return [
        pltpu.VMEM((rows, depth), bf16),
        pltpu.VMEM((2, tile, depth), bf16),
    ], [
        pltpu.SemaphoreType.DMA((n_kept,)),
        pltpu.SemaphoreType.DMA((2, n_dp, most)),
    ]


def tile_operands(kept, near, chunks):
    top = len(near)
    operands = [piece for piece, _ in kept] + [near[r] for r in range(top)]
    for piece in chunks:
        operands += [piece[r] for r in range(top, 2 * top)]
    return operands


def early_sums(places, scalars, kept, near, chunks, tiles, tile):
    rows = kept[0][0].shape[0]
    n_dp = 2 * len(near)
    depth = n_dp * near[0].shape[1]
    anywhere = pl.BlockSpec(memory_space=pl.ANY)
    operands = tile_operands(kept, near, chunks)
    buffers, semaphores = tile_scratch(rows, tile, depth, len(kept), n_dp, tiles)
    return pl.pallas_call(
        functools.partial(early_kernel, n_dp, tiles, len(chunks), [low for _, low in kept]),
        grid_spec=pltpu.PrefetchScalarGridSpec(
            num_scalar_prefetch=1,
            grid=(1,),
            in_specs=[anywhere] * len(operands),
            out_specs=[anywhere] * len(tiles),
            scratch_shapes=[
                *buffers,
                pltpu.VMEM((2, rows, tile), f32),
                *semaphores,
                pltpu.SemaphoreType.DMA((2,)),
            ],
        ),
        out_shape=[jax.ShapeDtypeStruct((rows, tile), f32)] * len(tiles),
        **params((1, 1)),
    )(jnp.concatenate([jnp.stack(places).astype(i32), scalars]), *operands)


def base(places, scalars, kept, near, chunks, tiles, tile, early, coef, block_a, held, token):
    rows = kept[0][0].shape[0]
    count, rank, ff = block_a.shape
    n_dp = 2 * len(near)
    depth = n_dp * near[0].shape[1]
    anywhere = pl.BlockSpec(memory_space=pl.ANY)
    operands = tile_operands(kept, near, chunks) + early
    in_specs = [anywhere] * len(operands)
    in_specs += [pl.BlockSpec(coef.shape, lambda i, s: (0, 0, 0)), anywhere]
    operands += [coef, block_a]
    aliases = {}
    if held is not None:
        in_specs += [anywhere, anywhere]
        operands += [token, held]
        aliases = {len(operands): 0}
    buffers, semaphores = tile_scratch(rows, tile, depth, len(kept), n_dp, tiles)
    return pl.pallas_call(
        functools.partial(
            base_kernel, n_dp, tiles, len(chunks), [low for _, low in kept], len(early), count
        ),
        grid_spec=pltpu.PrefetchScalarGridSpec(
            num_scalar_prefetch=1,
            grid=(1,),
            in_specs=in_specs,
            out_specs=[anywhere, pl.BlockSpec((8, 128), lambda i, s: (0, 0))],
            scratch_shapes=[
                *buffers,
                pltpu.VMEM((2, count, rank, tile), bf16),
                pltpu.VMEM((2, rows, tile), bf16),
                pltpu.VMEM((2, rows, tile), f32),
                *semaphores,
                pltpu.SemaphoreType.DMA((2,)),
                pltpu.SemaphoreType.DMA((2,)),
                pltpu.SemaphoreType.DMA((2,)),
            ],
        ),
        out_shape=[
            jax.ShapeDtypeStruct((rows, ff), bf16),
            jax.ShapeDtypeStruct((8, 128), f32),
        ],
        input_output_aliases=aliases,
        **params((1, 1)),
    )(jnp.concatenate([jnp.stack(places).astype(i32), scalars]), *operands)


def add_kernel(pieces, count, slots_ref, *refs):
    term_refs = refs[: 2 * pieces]
    a_ref, b_ref, terms, a, b, term_sem, a_sem, b_sem = refs[2 * pieces + 3 :]
    local, _, ff = a.shape
    both = terms.shape[2]
    cut = term_refs[0].shape[2]

    def load(k):
        lanes = (pl.ds(0, cut), pl.ds(cut, both - cut))
        return [
            pltpu.make_async_copy(
                term_refs[k // count * 2 + part].at[k % count],
                terms.at[k, :, lanes[part]],
                term_sem.at[k, part],
            )
            for part in range(2)
        ]

    def whole(slot):
        return [
            pltpu.make_async_copy(a.at[slot], a_ref.at[slot], a_sem.at[slot]),
            pltpu.make_async_copy(b.at[slot], b_ref.at[slot], b_sem.at[slot]),
        ]

    wanted = [slots_ref[k] for k in range(pieces * count)]
    owned = [(slot >= 0) & (slot < local) for slot in wanted]
    hit = []
    for j in range(local):
        any_here = wanted[0] == j
        for slot in wanted[1:]:
            any_here = any_here | (slot == j)
        hit.append(any_here)

    def clear(j):
        a[j] = jnp.zeros(a.shape[1:], f32)
        b[j] = jnp.zeros(b.shape[1:], f32)

    for k in range(pieces * count):
        pl.when(owned[k])(lambda k=k: start(load(k)))
    for j in range(local):
        pl.when(hit[j])(lambda j=j: clear(j))

    def add(k):
        wait(load(k))
        a[wanted[k]] += terms[k, :, :ff].astype(f32)
        b[wanted[k]] += terms[k, :, ff:].astype(f32)

    for k in range(pieces * count):
        pl.when(owned[k])(lambda k=k: add(k))
    for j in range(local):
        pl.when(hit[j])(lambda j=j: start(whole(j)))
    for j in range(local):
        pl.when(hit[j])(lambda j=j: wait(whole(j)))


def add_terms(slots, pieces, grad_a, grad_b, token):
    count, rank, _ = pieces[0].shape
    both = pieces[0].shape[2] + pieces[1].shape[2]
    anywhere = pl.BlockSpec(memory_space=pl.ANY)
    n = len(pieces) // 2
    local = grad_a.shape[0]
    return pl.pallas_call(
        functools.partial(add_kernel, n, count),
        grid_spec=pltpu.PrefetchScalarGridSpec(
            num_scalar_prefetch=1,
            grid=(1,),
            in_specs=[anywhere] * (2 * n + 3),
            out_specs=[anywhere] * 2,
            scratch_shapes=[
                pltpu.VMEM((n * count, rank, both), bf16),
                pltpu.VMEM(grad_a.shape, f32),
                pltpu.VMEM(grad_b.shape, f32),
                pltpu.SemaphoreType.DMA((n * count, 2)),
                pltpu.SemaphoreType.DMA((local,)),
                pltpu.SemaphoreType.DMA((local,)),
            ],
        ),
        out_shape=[
            jax.ShapeDtypeStruct(grad_a.shape, f32),
            jax.ShapeDtypeStruct(grad_b.shape, f32),
        ],
        input_output_aliases={2 * n + 2: 0, 2 * n + 3: 1},
        **params((1, 1)),
    )(slots, *pieces, token, grad_a, grad_b)


def on_device(
    n_groups,
    n_fsdp,
    n_dp,
    output_gradient,
    hidden,
    frozen_down_weight,
    adapter_first_factors,
    adapter_second_factors,
    island_live_rows,
    island_adapter_ids,
    owner_slot_adapters,
):
    rows, ff = hidden.shape
    d = output_gradient.shape[1]
    count = island_live_rows.shape[0]
    local = adapter_first_factors.shape[0]
    n_slots = owner_slot_adapters.shape[0]
    top = n_dp // 2
    me = lax.axis_index("dp")
    group = lax.axis_index("groups")

    def swap(value, bit, axis="dp", size=n_dp):
        return lax.ppermute(value, axis, [(i, i ^ bit) for i in range(size)])

    def spread(held):
        held = dict(held)
        bit = top // 2
        while bit:
            for r in list(held):
                held[r ^ bit] = swap(held[r], bit)
            bit //= 2
        return held

    match = island_adapter_ids[:, None] == owner_slot_adapters[None, :]
    slots = jnp.sum(jnp.where(match, jnp.arange(n_slots, dtype=i32)[None, :], 0), axis=1)
    far_slots = swap(slots, top)

    place = lax.axis_index("fsdp")
    line = n_fsdp <= 4
    height = rows // count
    pieces_of_kept, at = [(output_gradient, 0)], [None]

    def hop(*after, low=0, high=None):
        step = len(at) // 2
        if not line or step + 1 >= n_fsdp:
            return []
        if low == 0:
            ends[:] = next_ends or [output_gradient] * 2
            next_ends.clear()
        right = [(i, i + 1) for i in range(n_fsdp - 1)]
        left = [(i + 1, i) for i in range(n_fsdp - 1)]
        sent = []
        for piece, pairs, place_of in zip(ends, (right, left), (place - step - 1, place + step + 1)):
            piece = behind(piece[low:high], *after)
            sent.append(lax.ppermute(piece, "fsdp", pairs))
            pieces_of_kept.append((sent[-1], low))
            where.append(jnp.where(place_of < n_fsdp, place_of, -1))
        if high is None:
            at.extend([None, None])
            next_ends.extend(sent)
        return sent

    ends, next_ends, where = [], [], [place]
    first_hop = hop()

    share = ff // n_groups
    if share % 2048 == 0:
        unit, tile = share // 8, share // 4
        sizes = [2 * unit] * 4
    else:
        tile = share
        sizes = [share]
    parts = [(sum(sizes[:j]), size) for j, size in enumerate(sizes)]

    crossed = []
    turned = []

    def flat(*pieces):
        return [v for piece in pieces for v in piece.values()]

    def cross(*after):
        j = len(crossed)
        if j < len(parts):
            first_row, size = parts[j]
            piece = lax.dynamic_slice_in_dim(
                frozen_down_weight, group * share + first_row, size, axis=0
            )
            crossed.append({top: swap(behind(piece, *after), top)})

    def turn(*after):
        j = len(turned)
        if j < len(parts):
            piece = behind(crossed[j][top], *after)
            turned.append([])
            for shift in range(1, n_groups):
                ring = [(i, (i + shift) % n_groups) for i in range(n_groups)]
                turned[j].append({top: lax.ppermute(piece, "groups", ring)})

    def fill(chunks, *after):
        for piece in chunks:
            piece.update(spread({top: behind(piece[top], *after)}))

    cross(far_slots)

    first = jnp.swapaxes(adapter_first_factors, 1, 2)
    a_near = spread({0: first})
    b_near = spread({0: adapter_second_factors})
    near = sorted(a_near)
    a_near = [a_near[r] for r in near]
    b_near = [b_near[r] for r in near]
    def places(wanted):
        owner = wanted // local
        index = jnp.concatenate([wanted % local] * len(near))
        return index, jnp.where((owner ^ me) < top, owner ^ me, len(near))

    picked = pick(*places(far_slots), a_near, b_near)
    both_slots = spread({0: behind(jnp.concatenate([slots, far_slots]), picked)})
    past = [picked, *first_hop, *flat(both_slots, *crossed)]
    far = swap(behind(picked, *past[1:]), top)
    whole = spread({0: behind(frozen_down_weight, *past)})
    turn(*past)
    past = [far, *hop(*past), *flat(*turned[0])]

    ready = behind(slots, *flat(whole, both_slots), *past)
    part, block_a, grad_a, grad_b = project(
        *places(ready), a_near, b_near, far, hidden, output_gradient
    )
    third_hop = hop(*past)
    cross(*past)
    cross(*past)
    sums = [part]
    bit = 1
    while bit < n_fsdp:
        sums.append(swap(sums[-1], bit, "fsdp", n_fsdp))
        if 2 * bit < n_fsdp:
            sums.append(sums[-2] + sums[-1])
        bit *= 2
    total, other = sums[-2:]
    turn(part)
    past = [sums[2], *flat(*crossed[:3], *sum(turned[:2], [])), *third_hop]
    cross(*past)
    turn(*past)
    fill(crossed[:2], *past)

    order = [me ^ r for r in range(n_dp)]
    order = jnp.stack(order).astype(i32)

    def collect(named):
        chunks, tiles, places_of = [], [], []
        for shift, t in named:
            first_row = lax.rem(group + n_groups - shift, n_groups) * share
            places_of.append(first_row // tile + t)
            tiles.append([])
            for j, (first, size) in enumerate(parts):
                low, high = max(first, t * tile), min(first + size, (t + 1) * tile)
                if low < high:
                    if (shift, j) not in chunks:
                        chunks.append((shift, j))
                    tiles[-1].append((chunks.index((shift, j)), low - first, high - low))
        return places_of, [turned[j][shift - 1] if shift else crossed[j] for shift, j in chunks], tiles

    sums_of = {}

    def begin(*named):
        at = jnp.stack(where).astype(i32)
        places_of, chunks, tiles = collect(named)
        got = early_sums(
            places_of, jnp.concatenate([order, at]), pieces_of_kept, whole, chunks, tiles, tile
        )
        sums_of.update(zip(named, got))
        return got

    others = range(1, n_groups)
    ahead = line and share > tile
    begun = begin((0, 0), (0, 1)) if ahead else []
    live = behind(island_live_rows, *begun)
    low_terms, high_terms, coef = block_terms(live, total, other, hidden, output_gradient)
    past = [coef, *flat(*crossed, *sum(turned, []))]
    far_high = swap(high_terms, top)
    far_low = swap(low_terms, top)
    turn(*past)
    fill(crossed[2:], *past)
    for pieces in turned[:3]:
        fill(pieces, *past)
    if line:
        at = jnp.stack(where).astype(i32)
    else:
        pieces_of_kept = [(lax.all_gather(output_gradient, "fsdp", axis=1, tiled=True), 0)]
        at = jnp.zeros((1,), i32)

    relative = [both_slots[r][:count] for r in near] + [both_slots[r][count:] for r in near]
    relative = jnp.concatenate(relative) - me * local

    scalars = jnp.concatenate([order, at, island_live_rows])
    grad_hidden = token = None

    def multiply(*named):
        nonlocal grad_hidden, token
        named = sorted(named, key=lambda name: name not in sums_of)
        places_of, chunks, tiles = collect(named)
        grad_hidden, token = base(
            places_of, scalars, pieces_of_kept, whole, chunks, tiles, tile,
            [sums_of[name] for name in named if name in sums_of], coef, block_a, grad_hidden, token,
        )

    if share > tile:
        multiply(*[(0, t) for t in range(3)], *[(g, t) for g in others for t in range(2)])
        past = [token, far_high]
        for pieces in turned[3:]:
            fill(pieces, *past)
        multiply((0, 3), *[(g, t) for g in others for t in range(2, 4)])
    else:
        multiply(*[(g, 0) for g in range(n_groups)])

    near_low = spread({0: behind(low_terms, *past)})
    near_high = spread({0: behind(high_terms, *past)})
    all_high = spread({top: behind(far_high, *past)})
    all_low = spread({top: behind(far_low, token)})
    terms = [p for r in near for p in (near_low[r], near_high[r])]
    terms += [p for r in near for p in (all_low[r + top], all_high[r + top])]
    grad_a, grad_b = add_terms(relative, terms, grad_a, grad_b, token)
    return grad_hidden, jnp.swapaxes(grad_a, 1, 2), grad_b


def solution(mesh):
    placed = (
        P(("groups", "dp"), "fsdp"),
        P(("groups", "dp"), "fsdp"),
        P("fsdp", "dp"),
        P(("groups", "dp"), "fsdp", None),
        P(("groups", "dp"), None, "fsdp"),
        P(("groups", "dp")),
        P(("groups", "dp")),
        P("groups"),
    )
    sizes = [mesh.shape[name] for name in ("groups", "fsdp", "dp")]
    return jax.shard_map(
        functools.partial(on_device, *sizes),
        mesh=mesh,
        in_specs=placed,
        out_specs=(
            P(("groups", "dp"), "fsdp"),
            P(("groups", "dp"), "fsdp", None),
            P(("groups", "dp"), None, "fsdp"),
        ),
        check_vma=False,
    )
```
